32 devices in a mesh: grp: 2 (over y), seq: 4 (over z), head: 2 (over x), sub: 2 (over core).
Axes of the slice: x: 2, y: 2, z: 4, core: 2. Of those that a mesh axis runs over, the one named last changes fastest.
Arguments:
- hidden: bfloat16 [2048, 4096], P(('grp', 'seq'), ('head', 'sub')), parts along dimension 0, may hold values from -6 to 6
- inner_values: bfloat16 [2048, 8192], P(('grp', 'seq'), ('head', 'sub')), parts along dimension 0, may hold values from -0.29882812 to 0.29882812
- log_decay: float32 [2048, 128], P(('grp', 'seq'), ('head', 'sub')), parts along dimension 0, may hold values from -2 to 0
- skip_gain: float32 [128], P(('head', 'sub')), may hold values from 0.1 to 10
- cotangent: bfloat16 [2048, 8192], P(('grp', 'seq'), ('head', 'sub')), parts along dimension 0, may hold values from -6 to 6
- master: float32 [4096, 2048], P('seq', ('head', 'sub')), may hold values from -0.4 to 0.4
- mask_now: int32 [1024, 2048], P('seq', ('head', 'sub')), may hold values from 0 to 5
- mask_next: int32 [1024, 2048], P('seq', ('head', 'sub')), may hold values from 0 to 5
Outputs:
- ssd_output: bfloat16 [2048, 8192], P(('grp', 'seq'), ('head', 'sub')), parts along dimension 0
- new_weight: float32 [8192, 2048], P(('grp', 'seq'), ('head', 'sub')), parts along dimension 0
- sparse_weight: bfloat16 [8192, 2048], P(('grp', 'seq'), ('head', 'sub')), parts along dimension 0
The draws below stay inside these ranges and needn't reach their ends.
There are 2 independent parts, one for each index of `grp`. The reference program is written for one: setup_inputs(seed, part) draws one part's arguments, and reference() takes and returns one part's arrays. A program takes and returns all parts, laid end to end along the dimension named above; an argument that names none is the same for every part. Nothing has to cross between parts.
All inputs are finite; a program needn't handle non-finite values.
Results may differ from the reference program's by a relative error of at most 0.033.
Values may be sent and summed in bfloat16 or wider, within the bound.
No kernel may reach another device: no remote copies, remote signals or barrier semaphores. Data moves between devices by JAX's collectives and lax.ppermute only.
A program may use at most 128 MiB of HBM per device.

```python
import math
from functools import partial
import jax
import jax.numpy as jnp
import numpy as np
from jax import lax

D = 4096
HEADS = 128
HEAD_DIM = 64
STATE = 128
GROUPS = 8
SPAN = 256
TOK_DEV = 256
SEQUENCE_LENGTH = 1024


def draw_log_decay(key, part):
    key_rows = jax.random.split(jax.random.fold_in(key, 11), 10)
    fast_share = 0.5
    fast_heads = jax.random.bernoulli(key_rows[0], fast_share, (HEADS,))
    slow_rate = jnp.exp(jax.random.uniform(key_rows[1], (HEADS,), jnp.float32, math.log(0.02), math.log(0.2))) / SEQUENCE_LENGTH
    fast_rate = jax.random.uniform(key_rows[2], (HEADS,), jnp.float32, 2.3 / 50.0, 2.3 / 30.0)
    head_decay_rate = jnp.where(fast_heads, fast_rate, slow_rate)
    block_multiplier = jnp.exp(jax.random.uniform(key_rows[3], (SEQUENCE_LENGTH // TOK_DEV, 1), jnp.float32, -math.log(2.0), math.log(2.0)))
    block_multiplier = jnp.repeat(block_multiplier, TOK_DEV, axis=0)
    jitter_amplitude = jnp.exp(jax.random.uniform(key_rows[4], (SEQUENCE_LENGTH, HEADS), jnp.float32, math.log(0.5), math.log(1.5)))
    window_length = min(4 * TOK_DEV, SEQUENCE_LENGTH)
    windows = SEQUENCE_LENGTH // window_length
    window_blocks = window_length // SPAN
    block_pick = jax.random.randint(key_rows[5], (windows,), 0, window_blocks)
    offset_pick = jax.random.randint(key_rows[6], (windows,), 0, SPAN - 1)
    window_index = jnp.arange(windows, dtype=jnp.int32)
    first_position = window_index * window_length + block_pick * SPAN + offset_pick
    paired = window_index % 2 == 0
    paired_first = jax.random.uniform(key_rows[7], (windows,), jnp.float32, 1.155, 1.25)
    single_height = jax.random.uniform(key_rows[8], (windows,), jnp.float32, 1.3, 1.7)
    paired_second = jax.random.uniform(key_rows[9], (windows,), jnp.float32, 1.155, 1.25)
    first_height = jnp.where(paired, paired_first, single_height)
    second_height = jnp.where(paired, paired_second, 0.0)
    target_positions = jnp.arange(SEQUENCE_LENGTH, dtype=jnp.int32)
    first_hits = jnp.where(target_positions[:, None] == first_position[None, :], first_height[None, :], 0.0)
    second_hits = jnp.where(target_positions[:, None] == first_position[None, :] + 1, second_height[None, :], 0.0)
    spike_events = jnp.sum(first_hits + second_hits, axis=1)
    return -(head_decay_rate[None, :] * block_multiplier * jitter_amplitude) - spike_events[:, None]


def plant(values, rng, low, largest):
    shape = values.shape
    place = [jax.random.randint(jax.random.fold_in(rng, axis), (), 0, shape[axis]) for axis in range(len(shape))]
    values = values.at[tuple(place)].set(low)
    longest = shape.index(max(shape))
    place[longest] = (place[longest] + 1) % shape[longest]
    return values.at[tuple(place)].set(largest)


def raised(values, stream_key, source, target, blocks, factor):
    owner, partner = [(jnp.arange(values.shape[axis_at]) // (values.shape[axis_at] // blocks)).reshape([-1 if axis == axis_at else 1 for axis in range(values.ndim)]) for axis_at in (source, target)]
    chosen = jax.random.permutation(stream_key, blocks)[partner]
    strong = (owner == chosen) | (owner == (partner + blocks // 2) % blocks)
    return jnp.where(strong, factor * values, values)


def steps_of(stream_key, dims, cuts, least, top_value):
    level = 1.0
    for axis_at, parts in cuts:
        steps = jax.random.uniform(jax.random.fold_in(jax.random.fold_in(stream_key, 6), axis_at), (parts,), jnp.float32, least / len(cuts), top_value / len(cuts))
        level = level * jnp.repeat(jnp.exp(steps), dims[axis_at] // parts).reshape((-1,) + (1,) * (len(dims) - 1 - axis_at))
    return level


def noise(stream_key, shape, scale, most, cuts=(), held_as=jnp.bfloat16):
    level = steps_of(stream_key, shape, cuts, -0.22, 0.18) if cuts else 1.0
    values = jax.random.normal(stream_key, shape, jnp.float32) * scale * level
    return jnp.minimum(jnp.maximum(values, -most), most).astype(held_as)


def bell_draw_with(key, dims, scale, reach, cuts, heavy, kind=jnp.bfloat16):
    result = scale * jax.random.normal(key, dims, jnp.float32)
    if cuts:
        result = result * steps_of(key, dims, cuts, -0.22, 0.18)
    return jnp.clip(raised(result, jax.random.fold_in(key, 3), *heavy), -reach, reach).astype(kind)


def setup_inputs(seed: int = 0, part: int = 0) -> dict:
    keys = jax.random.split(jax.random.key(seed), 9)
    part_keys = jax.random.split(jax.random.fold_in(keys[8], part), 9)
    hidden = bell_draw_with(part_keys[0], (SEQUENCE_LENGTH, D), 1.0, 6.0, ((0, 4), (1, 4)), (0, 1, 4, 2.0))
    inner_values = noise(part_keys[1], (SEQUENCE_LENGTH, HEADS * HEAD_DIM), 0.05, 0.29882812, ((0, 4), (1, 4)))
    log_decay = draw_log_decay(jax.random.fold_in(jax.random.fold_in(keys[8], part), 71), part)
    skip_gain = jnp.clip(jnp.exp(math.log(10.0) - 4.6051702 * jax.random.uniform(keys[3], (HEADS,), jnp.float32) ** steps_of(keys[3], (HEADS,), ((0, 4),), -0.2, 0.2)), 0.1, 10.0)
    cotangent = noise(part_keys[4], (SEQUENCE_LENGTH, HEADS * HEAD_DIM), 1.0, 6.0, ((0, 4), (1, 4)))
    master = noise(keys[5], (D, 2 * GROUPS * STATE), 0.1, 0.4, ((0, 4), (1, 4)), jnp.float32)
    mask_now = plant(jax.random.randint(keys[6], (D // 4, 2 * GROUPS * STATE), 0, 6), jax.random.fold_in(keys[6], 1), 0, 5).astype(jnp.int32)
    mask_next = plant(jax.random.randint(keys[7], (D // 4, 2 * GROUPS * STATE), 0, 6), jax.random.fold_in(keys[7], 1), 0, 5).astype(jnp.int32)
    return dict(hidden=hidden, inner_values=inner_values, log_decay=log_decay, skip_gain=skip_gain, cotangent=cotangent, master=master, mask_now=mask_now, mask_next=mask_next)


PAIR_TABLE = np.array([[1, 1, 0, 0], [1, 0, 1, 0], [1, 0, 0, 1], [0, 1, 1, 0], [0, 1, 0, 1], [0, 0, 1, 1]], np.float32)
LEARN_RATE = 0.05
WEIGHT_DECAY = 10.0

def expand_mask(pattern_ids):
    group_rows, columns = pattern_ids.shape
    patterns = jnp.arange(6, dtype=jnp.int32)
    chosen = (pattern_ids[:, None, :] == patterns[None, :, None]).astype(jnp.float32)
    kept_mask = jnp.einsum('rpc,pk->rkc', chosen, jnp.asarray(PAIR_TABLE, jnp.float32))
    return kept_mask.reshape(group_rows * 4, columns)

def round_low(values):
    return lax.optimization_barrier(values.astype(jnp.bfloat16)).astype(jnp.float32)

def block_terms(log_block):
    cumulative = jnp.cumsum(log_block, axis=0)
    block_end = cumulative[-1]
    target_positions = jnp.arange(log_block.shape[0])
    causal = target_positions[:, None] >= target_positions[None, :]
    per_head = jnp.moveaxis(cumulative, 0, -1)
    spread = per_head[..., :, None] - per_head[..., None, :]
    decays = jnp.where(causal, jnp.exp(jnp.where(causal, spread, 0.0)), 0.0)
    return (cumulative, block_end, decays)

def forward_block(skip_group, running_state, inputs):
    value_block, log_block, write_block, read_block = inputs
    cumulative, block_end, decays = block_terms(log_block)
    scores = jnp.dot(read_block, write_block.T, preferred_element_type=jnp.float32)
    mixing = round_low(scores[None] * decays)
    value_wide = value_block.astype(jnp.float32)
    local_mix = jnp.einsum('hts,shp->thp', mixing, value_wide)
    write_low = round_low(write_block.astype(jnp.float32)[:, None, :] * jnp.exp(block_end[None, :] - cumulative)[:, :, None])
    read_low = round_low(read_block.astype(jnp.float32)[:, None, :] * jnp.exp(cumulative)[:, :, None])
    start_low = round_low(running_state)
    carried_in = jnp.einsum('thn,hnp->thp', read_low, start_low)
    output = (local_mix + carried_in + skip_group[None, :, None] * value_wide).astype(jnp.bfloat16)
    block_state = jnp.einsum('shn,shp->hnp', write_low, value_wide)
    new_state = jnp.exp(block_end)[:, None, None] * running_state + block_state
    return (new_state, (output, start_low.astype(jnp.bfloat16)))

def backward_block(adjoint, inputs):
    value_block, log_block, write_block, read_block, cotan_block, start_low = inputs
    cumulative, block_end, decays = block_terms(log_block)
    value_wide = value_block.astype(jnp.float32)
    cotan_wide = cotan_block.astype(jnp.float32)
    write_wide = write_block.astype(jnp.float32)
    read_wide = read_block.astype(jnp.float32)
    products = jnp.einsum('thp,shp->hts', cotan_wide, value_wide)
    back_mix = round_low(products * decays)
    grad_read = jnp.einsum('hts,sn->tn', back_mix, write_wide)
    grad_write = jnp.einsum('hts,tn->sn', back_mix, read_wide)
    adjoint_low = round_low(adjoint)
    grad_write = grad_write + lax.optimization_barrier(jnp.sum(jnp.einsum('shp,hnp->shn', value_wide, adjoint_low) * jnp.exp(block_end[None, :] - cumulative)[:, :, None], axis=1))
    grad_read = grad_read + lax.optimization_barrier(jnp.sum(jnp.einsum('thp,hnp->thn', cotan_wide, start_low.astype(jnp.float32)) * jnp.exp(cumulative)[:, :, None], axis=1))
    read_low = round_low(read_wide[:, None, :] * jnp.exp(cumulative)[:, :, None])
    new_adjoint = jnp.einsum('thn,thp->hnp', read_low, cotan_wide) + jnp.exp(block_end)[:, None, None] * adjoint
    return (new_adjoint, jnp.concatenate([grad_write, grad_read], axis=1).astype(jnp.bfloat16))

def group_pass(inputs):
    value_group, logs_group, cotan_group, proj_group, skip_group = inputs
    blocks = SEQUENCE_LENGTH // SPAN
    heads_group = HEADS // GROUPS
    value_blocks = value_group.reshape(blocks, SPAN, heads_group, HEAD_DIM)
    cotan_blocks = cotan_group.reshape(blocks, SPAN, heads_group, HEAD_DIM)
    log_blocks = logs_group.reshape(blocks, SPAN, heads_group)
    write_blocks = proj_group[:, :STATE].reshape(blocks, SPAN, STATE)
    read_blocks = proj_group[:, STATE:].reshape(blocks, SPAN, STATE)
    zero_state = jnp.zeros((heads_group, STATE, HEAD_DIM), jnp.float32)
    _, (outputs, starts) = lax.scan(partial(forward_block, skip_group), zero_state, (value_blocks, log_blocks, write_blocks, read_blocks))
    _, grads = lax.scan(backward_block, zero_state, (value_blocks, log_blocks, write_blocks, read_blocks, cotan_blocks, starts), reverse=True)
    return (outputs.reshape(SEQUENCE_LENGTH, heads_group, HEAD_DIM), grads.reshape(SEQUENCE_LENGTH, 2 * STATE))

def reference(hidden, inner_values, log_decay, skip_gain, cotangent, master, mask_now, mask_next):
    weight_scale = 2.0 / math.sqrt(D)
    keep_now = expand_mask(mask_now)
    effective = (master * keep_now * weight_scale).astype(jnp.bfloat16)
    projected = jnp.dot(hidden, effective, preferred_element_type=jnp.float32).astype(jnp.bfloat16)
    heads_group = HEADS // GROUPS
    value_groups = jnp.moveaxis(inner_values.reshape(SEQUENCE_LENGTH, GROUPS, heads_group, HEAD_DIM), 1, 0)
    cotan_groups = jnp.moveaxis(cotangent.reshape(SEQUENCE_LENGTH, GROUPS, heads_group, HEAD_DIM), 1, 0)
    log_groups = jnp.moveaxis(log_decay.reshape(SEQUENCE_LENGTH, GROUPS, heads_group), 1, 0)
    proj_groups = jnp.moveaxis(projected.reshape(SEQUENCE_LENGTH, GROUPS, 2 * STATE), 1, 0)
    skip_groups = skip_gain.reshape(GROUPS, heads_group)
    outputs, grads = lax.map(group_pass, (value_groups, log_groups, cotan_groups, proj_groups, skip_groups))
    ssd_output = jnp.moveaxis(outputs, 0, 1).reshape(SEQUENCE_LENGTH, HEADS * HEAD_DIM)
    grad_proj = jnp.moveaxis(grads, 0, 1).reshape(SEQUENCE_LENGTH, GROUPS * 2 * STATE)
    hidden_blocks = hidden.reshape(SEQUENCE_LENGTH // TOK_DEV, TOK_DEV, D)
    grad_blocks = grad_proj.reshape(SEQUENCE_LENGTH // TOK_DEV, TOK_DEV, GROUPS * 2 * STATE)

    def add_block(running, inputs):
        rows_in, grads_in = inputs
        term = jnp.dot(rows_in.T, grads_in, preferred_element_type=jnp.float32) * weight_scale
        return (running + round_low(term), None)
    gradient, _ = lax.scan(add_block, jnp.zeros(master.shape, jnp.float32), (hidden_blocks, grad_blocks))
    new_weight = master - LEARN_RATE * (gradient + WEIGHT_DECAY * (1.0 - keep_now) * master)
    sparse_weight = (new_weight * expand_mask(mask_next)).astype(jnp.bfloat16)
    return (ssd_output, new_weight, sparse_weight)
```

```python
import functools
import math

import jax
import jax.numpy as jnp
from jax import lax
from jax.experimental import pallas as pl
from jax.experimental.pallas import tpu as pltpu
from jax.sharding import PartitionSpec as P

D = 4096
STATE = 128
SPAN = 256
LEARN_RATE = 0.05
WEIGHT_DECAY = 10.0
WEIGHT_SCALE = 2.0 / math.sqrt(D)
KEEP_BITS = (0b000111, 0b011001, 0b101010, 0b110100)
OUT_OF_SIGHT = -1e30
VMEM_BYTES = 40 * 1024 * 1024

F32 = jnp.float32
BF16 = jnp.bfloat16
NT = (((1,), (1,)), ((), ()))


def call(kernel, out_shape, flops, moved, exps=0, **more):
    return pl.pallas_call(
        kernel,
        out_shape=out_shape,
        compiler_params=pltpu.CompilerParams(vmem_limit_bytes=VMEM_BYTES),
        cost_estimate=pl.CostEstimate(flops=flops, bytes_accessed=moved, transcendentals=exps),
        **more,
    )


def dot(a, b):
    return jnp.dot(a, b, preferred_element_type=F32)


def dot_nt(a, b):
    return lax.dot_general(a, b, NT, preferred_element_type=F32)


def turned(a):
    return a.astype(F32).T.astype(BF16)


def expanded(codes, rows):
    spread = (
        lax.broadcasted_iota(jnp.int32, (rows, rows // 4), 0) // 4
        == lax.broadcasted_iota(jnp.int32, (rows, rows // 4), 1)
    ).astype(F32)
    code = dot(spread.astype(BF16), codes.astype(F32).astype(BF16)).astype(jnp.int32)
    place = lax.broadcasted_iota(jnp.int32, (rows, 1), 0) % 4
    bits = jnp.where(
        place < 2,
        jnp.where(place == 0, KEEP_BITS[0], KEEP_BITS[1]),
        jnp.where(place == 2, KEEP_BITS[2], KEEP_BITS[3]),
    )
    return lax.shift_right_logical(jnp.broadcast_to(bits, code.shape), code) & 1


def weights_kernel(master_ref, now_ref, next_ref, effective_ref, decayed_ref, keep_ref):
    rows = master_ref.shape[0]
    master = master_ref[...]
    kept = expanded(now_ref[...], rows) == 1
    effective_ref[...] = jnp.where(kept, master * WEIGHT_SCALE, 0.0).astype(BF16)
    decayed_ref[...] = jnp.where(kept, master, master * (1.0 - LEARN_RATE * WEIGHT_DECAY))
    keep_ref[...] = expanded(next_ref[...], rows).astype(F32).astype(BF16)


def weights(master, mask_now, mask_next):
    rows, columns = master.shape
    block = min(rows, 256)
    full = pl.BlockSpec((block, columns), lambda i: (i, 0))
    quarter = pl.BlockSpec((block // 4, columns), lambda i: (i, 0))
    return call(
        weights_kernel,
        (
            jax.ShapeDtypeStruct((rows, columns), BF16),
            jax.ShapeDtypeStruct((rows, columns), F32),
            jax.ShapeDtypeStruct((rows, columns), BF16),
        ),
        flops=rows * columns * 150,
        moved=rows * columns * 14,
        grid=(rows // block,),
        in_specs=[full, quarter, quarter],
        out_specs=(full, full, full),
    )(master, mask_now, mask_next)


def lanes_of(left, right, wide):
    lane = lax.broadcasted_iota(jnp.int32, (left.shape[0], wide), 1)
    return jnp.where(lane < wide // 2, left, right)


def decays_of(col, row):
    half = SPAN // 2
    causal = lax.broadcasted_iota(jnp.int32, (half, half), 0) >= lax.broadcasted_iota(
        jnp.int32, (half, half), 1
    )
    top = jnp.exp(jnp.where(causal, col[:half] - row[:, :half], OUT_OF_SIGHT))
    low = jnp.exp(col[half:] - row[:, :half])
    end = jnp.exp(jnp.where(causal, col[half:] - row[:, half:], OUT_OF_SIGHT))
    return top, low, end


def before_kernel(
    x_ref, dy_ref, log_ref, logt_ref,
    xd_ref, yd_ref, mix_ref, mixt_ref, cum_ref, cumt_ref, end_ref,
):
    heads = log_ref.shape[2]
    half = SPAN // 2
    wide = x_ref.shape[1] // heads * 2
    row = lax.broadcasted_iota(jnp.int32, (SPAN, SPAN), 0)
    col = lax.broadcasted_iota(jnp.int32, (SPAN, SPAN), 1)
    cum = jnp.dot(
        (row >= col).astype(F32), log_ref[0],
        precision=lax.Precision.HIGHEST, preferred_element_type=F32,
    )
    cumt = jnp.dot(
        logt_ref[0], (row <= col).astype(F32),
        precision=lax.Precision.HIGHEST, preferred_element_type=F32,
    )
    cum_ref[0] = cum
    cumt_ref[0] = cumt
    end = cum[SPAN - 1 :, :]
    from_start = jnp.exp(cum)
    to_end = jnp.exp(end - cum)
    whole = jnp.exp(end)
    mix = [jnp.zeros((half, half), F32) for _ in range(3)]
    lane = lax.broadcasted_iota(jnp.int32, (SPAN, wide), 1)
    for pair in range(heads // 2):
        a, b = 2 * pair, 2 * pair + 1
        cut = slice(pair * wide, (pair + 1) * wide)
        x = x_ref[:, cut]
        dy = dy_ref[:, cut]
        wide_dy = dy.astype(F32)
        xd_ref[:, cut] = (
            x.astype(F32) * lanes_of(to_end[:, a : a + 1], to_end[:, b : b + 1], wide)
        ).astype(BF16)
        yd_ref[:, cut] = (
            wide_dy * lanes_of(from_start[:, a : a + 1], from_start[:, b : b + 1], wide)
        ).astype(BF16)
        end_ref[0, :, cut] = lanes_of(whole[:, a : a + 1], whole[:, b : b + 1], wide)
        for head, mine in ((a, lane < wide // 2), (b, lane >= wide // 2)):
            one = jnp.where(mine, wide_dy, 0.0).astype(BF16)
            decays = decays_of(cum[:, head : head + 1], cumt[head : head + 1, :])
            mix[0] += dot_nt(one[:half], x[:half]) * decays[0]
            both = dot_nt(one[half:], x)
            mix[1] += both[:, :half] * decays[1]
            mix[2] += both[:, half:] * decays[2]
    nothing = jnp.zeros((half, half), BF16)
    top, low, end_mix = (m.astype(BF16) for m in mix)
    topt, lowt, end_mixt = (m.T.astype(BF16) for m in mix)
    mix_ref[0, :half, :half] = top
    mix_ref[0, :half, half:] = nothing
    mix_ref[0, half:, :half] = low
    mix_ref[0, half:, half:] = end_mix
    mixt_ref[0, :half, :half] = topt
    mixt_ref[0, :half, half:] = lowt
    mixt_ref[0, half:, :half] = nothing
    mixt_ref[0, half:, half:] = end_mixt


def wide_spec(width):
    return pl.BlockSpec((SPAN, width), lambda g: (0, g))


def lead_spec(*shape):
    return pl.BlockSpec((1, *shape), lambda g: (g, *(0 for _ in shape)))


def before(values, cotan, logs, logs_t):
    groups, _, heads = logs.shape
    width = values.shape[1] // groups
    wide = wide_spec(width)
    return call(
        before_kernel,
        (
            jax.ShapeDtypeStruct(values.shape, BF16),
            jax.ShapeDtypeStruct(values.shape, BF16),
            jax.ShapeDtypeStruct((groups, SPAN, SPAN), BF16),
            jax.ShapeDtypeStruct((groups, SPAN, SPAN), BF16),
            jax.ShapeDtypeStruct((groups, SPAN, heads), F32),
            jax.ShapeDtypeStruct((groups, heads, SPAN), F32),
            jax.ShapeDtypeStruct((groups, 1, width), F32),
        ),
        flops=groups * heads * SPAN * SPAN * 260,
        moved=values.size * 8,
        exps=groups * heads * SPAN * SPAN,
        grid=(groups,),
        in_specs=[wide, wide, lead_spec(SPAN, heads), lead_spec(heads, SPAN)],
        out_specs=(
            wide, wide, lead_spec(SPAN, SPAN), lead_spec(SPAN, SPAN),
            lead_spec(SPAN, heads), lead_spec(heads, SPAN), lead_spec(1, width),
        ),
    )(values, cotan, logs, logs_t)


def partial_kernel(count, place_ref, *refs):
    pieces = refs[: -count - 1]
    weight_ref = refs[-count - 1]
    outs = refs[-count:]
    rows = pieces[0].shape[0]
    for number, piece in enumerate(pieces):
        term = dot(piece[...], weight_ref[...]).astype(BF16)
        block = place_ref[2 * number]
        start = pl.multiple_of(place_ref[2 * number + 1] * rows, rows)
        for target, out in enumerate(outs):

            @pl.when(block == target)
            def _(out=out, start=start, term=term):
                out[pl.ds(start, rows), :] = term


def partials(pieces, place, effective, count):
    columns = effective.shape[1]
    whole = pl.BlockSpec(memory_space=pltpu.VMEM)
    return call(
        functools.partial(partial_kernel, count),
        tuple(jax.ShapeDtypeStruct((SPAN, columns), BF16) for _ in range(count)),
        flops=2 * count * SPAN * effective.size,
        moved=count * SPAN * (effective.shape[0] + columns) * 2 + effective.size * 2,
        in_specs=[pl.BlockSpec(memory_space=pltpu.SMEM)] + [whole] * (len(pieces) + 1),
        out_specs=(whole,) * count,
    )(place, *pieces, effective)


def turn_kernel(place_ref, *refs):
    pieces, out_ref = refs[:-1], refs[-1]
    rows = pieces[0].shape[0]
    for number, piece in enumerate(pieces):
        at = place_ref[2 * number] * (SPAN // rows) + place_ref[2 * number + 1]
        out_ref[:, pl.ds(pl.multiple_of(at * rows, rows), rows)] = turned(piece[...])


def turn(pieces, place):
    whole = pl.BlockSpec(memory_space=pltpu.VMEM)
    tokens = sum(p.shape[0] for p in pieces)
    features = pieces[0].shape[1]
    return call(
        turn_kernel,
        jax.ShapeDtypeStruct((features, tokens), BF16),
        flops=tokens * features * 8,
        moved=tokens * features * 4,
        in_specs=[pl.BlockSpec(memory_space=pltpu.SMEM)] + [whole] * len(pieces),
        out_specs=whole,
    )(place, *pieces)


def states_kernel(*refs):
    (*terms, xd_ref, yd_ref, proj_ref, state_ref, adjoint_ref, state_low_ref, adjoint_low_ref) = refs
    total = terms[0][...].astype(F32)
    for term in terms[1:]:
        total += term[...].astype(F32)
    low = total.astype(BF16)
    proj_ref[...] = low
    write_t = turned(low[:, :STATE])
    read_t = turned(low[:, STATE:])
    state = dot(write_t, xd_ref[...])
    adjoint = dot(read_t, yd_ref[...])
    state_ref[0] = state
    adjoint_ref[0] = adjoint
    state_low_ref[0] = state.astype(BF16)
    adjoint_low_ref[0] = adjoint.astype(BF16)


def states(terms, xd, yd):
    columns = terms[0].shape[1]
    groups = columns // (2 * STATE)
    width = xd.shape[1] // groups
    pair, wide, lead = wide_spec(2 * STATE), wide_spec(width), lead_spec(STATE, width)
    shape = (groups, STATE, width)
    return call(
        states_kernel,
        (
            jax.ShapeDtypeStruct((SPAN, columns), BF16),
            jax.ShapeDtypeStruct(shape, F32),
            jax.ShapeDtypeStruct(shape, F32),
            jax.ShapeDtypeStruct(shape, BF16),
            jax.ShapeDtypeStruct(shape, BF16),
        ),
        flops=4 * SPAN * xd.shape[1] * STATE,
        moved=len(terms) * SPAN * columns * 2 + xd.size * 10,
        grid=(groups,),
        in_specs=[pair] * len(terms) + [wide, wide],
        out_specs=(pair, lead, lead, lead, lead),
    )(*terms, xd, yd)


def grads_kernel(proj_ref, xd_ref, yd_ref, mix_ref, mixt_ref, start_ref, adjoint_ref, out_ref):
    write = proj_ref[:, :STATE]
    read = proj_ref[:, STATE:]
    grad_write = dot(mixt_ref[0], read) + dot_nt(xd_ref[...], adjoint_ref[0])
    grad_read = dot(mix_ref[0], write) + dot_nt(yd_ref[...], start_ref[0])
    out_ref[:, :STATE] = grad_write.astype(BF16)
    out_ref[:, STATE:] = grad_read.astype(BF16)


def grads(proj, xd, yd, mix, mixt, start, adjoint):
    groups, _, width = start.shape
    pair, wide, lead = wide_spec(2 * STATE), wide_spec(width), lead_spec(STATE, width)
    square = lead_spec(SPAN, SPAN)
    return call(
        grads_kernel,
        jax.ShapeDtypeStruct(proj.shape, BF16),
        flops=4 * SPAN * xd.shape[1] * STATE,
        moved=xd.size * 8,
        grid=(groups,),
        in_specs=[pair, wide, wide, square, square, lead, lead],
        out_specs=pair,
    )(proj, xd, yd, mix, mixt, start, adjoint)


def output_kernel(proj_ref, x_ref, cum_ref, cumt_ref, start_ref, skip_ref, out_ref):
    heads = cum_ref.shape[2]
    half = SPAN // 2
    wide = x_ref.shape[1] // heads * 2
    write = proj_ref[:, :STATE]
    read = proj_ref[:, STATE:]
    cum = cum_ref[0]
    cumt = cumt_ref[0]
    from_start = jnp.exp(cum)
    scores = dot_nt(read, write)
    top, low, end = scores[:half, :half], scores[half:, :half], scores[half:, half:]
    lane = lax.broadcasted_iota(jnp.int32, (half, wide), 1)
    for pair in range(heads // 2):
        a, b = 2 * pair, 2 * pair + 1
        cut = slice(pair * wide, (pair + 1) * wide)
        x = x_ref[:, cut]
        upper, lower = [], []
        for head in (a, b):
            decays = decays_of(cum[:, head : head + 1], cumt[head : head + 1, :])
            upper.append(dot((top * decays[0]).astype(BF16), x[:half]))
            lower.append(
                dot((low * decays[1]).astype(BF16), x[:half])
                + dot((end * decays[2]).astype(BF16), x[half:])
            )
        carried = dot(read, start_ref[0, :, cut]) * lanes_of(
            from_start[:, a : a + 1], from_start[:, b : b + 1], wide
        )
        rest = carried + skip_ref[:, cut] * x.astype(F32)
        out_ref[:half, cut] = (
            jnp.where(lane < wide // 2, upper[0], upper[1]) + rest[:half]
        ).astype(BF16)
        out_ref[half:, cut] = (
            jnp.where(lane < wide // 2, lower[0], lower[1]) + rest[half:]
        ).astype(BF16)


def output(proj, values, cum, cumt, start, skip):
    groups, _, heads = cum.shape
    width = values.shape[1] // groups
    wide = wide_spec(width)
    return call(
        output_kernel,
        jax.ShapeDtypeStruct(values.shape, BF16),
        flops=groups * heads * SPAN * SPAN * 300,
        moved=values.size * 5,
        exps=groups * heads * SPAN * SPAN,
        grid=(groups,),
        in_specs=[
            wide_spec(2 * STATE), wide, lead_spec(SPAN, heads), lead_spec(heads, SPAN),
            lead_spec(STATE, width), pl.BlockSpec((1, width), lambda g: (0, g)),
        ],
        out_specs=wide,
    )(proj, values, cum, cumt, start, skip)


def update_kernel(turned_ref, *refs):
    (*blocks, decayed_ref, keep_ref, weight_ref, sparse_ref) = refs
    rows = blocks[0].shape[0]
    total = dot(turned_ref[:, :rows], blocks[0][...])
    for number in range(1, len(blocks)):
        total += dot(turned_ref[:, number * rows : (number + 1) * rows], blocks[number][...])
    weight = decayed_ref[...] - (LEARN_RATE * WEIGHT_SCALE) * total
    weight_ref[...] = weight
    sparse_ref[...] = (weight * keep_ref[...].astype(F32)).astype(BF16)


def update(turned_hidden, blocks, decayed, keep):
    rows, columns = decayed.shape
    tokens = turned_hidden.shape[1]
    step = min(rows, 256)
    full = pl.BlockSpec((step, columns), lambda i: (i, 0))
    return call(
        update_kernel,
        (jax.ShapeDtypeStruct((rows, columns), F32), jax.ShapeDtypeStruct((rows, columns), BF16)),
        flops=2 * tokens * rows * columns,
        moved=rows * columns * 12 + tokens * (rows + columns) * 2,
        grid=(rows // step,),
        in_specs=[pl.BlockSpec((step, tokens), lambda i: (i, 0))]
        + [pl.BlockSpec(b.shape, lambda i: (0, 0)) for b in blocks]
        + [full, full],
        out_specs=(full, full),
    )(turned_hidden, *blocks, decayed, keep)


def hidden_by_layer(hidden, seq, subs):
    z, sub = lax.axis_index("seq"), lax.axis_index("sub")
    j = lax.axis_index("head") * subs + sub
    rows = hidden.shape[0] // 2
    halves = [
        lax.dynamic_slice_in_dim(hidden, ((z + turn_by) % 2) * rows, rows, 0) for turn_by in (0, 1)
    ]
    pieces, place = [], []
    for turn_by in range(seq):
        pairs = [
            (source * seq + layer, layer * seq + (source + turn_by) % seq)
            for source in range(seq)
            for layer in range(seq)
        ]
        piece = lax.ppermute(halves[turn_by % 2], ("seq", "head", "sub"), pairs)
        pieces.append(piece)
        place += [(j - turn_by - z) % seq, sub]
        pieces.append(lax.ppermute(piece, "sub", [(0, 1), (1, 0)]))
        place += [((j ^ 1) - turn_by - z) % seq, 1 - sub]
    return pieces, jnp.stack(place).astype(jnp.int32)


def to_all(seq, distance):
    return [(source, (source + distance) % seq) for source in range(seq)]


def chain(own, own_low, decay, seq, step):
    arrived = jnp.zeros_like(own_low)
    message = own_low
    first = 0 if step > 0 else seq - 1
    for hop in range(seq - 1):
        source = first + hop * step
        if hop:
            message = (decay * arrived.astype(F32) + own).astype(BF16)
        arrived = arrived + lax.ppermute(message, "seq", [(source, source + step)])
    return arrived


def on_device(
    seq, heads_split, subs,
    hidden, inner_values, log_decay, skip_gain, cotangent, master, mask_now, mask_next,
):
    columns = master.shape[1]
    groups = columns // (2 * STATE)
    heads = log_decay.shape[1]
    head_width = inner_values.shape[1] // heads
    direct = seq == heads_split * subs and subs == 2

    if direct:
        pieces, place = hidden_by_layer(hidden, seq, subs)
    else:
        features = lax.all_gather(hidden, ("head", "sub"), axis=1, tiled=True)
        layer = lax.all_to_all(features, "seq", split_axis=1, concat_axis=0, tiled=True)

    effective, decayed, keep = weights(master, mask_now, mask_next)
    logs = log_decay.reshape(SPAN, groups, heads // groups).transpose(1, 0, 2)
    logs_t = log_decay.T.reshape(groups, heads // groups, SPAN)
    skip = jnp.repeat(skip_gain, head_width)[None, :]
    xd, yd, mix, mixt, cum, cumt, block_decay = before(inner_values, cotangent, logs, logs_t)

    if direct:
        parts = partials(pieces, place, effective, seq)
        terms = [parts[0]] + [
            lax.ppermute(parts[d], "seq", to_all(seq, d)) for d in range(1, seq)
        ]
        turned_hidden = turn(pieces, place)
    else:
        part = dot(layer, effective).astype(BF16)
        terms = [lax.psum_scatter(part, "seq", scatter_dimension=0, tiled=True)]
        turned_hidden = layer.T

    proj, state, adjoint, state_low, adjoint_low = states(terms, xd, yd)
    start = chain(state, state_low, block_decay, seq, 1)
    adjoint_in = chain(adjoint, adjoint_low, block_decay, seq, -1)
    grad = grads(proj, xd, yd, mix, mixt, start, adjoint_in)

    if direct:
        blocks = [grad] + [
            lax.ppermute(grad, "seq", to_all(seq, seq - d)) for d in range(1, seq)
        ]
    else:
        blocks = [lax.all_gather(grad, "seq", axis=0, tiled=True)]
    ssd_output = output(proj, inner_values, cum, cumt, start, skip)
    new_weight, sparse_weight = update(turned_hidden, blocks, decayed, keep)
    return ssd_output, new_weight, sparse_weight


def solution(mesh):
    by_position = P(("grp", "seq"), ("head", "sub"))
    by_row = P("seq", ("head", "sub"))
    return jax.shard_map(
        functools.partial(
            on_device, mesh.shape["seq"], mesh.shape["head"], mesh.shape["sub"]
        ),
        mesh=mesh,
        in_specs=(
            by_position, by_position, by_position, P(("head", "sub")), by_position,
            by_row, by_row, by_row,
        ),
        out_specs=(by_position, by_position, by_position),
        check_vma=False,
    )
```

```python
import functools
import math

import jax
import jax.numpy as jnp
from jax import lax
from jax.experimental import pallas as pl
from jax.experimental.pallas import tpu as pltpu
from jax.sharding import PartitionSpec as P

D = 4096
STATE = 128
SPAN = 256
LEARN_RATE = 0.05
WEIGHT_DECAY = 10.0
WEIGHT_SCALE = 2.0 / math.sqrt(D)
KEEP_BITS = (0b000111, 0b011001, 0b101010, 0b110100)
OUT_OF_SIGHT = -1e30
VMEM_BYTES = 40 * 1024 * 1024

F32 = jnp.float32
BF16 = jnp.bfloat16
NT = (((1,), (1,)), ((), ()))


def call(kernel, out_shape, flops, moved, exps=0, **more):
    return pl.pallas_call(
        kernel,
        out_shape=out_shape,
        compiler_params=pltpu.CompilerParams(vmem_limit_bytes=VMEM_BYTES),
        cost_estimate=pl.CostEstimate(flops=flops, bytes_accessed=moved, transcendentals=exps),
        **more,
    )


def dot(a, b):
    return jnp.dot(a, b, preferred_element_type=F32)


def dot_nt(a, b):
    return lax.dot_general(a, b, NT, preferred_element_type=F32)


def turned(a):
    return a.astype(F32).T.astype(BF16)


def expanded(codes, rows):
    spread = (
        lax.broadcasted_iota(jnp.int32, (rows, rows // 4), 0) // 4
        == lax.broadcasted_iota(jnp.int32, (rows, rows // 4), 1)
    ).astype(F32)
    code = dot(spread.astype(BF16), codes.astype(F32).astype(BF16)).astype(jnp.int32)
    place = lax.broadcasted_iota(jnp.int32, (rows, 1), 0) % 4
    bits = jnp.where(
        place < 2,
        jnp.where(place == 0, KEEP_BITS[0], KEEP_BITS[1]),
        jnp.where(place == 2, KEEP_BITS[2], KEEP_BITS[3]),
    )
    return lax.shift_right_logical(jnp.broadcast_to(bits, code.shape), code) & 1


def weights_kernel(master_ref, now_ref, next_ref, effective_ref, decayed_ref, keep_ref):
    rows = master_ref.shape[0]
    master = master_ref[...]
    kept = expanded(now_ref[...], rows) == 1
    effective_ref[...] = jnp.where(kept, master * WEIGHT_SCALE, 0.0).astype(BF16)
    decayed_ref[...] = jnp.where(kept, master, master * (1.0 - LEARN_RATE * WEIGHT_DECAY))
    keep_ref[...] = expanded(next_ref[...], rows).astype(F32).astype(BF16)


def weights(master, mask_now, mask_next):
    rows, columns = master.shape
    block = min(rows, 256)
    full = pl.BlockSpec((block, columns), lambda i: (i, 0))
    quarter = pl.BlockSpec((block // 4, columns), lambda i: (i, 0))
    return call(
        weights_kernel,
        (
            jax.ShapeDtypeStruct((rows, columns), BF16),
            jax.ShapeDtypeStruct((rows, columns), F32),
            jax.ShapeDtypeStruct((rows, columns), BF16),
        ),
        flops=rows * columns * 3000,
        moved=rows * columns * 14,
        grid=(rows // block,),
        in_specs=[full, quarter, quarter],
        out_specs=(full, full, full),
    )(master, mask_now, mask_next)


def lanes_of(left, right, wide):
    lane = lax.broadcasted_iota(jnp.int32, (left.shape[0], wide), 1)
    return jnp.where(lane < wide // 2, left, right)


def decays_of(col, row):
    half = SPAN // 2
    causal = lax.broadcasted_iota(jnp.int32, (half, half), 0) >= lax.broadcasted_iota(
        jnp.int32, (half, half), 1
    )
    top = jnp.exp(jnp.where(causal, col[:half] - row[:, :half], OUT_OF_SIGHT))
    low = jnp.exp(col[half:] - row[:, :half])
    end = jnp.exp(jnp.where(causal, col[half:] - row[:, half:], OUT_OF_SIGHT))
    return top, low, end


def before_kernel(
    x_ref, dy_ref, log_ref, logt_ref,
    xd_ref, yd_ref, mix_ref, mixt_ref, cum_ref, cumt_ref, end_ref,
):
    heads = log_ref.shape[2]
    half = SPAN // 2
    wide = x_ref.shape[1] // heads * 2
    row = lax.broadcasted_iota(jnp.int32, (SPAN, SPAN), 0)
    col = lax.broadcasted_iota(jnp.int32, (SPAN, SPAN), 1)
    cum = jnp.dot(
        (row >= col).astype(F32), log_ref[0],
        precision=lax.Precision.HIGHEST, preferred_element_type=F32,
    )
    cumt = jnp.dot(
        logt_ref[0], (row <= col).astype(F32),
        precision=lax.Precision.HIGHEST, preferred_element_type=F32,
    )
    cum_ref[0] = cum
    cumt_ref[0] = cumt
    end = cum[SPAN - 1 :, :]
    from_start = jnp.exp(cum)
    to_end = jnp.exp(end - cum)
    whole = jnp.exp(end)
    mix = [jnp.zeros((half, half), F32) for _ in range(3)]
    lane = lax.broadcasted_iota(jnp.int32, (SPAN, wide), 1)
    for pair in range(heads // 2):
        a, b = 2 * pair, 2 * pair + 1
        cut = slice(pair * wide, (pair + 1) * wide)
        x = x_ref[:, cut]
        dy = dy_ref[:, cut]
        wide_dy = dy.astype(F32)
        xd_ref[:, cut] = (
            x.astype(F32) * lanes_of(to_end[:, a : a + 1], to_end[:, b : b + 1], wide)
        ).astype(BF16)
        yd_ref[:, cut] = (
            wide_dy * lanes_of(from_start[:, a : a + 1], from_start[:, b : b + 1], wide)
        ).astype(BF16)
        end_ref[0, :, cut] = lanes_of(whole[:, a : a + 1], whole[:, b : b + 1], wide)
        for head, mine in ((a, lane < wide // 2), (b, lane >= wide // 2)):
            one = jnp.where(mine, wide_dy, 0.0).astype(BF16)
            decays = decays_of(cum[:, head : head + 1], cumt[head : head + 1, :])
            mix[0] += dot_nt(one[:half], x[:half]) * decays[0]
            both = dot_nt(one[half:], x)
            mix[1] += both[:, :half] * decays[1]
            mix[2] += both[:, half:] * decays[2]
    nothing = jnp.zeros((half, half), BF16)
    top, low, end_mix = (m.astype(BF16) for m in mix)
    topt, lowt, end_mixt = (m.T.astype(BF16) for m in mix)
    mix_ref[0, :half, :half] = top
    mix_ref[0, :half, half:] = nothing
    mix_ref[0, half:, :half] = low
    mix_ref[0, half:, half:] = end_mix
    mixt_ref[0, :half, :half] = topt
    mixt_ref[0, :half, half:] = lowt
    mixt_ref[0, half:, :half] = nothing
    mixt_ref[0, half:, half:] = end_mixt


def wide_spec(width):
    return pl.BlockSpec((SPAN, width), lambda g: (0, g))


def lead_spec(*shape):
    return pl.BlockSpec((1, *shape), lambda g: (g, *(0 for _ in shape)))


def before(values, cotan, logs, logs_t):
    groups, _, heads = logs.shape
    width = values.shape[1] // groups
    wide = wide_spec(width)
    return call(
        before_kernel,
        (
            jax.ShapeDtypeStruct(values.shape, BF16),
            jax.ShapeDtypeStruct(values.shape, BF16),
            jax.ShapeDtypeStruct((groups, SPAN, SPAN), BF16),
            jax.ShapeDtypeStruct((groups, SPAN, SPAN), BF16),
            jax.ShapeDtypeStruct((groups, SPAN, heads), F32),
            jax.ShapeDtypeStruct((groups, heads, SPAN), F32),
            jax.ShapeDtypeStruct((groups, 1, width), F32),
        ),
        flops=groups * heads * SPAN * SPAN * 2500,
        moved=values.size * 8,
        exps=groups * heads * SPAN * SPAN,
        grid=(groups,),
        in_specs=[wide, wide, lead_spec(SPAN, heads), lead_spec(heads, SPAN)],
        out_specs=(
            wide, wide, lead_spec(SPAN, SPAN), lead_spec(SPAN, SPAN),
            lead_spec(SPAN, heads), lead_spec(heads, SPAN), lead_spec(1, width),
        ),
    )(values, cotan, logs, logs_t)


def partial_kernel(parts, swap_ref, own_ref, sibling_ref, weight_ref, *outs):
    own = dot(own_ref[...], weight_ref[...]).astype(BF16)
    sibling = dot(sibling_ref[...], weight_ref[...]).astype(BF16)
    width = own.shape[1] // parts

    def put(first, second):
        for part in range(parts):
            cut = slice(part * width, (part + 1) * width)
            outs[2 * part][...] = first[:, cut]
            outs[2 * part + 1][...] = second[:, cut]

    @pl.when(swap_ref[0] == 0)
    def _():
        put(own, sibling)

    @pl.when(swap_ref[0] != 0)
    def _():
        put(sibling, own)


def partials(swap, own, sibling, effective, parts):
    tokens, columns = own.shape[0], effective.shape[1]
    whole = pl.BlockSpec(memory_space=pltpu.VMEM)
    outs = call(
        functools.partial(partial_kernel, parts),
        (jax.ShapeDtypeStruct((tokens, columns // parts), BF16),) * (2 * parts),
        flops=4 * tokens * effective.size,
        moved=(2 * own.size + effective.size + 2 * tokens * columns) * 2,
        in_specs=[pl.BlockSpec(memory_space=pltpu.SMEM), whole, whole, whole],
        out_specs=(whole,) * (2 * parts),
    )(swap, own, sibling, effective)
    return outs[0::2], outs[1::2]


def turn_kernel(place_ref, *refs):
    pieces, out_ref = refs[:-1], refs[-1]
    rows = pieces[0].shape[0]
    for number, piece in enumerate(pieces):
        start = pl.multiple_of(place_ref[number] * rows, rows)
        out_ref[:, pl.ds(start, rows)] = turned(piece[...])


def turn(pieces, place):
    whole = pl.BlockSpec(memory_space=pltpu.VMEM)
    tokens = sum(p.shape[0] for p in pieces)
    features = pieces[0].shape[1]
    return call(
        turn_kernel,
        jax.ShapeDtypeStruct((features, tokens), BF16),
        flops=tokens * features * 1000,
        moved=tokens * features * 4,
        in_specs=[pl.BlockSpec(memory_space=pltpu.SMEM)] + [whole] * len(pieces),
        out_specs=whole,
    )(place, *pieces)


def states_kernel(
    ahead_ref, *refs,
):
    (*terms, xd_ref, yd_ref, proj_ref, near_low_ref, near_ref, far_ref) = refs
    total = terms[0][...].astype(F32)
    for term in terms[1:]:
        total += term[...].astype(F32)
    low = total.astype(BF16)
    proj_ref[...] = low
    state = dot(turned(low[:, :STATE]), xd_ref[...])
    adjoint = dot(turned(low[:, STATE:]), yd_ref[...])

    def put(near, far):
        near_low_ref[0] = near.astype(BF16)
        near_ref[0] = near
        far_ref[0] = far

    @pl.when(ahead_ref[0] != 0)
    def _():
        put(state, adjoint)

    @pl.when(ahead_ref[0] == 0)
    def _():
        put(adjoint, state)


def states(ahead, whole_terms, part_terms, xd, yd, first, groups, width):
    pair = pl.BlockSpec((SPAN, 2 * STATE), lambda g: (0, g))
    pair_from = pl.BlockSpec((SPAN, 2 * STATE), lambda g: (0, g + first))
    wide = pl.BlockSpec((SPAN, width), lambda g: (0, g + first))
    lead = lead_spec(STATE, width)
    shape = (groups, STATE, width)
    return call(
        states_kernel,
        (
            jax.ShapeDtypeStruct((SPAN, groups * 2 * STATE), BF16),
            jax.ShapeDtypeStruct(shape, BF16),
            jax.ShapeDtypeStruct(shape, F32),
            jax.ShapeDtypeStruct(shape, F32),
        ),
        flops=4 * SPAN * groups * width * STATE,
        moved=groups * SPAN * (width * 4 + 4 * STATE * 5),
        grid=(groups,),
        in_specs=[pl.BlockSpec(memory_space=pltpu.SMEM)]
        + [pair_from] * len(whole_terms) + [pair] * len(part_terms) + [wide, wide],
        out_specs=(pair, lead, lead, lead),
    )(ahead, *whole_terms, *part_terms, xd, yd)


def grads_kernel(
    ahead_ref, proj_ref, xd_ref, yd_ref, mix_ref, mixt_ref, carried_ref, out_ref
):
    @pl.when(ahead_ref[0] != 0)
    def _():
        grad_read = dot(mix_ref[0], proj_ref[:, :STATE]) + dot_nt(yd_ref[...], carried_ref[0])
        out_ref[...] = grad_read.astype(BF16)

    @pl.when(ahead_ref[0] == 0)
    def _():
        grad_write = dot(mixt_ref[0], proj_ref[:, STATE:]) + dot_nt(xd_ref[...], carried_ref[0])
        out_ref[...] = grad_write.astype(BF16)


def grads(ahead, proj, xd, yd, mix, mixt, carried, first):
    groups, _, width = carried.shape
    pair = pl.BlockSpec((SPAN, 2 * STATE), lambda g: (0, g))
    wide = pl.BlockSpec((SPAN, width), lambda g: (0, g + first))
    square = pl.BlockSpec((1, SPAN, SPAN), lambda g: (g + first, 0, 0))
    return call(
        grads_kernel,
        jax.ShapeDtypeStruct((SPAN, groups * STATE), BF16),
        flops=2 * SPAN * groups * (width + SPAN) * STATE,
        moved=groups * SPAN * width * 5,
        grid=(groups,),
        in_specs=[
            pl.BlockSpec(memory_space=pltpu.SMEM), pair, wide, wide, square, square,
            lead_spec(STATE, width),
        ],
        out_specs=pl.BlockSpec((SPAN, STATE), lambda g: (0, g)),
    )(ahead, proj, xd, yd, mix, mixt, carried)


def output_kernel(proj_ref, x_ref, cum_ref, cumt_ref, start_ref, skip_ref, out_ref):
    heads = cum_ref.shape[2]
    half = SPAN // 2
    wide = x_ref.shape[1] // heads * 2
    write = proj_ref[:, :STATE]
    read = proj_ref[:, STATE:]
    cum = cum_ref[0]
    cumt = cumt_ref[0]
    from_start = jnp.exp(cum)
    scores = dot_nt(read, write)
    top, low, end = scores[:half, :half], scores[half:, :half], scores[half:, half:]
    lane = lax.broadcasted_iota(jnp.int32, (half, wide), 1)
    for pair in range(heads // 2):
        a, b = 2 * pair, 2 * pair + 1
        cut = slice(pair * wide, (pair + 1) * wide)
        x = x_ref[:, cut]
        upper, lower = [], []
        for head in (a, b):
            decays = decays_of(cum[:, head : head + 1], cumt[head : head + 1, :])
            upper.append(dot((top * decays[0]).astype(BF16), x[:half]))
            lower.append(
                dot((low * decays[1]).astype(BF16), x[:half])
                + dot((end * decays[2]).astype(BF16), x[half:])
            )
        carried = dot(read, start_ref[0, :, cut]) * lanes_of(
            from_start[:, a : a + 1], from_start[:, b : b + 1], wide
        )
        rest = carried + skip_ref[:, cut] * x.astype(F32)
        out_ref[:half, cut] = (
            jnp.where(lane < wide // 2, upper[0], upper[1]) + rest[:half]
        ).astype(BF16)
        out_ref[half:, cut] = (
            jnp.where(lane < wide // 2, lower[0], lower[1]) + rest[half:]
        ).astype(BF16)


def output(proj, values, cum, cumt, start, skip):
    groups, _, heads = cum.shape
    width = values.shape[1] // groups
    wide = wide_spec(width)
    return call(
        output_kernel,
        jax.ShapeDtypeStruct(values.shape, BF16),
        flops=groups * heads * SPAN * SPAN * 2000,
        moved=values.size * 5,
        exps=groups * heads * SPAN * SPAN,
        grid=(groups,),
        in_specs=[
            wide_spec(2 * STATE), wide, lead_spec(SPAN, heads), lead_spec(heads, SPAN),
            lead_spec(STATE, width), pl.BlockSpec((1, width), lambda g: (0, g)),
        ],
        out_specs=wide,
    )(proj, values, cum, cumt, start, skip)


def update_kernel(blocks, parts, ahead_ref, turned_ref, *refs):
    firsts, seconds = refs[: blocks * parts], refs[blocks * parts : 2 * blocks * parts]
    decayed_ref, keep_ref, weight_ref, sparse_ref, grad_ref = refs[2 * blocks * parts :]
    rows = firsts[0].shape[0]

    def put(block, reads, writes):
        column = 0
        for part in range(parts):
            read, write = reads[block * parts + part], writes[block * parts + part]
            for at in range(0, read.shape[1], STATE):
                here = pl.ds(block * rows, rows)
                grad_ref[here, column : column + STATE] = write[:, at : at + STATE]
                grad_ref[here, column + STATE : column + 2 * STATE] = read[:, at : at + STATE]
                column += 2 * STATE

    @pl.when(pl.program_id(0) == 0)
    def _():
        for block in range(blocks):

            @pl.when(ahead_ref[block] != 0)
            def _(block=block):
                put(block, firsts, seconds)

            @pl.when(ahead_ref[block] == 0)
            def _(block=block):
                put(block, seconds, firsts)

    total = dot(turned_ref[...], grad_ref[...])
    weight = decayed_ref[...] - (LEARN_RATE * WEIGHT_SCALE) * total
    weight_ref[...] = weight
    sparse_ref[...] = (weight * keep_ref[...].astype(F32)).astype(BF16)


def update(ahead, turned_hidden, firsts, seconds, decayed, keep):
    rows, columns = decayed.shape
    tokens = turned_hidden.shape[1]
    step = min(rows, 256)
    full = pl.BlockSpec((step, columns), lambda i: (i, 0))
    blocks, parts = len(firsts), len(firsts[0])
    pieces = [part for block in (*firsts, *seconds) for part in block]
    return call(
        functools.partial(update_kernel, blocks, parts),
        (jax.ShapeDtypeStruct((rows, columns), F32), jax.ShapeDtypeStruct((rows, columns), BF16)),
        flops=2 * tokens * rows * columns,
        moved=rows * columns * 12 + tokens * (rows + columns) * 2,
        grid=(rows // step,),
        in_specs=[
            pl.BlockSpec(memory_space=pltpu.SMEM),
            pl.BlockSpec((step, tokens), lambda i: (i, 0)),
        ]
        + [pl.BlockSpec(piece.shape, lambda i: (0, 0)) for piece in pieces]
        + [full, full],
        out_specs=(full, full),
        scratch_shapes=[pltpu.VMEM((tokens, columns), BF16)],
    )(ahead, turned_hidden, *pieces, decayed, keep)


def held(after, *before):
    return lax.optimization_barrier((after, *before))[0]


def scalars(*values):
    return jnp.stack([jnp.asarray(v).astype(jnp.int32) for v in values])


def to_all(seq, distance):
    return [(source, (source + distance) % seq) for source in range(seq)]


def line_pairs(seq, distance_of):
    return [
        (z * 2 + x, (z + distance_of[x]) % seq * 2 + x) for z in range(seq) for x in range(2)
    ]


def transpose_pairs(seq):
    pairs = []
    for z in range(seq):
        for layer in range(seq):
            distance = (z - layer) % seq
            pairs.append((z * seq + layer, layer * seq + distance % 2 * 2 + distance // 2))
    return pairs


SWAP = [(0, 1), (1, 0)]


def chain(own, own_low, decay, seq, step):
    arrived = jnp.zeros_like(own_low)
    message = own_low
    first = 0 if step > 0 else seq - 1
    for hop in range(seq - 1):
        source = first + hop * step
        if hop:
            message = (decay * arrived.astype(F32) + own).astype(BF16)
        arrived = arrived + lax.ppermute(message, "seq", [(source, source + step)])
    return arrived


def prepared(inner_values, log_decay, skip_gain, cotangent, groups):
    heads = log_decay.shape[1]
    logs = log_decay.reshape(SPAN, groups, heads // groups).transpose(1, 0, 2)
    logs_t = log_decay.T.reshape(groups, heads // groups, SPAN)
    skip = jnp.repeat(skip_gain, inner_values.shape[1] // heads)[None, :]
    return skip, before(inner_values, cotangent, logs, logs_t)


def on_device_general(
    seq, hidden, inner_values, log_decay, skip_gain, cotangent, master, mask_now, mask_next
):
    groups = master.shape[1] // (2 * STATE)
    effective, decayed, keep = weights(master, mask_now, mask_next)
    features = lax.all_gather(hidden, ("head", "sub"), axis=1, tiled=True)
    layer = lax.all_to_all(features, "seq", split_axis=1, concat_axis=0, tiled=True)
    skip, (xd, yd, mix, mixt, cum, cumt, decay) = prepared(
        inner_values, log_decay, skip_gain, cotangent, groups
    )
    part = dot(layer, effective).astype(BF16)
    terms = [lax.psum_scatter(part, "seq", scatter_dimension=0, tiled=True)]
    yes, no = scalars(1), scalars(0)
    proj, state_low, state, adjoint = states(yes, [], terms, xd, yd, 0, groups, decay.shape[2])
    start = chain(state, state_low, decay, seq, 1)
    adjoint_in = chain(adjoint, adjoint.astype(BF16), decay, seq, -1)
    grad_read = grads(yes, proj, xd, yd, mix, mixt, start, 0)
    grad_write = grads(no, proj, xd, yd, mix, mixt, adjoint_in, 0)
    reads, writes = (
        [[lax.all_gather(g, "seq", axis=0, tiled=True)]] for g in (grad_read, grad_write)
    )
    ssd_output = output(proj, inner_values, cum, cumt, start, skip)
    return ssd_output, *update(yes, layer.T, reads, writes, decayed, keep)


def on_device(
    seq, hidden, inner_values, log_decay, skip_gain, cotangent, master, mask_now, mask_next
):
    groups = master.shape[1] // (2 * STATE)
    z, x, core = (lax.axis_index(name) for name in ("seq", "head", "sub"))
    lower = z < seq // 2
    ahead = scalars(lower)
    behind = scalars(~lower)
    swap = scalars(core)

    own = lax.ppermute(hidden, ("seq", "head", "sub"), transpose_pairs(seq))
    effective, decayed, keep = weights(master, mask_now, mask_next)
    skip, (xd, yd, mix, mixt, cum, cumt, decay) = prepared(
        inner_values, log_decay, skip_gain, cotangent, groups
    )
    own = held(own, effective, xd)

    other = lax.ppermute(own, "head", SWAP)
    sibling = lax.ppermute(own, "sub", SWAP)
    early = [part for (part,) in partials(swap, own, sibling, effective, 1)]
    early = [
        lax.ppermute(early[0], ("seq", "head"), line_pairs(seq, (0, 1))),
        lax.ppermute(early[1], ("seq", "head"), line_pairs(seq, (2, 3))),
    ]
    other_sibling = lax.ppermute(other, "sub", SWAP)
    late = partials(swap, other, other_sibling, effective, PARTS)
    place = scalars(x + 2 * core, x + 2 * (1 - core), 1 - x + 2 * core, 3 - x - 2 * core)
    turned_hidden = turn((own, sibling, other, other_sibling), place)
    late = [
        [lax.ppermute(part, ("seq", "head"), line_pairs(seq, (1, 0))) for part in late[0]],
        [lax.ppermute(part, ("seq", "head"), line_pairs(seq, (3, 2))) for part in late[1]],
    ]

    each = groups // PARTS
    projs, starts = [], []
    firsts = [[] for _ in range(seq)]
    seconds = [[] for _ in range(seq)]
    for part in range(PARTS):
        at = part * each
        decay_part = decay[at : at + each]
        proj, near_low, near, far = states(
            ahead, early, [late[0][part], late[1][part]], xd, yd, at, each, decay.shape[2]
        )
        arrived = lax.ppermute(near_low, "seq", [(0, 1), (3, 2)])
        first = grads(ahead, proj, xd, yd, mix, mixt, arrived, at)
        message = (decay_part * arrived.astype(F32) + near).astype(BF16)
        middle = lax.ppermute(message, "seq", [(1, 2), (2, 1)])
        message = (decay_part * middle.astype(F32) + far).astype(BF16)
        last = middle + lax.ppermute(message, "seq", [(1, 0), (2, 3)])
        second = grads(behind, proj, xd, yd, mix, mixt, last, at)
        first = held(first, middle)
        for distance in range(seq):
            pairs = to_all(seq, seq - distance)
            firsts[distance].append(lax.ppermute(first, "seq", pairs) if distance else first)
            seconds[distance].append(lax.ppermute(second, "seq", pairs) if distance else second)
        projs.append(proj)
        starts.append(jnp.where(lower, arrived, last))

    proj = jnp.concatenate(projs, axis=1) if PARTS > 1 else projs[0]
    start = jnp.concatenate(starts, axis=0) if PARTS > 1 else starts[0]
    ssd_output = output(proj, inner_values, cum, cumt, start, skip)
    blocks_ahead = scalars(*((z + d) % seq < seq // 2 for d in range(seq)))
    new_weight, sparse_weight = update(
        blocks_ahead, turned_hidden, firsts, seconds, decayed, keep
    )
    return ssd_output, new_weight, sparse_weight


PARTS = 1


def solution(mesh):
    by_position = P(("grp", "seq"), ("head", "sub"))
    by_row = P("seq", ("head", "sub"))
    seq, head, sub = (mesh.shape[name] for name in ("seq", "head", "sub"))
    body = on_device if (seq, head, sub) == (4, 2, 2) else on_device_general
    return jax.shard_map(
        functools.partial(body, seq),
        mesh=mesh,
        in_specs=(
            by_position, by_position, by_position, P(("head", "sub")), by_position,
            by_row, by_row, by_row,
        ),
        out_specs=(by_position, by_position, by_position),
        check_vma=False,
    )
```

```python
import functools
import math

import jax
import jax.numpy as jnp
from jax import lax
from jax.experimental import pallas as pl
from jax.experimental.pallas import tpu as pltpu
from jax.sharding import PartitionSpec as P

D = 4096
STATE = 128
SPAN = 256
LEARN_RATE = 0.05
WEIGHT_DECAY = 10.0
WEIGHT_SCALE = 2.0 / math.sqrt(D)
KEEP_BITS = (0b000111, 0b011001, 0b101010, 0b110100)
OUT_OF_SIGHT = -1e30
VMEM_BYTES = 40 * 1024 * 1024

F32 = jnp.float32
BF16 = jnp.bfloat16
NT = (((1,), (1,)), ((), ()))


def call(kernel, out_shape, flops, moved, exps=0, **more):
    return pl.pallas_call(
        kernel,
        out_shape=out_shape,
        compiler_params=pltpu.CompilerParams(vmem_limit_bytes=VMEM_BYTES),
        cost_estimate=pl.CostEstimate(flops=flops, bytes_accessed=moved, transcendentals=exps),
        **more,
    )


def dot(a, b):
    return jnp.dot(a, b, preferred_element_type=F32)


def dot_nt(a, b):
    return lax.dot_general(a, b, NT, preferred_element_type=F32)


def turned(a):
    return a.astype(F32).T.astype(BF16)


def expanded(codes, rows):
    spread = (
        lax.broadcasted_iota(jnp.int32, (rows, rows // 4), 0) // 4
        == lax.broadcasted_iota(jnp.int32, (rows, rows // 4), 1)
    ).astype(F32)
    code = dot(spread.astype(BF16), codes.astype(F32).astype(BF16)).astype(jnp.int32)
    place = lax.broadcasted_iota(jnp.int32, (rows, 1), 0) % 4
    bits = jnp.where(
        place < 2,
        jnp.where(place == 0, KEEP_BITS[0], KEEP_BITS[1]),
        jnp.where(place == 2, KEEP_BITS[2], KEEP_BITS[3]),
    )
    return lax.shift_right_logical(jnp.broadcast_to(bits, code.shape), code) & 1


def weights_kernel(master_ref, now_ref, next_ref, effective_ref, decayed_ref, keep_ref):
    rows = master_ref.shape[0]
    master = master_ref[...]
    kept = expanded(now_ref[...], rows) == 1
    effective_ref[...] = jnp.where(kept, master * WEIGHT_SCALE, 0.0).astype(BF16)
    decayed_ref[...] = jnp.where(kept, master, master * (1.0 - LEARN_RATE * WEIGHT_DECAY))
    keep_ref[...] = expanded(next_ref[...], rows).astype(F32).astype(BF16)


def weights(master, mask_now, mask_next):
    rows, columns = master.shape
    block = min(rows, 256)
    full = pl.BlockSpec((block, columns), lambda i: (i, 0))
    quarter = pl.BlockSpec((block // 4, columns), lambda i: (i, 0))
    return call(
        weights_kernel,
        (
            jax.ShapeDtypeStruct((rows, columns), BF16),
            jax.ShapeDtypeStruct((rows, columns), F32),
            jax.ShapeDtypeStruct((rows, columns), BF16),
        ),
        flops=rows * columns * 3000,
        moved=rows * columns * 14,
        grid=(rows // block,),
        in_specs=[full, quarter, quarter],
        out_specs=(full, full, full),
    )(master, mask_now, mask_next)


def effective_kernel(master_ref, now_ref, effective_ref):
    kept = expanded(now_ref[...], master_ref.shape[0]) == 1
    effective_ref[...] = jnp.where(kept, master_ref[...] * WEIGHT_SCALE, 0.0).astype(BF16)


def effective_of(master, mask_now):
    rows, columns = master.shape
    block = min(rows, 256)
    full = pl.BlockSpec((block, columns), lambda i: (i, 0))
    return call(
        effective_kernel,
        jax.ShapeDtypeStruct((rows, columns), BF16),
        flops=rows * columns * 3000,
        moved=rows * columns * 7,
        grid=(rows // block,),
        in_specs=[full, pl.BlockSpec((block // 4, columns), lambda i: (i, 0))],
        out_specs=full,
    )(master, mask_now)


def lanes_of(left, right, wide):
    lane = lax.broadcasted_iota(jnp.int32, (left.shape[0], wide), 1)
    return jnp.where(lane < wide // 2, left, right)


def decays_of(col, row):
    half = SPAN // 2
    causal = lax.broadcasted_iota(jnp.int32, (half, half), 0) >= lax.broadcasted_iota(
        jnp.int32, (half, half), 1
    )
    top = jnp.exp(jnp.where(causal, col[:half] - row[:, :half], OUT_OF_SIGHT))
    low = jnp.exp(col[half:] - row[:, :half])
    end = jnp.exp(jnp.where(causal, col[half:] - row[:, half:], OUT_OF_SIGHT))
    return top, low, end


def before_kernel(
    x_ref, dy_ref, log_ref, logt_ref,
    xd_ref, yd_ref, mix_ref, mixt_ref, cum_ref, cumt_ref, end_ref,
):
    heads = log_ref.shape[2]
    half = SPAN // 2
    wide = x_ref.shape[1] // heads * 2
    row = lax.broadcasted_iota(jnp.int32, (SPAN, SPAN), 0)
    col = lax.broadcasted_iota(jnp.int32, (SPAN, SPAN), 1)
    cum = jnp.dot(
        (row >= col).astype(F32), log_ref[0],
        precision=lax.Precision.HIGHEST, preferred_element_type=F32,
    )
    cumt = jnp.dot(
        logt_ref[0], (row <= col).astype(F32),
        precision=lax.Precision.HIGHEST, preferred_element_type=F32,
    )
    cum_ref[0] = cum
    cumt_ref[0] = cumt
    end = cum[SPAN - 1 :, :]
    from_start = jnp.exp(cum)
    to_end = jnp.exp(end - cum)
    whole = jnp.exp(end)
    mix = [jnp.zeros((half, half), F32) for _ in range(3)]
    lane = lax.broadcasted_iota(jnp.int32, (SPAN, wide), 1)
    for pair in range(heads // 2):
        a, b = 2 * pair, 2 * pair + 1
        cut = slice(pair * wide, (pair + 1) * wide)
        x = x_ref[:, cut]
        dy = dy_ref[:, cut]
        wide_dy = dy.astype(F32)
        xd_ref[:, cut] = (
            x.astype(F32) * lanes_of(to_end[:, a : a + 1], to_end[:, b : b + 1], wide)
        ).astype(BF16)
        yd_ref[:, cut] = (
            wide_dy * lanes_of(from_start[:, a : a + 1], from_start[:, b : b + 1], wide)
        ).astype(BF16)
        end_ref[0, :, cut] = lanes_of(whole[:, a : a + 1], whole[:, b : b + 1], wide)
        for head, mine in ((a, lane < wide // 2), (b, lane >= wide // 2)):
            one = jnp.where(mine, wide_dy, 0.0).astype(BF16)
            decays = decays_of(cum[:, head : head + 1], cumt[head : head + 1, :])
            mix[0] += dot_nt(one[:half], x[:half]) * decays[0]
            both = dot_nt(one[half:], x)
            mix[1] += both[:, :half] * decays[1]
            mix[2] += both[:, half:] * decays[2]
    nothing = jnp.zeros((half, half), BF16)
    top, low, end_mix = (m.astype(BF16) for m in mix)
    topt, lowt, end_mixt = (m.T.astype(BF16) for m in mix)
    mix_ref[0, :half, :half] = top
    mix_ref[0, :half, half:] = nothing
    mix_ref[0, half:, :half] = low
    mix_ref[0, half:, half:] = end_mix
    mixt_ref[0, :half, :half] = topt
    mixt_ref[0, :half, half:] = lowt
    mixt_ref[0, half:, :half] = nothing
    mixt_ref[0, half:, half:] = end_mixt


def wide_spec(width):
    return pl.BlockSpec((SPAN, width), lambda g: (0, g))


def lead_spec(*shape):
    return pl.BlockSpec((1, *shape), lambda g: (g, *(0 for _ in shape)))


def before(values, cotan, logs, logs_t):
    groups, _, heads = logs.shape
    width = values.shape[1] // groups
    wide = wide_spec(width)
    return call(
        before_kernel,
        (
            jax.ShapeDtypeStruct(values.shape, BF16),
            jax.ShapeDtypeStruct(values.shape, BF16),
            jax.ShapeDtypeStruct((groups, SPAN, SPAN), BF16),
            jax.ShapeDtypeStruct((groups, SPAN, SPAN), BF16),
            jax.ShapeDtypeStruct((groups, SPAN, heads), F32),
            jax.ShapeDtypeStruct((groups, heads, SPAN), F32),
            jax.ShapeDtypeStruct((groups, 1, width), F32),
        ),
        flops=groups * heads * SPAN * SPAN * 2500,
        moved=values.size * 8,
        exps=groups * heads * SPAN * SPAN,
        grid=(groups,),
        in_specs=[wide, wide, lead_spec(SPAN, heads), lead_spec(heads, SPAN)],
        out_specs=(
            wide, wide, lead_spec(SPAN, SPAN), lead_spec(SPAN, SPAN),
            lead_spec(SPAN, heads), lead_spec(heads, SPAN), lead_spec(1, width),
        ),
    )(values, cotan, logs, logs_t)


def partial_kernel(parts, hidden_ref, *refs):
    weight_refs, outs = refs[:2], refs[2:]
    for number, weight_ref in enumerate(weight_refs):
        term = dot(hidden_ref[...], weight_ref[...]).astype(BF16)
        width = term.shape[1] // parts
        for part in range(parts):
            outs[number * parts + part][...] = term[:, part * width : (part + 1) * width]


def partials(hidden, effective, sibling_effective, parts):
    tokens, columns = hidden.shape[0], effective.shape[1]
    whole = pl.BlockSpec(memory_space=pltpu.VMEM)
    outs = call(
        functools.partial(partial_kernel, parts),
        (jax.ShapeDtypeStruct((tokens, columns // parts), BF16),) * (2 * parts),
        flops=4 * tokens * effective.size,
        moved=(hidden.size + 2 * effective.size + 2 * tokens * columns) * 2,
        in_specs=[whole] * 3,
        out_specs=(whole,) * (2 * parts),
    )(hidden, effective, sibling_effective)
    return outs[:parts], outs[parts:]


def turn_kernel(place_ref, *refs):
    pieces, out_ref = refs[:-1], refs[-1]
    rows = pieces[0].shape[0]
    for number, piece in enumerate(pieces):
        start = pl.multiple_of(place_ref[number] * rows, rows)
        out_ref[:, pl.ds(start, rows)] = turned(piece[...])


def turn(pieces, place):
    whole = pl.BlockSpec(memory_space=pltpu.VMEM)
    tokens = sum(p.shape[0] for p in pieces)
    features = pieces[0].shape[1]
    return call(
        turn_kernel,
        jax.ShapeDtypeStruct((features, tokens), BF16),
        flops=tokens * features * 1000,
        moved=tokens * features * 4,
        in_specs=[pl.BlockSpec(memory_space=pltpu.SMEM)] + [whole] * len(pieces),
        out_specs=whole,
    )(place, *pieces)


def states_kernel(
    ahead_ref, *refs,
):
    (*terms, xd_ref, yd_ref, proj_ref, near_low_ref, near_ref, far_ref) = refs
    total = terms[0][...].astype(F32)
    for term in terms[1:]:
        total += term[...].astype(F32)
    low = total.astype(BF16)
    proj_ref[...] = low
    state = dot(turned(low[:, :STATE]), xd_ref[...])
    adjoint = dot(turned(low[:, STATE:]), yd_ref[...])

    def put(near, far):
        near_low_ref[0] = near.astype(BF16)
        near_ref[0] = near
        far_ref[0] = far

    @pl.when(ahead_ref[0] != 0)
    def _():
        put(state, adjoint)

    @pl.when(ahead_ref[0] == 0)
    def _():
        put(adjoint, state)


def states(ahead, whole_terms, part_terms, xd, yd, first, groups, width):
    pair = pl.BlockSpec((SPAN, 2 * STATE), lambda g: (0, g))
    pair_from = pl.BlockSpec((SPAN, 2 * STATE), lambda g: (0, g + first))
    wide = pl.BlockSpec((SPAN, width), lambda g: (0, g + first))
    lead = lead_spec(STATE, width)
    shape = (groups, STATE, width)
    return call(
        states_kernel,
        (
            jax.ShapeDtypeStruct((SPAN, groups * 2 * STATE), BF16),
            jax.ShapeDtypeStruct(shape, BF16),
            jax.ShapeDtypeStruct(shape, F32),
            jax.ShapeDtypeStruct(shape, F32),
        ),
        flops=4 * SPAN * groups * width * STATE,
        moved=groups * SPAN * (width * 4 + 4 * STATE * 5),
        grid=(groups,),
        in_specs=[pl.BlockSpec(memory_space=pltpu.SMEM)]
        + [pair_from] * len(whole_terms) + [pair] * len(part_terms) + [wide, wide],
        out_specs=(pair, lead, lead, lead),
    )(ahead, *whole_terms, *part_terms, xd, yd)


def either(ahead_ref, near, far, body):
    @pl.when(ahead_ref[0] != 0)
    def _():
        body(near, far)

    @pl.when(ahead_ref[0] == 0)
    def _():
        body(far, near)


def added(refs):
    total = refs[0][0]
    for ref in refs[1:]:
        total += ref[0]
    return total


def grads_kernel(ahead_ref, proj_ref, xd_ref, yd_ref, mix_ref, mixt_ref, near_ref, *refs):
    (*far_refs, out_ref) = refs

    def body(start, adjoint):
        write, read = proj_ref[:, :STATE], proj_ref[:, STATE:]
        grad_write = dot(mixt_ref[0], read) + dot_nt(xd_ref[...], added(adjoint))
        grad_read = dot(mix_ref[0], write) + dot_nt(yd_ref[...], added(start))
        out_ref[:, :STATE] = grad_write.astype(BF16)
        out_ref[:, STATE:] = grad_read.astype(BF16)

    either(ahead_ref, [near_ref], far_refs, body)


def grads(ahead, proj, xd, yd, mix, mixt, near, far, first):
    groups, _, width = near.shape
    pair = pl.BlockSpec((SPAN, 2 * STATE), lambda g: (0, g))
    wide = pl.BlockSpec((SPAN, width), lambda g: (0, g + first))
    square = pl.BlockSpec((1, SPAN, SPAN), lambda g: (g + first, 0, 0))
    return call(
        grads_kernel,
        jax.ShapeDtypeStruct(proj.shape, BF16),
        flops=4 * SPAN * groups * (width + SPAN) * STATE,
        moved=groups * SPAN * width * 8,
        grid=(groups,),
        in_specs=[pl.BlockSpec(memory_space=pltpu.SMEM), pair, wide, wide, square, square]
        + [lead_spec(STATE, width)] * (1 + len(far)),
        out_specs=pair,
    )(ahead, proj, xd, yd, mix, mixt, near, *far)


def output_kernel(parts, hops, ahead_ref, x_ref, cum_ref, cumt_ref, skip_ref, *refs):
    (*refs, out_ref, proj_ref, start_ref) = refs
    projs, nears = refs[:parts], refs[parts : 2 * parts]
    fars = [refs[2 * parts + hops * p : 2 * parts + hops * (p + 1)] for p in range(parts)]
    each = projs[0].shape[1] // (2 * STATE)
    for group in range(parts * each):
        part, at = divmod(group, each)

        @pl.when(pl.program_id(0) == group)
        def _(part=part, at=at):
            proj_ref[...] = projs[part][:, at * 2 * STATE : (at + 1) * 2 * STATE]

            def put(start, _):
                start_ref[...] = added([ref.at[at : at + 1] for ref in start])

            either(ahead_ref, [nears[part]], fars[part], put)

    heads = cum_ref.shape[2]
    half = SPAN // 2
    wide = x_ref.shape[1] // heads * 2
    write = proj_ref[:, :STATE]
    read = proj_ref[:, STATE:]
    cum = cum_ref[0]
    cumt = cumt_ref[0]
    from_start = jnp.exp(cum)
    scores = dot_nt(read, write)
    top, low, end = scores[:half, :half], scores[half:, :half], scores[half:, half:]
    lane = lax.broadcasted_iota(jnp.int32, (half, wide), 1)
    for pair in range(heads // 2):
        a, b = 2 * pair, 2 * pair + 1
        cut = slice(pair * wide, (pair + 1) * wide)
        x = x_ref[:, cut]
        upper, lower = [], []
        for head in (a, b):
            decays = decays_of(cum[:, head : head + 1], cumt[head : head + 1, :])
            upper.append(dot((top * decays[0]).astype(BF16), x[:half]))
            lower.append(
                dot((low * decays[1]).astype(BF16), x[:half])
                + dot((end * decays[2]).astype(BF16), x[half:])
            )
        carried = dot(read, start_ref[:, cut]) * lanes_of(
            from_start[:, a : a + 1], from_start[:, b : b + 1], wide
        )
        rest = carried + skip_ref[:, cut] * x.astype(F32)
        out_ref[:half, cut] = (
            jnp.where(lane < wide // 2, upper[0], upper[1]) + rest[:half]
        ).astype(BF16)
        out_ref[half:, cut] = (
            jnp.where(lane < wide // 2, lower[0], lower[1]) + rest[half:]
        ).astype(BF16)


def output(ahead, values, cum, cumt, skip, projs, nears, fars):
    groups, _, heads = cum.shape
    width = values.shape[1] // groups
    wide = wide_spec(width)
    pieces = [*projs, *nears, *(ref for far in fars for ref in far)]
    return call(
        functools.partial(output_kernel, len(projs), len(fars[0])),
        jax.ShapeDtypeStruct(values.shape, BF16),
        flops=groups * heads * SPAN * SPAN * 2000,
        moved=values.size * 5,
        exps=groups * heads * SPAN * SPAN,
        grid=(groups,),
        in_specs=[
            pl.BlockSpec(memory_space=pltpu.SMEM), wide, lead_spec(SPAN, heads),
            lead_spec(heads, SPAN), pl.BlockSpec((1, width), lambda g: (0, g)),
        ]
        + [pl.BlockSpec(memory_space=pltpu.VMEM)] * len(pieces),
        out_specs=wide,
        scratch_shapes=[
            pltpu.VMEM((SPAN, 2 * STATE), BF16), pltpu.VMEM((STATE, width), BF16)
        ],
    )(ahead, values, cum, cumt, skip, *pieces)


def update_kernel(blocks, turned_ref, *refs):
    (*pieces, decayed_ref, keep_ref, weight_ref, sparse_ref, grad_ref) = refs
    parts = len(pieces) // blocks
    rows, width = pieces[0].shape

    @pl.when(pl.program_id(0) == 0)
    def _():
        for number, piece in enumerate(pieces):
            block, part = divmod(number, parts)
            grad_ref[block * rows : (block + 1) * rows, part * width : (part + 1) * width] = piece[
                ...
            ]

    total = dot(turned_ref[...], grad_ref[...])
    weight = decayed_ref[...] - (LEARN_RATE * WEIGHT_SCALE) * total
    weight_ref[...] = weight
    sparse_ref[...] = (weight * keep_ref[...].astype(F32)).astype(BF16)


def update(turned_hidden, grad_blocks, decayed, keep):
    rows, columns = decayed.shape
    tokens = turned_hidden.shape[1]
    step = min(rows, 256)
    full = pl.BlockSpec((step, columns), lambda i: (i, 0))
    pieces = [part for block in grad_blocks for part in block]
    return call(
        functools.partial(update_kernel, len(grad_blocks)),
        (jax.ShapeDtypeStruct((rows, columns), F32), jax.ShapeDtypeStruct((rows, columns), BF16)),
        flops=2 * tokens * rows * columns,
        moved=rows * columns * 12 + tokens * (rows + columns) * 2,
        grid=(rows // step,),
        in_specs=[pl.BlockSpec((step, tokens), lambda i: (i, 0))]
        + [pl.BlockSpec(piece.shape, lambda i: (0, 0)) for piece in pieces]
        + [full, full],
        out_specs=(full, full),
        scratch_shapes=[pltpu.VMEM((tokens, columns), BF16)],
    )(turned_hidden, *pieces, decayed, keep)


def held(after, *before):
    return lax.optimization_barrier((after, *before))[0]


def scalars(*values):
    return jnp.stack([jnp.asarray(v).astype(jnp.int32) for v in values])


def to_all(seq, distance):
    return [(source, (source + distance) % seq) for source in range(seq)]


def block_pairs(seq, near, same_core):
    return [
        (
            (z * 2 + x) * 2 + core,
            ((z + (x if near else 1 - x) + 2 * core) % seq * 2 + x) * 2
            + (core if same_core else 1 - core),
        )
        for z in range(seq)
        for x in range(2)
        for core in range(2)
    ]


def transpose_pairs(seq):
    pairs = []
    for z in range(seq):
        for layer in range(seq):
            distance = (z - layer) % seq
            pairs.append((z * seq + layer, layer * seq + distance % 2 * 2 + distance // 2))
    return pairs


SWAP = [(0, 1), (1, 0)]


def chain(own, own_low, decay, seq, step):
    arrived = jnp.zeros_like(own_low)
    message = own_low
    first = 0 if step > 0 else seq - 1
    for hop in range(seq - 1):
        source = first + hop * step
        if hop:
            message = (decay * arrived.astype(F32) + own).astype(BF16)
        arrived = arrived + lax.ppermute(message, "seq", [(source, source + step)])
    return arrived


def prepared(inner_values, log_decay, skip_gain, cotangent, groups):
    heads = log_decay.shape[1]
    logs = log_decay.reshape(SPAN, groups, heads // groups).transpose(1, 0, 2)
    logs_t = log_decay.T.reshape(groups, heads // groups, SPAN)
    skip = jnp.repeat(skip_gain, inner_values.shape[1] // heads)[None, :]
    return skip, before(inner_values, cotangent, logs, logs_t)


def on_device_general(
    seq, hidden, inner_values, log_decay, skip_gain, cotangent, master, mask_now, mask_next
):
    groups = master.shape[1] // (2 * STATE)
    effective, decayed, keep = weights(master, mask_now, mask_next)
    features = lax.all_gather(hidden, ("head", "sub"), axis=1, tiled=True)
    layer = lax.all_to_all(features, "seq", split_axis=1, concat_axis=0, tiled=True)
    skip, (xd, yd, mix, mixt, cum, cumt, decay) = prepared(
        inner_values, log_decay, skip_gain, cotangent, groups
    )
    part = dot(layer, effective).astype(BF16)
    terms = [lax.psum_scatter(part, "seq", scatter_dimension=0, tiled=True)]
    yes = scalars(1)
    proj, state_low, state, adjoint = states(yes, [], terms, xd, yd, 0, groups, decay.shape[2])
    start = chain(state, state_low, decay, seq, 1)
    adjoint_in = chain(adjoint, adjoint.astype(BF16), decay, seq, -1)
    grad = grads(yes, proj, xd, yd, mix, mixt, start, [adjoint_in], 0)
    blocks = [[lax.all_gather(grad, "seq", axis=0, tiled=True)]]
    ssd_output = output(
        yes, inner_values, cum, cumt, skip, [proj], [start], [[adjoint_in]]
    )
    return ssd_output, *update(layer.T, blocks, decayed, keep)


def on_device(
    seq, hidden, inner_values, log_decay, skip_gain, cotangent, master, mask_now, mask_next
):
    groups = master.shape[1] // (2 * STATE)
    z, x, core = (lax.axis_index(name) for name in ("seq", "head", "sub"))
    ahead = scalars(z < seq // 2)

    own = lax.ppermute(hidden, ("seq", "head", "sub"), transpose_pairs(seq))
    effective, decayed, keep = weights(master, mask_now, mask_next)
    skip, (xd, yd, mix, mixt, cum, cumt, decay) = prepared(
        inner_values, log_decay, skip_gain, cotangent, groups
    )
    sibling_effective = effective_of(
        lax.ppermute(master, "sub", SWAP), lax.ppermute(mask_now, "sub", SWAP)
    )
    own = held(own, effective, sibling_effective)

    axes = ("seq", "head", "sub")
    other = lax.ppermute(own, "head", SWAP)
    (same,), (cross,) = partials(own, effective, sibling_effective, 1)
    same = lax.ppermute(same, axes, block_pairs(seq, True, True))
    cross = lax.ppermute(held(cross, same), axes, block_pairs(seq, True, False))
    early = [same, cross]
    other = held(other, same)
    sames, crosses = partials(other, effective, sibling_effective, PARTS)
    late = []
    for same, cross in zip(sames, crosses):
        last = late[-1] if late else early
        same, cross = held(same, *last), held(cross, *last)
        late.append(
            [
                lax.ppermute(same, axes, block_pairs(seq, False, True)),
                lax.ppermute(cross, axes, block_pairs(seq, False, False)),
            ]
        )
    own, other = held(own, sames[0]), held(other, sames[0])
    pieces = (
        own, lax.ppermute(own, "sub", SWAP), other, lax.ppermute(other, "sub", SWAP)
    )
    place = scalars(x + 2 * core, x + 2 * (1 - core), 1 - x + 2 * core, 3 - x - 2 * core)
    turned_hidden = turn(pieces, place)

    each = groups // PARTS
    spans = range(PARTS)
    projs, messages, nears, fars = zip(
        *(
            states(ahead, early, late[p], xd, yd, p * each, each, decay.shape[2])
            for p in spans
        )
    )
    decays = [decay[p * each : (p + 1) * each] for p in spans]
    arrived = [[] for _ in spans]
    hops = (([(0, 1), (3, 2)], nears), ([(1, 2), (2, 1)], fars), ([(1, 0), (2, 3)], None))
    messages = list(messages)
    for pairs, own_terms in hops:
        for p in spans:
            message = messages[p]
            if p:
                message = held(message, arrived[p - 1][-1])
            arrived[p].append(lax.ppermute(message, "seq", pairs))
        for p in spans:
            if own_terms:
                carried = decays[p] * arrived[p][-1].astype(F32)
                messages[p] = (carried + own_terms[p]).astype(BF16)
    blocks = [[] for _ in range(seq)]
    for p in spans:
        grad = grads(
            ahead, projs[p], xd, yd, mix, mixt, arrived[p][0], arrived[p][1:], p * each
        )
        for distance in range(seq):
            pairs = to_all(seq, seq - distance)
            blocks[distance].append(lax.ppermute(grad, "seq", pairs) if distance else grad)

    ssd_output = output(
        ahead, inner_values, cum, cumt, skip,
        projs, [a[0] for a in arrived], [a[1:] for a in arrived],
    )
    new_weight, sparse_weight = update(turned_hidden, blocks, decayed, keep)
    return ssd_output, new_weight, sparse_weight


PARTS = 2


def solution(mesh):
    by_position = P(("grp", "seq"), ("head", "sub"))
    by_row = P("seq", ("head", "sub"))
    seq, head, sub = (mesh.shape[name] for name in ("seq", "head", "sub"))
    body = on_device if (seq, head, sub) == (4, 2, 2) else on_device_general
    return jax.shard_map(
        functools.partial(body, seq),
        mesh=mesh,
        in_specs=(
            by_position, by_position, by_position, P(("head", "sub")), by_position,
            by_row, by_row, by_row,
        ),
        out_specs=(by_position, by_position, by_position),
        check_vma=False,
    )
```

```python
import functools
import math

import jax
import jax.numpy as jnp
from jax import lax
from jax.experimental import pallas as pl
from jax.experimental.pallas import tpu as pltpu
from jax.sharding import PartitionSpec as P

D = 4096
STATE = 128
SPAN = 256
LEARN_RATE = 0.05
WEIGHT_DECAY = 10.0
WEIGHT_SCALE = 2.0 / math.sqrt(D)
KEEP_BITS = (0b000111, 0b011001, 0b101010, 0b110100)
OUT_OF_SIGHT = -1e30
MIB = 1024 * 1024

F32 = jnp.float32
BF16 = jnp.bfloat16
NT = (((1,), (1,)), ((), ()))


def call(kernel, out_shape, flops, moved, exps=0, vmem=16 * MIB, **more):
    return pl.pallas_call(
        kernel,
        out_shape=out_shape,
        compiler_params=pltpu.CompilerParams(vmem_limit_bytes=vmem),
        cost_estimate=pl.CostEstimate(flops=flops, bytes_accessed=moved, transcendentals=exps),
        **more,
    )


def dot(a, b):
    return jnp.dot(a, b, preferred_element_type=F32)


def dot_nt(a, b):
    return lax.dot_general(a, b, NT, preferred_element_type=F32)


def turned(a):
    return a.astype(F32).T.astype(BF16)


def expanded(codes, rows):
    spread = (
        lax.broadcasted_iota(jnp.int32, (rows, rows // 4), 0) // 4
        == lax.broadcasted_iota(jnp.int32, (rows, rows // 4), 1)
    ).astype(F32)
    code = dot(spread.astype(BF16), codes.astype(F32).astype(BF16)).astype(jnp.int32)
    place = lax.broadcasted_iota(jnp.int32, (rows, 1), 0) % 4
    bits = jnp.where(
        place < 2,
        jnp.where(place == 0, KEEP_BITS[0], KEEP_BITS[1]),
        jnp.where(place == 2, KEEP_BITS[2], KEEP_BITS[3]),
    )
    return lax.shift_right_logical(jnp.broadcast_to(bits, code.shape), code) & 1


def weights_kernel(master_ref, now_ref, next_ref, effective_ref, decayed_ref, keep_ref):
    rows = master_ref.shape[0]
    master = master_ref[...]
    kept = expanded(now_ref[...], rows) == 1
    effective_ref[...] = jnp.where(kept, master * WEIGHT_SCALE, 0.0).astype(BF16)
    decayed_ref[...] = jnp.where(kept, master, master * (1.0 - LEARN_RATE * WEIGHT_DECAY))
    keep_ref[...] = expanded(next_ref[...], rows).astype(F32).astype(BF16)


def weights(master, mask_now, mask_next):
    rows, columns = master.shape
    block = min(rows, 256)
    full = pl.BlockSpec((block, columns), lambda i: (i, 0))
    quarter = pl.BlockSpec((block // 4, columns), lambda i: (i, 0))
    return call(
        weights_kernel,
        (
            jax.ShapeDtypeStruct((rows, columns), BF16),
            jax.ShapeDtypeStruct((rows, columns), F32),
            jax.ShapeDtypeStruct((rows, columns), BF16),
        ),
        flops=rows * columns * 3000,
        moved=rows * columns * 14,
        grid=(rows // block,),
        in_specs=[full, quarter, quarter],
        out_specs=(full, full, full),
    )(master, mask_now, mask_next)


def effective_kernel(master_ref, now_ref, effective_ref):
    kept = expanded(now_ref[...], master_ref.shape[0]) == 1
    effective_ref[...] = jnp.where(kept, master_ref[...] * WEIGHT_SCALE, 0.0).astype(BF16)


def effective_of(master, mask_now):
    rows, columns = master.shape
    block = min(rows, 256)
    full = pl.BlockSpec((block, columns), lambda i: (i, 0))
    return call(
        effective_kernel,
        jax.ShapeDtypeStruct((rows, columns), BF16),
        flops=rows * columns * 3000,
        moved=rows * columns * 7,
        grid=(rows // block,),
        in_specs=[full, pl.BlockSpec((block // 4, columns), lambda i: (i, 0))],
        out_specs=full,
    )(master, mask_now)


def lanes_of(left, right, wide):
    lane = lax.broadcasted_iota(jnp.int32, (left.shape[0], wide), 1)
    return jnp.where(lane < wide // 2, left, right)


def decays_of(col, row):
    half = SPAN // 2
    causal = lax.broadcasted_iota(jnp.int32, (half, half), 0) >= lax.broadcasted_iota(
        jnp.int32, (half, half), 1
    )
    top = jnp.exp(jnp.where(causal, col[:half] - row[:, :half], OUT_OF_SIGHT))
    low = jnp.exp(col[half:] - row[:, :half])
    end = jnp.exp(jnp.where(causal, col[half:] - row[:, half:], OUT_OF_SIGHT))
    return top, low, end


def before_kernel(
    x_ref, dy_ref, log_ref, logt_ref,
    xd_ref, yd_ref, mix_ref, mixt_ref, cum_ref, cumt_ref, end_ref,
):
    heads = log_ref.shape[2]
    half = SPAN // 2
    wide = x_ref.shape[1] // heads * 2
    row = lax.broadcasted_iota(jnp.int32, (SPAN, SPAN), 0)
    col = lax.broadcasted_iota(jnp.int32, (SPAN, SPAN), 1)
    cum = jnp.dot(
        (row >= col).astype(F32), log_ref[0],
        precision=lax.Precision.HIGHEST, preferred_element_type=F32,
    )
    cumt = jnp.dot(
        logt_ref[0], (row <= col).astype(F32),
        precision=lax.Precision.HIGHEST, preferred_element_type=F32,
    )
    cum_ref[0] = cum
    cumt_ref[0] = cumt
    end = cum[SPAN - 1 :, :]
    from_start = jnp.exp(cum)
    to_end = jnp.exp(end - cum)
    whole = jnp.exp(end)
    mix = [jnp.zeros((half, half), F32) for _ in range(3)]
    lane = lax.broadcasted_iota(jnp.int32, (SPAN, wide), 1)
    for pair in range(heads // 2):
        a, b = 2 * pair, 2 * pair + 1
        cut = slice(pair * wide, (pair + 1) * wide)
        x = x_ref[:, cut]
        dy = dy_ref[:, cut]
        wide_dy = dy.astype(F32)
        xd_ref[:, cut] = (
            x.astype(F32) * lanes_of(to_end[:, a : a + 1], to_end[:, b : b + 1], wide)
        ).astype(BF16)
        yd_ref[:, cut] = (
            wide_dy * lanes_of(from_start[:, a : a + 1], from_start[:, b : b + 1], wide)
        ).astype(BF16)
        end_ref[0, :, cut] = lanes_of(whole[:, a : a + 1], whole[:, b : b + 1], wide)
        for head, mine in ((a, lane < wide // 2), (b, lane >= wide // 2)):
            one = jnp.where(mine, wide_dy, 0.0).astype(BF16)
            decays = decays_of(cum[:, head : head + 1], cumt[head : head + 1, :])
            mix[0] += dot_nt(one[:half], x[:half]) * decays[0]
            both = dot_nt(one[half:], x)
            mix[1] += both[:, :half] * decays[1]
            mix[2] += both[:, half:] * decays[2]
    nothing = jnp.zeros((half, half), BF16)
    top, low, end_mix = (m.astype(BF16) for m in mix)
    topt, lowt, end_mixt = (m.T.astype(BF16) for m in mix)
    mix_ref[0, :half, :half] = top
    mix_ref[0, :half, half:] = nothing
    mix_ref[0, half:, :half] = low
    mix_ref[0, half:, half:] = end_mix
    mixt_ref[0, :half, :half] = topt
    mixt_ref[0, :half, half:] = lowt
    mixt_ref[0, half:, :half] = nothing
    mixt_ref[0, half:, half:] = end_mixt


def wide_spec(width):
    return pl.BlockSpec((SPAN, width), lambda g: (0, g))


def lead_spec(*shape):
    return pl.BlockSpec((1, *shape), lambda g: (g, *(0 for _ in shape)))


def before(values, cotan, logs, logs_t):
    groups, _, heads = logs.shape
    width = values.shape[1] // groups
    wide = wide_spec(width)
    return call(
        before_kernel,
        (
            jax.ShapeDtypeStruct(values.shape, BF16),
            jax.ShapeDtypeStruct(values.shape, BF16),
            jax.ShapeDtypeStruct((groups, SPAN, SPAN), BF16),
            jax.ShapeDtypeStruct((groups, SPAN, SPAN), BF16),
            jax.ShapeDtypeStruct((groups, SPAN, heads), F32),
            jax.ShapeDtypeStruct((groups, heads, SPAN), F32),
            jax.ShapeDtypeStruct((groups, 1, width), F32),
        ),
        flops=groups * heads * SPAN * SPAN * 2500,
        moved=values.size * 8,
        exps=groups * heads * SPAN * SPAN,
        grid=(groups,),
        in_specs=[wide, wide, lead_spec(SPAN, heads), lead_spec(heads, SPAN)],
        out_specs=(
            wide, wide, lead_spec(SPAN, SPAN), lead_spec(SPAN, SPAN),
            lead_spec(SPAN, heads), lead_spec(heads, SPAN), lead_spec(1, width),
        ),
    )(values, cotan, logs, logs_t)


def partial_kernel(hidden_ref, weight_ref, sibling_weight_ref, out_ref, sibling_out_ref):
    out_ref[...] = dot(hidden_ref[...], weight_ref[...]).astype(BF16)
    sibling_out_ref[...] = dot(hidden_ref[...], sibling_weight_ref[...]).astype(BF16)


def partials(hidden, effective, sibling_effective):
    tokens, columns = hidden.shape[0], effective.shape[1]
    whole = pl.BlockSpec(memory_space=pltpu.VMEM)
    return call(
        partial_kernel,
        (jax.ShapeDtypeStruct((tokens, columns), BF16),) * 2,
        flops=4 * tokens * effective.size,
        moved=(hidden.size + 2 * effective.size + 2 * tokens * columns) * 2,
        in_specs=[whole] * 3,
        out_specs=(whole,) * 2,
    )(hidden, effective, sibling_effective)


def turn_kernel(hidden_ref, out_ref):
    out_ref[...] = turned(hidden_ref[...])


def turn(hidden):
    tokens, features = hidden.shape
    whole = pl.BlockSpec(memory_space=pltpu.VMEM)
    return call(
        turn_kernel,
        jax.ShapeDtypeStruct((features, tokens), BF16),
        flops=tokens * features * 2000,
        moved=tokens * features * 4,
        in_specs=[whole],
        out_specs=whole,
    )(hidden)


def states_kernel(
    ahead_ref, *refs,
):
    (*terms, xd_ref, yd_ref, proj_ref, near_low_ref, near_ref, far_ref) = refs
    total = terms[0][...].astype(F32)
    for term in terms[1:]:
        total += term[...].astype(F32)
    low = total.astype(BF16)
    proj_ref[...] = low
    state = dot(turned(low[:, :STATE]), xd_ref[...])
    adjoint = dot(turned(low[:, STATE:]), yd_ref[...])

    def put(near, far):
        near_low_ref[0] = near.astype(BF16)
        near_ref[0] = near
        far_ref[0] = far

    @pl.when(ahead_ref[0] != 0)
    def _():
        put(state, adjoint)

    @pl.when(ahead_ref[0] == 0)
    def _():
        put(adjoint, state)


def states(ahead, terms, xd, yd, first, groups, width):
    pair = pl.BlockSpec((SPAN, 2 * STATE), lambda g: (0, g))
    pair_from = pl.BlockSpec((SPAN, 2 * STATE), lambda g: (0, g + first))
    wide = pl.BlockSpec((SPAN, width), lambda g: (0, g + first))
    lead = lead_spec(STATE, width)
    shape = (groups, STATE, width)
    return call(
        states_kernel,
        (
            jax.ShapeDtypeStruct((SPAN, groups * 2 * STATE), BF16),
            jax.ShapeDtypeStruct(shape, BF16),
            jax.ShapeDtypeStruct(shape, F32),
            jax.ShapeDtypeStruct(shape, F32),
        ),
        flops=4 * SPAN * groups * width * STATE,
        moved=groups * SPAN * (width * 4 + 4 * STATE * 5),
        grid=(groups,),
        in_specs=[pl.BlockSpec(memory_space=pltpu.SMEM)]
        + [pair_from] * len(terms) + [wide, wide],
        out_specs=(pair, lead, lead, lead),
    )(ahead, *terms, xd, yd)


def either(ahead_ref, near, far, body):
    @pl.when(ahead_ref[0] != 0)
    def _():
        body(near, far)

    @pl.when(ahead_ref[0] == 0)
    def _():
        body(far, near)


def added(refs):
    total = refs[0][0]
    for ref in refs[1:]:
        total += ref[0]
    return total


def grads_kernel(ahead_ref, proj_ref, xd_ref, yd_ref, mix_ref, mixt_ref, near_ref, *refs):
    (*far_refs, out_ref) = refs

    def body(start, adjoint):
        write, read = proj_ref[:, :STATE], proj_ref[:, STATE:]
        grad_write = dot(mixt_ref[0], read) + dot_nt(xd_ref[...], added(adjoint))
        grad_read = dot(mix_ref[0], write) + dot_nt(yd_ref[...], added(start))
        out_ref[:, :STATE] = grad_write.astype(BF16)
        out_ref[:, STATE:] = grad_read.astype(BF16)

    either(ahead_ref, [near_ref], far_refs, body)


def grads(ahead, proj, xd, yd, mix, mixt, near, far, first):
    groups, _, width = near.shape
    pair = pl.BlockSpec((SPAN, 2 * STATE), lambda g: (0, g))
    wide = pl.BlockSpec((SPAN, width), lambda g: (0, g + first))
    square = pl.BlockSpec((1, SPAN, SPAN), lambda g: (g + first, 0, 0))
    return call(
        grads_kernel,
        jax.ShapeDtypeStruct(proj.shape, BF16),
        flops=4 * SPAN * groups * (width + SPAN) * STATE,
        moved=groups * SPAN * width * 8,
        grid=(groups,),
        in_specs=[pl.BlockSpec(memory_space=pltpu.SMEM), pair, wide, wide, square, square]
        + [lead_spec(STATE, width)] * (1 + len(far)),
        out_specs=pair,
    )(ahead, proj, xd, yd, mix, mixt, near, *far)


def output_kernel(parts, hops, ahead_ref, x_ref, cum_ref, cumt_ref, skip_ref, *refs):
    (*refs, out_ref, proj_ref, start_ref) = refs
    projs, nears = refs[:parts], refs[parts : 2 * parts]
    fars = [refs[2 * parts + hops * p : 2 * parts + hops * (p + 1)] for p in range(parts)]
    each = projs[0].shape[1] // (2 * STATE)
    for group in range(parts * each):
        part, at = divmod(group, each)

        @pl.when(pl.program_id(0) == group)
        def _(part=part, at=at):
            proj_ref[...] = projs[part][:, at * 2 * STATE : (at + 1) * 2 * STATE]

            def put(start, _):
                start_ref[...] = added([ref.at[at : at + 1] for ref in start])

            either(ahead_ref, [nears[part]], fars[part], put)

    heads = cum_ref.shape[2]
    half = SPAN // 2
    wide = x_ref.shape[1] // heads * 2
    write = proj_ref[:, :STATE]
    read = proj_ref[:, STATE:]
    cum = cum_ref[0]
    cumt = cumt_ref[0]
    from_start = jnp.exp(cum)
    scores = dot_nt(read, write)
    top, low, end = scores[:half, :half], scores[half:, :half], scores[half:, half:]
    lane = lax.broadcasted_iota(jnp.int32, (half, wide), 1)
    for pair in range(heads // 2):
        a, b = 2 * pair, 2 * pair + 1
        cut = slice(pair * wide, (pair + 1) * wide)
        x = x_ref[:, cut]
        upper, lower = [], []
        for head in (a, b):
            decays = decays_of(cum[:, head : head + 1], cumt[head : head + 1, :])
            upper.append(dot((top * decays[0]).astype(BF16), x[:half]))
            lower.append(
                dot((low * decays[1]).astype(BF16), x[:half])
                + dot((end * decays[2]).astype(BF16), x[half:])
            )
        carried = dot(read, start_ref[:, cut]) * lanes_of(
            from_start[:, a : a + 1], from_start[:, b : b + 1], wide
        )
        skip = skip_ref[0]
        gain = lanes_of(skip[:, a : a + 1], skip[:, b : b + 1], wide)
        rest = carried + gain * x.astype(F32)
        out_ref[:half, cut] = (
            jnp.where(lane < wide // 2, upper[0], upper[1]) + rest[:half]
        ).astype(BF16)
        out_ref[half:, cut] = (
            jnp.where(lane < wide // 2, lower[0], lower[1]) + rest[half:]
        ).astype(BF16)


def output(ahead, values, cum, cumt, skip, projs, nears, fars):
    groups, _, heads = cum.shape
    width = values.shape[1] // groups
    wide = wide_spec(width)
    pieces = [*projs, *nears, *(ref for far in fars for ref in far)]
    return call(
        functools.partial(output_kernel, len(projs), len(fars[0])),
        jax.ShapeDtypeStruct(values.shape, BF16),
        flops=groups * heads * SPAN * SPAN * 2000,
        moved=values.size * 5,
        exps=groups * heads * SPAN * SPAN,
        grid=(groups,),
        in_specs=[
            pl.BlockSpec(memory_space=pltpu.SMEM), wide, lead_spec(SPAN, heads),
            lead_spec(heads, SPAN), lead_spec(1, heads),
        ]
        + [pl.BlockSpec(memory_space=pltpu.VMEM)] * len(pieces),
        out_specs=wide,
        scratch_shapes=[
            pltpu.VMEM((SPAN, 2 * STATE), BF16), pltpu.VMEM((STATE, width), BF16)
        ],
    )(ahead, values, cum, cumt, skip, *pieces)


def update_kernel(blocks, spots, place_ref, *refs):
    turned_refs, pieces = refs[:spots], refs[spots:-5]
    decayed_ref, keep_ref, weight_ref, sparse_ref, grad_ref = refs[-5:]
    parts = len(pieces) // blocks
    rows, width = pieces[0].shape

    @pl.when(pl.program_id(0) == 0)
    def _():
        for number, piece in enumerate(pieces):
            block, part = divmod(number, parts)
            start = pl.multiple_of(place_ref[block] * rows, rows)
            grad_ref[pl.ds(start, rows), part * width : (part + 1) * width] = piece[...]

    total = dot(turned_refs[0][...], grad_ref[:rows, :])
    for spot in range(1, spots):
        total += dot(turned_refs[spot][...], grad_ref[spot * rows : (spot + 1) * rows, :])
    weight = decayed_ref[...] - (LEARN_RATE * WEIGHT_SCALE) * total
    weight_ref[...] = weight
    sparse_ref[...] = (weight * keep_ref[...].astype(F32)).astype(BF16)


def update(place, turned_hidden, grad_blocks, decayed, keep, vmem):
    rows, columns = decayed.shape
    tokens = turned_hidden[0].shape[1]
    step = min(rows, 256)
    full = pl.BlockSpec((step, columns), lambda i: (i, 0))
    pieces = [part for block in grad_blocks for part in block]
    return call(
        functools.partial(update_kernel, len(grad_blocks), len(turned_hidden)),
        (jax.ShapeDtypeStruct((rows, columns), F32), jax.ShapeDtypeStruct((rows, columns), BF16)),
        flops=2 * len(turned_hidden) * tokens * rows * columns,
        moved=rows * columns * 12 + len(turned_hidden) * tokens * (rows + columns) * 2,
        vmem=vmem,
        grid=(rows // step,),
        in_specs=[pl.BlockSpec(memory_space=pltpu.SMEM)]
        + [pl.BlockSpec((step, tokens), lambda i: (i, 0))] * len(turned_hidden)
        + [pl.BlockSpec(piece.shape, lambda i: (0, 0)) for piece in pieces]
        + [full, full],
        out_specs=(full, full),
        scratch_shapes=[pltpu.VMEM((len(turned_hidden) * tokens, columns), BF16)],
    )(place, *turned_hidden, *pieces, decayed, keep)


def held(after, *before):
    return lax.optimization_barrier((after, *before))[0]


def scalars(*values):
    return jnp.stack([jnp.asarray(v).astype(jnp.int32) for v in values])


def to_all(seq, distance):
    return [(source, (source + distance) % seq) for source in range(seq)]


def block_pairs(seq, near, same_core):
    return [
        (
            (z * 2 + x) * 2 + core,
            ((z + (x if near else 1 - x) + 2 * core) % seq * 2 + x) * 2
            + (core if same_core else 1 - core),
        )
        for z in range(seq)
        for x in range(2)
        for core in range(2)
    ]


def transpose_pairs(seq):
    change, straight, changed = [], [], []
    for z in range(seq):
        for x in range(2):
            for core in range(2):
                layer = 2 * x + core
                distance = (z - layer) % seq
                here = (z * 2 + x) * 2 + core
                beside = (z * 2 + 1 - x) * 2 + core
                target = (layer * 2 + distance % 2) * 2 + distance // 2
                if distance % 2 == x:
                    straight.append((here, target))
                else:
                    change.append((here, beside))
                    changed.append((beside, target))
    return change, straight, changed


SWAP = [(0, 1), (1, 0)]


def chain(own, own_low, decay, seq, step):
    arrived = jnp.zeros_like(own_low)
    message = own_low
    first = 0 if step > 0 else seq - 1
    for hop in range(seq - 1):
        source = first + hop * step
        if hop:
            message = (decay * arrived.astype(F32) + own).astype(BF16)
        arrived = arrived + lax.ppermute(message, "seq", [(source, source + step)])
    return arrived


def prepared(inner_values, log_decay, skip_gain, cotangent, groups):
    heads = log_decay.shape[1]
    logs = log_decay.reshape(SPAN, groups, heads // groups).transpose(1, 0, 2)
    logs_t = log_decay.T.reshape(groups, heads // groups, SPAN)
    skip = skip_gain.reshape(groups, 1, heads // groups)
    return skip, before(inner_values, cotangent, logs, logs_t)


def on_device_general(
    seq, hidden, inner_values, log_decay, skip_gain, cotangent, master, mask_now, mask_next
):
    groups = master.shape[1] // (2 * STATE)
    effective, decayed, keep = weights(master, mask_now, mask_next)
    features = lax.all_gather(hidden, ("head", "sub"), axis=1, tiled=True)
    layer = lax.all_to_all(features, "seq", split_axis=1, concat_axis=0, tiled=True)
    skip, (xd, yd, mix, mixt, cum, cumt, decay) = prepared(
        inner_values, log_decay, skip_gain, cotangent, groups
    )
    part = dot(layer, effective).astype(BF16)
    terms = [lax.psum_scatter(part, "seq", scatter_dimension=0, tiled=True)]
    yes = scalars(1)
    proj, state_low, state, adjoint = states(yes, terms, xd, yd, 0, groups, decay.shape[2])
    start = chain(state, state_low, decay, seq, 1)
    adjoint_in = chain(adjoint, adjoint.astype(BF16), decay, seq, -1)
    grad = grads(yes, proj, xd, yd, mix, mixt, start, [adjoint_in], 0)
    blocks = [[lax.all_gather(grad, "seq", axis=0, tiled=True)]]
    ssd_output = output(
        yes, inner_values, cum, cumt, skip, [proj], [start], [[adjoint_in]]
    )
    place = scalars(0)
    return ssd_output, *update(place, [layer.T], blocks, decayed, keep, 40 * MIB)


def on_device(
    seq, hidden, inner_values, log_decay, skip_gain, cotangent, master, mask_now, mask_next
):
    groups = master.shape[1] // (2 * STATE)
    z, x, core = (lax.axis_index(name) for name in ("seq", "head", "sub"))
    ahead = scalars(z < seq // 2)

    axes = ("seq", "head", "sub")
    change, straight, changed = transpose_pairs(seq)
    beside = lax.ppermute(hidden, axes, change)
    own = lax.ppermute(hidden, axes, straight)
    own = own + lax.ppermute(beside, axes, changed)

    effective, decayed, keep = weights(master, mask_now, mask_next)
    sibling_effective = effective_of(
        lax.ppermute(master, "sub", SWAP), lax.ppermute(mask_now, "sub", SWAP)
    )
    skip, (xd, yd, mix, mixt, cum, cumt, decay) = prepared(
        inner_values, log_decay, skip_gain, cotangent, groups
    )
    own = held(own, effective, sibling_effective)

    other = lax.ppermute(own, "head", SWAP)
    same, cross = partials(own, effective, sibling_effective)
    terms = [
        lax.ppermute(same, axes, block_pairs(seq, True, True)),
        lax.ppermute(cross, axes, block_pairs(seq, True, False)),
    ]
    own_turned = turn(held(own, same))
    other = held(other, xd, own_turned, *terms)
    same, cross = partials(other, effective, sibling_effective)
    terms += [
        lax.ppermute(same, axes, block_pairs(seq, False, True)),
        lax.ppermute(cross, axes, block_pairs(seq, False, False)),
    ]
    each = groups // PARTS
    spans = range(PARTS)
    projs, messages, nears, fars = zip(
        *(
            states(ahead, terms, xd, yd, p * each, each, decay.shape[2])
            for p in spans
        )
    )
    other_turned = turn(held(other, nears[0]))
    own_turned = held(own_turned, nears[0])
    turned_hidden = [
        own_turned, lax.ppermute(own_turned, "sub", SWAP),
        other_turned, lax.ppermute(other_turned, "sub", SWAP),
    ]
    decays = [decay[p * each : (p + 1) * each] for p in spans]
    arrived = [[] for _ in spans]
    hops = (([(0, 1), (3, 2)], nears), ([(1, 2), (2, 1)], fars), ([(1, 0), (2, 3)], None))
    messages = list(messages)
    for pairs, own_terms in hops:
        for p in spans:
            message = messages[p]
            if p:
                message = held(message, arrived[p - 1][-1])
            arrived[p].append(lax.ppermute(message, "seq", pairs))
        for p in spans:
            if own_terms:
                carried = decays[p] * arrived[p][-1].astype(F32)
                messages[p] = (carried + own_terms[p]).astype(BF16)
    blocks = [[] for _ in range(seq)]
    for p in spans:
        grad = grads(
            ahead, projs[p], xd, yd, mix, mixt, arrived[p][0], arrived[p][1:], p * each
        )
        for distance in range(seq):
            pairs = to_all(seq, seq - distance)
            blocks[distance].append(lax.ppermute(grad, "seq", pairs) if distance else grad)

    ssd_output = output(
        ahead, inner_values, cum, cumt, skip,
        projs, [a[0] for a in arrived], [a[1:] for a in arrived],
    )
    place = scalars(*(2 * ((d - x) % 2) + (core != d // 2) for d in range(seq)))
    new_weight, sparse_weight = update(
        place, turned_hidden, blocks, decayed, keep, 16 * MIB
    )
    return ssd_output, new_weight, sparse_weight


PARTS = 2


def solution(mesh):
    by_position = P(("grp", "seq"), ("head", "sub"))
    by_row = P("seq", ("head", "sub"))
    seq, head, sub = (mesh.shape[name] for name in ("seq", "head", "sub"))
    body = on_device if (seq, head, sub) == (4, 2, 2) else on_device_general
    return jax.shard_map(
        functools.partial(body, seq),
        mesh=mesh,
        in_specs=(
            by_position, by_position, by_position, P(("head", "sub")), by_position,
            by_row, by_row, by_row,
        ),
        out_specs=(by_position, by_position, by_position),
        check_vma=False,
    )
```

```python
import functools
import math

import jax
import jax.numpy as jnp
from jax import lax
from jax.experimental import pallas as pl
from jax.experimental.pallas import tpu as pltpu
from jax.sharding import PartitionSpec as P

D = 4096
STATE = 128
SPAN = 256
LEARN_RATE = 0.05
WEIGHT_DECAY = 10.0
WEIGHT_SCALE = 2.0 / math.sqrt(D)
KEEP_BITS = (0b000111, 0b011001, 0b101010, 0b110100)
OUT_OF_SIGHT = -1e30
MIB = 1024 * 1024

F32 = jnp.float32
BF16 = jnp.bfloat16
NT = (((1,), (1,)), ((), ()))


def call(kernel, out_shape, flops, moved, exps=0, vmem=16 * MIB, **more):
    return pl.pallas_call(
        kernel,
        out_shape=out_shape,
        compiler_params=pltpu.CompilerParams(vmem_limit_bytes=vmem),
        cost_estimate=pl.CostEstimate(flops=flops, bytes_accessed=moved, transcendentals=exps),
        **more,
    )


def dot(a, b):
    return jnp.dot(a, b, preferred_element_type=F32)


def dot_nt(a, b):
    return lax.dot_general(a, b, NT, preferred_element_type=F32)


def turned(a):
    return a.astype(F32).T.astype(BF16)


def expanded(codes, rows):
    spread = (
        lax.broadcasted_iota(jnp.int32, (rows, rows // 4), 0) // 4
        == lax.broadcasted_iota(jnp.int32, (rows, rows // 4), 1)
    ).astype(F32)
    code = dot(spread.astype(BF16), codes.astype(F32).astype(BF16)).astype(jnp.int32)
    place = lax.broadcasted_iota(jnp.int32, (rows, 1), 0) % 4
    bits = jnp.where(
        place < 2,
        jnp.where(place == 0, KEEP_BITS[0], KEEP_BITS[1]),
        jnp.where(place == 2, KEEP_BITS[2], KEEP_BITS[3]),
    )
    return lax.shift_right_logical(jnp.broadcast_to(bits, code.shape), code) & 1


def weights_kernel(master_ref, now_ref, next_ref, effective_ref, decayed_ref, keep_ref):
    rows = master_ref.shape[0]
    master = master_ref[...]
    kept = expanded(now_ref[...], rows) == 1
    effective_ref[...] = jnp.where(kept, master * WEIGHT_SCALE, 0.0).astype(BF16)
    decayed_ref[...] = jnp.where(kept, master, master * (1.0 - LEARN_RATE * WEIGHT_DECAY))
    keep_ref[...] = expanded(next_ref[...], rows).astype(F32).astype(BF16)


def weights(master, mask_now, mask_next):
    rows, columns = master.shape
    block = min(rows, 256)
    full = pl.BlockSpec((block, columns), lambda i: (i, 0))
    quarter = pl.BlockSpec((block // 4, columns), lambda i: (i, 0))
    return call(
        weights_kernel,
        (
            jax.ShapeDtypeStruct((rows, columns), BF16),
            jax.ShapeDtypeStruct((rows, columns), F32),
            jax.ShapeDtypeStruct((rows, columns), BF16),
        ),
        flops=rows * columns * 3000,
        moved=rows * columns * 14,
        grid=(rows // block,),
        in_specs=[full, quarter, quarter],
        out_specs=(full, full, full),
    )(master, mask_now, mask_next)


def effective_kernel(master_ref, now_ref, effective_ref):
    kept = expanded(now_ref[...], master_ref.shape[0]) == 1
    effective_ref[...] = jnp.where(kept, master_ref[...] * WEIGHT_SCALE, 0.0).astype(BF16)


def effective_of(master, mask_now):
    rows, columns = master.shape
    block = min(rows, 256)
    full = pl.BlockSpec((block, columns), lambda i: (i, 0))
    return call(
        effective_kernel,
        jax.ShapeDtypeStruct((rows, columns), BF16),
        flops=rows * columns * 3000,
        moved=rows * columns * 7,
        grid=(rows // block,),
        in_specs=[full, pl.BlockSpec((block // 4, columns), lambda i: (i, 0))],
        out_specs=full,
    )(master, mask_now)


def lanes_of(left, right, wide):
    lane = lax.broadcasted_iota(jnp.int32, (left.shape[0], wide), 1)
    return jnp.where(lane < wide // 2, left, right)


def decays_of(col, row):
    half = SPAN // 2
    causal = lax.broadcasted_iota(jnp.int32, (half, half), 0) >= lax.broadcasted_iota(
        jnp.int32, (half, half), 1
    )
    top = jnp.exp(jnp.where(causal, col[:half] - row[:, :half], OUT_OF_SIGHT))
    low = jnp.exp(col[half:] - row[:, :half])
    end = jnp.exp(jnp.where(causal, col[half:] - row[:, half:], OUT_OF_SIGHT))
    return top, low, end


def before_kernel(
    x_ref, dy_ref, logt_ref,
    xd_ref, yd_ref, mix_ref, mixt_ref, cum_ref, cumt_ref, end_ref, tall_ref,
):
    heads = cum_ref.shape[2]
    half = SPAN // 2
    wide = x_ref.shape[1] // heads * 2
    row = lax.broadcasted_iota(jnp.int32, (SPAN, SPAN), 0)
    col = lax.broadcasted_iota(jnp.int32, (SPAN, SPAN), 1)
    first = pl.multiple_of(pl.program_id(0) * heads, heads)
    cumt = jnp.dot(
        logt_ref[pl.ds(first, heads), :], (row <= col).astype(F32),
        precision=lax.Precision.HIGHEST, preferred_element_type=F32,
    )
    tall_ref[...] = jnp.zeros_like(tall_ref)
    tall_ref[:heads, :] = cumt
    cum = tall_ref[...].T[:, :heads]
    cum_ref[0] = cum
    cumt_ref[0] = cumt
    end = cum[SPAN - 1 :, :]
    from_start = jnp.exp(cum)
    to_end = jnp.exp(end - cum)
    whole = jnp.exp(end)
    mix = [jnp.zeros((half, half), F32) for _ in range(3)]
    lane = lax.broadcasted_iota(jnp.int32, (SPAN, wide), 1)
    for pair in range(heads // 2):
        a, b = 2 * pair, 2 * pair + 1
        cut = slice(pair * wide, (pair + 1) * wide)
        x = x_ref[:, cut]
        dy = dy_ref[:, cut]
        wide_dy = dy.astype(F32)
        xd_ref[:, cut] = (
            x.astype(F32) * lanes_of(to_end[:, a : a + 1], to_end[:, b : b + 1], wide)
        ).astype(BF16)
        yd_ref[:, cut] = (
            wide_dy * lanes_of(from_start[:, a : a + 1], from_start[:, b : b + 1], wide)
        ).astype(BF16)
        end_ref[0, :, cut] = lanes_of(whole[:, a : a + 1], whole[:, b : b + 1], wide)
        for head, mine in ((a, lane < wide // 2), (b, lane >= wide // 2)):
            one = jnp.where(mine, wide_dy, 0.0).astype(BF16)
            decays = decays_of(cum[:, head : head + 1], cumt[head : head + 1, :])
            mix[0] += dot_nt(one[:half], x[:half]) * decays[0]
            both = dot_nt(one[half:], x)
            mix[1] += both[:, :half] * decays[1]
            mix[2] += both[:, half:] * decays[2]
    nothing = jnp.zeros((half, half), BF16)
    top, low, end_mix = (m.astype(BF16) for m in mix)
    topt, lowt, end_mixt = (m.T.astype(BF16) for m in mix)
    mix_ref[0, :half, :half] = top
    mix_ref[0, :half, half:] = nothing
    mix_ref[0, half:, :half] = low
    mix_ref[0, half:, half:] = end_mix
    mixt_ref[0, :half, :half] = topt
    mixt_ref[0, :half, half:] = lowt
    mixt_ref[0, half:, :half] = nothing
    mixt_ref[0, half:, half:] = end_mixt


def wide_spec(width):
    return pl.BlockSpec((SPAN, width), lambda g: (0, g))


def lead_spec(*shape):
    return pl.BlockSpec((1, *shape), lambda g: (g, *(0 for _ in shape)))


def before(values, cotan, logs_t, groups):
    heads = logs_t.shape[0] // groups
    width = values.shape[1] // groups
    wide = wide_spec(width)
    return call(
        before_kernel,
        (
            jax.ShapeDtypeStruct(values.shape, BF16),
            jax.ShapeDtypeStruct(values.shape, BF16),
            jax.ShapeDtypeStruct((groups, SPAN, SPAN), BF16),
            jax.ShapeDtypeStruct((groups, SPAN, SPAN), BF16),
            jax.ShapeDtypeStruct((groups, SPAN, heads), F32),
            jax.ShapeDtypeStruct((groups, heads, SPAN), F32),
            jax.ShapeDtypeStruct((groups, 1, width), F32),
        ),
        flops=groups * heads * SPAN * SPAN * 2500,
        moved=values.size * 8,
        exps=groups * heads * SPAN * SPAN,
        grid=(groups,),
        in_specs=[wide, wide, pl.BlockSpec(logs_t.shape, lambda g: (0, 0))],
        out_specs=(
            wide, wide, lead_spec(SPAN, SPAN), lead_spec(SPAN, SPAN),
            lead_spec(SPAN, heads), lead_spec(heads, SPAN), lead_spec(1, width),
        ),
        scratch_shapes=[pltpu.VMEM((STATE, SPAN), F32)],
    )(values, cotan, logs_t)


def partial_kernel(hidden_ref, weight_ref, sibling_weight_ref, out_ref, sibling_out_ref):
    out_ref[...] = dot(hidden_ref[...], weight_ref[...]).astype(BF16)
    sibling_out_ref[...] = dot(hidden_ref[...], sibling_weight_ref[...]).astype(BF16)


def partials(hidden, effective, sibling_effective):
    tokens, columns = hidden.shape[0], effective.shape[1]
    whole = pl.BlockSpec(memory_space=pltpu.VMEM)
    return call(
        partial_kernel,
        (jax.ShapeDtypeStruct((tokens, columns), BF16),) * 2,
        flops=4 * tokens * effective.size,
        moved=(hidden.size + 2 * effective.size + 2 * tokens * columns) * 2,
        in_specs=[whole] * 3,
        out_specs=(whole,) * 2,
    )(hidden, effective, sibling_effective)


def turn_kernel(hidden_ref, out_ref):
    out_ref[...] = turned(hidden_ref[...])


def turn(hidden):
    tokens, features = hidden.shape
    whole = pl.BlockSpec(memory_space=pltpu.VMEM)
    return call(
        turn_kernel,
        jax.ShapeDtypeStruct((features, tokens), BF16),
        flops=tokens * features * 2000,
        moved=tokens * features * 4,
        in_specs=[whole],
        out_specs=whole,
    )(hidden)


def either(ahead, first, second, body):
    if ahead:
        return body(first, second)
    lower = lax.axis_index("seq") < lax.axis_size("seq") // 2

    @pl.when(lower)
    def _():
        body(first, second)

    @pl.when(jnp.logical_not(lower))
    def _():
        body(second, first)


def states_kernel(both, *refs):
    (*terms, xd_ref, yd_ref, proj_ref, near_low_ref, near_ref, far_ref) = refs
    total = terms[0][...].astype(F32)
    for term in terms[1:]:
        total += term[...].astype(F32)
    low = total.astype(BF16)
    proj_ref[...] = low
    state = dot(turned(low[:, :STATE]), xd_ref[...])
    adjoint = dot(turned(low[:, STATE:]), yd_ref[...])

    def put(near, far):
        near_low_ref[0] = near.astype(BF16)
        near_ref[0] = near
        far_ref[0] = far

    either(both, state, adjoint, put)


def states(ahead, terms, xd, yd, first, groups, width):
    pair = pl.BlockSpec((SPAN, 2 * STATE), lambda g: (0, g))
    pair_from = pl.BlockSpec((SPAN, 2 * STATE), lambda g: (0, g + first))
    wide = pl.BlockSpec((SPAN, width), lambda g: (0, g + first))
    lead = lead_spec(STATE, width)
    shape = (groups, STATE, width)
    return call(
        functools.partial(states_kernel, ahead),
        (
            jax.ShapeDtypeStruct((SPAN, groups * 2 * STATE), BF16),
            jax.ShapeDtypeStruct(shape, BF16),
            jax.ShapeDtypeStruct(shape, F32),
            jax.ShapeDtypeStruct(shape, F32),
        ),
        flops=4 * SPAN * groups * width * STATE,
        moved=groups * SPAN * (width * 4 + 4 * STATE * 5),
        grid=(groups,),
        in_specs=[pair_from] * len(terms) + [wide, wide],
        out_specs=(pair, lead, lead, lead),
    )(*terms, xd, yd)


def added(refs):
    total = refs[0][0]
    for ref in refs[1:]:
        total += ref[0]
    return total


def message_kernel(decay_ref, arrived_ref, own_ref, out_ref):
    out_ref[0] = (decay_ref[0] * arrived_ref[0].astype(F32) + own_ref[0]).astype(BF16)


def handed_on(decay, arrived, own, first):
    groups, _, width = arrived.shape
    lead = lead_spec(STATE, width)
    return call(
        message_kernel,
        jax.ShapeDtypeStruct(arrived.shape, BF16),
        flops=2 * arrived.size,
        moved=8 * arrived.size,
        grid=(groups,),
        in_specs=[pl.BlockSpec((1, 1, width), lambda g: (g + first, 0, 0)), lead, lead],
        out_specs=lead,
    )(decay, arrived, own)


def grads_kernel(ahead, proj_ref, xd_ref, yd_ref, mix_ref, mixt_ref, near_ref, *refs):
    (*far_refs, out_ref) = refs

    def body(start, adjoint):
        write, read = proj_ref[:, :STATE], proj_ref[:, STATE:]
        grad_write = dot(mixt_ref[0], read) + dot_nt(xd_ref[...], added(adjoint))
        grad_read = dot(mix_ref[0], write) + dot_nt(yd_ref[...], added(start))
        out_ref[:, :STATE] = grad_write.astype(BF16)
        out_ref[:, STATE:] = grad_read.astype(BF16)

    either(ahead, [near_ref], far_refs, body)


def grads(ahead, proj, xd, yd, mix, mixt, near, far, first):
    groups, _, width = near.shape
    pair = pl.BlockSpec((SPAN, 2 * STATE), lambda g: (0, g))
    wide = pl.BlockSpec((SPAN, width), lambda g: (0, g + first))
    square = pl.BlockSpec((1, SPAN, SPAN), lambda g: (g + first, 0, 0))
    return call(
        functools.partial(grads_kernel, ahead),
        jax.ShapeDtypeStruct(proj.shape, BF16),
        flops=4 * SPAN * groups * (width + SPAN) * STATE,
        moved=groups * SPAN * width * 8,
        grid=(groups,),
        in_specs=[pair, wide, wide, square, square]
        + [lead_spec(STATE, width)] * (1 + len(far)),
        out_specs=pair,
    )(proj, xd, yd, mix, mixt, near, *far)


def output_kernel(parts, hops, ahead, skip_ref, x_ref, cum_ref, cumt_ref, *refs):
    (*refs, out_ref, proj_ref, start_ref) = refs
    projs, nears = refs[:parts], refs[parts : 2 * parts]
    fars = [refs[2 * parts + hops * p : 2 * parts + hops * (p + 1)] for p in range(parts)]
    each = projs[0].shape[1] // (2 * STATE)
    for group in range(parts * each):
        part, at = divmod(group, each)

        @pl.when(pl.program_id(0) == group)
        def _(part=part, at=at):
            proj_ref[...] = projs[part][:, at * 2 * STATE : (at + 1) * 2 * STATE]

            def put(start, _):
                start_ref[...] = added([ref.at[at : at + 1] for ref in start])

            either(ahead, [nears[part]], fars[part], put)

    heads = cum_ref.shape[2]
    half = SPAN // 2
    wide = x_ref.shape[1] // heads * 2
    write = proj_ref[:, :STATE]
    read = proj_ref[:, STATE:]
    cum = cum_ref[0]
    cumt = cumt_ref[0]
    from_start = jnp.exp(cum)
    scores = dot_nt(read, write)
    top, low, end = scores[:half, :half], scores[half:, :half], scores[half:, half:]
    lane = lax.broadcasted_iota(jnp.int32, (half, wide), 1)
    for pair in range(heads // 2):
        a, b = 2 * pair, 2 * pair + 1
        cut = slice(pair * wide, (pair + 1) * wide)
        x = x_ref[:, cut]
        upper, lower = [], []
        for head in (a, b):
            decays = decays_of(cum[:, head : head + 1], cumt[head : head + 1, :])
            upper.append(dot((top * decays[0]).astype(BF16), x[:half]))
            lower.append(
                dot((low * decays[1]).astype(BF16), x[:half])
                + dot((end * decays[2]).astype(BF16), x[half:])
            )
        carried = dot(read, start_ref[:, cut]) * lanes_of(
            from_start[:, a : a + 1], from_start[:, b : b + 1], wide
        )
        head = pl.program_id(0) * heads + a
        gain = jnp.where(
            lax.broadcasted_iota(jnp.int32, (1, wide), 1) < wide // 2,
            skip_ref[head], skip_ref[head + 1],
        )
        rest = carried + gain * x.astype(F32)
        out_ref[:half, cut] = (
            jnp.where(lane < wide // 2, upper[0], upper[1]) + rest[:half]
        ).astype(BF16)
        out_ref[half:, cut] = (
            jnp.where(lane < wide // 2, lower[0], lower[1]) + rest[half:]
        ).astype(BF16)


def output(ahead, values, cum, cumt, skip, projs, nears, fars):
    groups, _, heads = cum.shape
    width = values.shape[1] // groups
    wide = wide_spec(width)
    pieces = [*projs, *nears, *(ref for far in fars for ref in far)]
    return call(
        functools.partial(output_kernel, len(projs), len(fars[0]), ahead),
        jax.ShapeDtypeStruct(values.shape, BF16),
        flops=groups * heads * SPAN * SPAN * 2000,
        moved=values.size * 5,
        exps=groups * heads * SPAN * SPAN,
        grid=(groups,),
        in_specs=[
            pl.BlockSpec(memory_space=pltpu.SMEM), wide, lead_spec(SPAN, heads),
            lead_spec(heads, SPAN),
        ]
        + [pl.BlockSpec(memory_space=pltpu.VMEM)] * len(pieces),
        out_specs=wide,
        scratch_shapes=[
            pltpu.VMEM((SPAN, 2 * STATE), BF16), pltpu.VMEM((STATE, width), BF16)
        ],
    )(skip, values, cum, cumt, *pieces)


def spot_of(block, spots):
    if spots == 1:
        return 0
    other_x = (lax.axis_index("head") != block % 2).astype(jnp.int32)
    other_core = (lax.axis_index("sub") != block // 2).astype(jnp.int32)
    return 2 * other_x + other_core


def update_kernel(blocks, spots, *refs):
    turned_refs, pieces = refs[:spots], refs[spots:-5]
    decayed_ref, keep_ref, weight_ref, sparse_ref, grad_ref = refs[-5:]
    parts = len(pieces) // blocks
    rows, width = pieces[0].shape

    @pl.when(pl.program_id(0) == 0)
    def _():
        for number, piece in enumerate(pieces):
            block, part = divmod(number, parts)
            start = pl.multiple_of(spot_of(block, spots) * rows, rows)
            grad_ref[pl.ds(start, rows), part * width : (part + 1) * width] = piece[...]

    total = dot(turned_refs[0][...], grad_ref[:rows, :])
    for spot in range(1, spots):
        total += dot(turned_refs[spot][...], grad_ref[spot * rows : (spot + 1) * rows, :])
    weight = decayed_ref[...] - (LEARN_RATE * WEIGHT_SCALE) * total
    weight_ref[...] = weight
    sparse_ref[...] = (weight * keep_ref[...].astype(F32)).astype(BF16)


def update(turned_hidden, grad_blocks, decayed, keep, vmem):
    rows, columns = decayed.shape
    tokens = turned_hidden[0].shape[1]
    step = min(rows, 256)
    full = pl.BlockSpec((step, columns), lambda i: (i, 0))
    pieces = [part for block in grad_blocks for part in block]
    return call(
        functools.partial(update_kernel, len(grad_blocks), len(turned_hidden)),
        (jax.ShapeDtypeStruct((rows, columns), F32), jax.ShapeDtypeStruct((rows, columns), BF16)),
        flops=2 * len(turned_hidden) * tokens * rows * columns,
        moved=rows * columns * 12 + len(turned_hidden) * tokens * (rows + columns) * 2,
        vmem=vmem,
        grid=(rows // step,),
        in_specs=[pl.BlockSpec((step, tokens), lambda i: (i, 0))] * len(turned_hidden)
        + [pl.BlockSpec(piece.shape, lambda i: (0, 0)) for piece in pieces]
        + [full, full],
        out_specs=(full, full),
        scratch_shapes=[pltpu.VMEM((len(turned_hidden) * tokens, columns), BF16)],
    )(*turned_hidden, *pieces, decayed, keep)


def held(after, *before):
    return lax.optimization_barrier((after, *before))[0]


def to_all(seq, distance):
    return [(source, (source + distance) % seq) for source in range(seq)]


def block_pairs(seq, near, same_core):
    return [
        (
            (z * 2 + x) * 2 + core,
            ((z + (x if near else 1 - x) + 2 * core) % seq * 2 + x) * 2
            + (core if same_core else 1 - core),
        )
        for z in range(seq)
        for x in range(2)
        for core in range(2)
    ]


def transpose_pairs(seq):
    pairs = []
    for z in range(seq):
        for layer in range(seq):
            distance = (z - layer) % seq
            pairs.append((z * seq + layer, layer * seq + distance % 2 * 2 + distance // 2))
    return pairs


SWAP = [(0, 1), (1, 0)]


def chain(own, own_low, decay, seq, step):
    arrived = jnp.zeros_like(own_low)
    message = own_low
    first = 0 if step > 0 else seq - 1
    for hop in range(seq - 1):
        source = first + hop * step
        if hop:
            message = handed_on(decay, arrived, own, 0)
        arrived = arrived + lax.ppermute(message, "seq", [(source, source + step)])
    return arrived


def on_device_general(
    seq, hidden, inner_values, log_decay, skip_gain, cotangent, master, mask_now, mask_next
):
    groups = master.shape[1] // (2 * STATE)
    effective, decayed, keep = weights(master, mask_now, mask_next)
    features = lax.all_gather(hidden, ("head", "sub"), axis=1, tiled=True)
    layer = lax.all_to_all(features, "seq", split_axis=1, concat_axis=0, tiled=True)
    xd, yd, mix, mixt, cum, cumt, decay = before(
        inner_values, cotangent, log_decay.T, groups
    )
    part = dot(layer, effective).astype(BF16)
    terms = [lax.psum_scatter(part, "seq", scatter_dimension=0, tiled=True)]
    proj, state_low, state, adjoint = states(True, terms, xd, yd, 0, groups, decay.shape[2])
    start = chain(state, state_low, decay, seq, 1)
    adjoint_in = chain(adjoint, adjoint.astype(BF16), decay, seq, -1)
    grad = grads(True, proj, xd, yd, mix, mixt, start, [adjoint_in], 0)
    blocks = [[lax.all_gather(grad, "seq", axis=0, tiled=True)]]
    ssd_output = output(
        True, inner_values, cum, cumt, skip_gain, [proj], [start], [[adjoint_in]]
    )
    return ssd_output, *update([layer.T], blocks, decayed, keep, 40 * MIB)


def on_device(
    seq, hidden, inner_values, log_decay, skip_gain, cotangent, master, mask_now, mask_next
):
    groups = master.shape[1] // (2 * STATE)
    axes = ("seq", "head", "sub")
    own = lax.ppermute(hidden, axes, transpose_pairs(seq))
    effective, decayed, keep = weights(master, mask_now, mask_next)
    sibling_effective = effective_of(
        lax.ppermute(master, "sub", SWAP), lax.ppermute(mask_now, "sub", SWAP)
    )
    xd, yd, mix, mixt, cum, cumt, decay = before(
        inner_values, cotangent, log_decay.T, groups
    )
    own = held(own, effective, sibling_effective)

    other = lax.ppermute(own, "head", SWAP)
    same, cross = partials(own, effective, sibling_effective)
    terms = [
        lax.ppermute(same, axes, block_pairs(seq, True, True)),
        lax.ppermute(cross, axes, block_pairs(seq, True, False)),
    ]
    own_turned = turn(held(own, same))
    other = held(other, xd, own_turned, *terms)
    same, cross = partials(other, effective, sibling_effective)
    terms += [
        lax.ppermute(same, axes, block_pairs(seq, False, True)),
        lax.ppermute(cross, axes, block_pairs(seq, False, False)),
    ]
    each = groups // PARTS
    spans = range(PARTS)
    projs, messages, nears, fars = zip(
        *(
            states(None, terms, xd, yd, p * each, each, decay.shape[2])
            for p in spans
        )
    )
    other_turned = turn(held(other, nears[0]))
    own_turned = held(own_turned, nears[0])
    turned_hidden = [
        own_turned, lax.ppermute(own_turned, "sub", SWAP),
        other_turned, lax.ppermute(other_turned, "sub", SWAP),
    ]
    arrived = [[] for _ in spans]
    hops = (([(0, 1), (3, 2)], nears), ([(1, 2), (2, 1)], fars), ([(1, 0), (2, 3)], None))
    messages = list(messages)
    for pairs, own_terms in hops:
        for p in spans:
            message = messages[p]
            if p:
                message = held(message, arrived[p - 1][-1])
            arrived[p].append(lax.ppermute(message, "seq", pairs))
        for p in spans:
            if own_terms:
                messages[p] = handed_on(decay, arrived[p][-1], own_terms[p], p * each)
    blocks = [[] for _ in range(seq)]
    for p in spans:
        grad = grads(
            None, projs[p], xd, yd, mix, mixt, arrived[p][0], arrived[p][1:], p * each
        )
        for distance in range(seq):
            pairs = to_all(seq, seq - distance)
            blocks[distance].append(lax.ppermute(grad, "seq", pairs) if distance else grad)

    ssd_output = output(
        None, inner_values, cum, cumt, skip_gain,
        projs, [a[0] for a in arrived], [a[1:] for a in arrived],
    )
    new_weight, sparse_weight = update(turned_hidden, blocks, decayed, keep, 16 * MIB)
    return ssd_output, new_weight, sparse_weight


PARTS = 2


def solution(mesh):
    by_position = P(("grp", "seq"), ("head", "sub"))
    by_row = P("seq", ("head", "sub"))
    seq, head, sub = (mesh.shape[name] for name in ("seq", "head", "sub"))
    body = on_device if (seq, head, sub) == (4, 2, 2) else on_device_general
    return jax.shard_map(
        functools.partial(body, seq),
        mesh=mesh,
        in_specs=(
            by_position, by_position, by_position, P(("head", "sub")), by_position,
            by_row, by_row, by_row,
        ),
        out_specs=(by_position, by_position, by_position),
        check_vma=False,
    )
```

```python
import functools
import math

import jax
import jax.numpy as jnp
from jax import lax
from jax.experimental import pallas as pl
from jax.experimental.pallas import tpu as pltpu
from jax.sharding import PartitionSpec as P

D = 4096
STATE = 128
SPAN = 256
LEARN_RATE = 0.05
WEIGHT_DECAY = 10.0
WEIGHT_SCALE = 2.0 / math.sqrt(D)
KEEP_BITS = (0b000111, 0b011001, 0b101010, 0b110100)
OUT_OF_SIGHT = -1e30
MIB = 1024 * 1024

F32 = jnp.float32
BF16 = jnp.bfloat16
NT = (((1,), (1,)), ((), ()))


def call(kernel, out_shape, flops, moved, exps=0, vmem=16 * MIB, **more):
    return pl.pallas_call(
        kernel,
        out_shape=out_shape,
        compiler_params=pltpu.CompilerParams(vmem_limit_bytes=vmem),
        cost_estimate=pl.CostEstimate(flops=flops, bytes_accessed=moved, transcendentals=exps),
        **more,
    )


def dot(a, b):
    return jnp.dot(a, b, preferred_element_type=F32)


def dot_nt(a, b):
    return lax.dot_general(a, b, NT, preferred_element_type=F32)


def turned(a):
    return a.astype(F32).T.astype(BF16)


def expanded(codes, rows):
    spread = (
        lax.broadcasted_iota(jnp.int32, (rows, rows // 4), 0) // 4
        == lax.broadcasted_iota(jnp.int32, (rows, rows // 4), 1)
    ).astype(F32)
    code = dot(spread.astype(BF16), codes.astype(F32).astype(BF16)).astype(jnp.int32)
    place = lax.broadcasted_iota(jnp.int32, (rows, 1), 0) % 4
    bits = jnp.where(
        place < 2,
        jnp.where(place == 0, KEEP_BITS[0], KEEP_BITS[1]),
        jnp.where(place == 2, KEEP_BITS[2], KEEP_BITS[3]),
    )
    return lax.shift_right_logical(jnp.broadcast_to(bits, code.shape), code) & 1


def weights_kernel(master_ref, now_ref, next_ref, effective_ref, decayed_ref, keep_ref):
    rows = master_ref.shape[0]
    master = master_ref[...]
    kept = expanded(now_ref[...], rows) == 1
    effective_ref[...] = jnp.where(kept, master * WEIGHT_SCALE, 0.0).astype(BF16)
    decayed_ref[...] = jnp.where(kept, master, master * (1.0 - LEARN_RATE * WEIGHT_DECAY))
    keep_ref[...] = expanded(next_ref[...], rows).astype(F32).astype(BF16)


def weights(master, mask_now, mask_next):
    rows, columns = master.shape
    block = min(rows, 256)
    full = pl.BlockSpec((block, columns), lambda i: (i, 0))
    quarter = pl.BlockSpec((block // 4, columns), lambda i: (i, 0))
    return call(
        weights_kernel,
        (
            jax.ShapeDtypeStruct((rows, columns), BF16),
            jax.ShapeDtypeStruct((rows, columns), F32),
            jax.ShapeDtypeStruct((rows, columns), BF16),
        ),
        flops=rows * columns * 3000,
        moved=rows * columns * 14,
        grid=(rows // block,),
        in_specs=[full, quarter, quarter],
        out_specs=(full, full, full),
    )(master, mask_now, mask_next)


def effective_kernel(master_ref, now_ref, effective_ref):
    kept = expanded(now_ref[...], master_ref.shape[0]) == 1
    effective_ref[...] = jnp.where(kept, master_ref[...] * WEIGHT_SCALE, 0.0).astype(BF16)


def effective_of(master, mask_now):
    rows, columns = master.shape
    block = min(rows, 256)
    full = pl.BlockSpec((block, columns), lambda i: (i, 0))
    return call(
        effective_kernel,
        jax.ShapeDtypeStruct((rows, columns), BF16),
        flops=rows * columns * 3000,
        moved=rows * columns * 7,
        grid=(rows // block,),
        in_specs=[full, pl.BlockSpec((block // 4, columns), lambda i: (i, 0))],
        out_specs=full,
    )(master, mask_now)


def lanes_of(left, right, wide):
    lane = lax.broadcasted_iota(jnp.int32, (left.shape[0], wide), 1)
    return jnp.where(lane < wide // 2, left, right)


def decays_of(col, row):
    half = SPAN // 2
    causal = lax.broadcasted_iota(jnp.int32, (half, half), 0) >= lax.broadcasted_iota(
        jnp.int32, (half, half), 1
    )
    top = jnp.exp(jnp.where(causal, col[:half] - row[:, :half], OUT_OF_SIGHT))
    low = jnp.exp(col[half:] - row[:, :half])
    end = jnp.exp(jnp.where(causal, col[half:] - row[:, half:], OUT_OF_SIGHT))
    return top, low, end


def before_kernel(
    x_ref, dy_ref, logt_ref,
    xd_ref, yd_ref, mix_ref, mixt_ref, cum_ref, cumt_ref, end_ref, tall_ref,
):
    heads = cum_ref.shape[2]
    half = SPAN // 2
    wide = x_ref.shape[1] // heads * 2
    row = lax.broadcasted_iota(jnp.int32, (SPAN, SPAN), 0)
    col = lax.broadcasted_iota(jnp.int32, (SPAN, SPAN), 1)
    first = pl.multiple_of(pl.program_id(0) * heads, heads)
    cumt = jnp.dot(
        logt_ref[pl.ds(first, heads), :], (row <= col).astype(F32),
        precision=lax.Precision.HIGHEST, preferred_element_type=F32,
    )
    tall_ref[...] = jnp.zeros_like(tall_ref)
    tall_ref[:heads, :] = cumt
    cum = tall_ref[...].T[:, :heads]
    cum_ref[0] = cum
    cumt_ref[0] = cumt
    end = cum[SPAN - 1 :, :]
    from_start = jnp.exp(cum)
    to_end = jnp.exp(end - cum)
    whole = jnp.exp(end)
    mix = [jnp.zeros((half, half), F32) for _ in range(3)]
    lane = lax.broadcasted_iota(jnp.int32, (SPAN, wide), 1)
    for pair in range(heads // 2):
        a, b = 2 * pair, 2 * pair + 1
        cut = slice(pair * wide, (pair + 1) * wide)
        x = x_ref[:, cut]
        dy = dy_ref[:, cut]
        wide_dy = dy.astype(F32)
        xd_ref[:, cut] = (
            x.astype(F32) * lanes_of(to_end[:, a : a + 1], to_end[:, b : b + 1], wide)
        ).astype(BF16)
        yd_ref[:, cut] = (
            wide_dy * lanes_of(from_start[:, a : a + 1], from_start[:, b : b + 1], wide)
        ).astype(BF16)
        end_ref[0, :, cut] = lanes_of(whole[:, a : a + 1], whole[:, b : b + 1], wide)
        for head, mine in ((a, lane < wide // 2), (b, lane >= wide // 2)):
            one = jnp.where(mine, wide_dy, 0.0).astype(BF16)
            decays = decays_of(cum[:, head : head + 1], cumt[head : head + 1, :])
            mix[0] += dot_nt(one[:half], x[:half]) * decays[0]
            both = dot_nt(one[half:], x)
            mix[1] += both[:, :half] * decays[1]
            mix[2] += both[:, half:] * decays[2]
    nothing = jnp.zeros((half, half), BF16)
    top, low, end_mix = (m.astype(BF16) for m in mix)
    topt, lowt, end_mixt = (m.T.astype(BF16) for m in mix)
    mix_ref[0, :half, :half] = top
    mix_ref[0, :half, half:] = nothing
    mix_ref[0, half:, :half] = low
    mix_ref[0, half:, half:] = end_mix
    mixt_ref[0, :half, :half] = topt
    mixt_ref[0, :half, half:] = lowt
    mixt_ref[0, half:, :half] = nothing
    mixt_ref[0, half:, half:] = end_mixt


def wide_spec(width):
    return pl.BlockSpec((SPAN, width), lambda g: (0, g))


def lead_spec(*shape):
    return pl.BlockSpec((1, *shape), lambda g: (g, *(0 for _ in shape)))


def before(values, cotan, logs_t, groups):
    heads = logs_t.shape[0] // groups
    width = values.shape[1] // groups
    wide = wide_spec(width)
    return call(
        before_kernel,
        (
            jax.ShapeDtypeStruct(values.shape, BF16),
            jax.ShapeDtypeStruct(values.shape, BF16),
            jax.ShapeDtypeStruct((groups, SPAN, SPAN), BF16),
            jax.ShapeDtypeStruct((groups, SPAN, SPAN), BF16),
            jax.ShapeDtypeStruct((groups, SPAN, heads), F32),
            jax.ShapeDtypeStruct((groups, heads, SPAN), F32),
            jax.ShapeDtypeStruct((groups, 1, width), F32),
        ),
        flops=groups * heads * SPAN * SPAN * 2500,
        moved=values.size * 8,
        exps=groups * heads * SPAN * SPAN,
        grid=(groups,),
        in_specs=[wide, wide, pl.BlockSpec(logs_t.shape, lambda g: (0, 0))],
        out_specs=(
            wide, wide, lead_spec(SPAN, SPAN), lead_spec(SPAN, SPAN),
            lead_spec(SPAN, heads), lead_spec(heads, SPAN), lead_spec(1, width),
        ),
        scratch_shapes=[pltpu.VMEM((STATE, SPAN), F32)],
    )(values, cotan, logs_t)


def partial_kernel(top_ref, low_ref, weight_ref, sibling_weight_ref, out_ref, sibling_out_ref):
    rows = top_ref.shape[0]
    for weight, out in ((weight_ref, out_ref), (sibling_weight_ref, sibling_out_ref)):
        out[:rows, :] = dot(top_ref[...], weight[...]).astype(BF16)
        out[rows:, :] = dot(low_ref[...], weight[...]).astype(BF16)


def partials(halves, effective, sibling_effective):
    rows, columns = halves[0].shape[0], effective.shape[1]
    whole = pl.BlockSpec(memory_space=pltpu.VMEM)
    return call(
        partial_kernel,
        (jax.ShapeDtypeStruct((2 * rows, columns), BF16),) * 2,
        flops=8 * rows * effective.size,
        moved=(2 * halves[0].size + 2 * effective.size + 4 * rows * columns) * 2,
        in_specs=[whole] * 4,
        out_specs=(whole,) * 2,
    )(*halves, effective, sibling_effective)


def turn_kernel(top_ref, low_ref, out_ref):
    rows = top_ref.shape[0]
    out_ref[:, :rows] = turned(top_ref[...])
    out_ref[:, rows:] = turned(low_ref[...])


def turn(halves):
    rows, features = halves[0].shape
    whole = pl.BlockSpec(memory_space=pltpu.VMEM)
    return call(
        turn_kernel,
        jax.ShapeDtypeStruct((features, 2 * rows), BF16),
        flops=rows * features * 4000,
        moved=rows * features * 8,
        in_specs=[whole, whole],
        out_specs=whole,
    )(*halves)


def either(ahead, first, second, body):
    if ahead:
        return body(first, second)
    lower = lax.axis_index("seq") < lax.axis_size("seq") // 2

    @pl.when(lower)
    def _():
        body(first, second)

    @pl.when(jnp.logical_not(lower))
    def _():
        body(second, first)


def states_kernel(both, *refs):
    (*terms, xd_ref, yd_ref, proj_ref, near_low_ref, near_ref, far_ref) = refs
    total = terms[0][...].astype(F32)
    for term in terms[1:]:
        total += term[...].astype(F32)
    low = total.astype(BF16)
    proj_ref[...] = low
    state = dot(turned(low[:, :STATE]), xd_ref[...])
    adjoint = dot(turned(low[:, STATE:]), yd_ref[...])

    def put(near, far):
        near_low_ref[0] = near.astype(BF16)
        near_ref[0] = near
        far_ref[0] = far

    either(both, state, adjoint, put)


def states(ahead, terms, xd, yd, first, groups, width):
    pair = pl.BlockSpec((SPAN, 2 * STATE), lambda g: (0, g))
    pair_from = pl.BlockSpec((SPAN, 2 * STATE), lambda g: (0, g + first))
    wide = pl.BlockSpec((SPAN, width), lambda g: (0, g + first))
    lead = lead_spec(STATE, width)
    shape = (groups, STATE, width)
    return call(
        functools.partial(states_kernel, ahead),
        (
            jax.ShapeDtypeStruct((SPAN, groups * 2 * STATE), BF16),
            jax.ShapeDtypeStruct(shape, BF16),
            jax.ShapeDtypeStruct(shape, F32),
            jax.ShapeDtypeStruct(shape, F32),
        ),
        flops=4 * SPAN * groups * width * STATE,
        moved=groups * SPAN * (width * 4 + 4 * STATE * 5),
        grid=(groups,),
        in_specs=[pair_from] * len(terms) + [wide, wide],
        out_specs=(pair, lead, lead, lead),
    )(*terms, xd, yd)


def added(refs):
    total = refs[0][0]
    for ref in refs[1:]:
        total += ref[0]
    return total


def message_kernel(decay_ref, arrived_ref, own_ref, out_ref):
    out_ref[0] = (decay_ref[0] * arrived_ref[0].astype(F32) + own_ref[0]).astype(BF16)


def handed_on(decay, arrived, own, first):
    groups, _, width = arrived.shape
    lead = lead_spec(STATE, width)
    return call(
        message_kernel,
        jax.ShapeDtypeStruct(arrived.shape, BF16),
        flops=2 * arrived.size,
        moved=8 * arrived.size,
        grid=(groups,),
        in_specs=[pl.BlockSpec((1, 1, width), lambda g: (g + first, 0, 0)), lead, lead],
        out_specs=lead,
    )(decay, arrived, own)


def grads_kernel(ahead, proj_ref, xd_ref, yd_ref, mix_ref, mixt_ref, near_ref, *refs):
    (*far_refs, out_ref) = refs

    def body(start, adjoint):
        write, read = proj_ref[:, :STATE], proj_ref[:, STATE:]
        grad_write = dot(mixt_ref[0], read) + dot_nt(xd_ref[...], added(adjoint))
        grad_read = dot(mix_ref[0], write) + dot_nt(yd_ref[...], added(start))
        out_ref[:, :STATE] = grad_write.astype(BF16)
        out_ref[:, STATE:] = grad_read.astype(BF16)

    either(ahead, [near_ref], far_refs, body)


def grads(ahead, proj, xd, yd, mix, mixt, near, far, first):
    groups, _, width = near.shape
    pair = pl.BlockSpec((SPAN, 2 * STATE), lambda g: (0, g))
    wide = pl.BlockSpec((SPAN, width), lambda g: (0, g + first))
    square = pl.BlockSpec((1, SPAN, SPAN), lambda g: (g + first, 0, 0))
    return call(
        functools.partial(grads_kernel, ahead),
        jax.ShapeDtypeStruct(proj.shape, BF16),
        flops=4 * SPAN * groups * (width + SPAN) * STATE,
        moved=groups * SPAN * width * 8,
        grid=(groups,),
        in_specs=[pair, wide, wide, square, square]
        + [lead_spec(STATE, width)] * (1 + len(far)),
        out_specs=pair,
    )(proj, xd, yd, mix, mixt, near, *far)


def output_kernel(
    ahead, first, skip_ref, x_ref, cum_ref, cumt_ref, proj_ref, near_ref, *refs
):
    (*far_refs, out_ref, start_ref) = refs
    far_refs = [ref for ref in far_refs if ref.shape[1:] == near_ref.shape[1:]]

    def put(start, _):
        start_ref[...] = added(start)

    either(ahead, [near_ref], far_refs, put)

    heads = cum_ref.shape[2]
    half = SPAN // 2
    wide = x_ref.shape[1] // heads * 2
    write = proj_ref[:, :STATE]
    read = proj_ref[:, STATE:]
    cum = cum_ref[0]
    cumt = cumt_ref[0]
    from_start = jnp.exp(cum)
    scores = dot_nt(read, write)
    top, low, end = scores[:half, :half], scores[half:, :half], scores[half:, half:]
    lane = lax.broadcasted_iota(jnp.int32, (half, wide), 1)
    for pair in range(heads // 2):
        a, b = 2 * pair, 2 * pair + 1
        cut = slice(pair * wide, (pair + 1) * wide)
        x = x_ref[:, cut]
        upper, lower = [], []
        for head in (a, b):
            decays = decays_of(cum[:, head : head + 1], cumt[head : head + 1, :])
            upper.append(dot((top * decays[0]).astype(BF16), x[:half]))
            lower.append(
                dot((low * decays[1]).astype(BF16), x[:half])
                + dot((end * decays[2]).astype(BF16), x[half:])
            )
        carried = dot(read, start_ref[:, cut]) * lanes_of(
            from_start[:, a : a + 1], from_start[:, b : b + 1], wide
        )
        head = (pl.program_id(0) + first) * heads + a
        gain = jnp.where(
            lax.broadcasted_iota(jnp.int32, (1, wide), 1) < wide // 2,
            skip_ref[head], skip_ref[head + 1],
        )
        rest = carried + gain * x.astype(F32)
        out_ref[:half, cut] = (
            jnp.where(lane < wide // 2, upper[0], upper[1]) + rest[:half]
        ).astype(BF16)
        out_ref[half:, cut] = (
            jnp.where(lane < wide // 2, lower[0], lower[1]) + rest[half:]
        ).astype(BF16)


def output(ahead, values, cum, cumt, skip, proj, near, far, first, earlier):
    groups, _, width = near.shape
    heads = cum.shape[2]
    wide = pl.BlockSpec((SPAN, width), lambda g: (0, g + first))
    lead = lead_spec(STATE, width)
    earlier = [] if earlier is None else [earlier]
    return call(
        functools.partial(output_kernel, ahead, first),
        jax.ShapeDtypeStruct(values.shape, BF16),
        flops=groups * heads * SPAN * SPAN * 2000,
        moved=groups * SPAN * width * 10,
        exps=groups * heads * SPAN * SPAN,
        grid=(groups,),
        in_specs=[
            pl.BlockSpec(memory_space=pltpu.SMEM), wide,
            pl.BlockSpec((1, SPAN, heads), lambda g: (g + first, 0, 0)),
            pl.BlockSpec((1, heads, SPAN), lambda g: (g + first, 0, 0)),
            pl.BlockSpec((SPAN, 2 * STATE), lambda g: (0, g)),
        ]
        + [lead] * (1 + len(far))
        + [pl.BlockSpec(memory_space=pl.ANY)] * len(earlier),
        out_specs=wide,
        scratch_shapes=[pltpu.VMEM((STATE, width), BF16)],
        input_output_aliases={6 + len(far): 0} if earlier else {},
    )(skip, values, cum, cumt, proj, near, *far, *earlier)


def spot_of(block, spots):
    if spots == 1:
        return 0
    other_x = (lax.axis_index("head") != block % 2).astype(jnp.int32)
    other_core = (lax.axis_index("sub") != block // 2).astype(jnp.int32)
    return 2 * other_x + other_core


def update_kernel(blocks, spots, *refs):
    turned_refs, pieces = refs[:spots], refs[spots : spots + blocks]
    decayed_ref, keep_ref = refs[spots + blocks : spots + blocks + 2]
    weight_ref, sparse_ref, grad_ref = refs[-3:]
    rows = pieces[0].shape[0]

    @pl.when(pl.program_id(0) == 0)
    def _():
        for block, piece in enumerate(pieces):
            start = pl.multiple_of(spot_of(block, spots) * rows, rows)
            grad_ref[pl.ds(start, rows), :] = piece[...]

    total = dot(turned_refs[0][...], grad_ref[:rows, :])
    for spot in range(1, spots):
        total += dot(turned_refs[spot][...], grad_ref[spot * rows : (spot + 1) * rows, :])
    weight = decayed_ref[...] - (LEARN_RATE * WEIGHT_SCALE) * total
    weight_ref[...] = weight
    sparse_ref[...] = (weight * keep_ref[...].astype(F32)).astype(BF16)


def update(turned_hidden, grad_blocks, decayed, keep, part, earlier, vmem):
    rows, columns = decayed.shape
    width = grad_blocks[0].shape[1]
    tokens = turned_hidden[0].shape[1]
    spots, blocks = len(turned_hidden), len(grad_blocks)
    step = min(rows, 256)
    full = pl.BlockSpec((step, width), lambda i: (i, part))
    earlier = earlier or ()
    return call(
        functools.partial(update_kernel, blocks, spots),
        (jax.ShapeDtypeStruct((rows, columns), F32), jax.ShapeDtypeStruct((rows, columns), BF16)),
        flops=2 * spots * tokens * rows * width,
        moved=rows * width * 12 + spots * tokens * (rows + width) * 2,
        vmem=vmem,
        grid=(rows // step,),
        in_specs=[pl.BlockSpec((step, tokens), lambda i: (i, 0))] * spots
        + [pl.BlockSpec(piece.shape, lambda i: (0, 0)) for piece in grad_blocks]
        + [full, full]
        + [pl.BlockSpec(memory_space=pl.ANY)] * len(earlier),
        out_specs=(full, full),
        scratch_shapes=[pltpu.VMEM((spots * tokens, width), BF16)],
        input_output_aliases={spots + blocks + 2 + i: i for i in range(len(earlier))},
    )(*turned_hidden, *grad_blocks, decayed, keep, *earlier)


def held(after, *before):
    return lax.optimization_barrier((after, *before))[0]


def to_all(seq, distance):
    return [(source, (source + distance) % seq) for source in range(seq)]


def block_pairs(seq, near, same_core):
    return [
        (
            (z * 2 + x) * 2 + core,
            ((z + (x if near else 1 - x) + 2 * core) % seq * 2 + x) * 2
            + (core if same_core else 1 - core),
        )
        for z in range(seq)
        for x in range(2)
        for core in range(2)
    ]


def transpose_pairs(seq, changed):
    pairs = []
    for z in range(seq):
        for x in range(2):
            for core in range(2):
                layer = 2 * x + core
                distance = (z - layer) % seq
                source = (z * 2 + (1 - x if changed else x)) * 2 + core
                pairs.append((source, (layer * 2 + distance % 2) * 2 + distance // 2))
    return pairs


SWAP = [(0, 1), (1, 0)]


def chain(own, own_low, decay, seq, step):
    arrived = jnp.zeros_like(own_low)
    message = own_low
    first = 0 if step > 0 else seq - 1
    for hop in range(seq - 1):
        source = first + hop * step
        if hop:
            message = handed_on(decay, arrived, own, 0)
        arrived = arrived + lax.ppermute(message, "seq", [(source, source + step)])
    return arrived


def on_device_general(
    seq, hidden, inner_values, log_decay, skip_gain, cotangent, master, mask_now, mask_next
):
    groups = master.shape[1] // (2 * STATE)
    effective, decayed, keep = weights(master, mask_now, mask_next)
    features = lax.all_gather(hidden, ("head", "sub"), axis=1, tiled=True)
    layer = lax.all_to_all(features, "seq", split_axis=1, concat_axis=0, tiled=True)
    xd, yd, mix, mixt, cum, cumt, decay = before(
        inner_values, cotangent, log_decay.T, groups
    )
    part = dot(layer, effective).astype(BF16)
    terms = [lax.psum_scatter(part, "seq", scatter_dimension=0, tiled=True)]
    proj, state_low, state, adjoint = states(True, terms, xd, yd, 0, groups, decay.shape[2])
    start = chain(state, state_low, decay, seq, 1)
    adjoint_in = chain(adjoint, adjoint.astype(BF16), decay, seq, -1)
    grad = grads(True, proj, xd, yd, mix, mixt, start, [adjoint_in], 0)
    blocks = [lax.all_gather(grad, "seq", axis=0, tiled=True)]
    ssd_output = output(
        True, inner_values, cum, cumt, skip_gain, proj, start, [adjoint_in], 0, None
    )
    return ssd_output, *update([layer.T], blocks, decayed, keep, 0, None, 40 * MIB)


def on_device(
    seq, hidden, inner_values, log_decay, skip_gain, cotangent, master, mask_now, mask_next
):
    groups = master.shape[1] // (2 * STATE)
    axes = ("seq", "head", "sub")
    rows = hidden.shape[0] // 2
    beside = lax.ppermute(hidden[rows:], "head", SWAP)
    top = lax.ppermute(hidden[:rows], axes, transpose_pairs(seq, False))
    low = lax.ppermute(beside, axes, transpose_pairs(seq, True))
    effective, decayed, keep = weights(master, mask_now, mask_next)
    sibling_effective = effective_of(
        lax.ppermute(master, "sub", SWAP), lax.ppermute(mask_now, "sub", SWAP)
    )
    xd, yd, mix, mixt, cum, cumt, decay = before(
        inner_values, cotangent, log_decay.T, groups
    )
    top, low = held(top, effective, sibling_effective), held(low, effective, sibling_effective)

    own = [top, low]
    other = [lax.ppermute(half, "head", SWAP) for half in own]
    same, cross = partials(own, effective, sibling_effective)
    terms = [
        lax.ppermute(same, axes, block_pairs(seq, True, True)),
        lax.ppermute(cross, axes, block_pairs(seq, True, False)),
    ]
    own_turned = turn([held(top, same), low])
    other[0] = held(other[0], xd, own_turned, *terms)
    same, cross = partials(other, effective, sibling_effective)
    terms += [
        lax.ppermute(same, axes, block_pairs(seq, False, True)),
        lax.ppermute(cross, axes, block_pairs(seq, False, False)),
    ]

    each = groups // PARTS
    spans = range(PARTS)
    projs, messages, nears, fars = zip(
        *(
            states(None, terms, xd, yd, p * each, each, decay.shape[2])
            for p in spans
        )
    )
    other_turned = turn([held(other[0], nears[0]), other[1]])
    own_turned = held(own_turned, nears[0])
    turned_hidden = [
        own_turned, lax.ppermute(own_turned, "sub", SWAP),
        other_turned, lax.ppermute(other_turned, "sub", SWAP),
    ]
    arrived = [[] for _ in spans]
    hops = (([(0, 1), (3, 2)], nears), ([(1, 2), (2, 1)], fars), ([(1, 0), (2, 3)], None))
    messages = list(messages)
    for pairs, own_terms in hops:
        for p in spans:
            message = messages[p]
            if p:
                message = held(message, arrived[p - 1][-1], messages[p - 1])
            arrived[p].append(lax.ppermute(message, "seq", pairs))
            if own_terms:
                messages[p] = handed_on(decay, arrived[p][-1], own_terms[p], p * each)
    grad_inputs = [held(projs[0], *turned_hidden), *projs[1:]]
    blocks = []
    for p in spans:
        grad = grads(
            None, grad_inputs[p], xd, yd, mix, mixt, arrived[p][0], arrived[p][1:], p * each
        )
        blocks.append(
            [grad]
            + [
                lax.ppermute(grad, "seq", to_all(seq, seq - distance))
                for distance in range(1, seq)
            ]
        )
    after = [blocks[-1][0], *blocks[0]]
    decayed, cum = held(decayed, *after), held(cum, *after)
    ssd_output = updated = None
    for p in spans:
        ssd_output = output(
            None, inner_values, cum, cumt, skip_gain,
            projs[p], arrived[p][0], arrived[p][1:], p * each, ssd_output,
        )
        updated = update(turned_hidden, blocks[p], decayed, keep, p, updated, 16 * MIB)
    return ssd_output, *updated


PARTS = 2


def solution(mesh):
    by_position = P(("grp", "seq"), ("head", "sub"))
    by_row = P("seq", ("head", "sub"))
    seq, head, sub = (mesh.shape[name] for name in ("seq", "head", "sub"))
    body = on_device if (seq, head, sub) == (4, 2, 2) else on_device_general
    return jax.shard_map(
        functools.partial(body, seq),
        mesh=mesh,
        in_specs=(
            by_position, by_position, by_position, P(("head", "sub")), by_position,
            by_row, by_row, by_row,
        ),
        out_specs=(by_position, by_position, by_position),
        check_vma=False,
    )
```

```python
import functools
import math

import jax
import jax.numpy as jnp
from jax import lax
from jax.experimental import pallas as pl
from jax.experimental.pallas import tpu as pltpu
from jax.sharding import PartitionSpec as P

D = 4096
STATE = 128
SPAN = 256
LEARN_RATE = 0.05
WEIGHT_DECAY = 10.0
WEIGHT_SCALE = 2.0 / math.sqrt(D)
KEEP_BITS = (0b000111, 0b011001, 0b101010, 0b110100)
OUT_OF_SIGHT = -1e30
MIB = 1024 * 1024

F32 = jnp.float32
BF16 = jnp.bfloat16
NT = (((1,), (1,)), ((), ()))


def call(kernel, out_shape, flops, moved, exps=0, vmem=16 * MIB, **more):
    return pl.pallas_call(
        kernel,
        out_shape=out_shape,
        compiler_params=pltpu.CompilerParams(vmem_limit_bytes=vmem),
        cost_estimate=pl.CostEstimate(flops=flops, bytes_accessed=moved, transcendentals=exps),
        **more,
    )


def dot(a, b):
    return jnp.dot(a, b, preferred_element_type=F32)


def dot_nt(a, b):
    return lax.dot_general(a, b, NT, preferred_element_type=F32)


def turned(a):
    return a.astype(F32).T.astype(BF16)


def expanded(codes, rows):
    spread = (
        lax.broadcasted_iota(jnp.int32, (rows, rows // 4), 0) // 4
        == lax.broadcasted_iota(jnp.int32, (rows, rows // 4), 1)
    ).astype(F32)
    code = dot(spread.astype(BF16), codes.astype(F32).astype(BF16)).astype(jnp.int32)
    place = lax.broadcasted_iota(jnp.int32, (rows, 1), 0) % 4
    bits = jnp.where(
        place < 2,
        jnp.where(place == 0, KEEP_BITS[0], KEEP_BITS[1]),
        jnp.where(place == 2, KEEP_BITS[2], KEEP_BITS[3]),
    )
    return lax.shift_right_logical(jnp.broadcast_to(bits, code.shape), code) & 1


def weights_kernel(master_ref, now_ref, next_ref, effective_ref, decayed_ref, keep_ref):
    rows = master_ref.shape[0]
    master = master_ref[...]
    kept = expanded(now_ref[...], rows) == 1
    effective_ref[...] = jnp.where(kept, master * WEIGHT_SCALE, 0.0).astype(BF16)
    decayed_ref[...] = jnp.where(kept, master, master * (1.0 - LEARN_RATE * WEIGHT_DECAY))
    keep_ref[...] = expanded(next_ref[...], rows).astype(F32).astype(BF16)


def weights(master, mask_now, mask_next):
    rows, columns = master.shape
    block = min(rows, 256)
    full = pl.BlockSpec((block, columns), lambda i: (i, 0))
    quarter = pl.BlockSpec((block // 4, columns), lambda i: (i, 0))
    return call(
        weights_kernel,
        (
            jax.ShapeDtypeStruct((rows, columns), BF16),
            jax.ShapeDtypeStruct((rows, columns), F32),
            jax.ShapeDtypeStruct((rows, columns), BF16),
        ),
        flops=rows * columns * 3000,
        moved=rows * columns * 14,
        grid=(rows // block,),
        in_specs=[full, quarter, quarter],
        out_specs=(full, full, full),
    )(master, mask_now, mask_next)


def effective_kernel(master_ref, now_ref, effective_ref):
    kept = expanded(now_ref[...], master_ref.shape[0]) == 1
    effective_ref[...] = jnp.where(kept, master_ref[...] * WEIGHT_SCALE, 0.0).astype(BF16)


def effective_of(master, mask_now):
    rows, columns = master.shape
    block = min(rows, 256)
    full = pl.BlockSpec((block, columns), lambda i: (i, 0))
    return call(
        effective_kernel,
        jax.ShapeDtypeStruct((rows, columns), BF16),
        flops=rows * columns * 3000,
        moved=rows * columns * 7,
        grid=(rows // block,),
        in_specs=[full, pl.BlockSpec((block // 4, columns), lambda i: (i, 0))],
        out_specs=full,
    )(master, mask_now)


def lanes_of(left, right, wide):
    lane = lax.broadcasted_iota(jnp.int32, (left.shape[0], wide), 1)
    return jnp.where(lane < wide // 2, left, right)


def decays_of(col, row):
    half = SPAN // 2
    causal = lax.broadcasted_iota(jnp.int32, (half, half), 0) >= lax.broadcasted_iota(
        jnp.int32, (half, half), 1
    )
    top = jnp.exp(jnp.where(causal, col[:half] - row[:, :half], OUT_OF_SIGHT))
    low = jnp.exp(col[half:] - row[:, :half])
    end = jnp.exp(jnp.where(causal, col[half:] - row[:, half:], OUT_OF_SIGHT))
    return top, low, end


def before_kernel(
    x_ref, dy_ref, logt_ref,
    xd_ref, yd_ref, mix_ref, mixt_ref, cum_ref, cumt_ref, end_ref, tall_ref,
):
    heads = cum_ref.shape[2]
    half = SPAN // 2
    wide = x_ref.shape[1] // heads * 2
    row = lax.broadcasted_iota(jnp.int32, (SPAN, SPAN), 0)
    col = lax.broadcasted_iota(jnp.int32, (SPAN, SPAN), 1)
    first = pl.multiple_of(pl.program_id(0) * heads, heads)
    cumt = jnp.dot(
        logt_ref[pl.ds(first, heads), :], (row <= col).astype(F32),
        precision=lax.Precision.HIGHEST, preferred_element_type=F32,
    )
    tall_ref[...] = jnp.zeros_like(tall_ref)
    tall_ref[:heads, :] = cumt
    cum = tall_ref[...].T[:, :heads]
    cum_ref[0] = cum
    cumt_ref[0] = cumt
    end = cum[SPAN - 1 :, :]
    from_start = jnp.exp(cum)
    to_end = jnp.exp(end - cum)
    whole = jnp.exp(end)
    mix = [jnp.zeros((half, half), F32) for _ in range(3)]
    lane = lax.broadcasted_iota(jnp.int32, (SPAN, wide), 1)
    for pair in range(heads // 2):
        a, b = 2 * pair, 2 * pair + 1
        cut = slice(pair * wide, (pair + 1) * wide)
        x = x_ref[:, cut]
        dy = dy_ref[:, cut]
        wide_dy = dy.astype(F32)
        xd_ref[:, cut] = (
            x.astype(F32) * lanes_of(to_end[:, a : a + 1], to_end[:, b : b + 1], wide)
        ).astype(BF16)
        yd_ref[:, cut] = (
            wide_dy * lanes_of(from_start[:, a : a + 1], from_start[:, b : b + 1], wide)
        ).astype(BF16)
        end_ref[0, :, cut] = lanes_of(whole[:, a : a + 1], whole[:, b : b + 1], wide)
        for head, mine in ((a, lane < wide // 2), (b, lane >= wide // 2)):
            one = jnp.where(mine, wide_dy, 0.0).astype(BF16)
            decays = decays_of(cum[:, head : head + 1], cumt[head : head + 1, :])
            mix[0] += dot_nt(one[:half], x[:half]) * decays[0]
            both = dot_nt(one[half:], x)
            mix[1] += both[:, :half] * decays[1]
            mix[2] += both[:, half:] * decays[2]
    nothing = jnp.zeros((half, half), BF16)
    top, low, end_mix = (m.astype(BF16) for m in mix)
    topt, lowt, end_mixt = (m.T.astype(BF16) for m in mix)
    mix_ref[0, :half, :half] = top
    mix_ref[0, :half, half:] = nothing
    mix_ref[0, half:, :half] = low
    mix_ref[0, half:, half:] = end_mix
    mixt_ref[0, :half, :half] = topt
    mixt_ref[0, :half, half:] = lowt
    mixt_ref[0, half:, :half] = nothing
    mixt_ref[0, half:, half:] = end_mixt


def wide_spec(width):
    return pl.BlockSpec((SPAN, width), lambda g: (0, g))


def lead_spec(*shape):
    return pl.BlockSpec((1, *shape), lambda g: (g, *(0 for _ in shape)))


def before(values, cotan, logs_t, groups):
    heads = logs_t.shape[0] // groups
    width = values.shape[1] // groups
    wide = wide_spec(width)
    return call(
        before_kernel,
        (
            jax.ShapeDtypeStruct(values.shape, BF16),
            jax.ShapeDtypeStruct(values.shape, BF16),
            jax.ShapeDtypeStruct((groups, SPAN, SPAN), BF16),
            jax.ShapeDtypeStruct((groups, SPAN, SPAN), BF16),
            jax.ShapeDtypeStruct((groups, SPAN, heads), F32),
            jax.ShapeDtypeStruct((groups, heads, SPAN), F32),
            jax.ShapeDtypeStruct((groups, 1, width), F32),
        ),
        flops=groups * heads * SPAN * SPAN * 2500,
        moved=values.size * 8,
        exps=groups * heads * SPAN * SPAN,
        grid=(groups,),
        in_specs=[wide, wide, pl.BlockSpec(logs_t.shape, lambda g: (0, 0))],
        out_specs=(
            wide, wide, lead_spec(SPAN, SPAN), lead_spec(SPAN, SPAN),
            lead_spec(SPAN, heads), lead_spec(heads, SPAN), lead_spec(1, width),
        ),
        scratch_shapes=[pltpu.VMEM((STATE, SPAN), F32)],
    )(values, cotan, logs_t)


def partial_kernel(parts, *refs):
    (*pieces, weight_ref, sibling_weight_ref) = refs[: -2 * parts]
    outs = refs[-2 * parts :]
    width = outs[0].shape[1]
    start = 0
    for piece in pieces:
        rows = slice(start, start + piece.shape[0])
        start += piece.shape[0]
        for number, weight in enumerate((weight_ref, sibling_weight_ref)):
            term = dot(piece[...], weight[...]).astype(BF16)
            for part in range(parts):
                outs[number * parts + part][rows, :] = term[:, part * width : (part + 1) * width]


def partials(pieces, effective, sibling_effective, parts):
    rows, columns = sum(piece.shape[0] for piece in pieces), effective.shape[1]
    whole = pl.BlockSpec(memory_space=pltpu.VMEM)
    outs = call(
        functools.partial(partial_kernel, parts),
        (jax.ShapeDtypeStruct((rows, columns // parts), BF16),) * (2 * parts),
        flops=4 * rows * effective.size,
        moved=(rows * effective.shape[0] + 2 * effective.size + 2 * rows * columns) * 2,
        in_specs=[whole] * (len(pieces) + 2),
        out_specs=(whole,) * (2 * parts),
    )(*pieces, effective, sibling_effective)
    return outs[:parts], outs[parts:]


def turn_kernel(*refs):
    (*pieces, out_ref) = refs
    start = 0
    for piece in pieces:
        out_ref[:, start : start + piece.shape[0]] = turned(piece[...])
        start += piece.shape[0]


def turn(pieces):
    rows, features = sum(piece.shape[0] for piece in pieces), pieces[0].shape[1]
    whole = pl.BlockSpec(memory_space=pltpu.VMEM)
    return call(
        turn_kernel,
        jax.ShapeDtypeStruct((features, rows), BF16),
        flops=rows * features * 2000,
        moved=rows * features * 4,
        in_specs=[whole] * len(pieces),
        out_specs=whole,
    )(*pieces)


def either(ahead, first, second, body):
    if ahead:
        return body(first, second)
    lower = lax.axis_index("seq") < lax.axis_size("seq") // 2

    @pl.when(lower)
    def _():
        body(first, second)

    @pl.when(jnp.logical_not(lower))
    def _():
        body(second, first)


def states_kernel(both, *refs):
    (*terms, xd_ref, yd_ref, proj_ref, near_low_ref, near_ref, far_ref) = refs
    total = terms[0][...].astype(F32)
    for term in terms[1:]:
        total += term[...].astype(F32)
    low = total.astype(BF16)
    proj_ref[...] = low
    state = dot(turned(low[:, :STATE]), xd_ref[...])
    adjoint = dot(turned(low[:, STATE:]), yd_ref[...])

    def put(near, far):
        near_low_ref[0] = near.astype(BF16)
        near_ref[0] = near
        far_ref[0] = far

    either(both, state, adjoint, put)


def states(ahead, terms, part_terms, xd, yd, first, groups, width):
    pair = pl.BlockSpec((SPAN, 2 * STATE), lambda g: (0, g))
    pair_from = pl.BlockSpec((SPAN, 2 * STATE), lambda g: (0, g + first))
    wide = pl.BlockSpec((SPAN, width), lambda g: (0, g + first))
    lead = lead_spec(STATE, width)
    shape = (groups, STATE, width)
    return call(
        functools.partial(states_kernel, ahead),
        (
            jax.ShapeDtypeStruct((SPAN, groups * 2 * STATE), BF16),
            jax.ShapeDtypeStruct(shape, BF16),
            jax.ShapeDtypeStruct(shape, F32),
            jax.ShapeDtypeStruct(shape, F32),
        ),
        flops=4 * SPAN * groups * width * STATE,
        moved=groups * SPAN * (width * 4 + 4 * STATE * 5),
        grid=(groups,),
        in_specs=[pair_from] * len(terms) + [pair] * len(part_terms) + [wide, wide],
        out_specs=(pair, lead, lead, lead),
    )(*terms, *part_terms, xd, yd)


def added(refs):
    total = refs[0][0]
    for ref in refs[1:]:
        total += ref[0]
    return total


def message_kernel(decay_ref, arrived_ref, own_ref, out_ref):
    out_ref[0] = (decay_ref[0] * arrived_ref[0].astype(F32) + own_ref[0]).astype(BF16)


def handed_on(decay, arrived, own, first):
    groups, _, width = arrived.shape
    lead = lead_spec(STATE, width)
    return call(
        message_kernel,
        jax.ShapeDtypeStruct(arrived.shape, BF16),
        flops=2 * arrived.size,
        moved=8 * arrived.size,
        grid=(groups,),
        in_specs=[pl.BlockSpec((1, 1, width), lambda g: (g + first, 0, 0)), lead, lead],
        out_specs=lead,
    )(decay, arrived, own)


def grads_kernel(ahead, proj_ref, xd_ref, yd_ref, mix_ref, mixt_ref, near_ref, *refs):
    (*far_refs, out_ref) = refs

    def body(start, adjoint):
        write, read = proj_ref[:, :STATE], proj_ref[:, STATE:]
        grad_write = dot(mixt_ref[0], read) + dot_nt(xd_ref[...], added(adjoint))
        grad_read = dot(mix_ref[0], write) + dot_nt(yd_ref[...], added(start))
        out_ref[:, :STATE] = grad_write.astype(BF16)
        out_ref[:, STATE:] = grad_read.astype(BF16)

    either(ahead, [near_ref], far_refs, body)


def grads(ahead, proj, xd, yd, mix, mixt, near, far, first):
    groups, _, width = near.shape
    pair = pl.BlockSpec((SPAN, 2 * STATE), lambda g: (0, g))
    wide = pl.BlockSpec((SPAN, width), lambda g: (0, g + first))
    square = pl.BlockSpec((1, SPAN, SPAN), lambda g: (g + first, 0, 0))
    return call(
        functools.partial(grads_kernel, ahead),
        jax.ShapeDtypeStruct(proj.shape, BF16),
        flops=4 * SPAN * groups * (width + SPAN) * STATE,
        moved=groups * SPAN * width * 8,
        grid=(groups,),
        in_specs=[pair, wide, wide, square, square]
        + [lead_spec(STATE, width)] * (1 + len(far)),
        out_specs=pair,
    )(proj, xd, yd, mix, mixt, near, *far)


def output_kernel(parts, hops, ahead, skip_ref, x_ref, cum_ref, cumt_ref, *refs):
    (*refs, out_ref, proj_ref, start_ref) = refs
    projs, nears = refs[:parts], refs[parts : 2 * parts]
    fars = [refs[2 * parts + hops * p : 2 * parts + hops * (p + 1)] for p in range(parts)]
    each = projs[0].shape[1] // (2 * STATE)
    for group in range(parts * each):
        part, at = divmod(group, each)

        @pl.when(pl.program_id(0) == group)
        def _(part=part, at=at):
            proj_ref[...] = projs[part][:, at * 2 * STATE : (at + 1) * 2 * STATE]

            def put(start, _):
                start_ref[...] = added([ref.at[at : at + 1] for ref in start])

            either(ahead, [nears[part]], fars[part], put)

    heads = cum_ref.shape[2]
    half = SPAN // 2
    wide = x_ref.shape[1] // heads * 2
    write = proj_ref[:, :STATE]
    read = proj_ref[:, STATE:]
    cum = cum_ref[0]
    cumt = cumt_ref[0]
    from_start = jnp.exp(cum)
    scores = dot_nt(read, write)
    top, low, end = scores[:half, :half], scores[half:, :half], scores[half:, half:]
    lane = lax.broadcasted_iota(jnp.int32, (half, wide), 1)
    for pair in range(heads // 2):
        a, b = 2 * pair, 2 * pair + 1
        cut = slice(pair * wide, (pair + 1) * wide)
        x = x_ref[:, cut]
        upper, lower = [], []
        for head in (a, b):
            decays = decays_of(cum[:, head : head + 1], cumt[head : head + 1, :])
            upper.append(dot((top * decays[0]).astype(BF16), x[:half]))
            lower.append(
                dot((low * decays[1]).astype(BF16), x[:half])
                + dot((end * decays[2]).astype(BF16), x[half:])
            )
        carried = dot(read, start_ref[:, cut]) * lanes_of(
            from_start[:, a : a + 1], from_start[:, b : b + 1], wide
        )
        head = pl.program_id(0) * heads + a
        gain = jnp.where(
            lax.broadcasted_iota(jnp.int32, (1, wide), 1) < wide // 2,
            skip_ref[head], skip_ref[head + 1],
        )
        rest = carried + gain * x.astype(F32)
        out_ref[:half, cut] = (
            jnp.where(lane < wide // 2, upper[0], upper[1]) + rest[:half]
        ).astype(BF16)
        out_ref[half:, cut] = (
            jnp.where(lane < wide // 2, lower[0], lower[1]) + rest[half:]
        ).astype(BF16)


def output(ahead, values, cum, cumt, skip, projs, nears, fars):
    groups, _, heads = cum.shape
    width = values.shape[1] // groups
    wide = wide_spec(width)
    pieces = [*projs, *nears, *(ref for far in fars for ref in far)]
    return call(
        functools.partial(output_kernel, len(projs), len(fars[0]), ahead),
        jax.ShapeDtypeStruct(values.shape, BF16),
        flops=groups * heads * SPAN * SPAN * 2000,
        moved=values.size * 5,
        exps=groups * heads * SPAN * SPAN,
        grid=(groups,),
        in_specs=[
            pl.BlockSpec(memory_space=pltpu.SMEM), wide, lead_spec(SPAN, heads),
            lead_spec(heads, SPAN),
        ]
        + [pl.BlockSpec(memory_space=pltpu.VMEM)] * len(pieces),
        out_specs=wide,
        scratch_shapes=[
            pltpu.VMEM((SPAN, 2 * STATE), BF16), pltpu.VMEM((STATE, width), BF16)
        ],
    )(skip, values, cum, cumt, *pieces)


def spot_of(block, spots):
    if spots == 1:
        return 0
    other_x = (lax.axis_index("head") != block % 2).astype(jnp.int32)
    other_core = (lax.axis_index("sub") != block // 2).astype(jnp.int32)
    return 2 * other_x + other_core


def update_kernel(blocks, spots, *refs):
    turned_refs, pieces = refs[:spots], refs[spots:-5]
    decayed_ref, keep_ref, weight_ref, sparse_ref, grad_ref = refs[-5:]
    parts = len(pieces) // blocks
    rows, width = pieces[0].shape

    @pl.when(pl.program_id(0) == 0)
    def _():
        for number, piece in enumerate(pieces):
            block, part = divmod(number, parts)
            start = pl.multiple_of(spot_of(block, spots) * rows, rows)
            grad_ref[pl.ds(start, rows), part * width : (part + 1) * width] = piece[...]

    total = dot(turned_refs[0][...], grad_ref[:rows, :])
    for spot in range(1, spots):
        total += dot(turned_refs[spot][...], grad_ref[spot * rows : (spot + 1) * rows, :])
    weight = decayed_ref[...] - (LEARN_RATE * WEIGHT_SCALE) * total
    weight_ref[...] = weight
    sparse_ref[...] = (weight * keep_ref[...].astype(F32)).astype(BF16)


def update(turned_hidden, grad_blocks, decayed, keep, vmem):
    rows, columns = decayed.shape
    tokens = turned_hidden[0].shape[1]
    step = min(rows, 256)
    full = pl.BlockSpec((step, columns), lambda i: (i, 0))
    pieces = [part for block in grad_blocks for part in block]
    return call(
        functools.partial(update_kernel, len(grad_blocks), len(turned_hidden)),
        (jax.ShapeDtypeStruct((rows, columns), F32), jax.ShapeDtypeStruct((rows, columns), BF16)),
        flops=2 * len(turned_hidden) * tokens * rows * columns,
        moved=rows * columns * 12 + len(turned_hidden) * tokens * (rows + columns) * 2,
        vmem=vmem,
        grid=(rows // step,),
        in_specs=[pl.BlockSpec((step, tokens), lambda i: (i, 0))] * len(turned_hidden)
        + [pl.BlockSpec(piece.shape, lambda i: (0, 0)) for piece in pieces]
        + [full, full],
        out_specs=(full, full),
        scratch_shapes=[pltpu.VMEM((len(turned_hidden) * tokens, columns), BF16)],
    )(*turned_hidden, *pieces, decayed, keep)


def held(after, *before):
    return lax.optimization_barrier((after, *before))[0]


def to_all(seq, distance):
    return [(source, (source + distance) % seq) for source in range(seq)]


def block_pairs(seq, near, same_core):
    return [
        (
            (z * 2 + x) * 2 + core,
            ((z + (x if near else 1 - x) + 2 * core) % seq * 2 + x) * 2
            + (core if same_core else 1 - core),
        )
        for z in range(seq)
        for x in range(2)
        for core in range(2)
    ]


def transpose_pairs(seq, changed):
    pairs = []
    for z in range(seq):
        for x in range(2):
            for core in range(2):
                layer = 2 * x + core
                distance = (z - layer) % seq
                source = (z * 2 + (1 - x if changed else x)) * 2 + core
                pairs.append((source, (layer * 2 + distance % 2) * 2 + distance // 2))
    return pairs


SWAP = [(0, 1), (1, 0)]


def chain(own, own_low, decay, seq, step):
    arrived = jnp.zeros_like(own_low)
    message = own_low
    first = 0 if step > 0 else seq - 1
    for hop in range(seq - 1):
        source = first + hop * step
        if hop:
            message = handed_on(decay, arrived, own, 0)
        arrived = arrived + lax.ppermute(message, "seq", [(source, source + step)])
    return arrived


def on_device_general(
    seq, hidden, inner_values, log_decay, skip_gain, cotangent, master, mask_now, mask_next
):
    groups = master.shape[1] // (2 * STATE)
    effective, decayed, keep = weights(master, mask_now, mask_next)
    features = lax.all_gather(hidden, ("head", "sub"), axis=1, tiled=True)
    layer = lax.all_to_all(features, "seq", split_axis=1, concat_axis=0, tiled=True)
    xd, yd, mix, mixt, cum, cumt, decay = before(
        inner_values, cotangent, log_decay.T, groups
    )
    part = dot(layer, effective).astype(BF16)
    terms = [lax.psum_scatter(part, "seq", scatter_dimension=0, tiled=True)]
    proj, state_low, state, adjoint = states(True, terms, [], xd, yd, 0, groups, decay.shape[2])
    start = chain(state, state_low, decay, seq, 1)
    adjoint_in = chain(adjoint, adjoint.astype(BF16), decay, seq, -1)
    grad = grads(True, proj, xd, yd, mix, mixt, start, [adjoint_in], 0)
    blocks = [[lax.all_gather(grad, "seq", axis=0, tiled=True)]]
    ssd_output = output(
        True, inner_values, cum, cumt, skip_gain, [proj], [start], [[adjoint_in]]
    )
    return ssd_output, *update([layer.T], blocks, decayed, keep, 40 * MIB)


def on_device(
    seq, hidden, inner_values, log_decay, skip_gain, cotangent, master, mask_now, mask_next
):
    groups = master.shape[1] // (2 * STATE)
    axes = ("seq", "head", "sub")
    rows = hidden.shape[0] * 3 // 4
    beside = lax.ppermute(hidden[rows:], "head", SWAP)
    top = lax.ppermute(hidden[:rows], axes, transpose_pairs(seq, False))
    low = lax.ppermute(beside, axes, transpose_pairs(seq, True))
    effective, decayed, keep = weights(master, mask_now, mask_next)
    sibling_effective = effective_of(
        lax.ppermute(master, "sub", SWAP), lax.ppermute(mask_now, "sub", SWAP)
    )
    xd, yd, mix, mixt, cum, cumt, decay = before(
        inner_values, cotangent, log_decay.T, groups
    )
    top, low = held(top, effective, sibling_effective), held(low, effective, sibling_effective)

    own = [top, low]
    other = [lax.ppermute(piece, "head", SWAP) for piece in own]
    (same,), (cross,) = partials(own, effective, sibling_effective, 1)
    terms = [
        lax.ppermute(same, axes, block_pairs(seq, True, True)),
        lax.ppermute(cross, axes, block_pairs(seq, True, False)),
    ]
    own_turned = turn([held(top, same), low])
    other[0] = held(other[0], xd, own_turned, *terms)
    late = []
    sames, crosses = partials(other, effective, sibling_effective, PARTS)
    for same, cross in zip(sames, crosses):
        if late:
            same, cross = held(same, *late[-1]), held(cross, *late[-1])
        late.append(
            [
                lax.ppermute(same, axes, block_pairs(seq, False, True)),
                lax.ppermute(cross, axes, block_pairs(seq, False, False)),
            ]
        )

    each = groups // PARTS
    spans = range(PARTS)
    projs, messages, nears, fars = zip(
        *(
            states(None, terms, late[p], xd, yd, p * each, each, decay.shape[2])
            for p in spans
        )
    )
    other_turned = turn([held(other[0], nears[0]), other[1]])
    own_turned = held(own_turned, nears[0])
    turned_hidden = [
        own_turned, lax.ppermute(own_turned, "sub", SWAP),
        other_turned, lax.ppermute(other_turned, "sub", SWAP),
    ]
    arrived = [[] for _ in spans]
    hops = (([(0, 1), (3, 2)], nears), ([(1, 2), (2, 1)], fars), ([(1, 0), (2, 3)], None))
    messages = list(messages)
    for pairs, own_terms in hops:
        for p in spans:
            message = messages[p]
            if p:
                message = held(message, arrived[p - 1][-1])
            arrived[p].append(lax.ppermute(message, "seq", pairs))
        for p in spans:
            if own_terms:
                messages[p] = handed_on(decay, arrived[p][-1], own_terms[p], p * each)
    blocks = [[] for _ in range(seq)]
    for p in spans:
        grad = grads(
            None, projs[p], xd, yd, mix, mixt, arrived[p][0], arrived[p][1:], p * each
        )
        blocks[0].append(grad)
        for distance in range(seq - 1, 0, -1):
            pairs = to_all(seq, seq - distance)
            if p == 0 and distance == 1:
                grad = held(grad, arrived[-1][-1])
            blocks[distance].append(lax.ppermute(grad, "seq", pairs))

    ssd_output = output(
        None, inner_values, cum, cumt, skip_gain,
        projs, [a[0] for a in arrived], [a[1:] for a in arrived],
    )
    new_weight, sparse_weight = update(turned_hidden, blocks, decayed, keep, 16 * MIB)
    return ssd_output, new_weight, sparse_weight


PARTS = 2


def solution(mesh):
    by_position = P(("grp", "seq"), ("head", "sub"))
    by_row = P("seq", ("head", "sub"))
    seq, head, sub = (mesh.shape[name] for name in ("seq", "head", "sub"))
    body = on_device if (seq, head, sub) == (4, 2, 2) else on_device_general
    return jax.shard_map(
        functools.partial(body, seq),
        mesh=mesh,
        in_specs=(
            by_position, by_position, by_position, P(("head", "sub")), by_position,
            by_row, by_row, by_row,
        ),
        out_specs=(by_position, by_position, by_position),
        check_vma=False,
    )
```

```python
import functools
import math

import jax
import jax.numpy as jnp
from jax import lax
from jax.experimental import pallas as pl
from jax.experimental.pallas import tpu as pltpu
from jax.sharding import PartitionSpec as P

D = 4096
STATE = 128
SPAN = 256
LEARN_RATE = 0.05
WEIGHT_DECAY = 10.0
WEIGHT_SCALE = 2.0 / math.sqrt(D)
KEEP_BITS = (0b000111, 0b011001, 0b101010, 0b110100)
OUT_OF_SIGHT = -1e30
MIB = 1024 * 1024

F32 = jnp.float32
BF16 = jnp.bfloat16
NT = (((1,), (1,)), ((), ()))


def call(kernel, out_shape, flops, moved, exps=0, vmem=16 * MIB, **more):
    return pl.pallas_call(
        kernel,
        out_shape=out_shape,
        compiler_params=pltpu.CompilerParams(vmem_limit_bytes=vmem),
        cost_estimate=pl.CostEstimate(flops=flops, bytes_accessed=moved, transcendentals=exps),
        **more,
    )


def dot(a, b):
    return jnp.dot(a, b, preferred_element_type=F32)


def dot_nt(a, b):
    return lax.dot_general(a, b, NT, preferred_element_type=F32)


def turned(a):
    return a.astype(F32).T.astype(BF16)


def expanded(codes, rows):
    spread = (
        lax.broadcasted_iota(jnp.int32, (rows, rows // 4), 0) // 4
        == lax.broadcasted_iota(jnp.int32, (rows, rows // 4), 1)
    ).astype(F32)
    code = dot(spread.astype(BF16), codes.astype(F32).astype(BF16)).astype(jnp.int32)
    place = lax.broadcasted_iota(jnp.int32, (rows, 1), 0) % 4
    bits = jnp.where(
        place < 2,
        jnp.where(place == 0, KEEP_BITS[0], KEEP_BITS[1]),
        jnp.where(place == 2, KEEP_BITS[2], KEEP_BITS[3]),
    )
    return lax.shift_right_logical(jnp.broadcast_to(bits, code.shape), code) & 1


def weights_kernel(master_ref, now_ref, next_ref, effective_ref, decayed_ref, keep_ref):
    rows = master_ref.shape[0]
    master = master_ref[...]
    kept = expanded(now_ref[...], rows) == 1
    effective_ref[...] = jnp.where(kept, master * WEIGHT_SCALE, 0.0).astype(BF16)
    decayed_ref[...] = jnp.where(kept, master, master * (1.0 - LEARN_RATE * WEIGHT_DECAY))
    keep_ref[...] = expanded(next_ref[...], rows).astype(F32).astype(BF16)


def weights(master, mask_now, mask_next):
    rows, columns = master.shape
    block = min(rows, 256)
    full = pl.BlockSpec((block, columns), lambda i: (i, 0))
    quarter = pl.BlockSpec((block // 4, columns), lambda i: (i, 0))
    return call(
        weights_kernel,
        (
            jax.ShapeDtypeStruct((rows, columns), BF16),
            jax.ShapeDtypeStruct((rows, columns), F32),
            jax.ShapeDtypeStruct((rows, columns), BF16),
        ),
        flops=rows * columns * 3000,
        moved=rows * columns * 14,
        grid=(rows // block,),
        in_specs=[full, quarter, quarter],
        out_specs=(full, full, full),
    )(master, mask_now, mask_next)


def effective_kernel(master_ref, now_ref, effective_ref):
    kept = expanded(now_ref[...], master_ref.shape[0]) == 1
    effective_ref[...] = jnp.where(kept, master_ref[...] * WEIGHT_SCALE, 0.0).astype(BF16)


def effective_of(master, mask_now):
    rows, columns = master.shape
    block = min(rows, 256)
    full = pl.BlockSpec((block, columns), lambda i: (i, 0))
    return call(
        effective_kernel,
        jax.ShapeDtypeStruct((rows, columns), BF16),
        flops=rows * columns * 3000,
        moved=rows * columns * 7,
        grid=(rows // block,),
        in_specs=[full, pl.BlockSpec((block // 4, columns), lambda i: (i, 0))],
        out_specs=full,
    )(master, mask_now)


def lanes_of(left, right, wide):
    lane = lax.broadcasted_iota(jnp.int32, (left.shape[0], wide), 1)
    return jnp.where(lane < wide // 2, left, right)


def decays_of(col, row):
    half = SPAN // 2
    causal = lax.broadcasted_iota(jnp.int32, (half, half), 0) >= lax.broadcasted_iota(
        jnp.int32, (half, half), 1
    )
    top = jnp.exp(jnp.where(causal, col[:half] - row[:, :half], OUT_OF_SIGHT))
    low = jnp.exp(col[half:] - row[:, :half])
    end = jnp.exp(jnp.where(causal, col[half:] - row[:, half:], OUT_OF_SIGHT))
    return top, low, end


def before_kernel(
    x_ref, dy_ref, logt_ref,
    xd_ref, yd_ref, mix_ref, mixt_ref, cum_ref, cumt_ref, end_ref, tall_ref,
):
    heads = cum_ref.shape[2]
    half = SPAN // 2
    wide = x_ref.shape[1] // heads * 2
    row = lax.broadcasted_iota(jnp.int32, (SPAN, SPAN), 0)
    col = lax.broadcasted_iota(jnp.int32, (SPAN, SPAN), 1)
    first = pl.multiple_of(pl.program_id(0) * heads, heads)
    cumt = jnp.dot(
        logt_ref[pl.ds(first, heads), :], (row <= col).astype(F32),
        precision=lax.Precision.HIGHEST, preferred_element_type=F32,
    )
    tall_ref[...] = jnp.zeros_like(tall_ref)
    tall_ref[:heads, :] = cumt
    cum = tall_ref[...].T[:, :heads]
    cum_ref[0] = cum
    cumt_ref[0] = cumt
    end = cum[SPAN - 1 :, :]
    from_start = jnp.exp(cum)
    to_end = jnp.exp(end - cum)
    whole = jnp.exp(end)
    mix = [jnp.zeros((half, half), F32) for _ in range(3)]
    lane = lax.broadcasted_iota(jnp.int32, (SPAN, wide), 1)
    for pair in range(heads // 2):
        a, b = 2 * pair, 2 * pair + 1
        cut = slice(pair * wide, (pair + 1) * wide)
        x = x_ref[:, cut]
        dy = dy_ref[:, cut]
        wide_dy = dy.astype(F32)
        xd_ref[:, cut] = (
            x.astype(F32) * lanes_of(to_end[:, a : a + 1], to_end[:, b : b + 1], wide)
        ).astype(BF16)
        yd_ref[:, cut] = (
            wide_dy * lanes_of(from_start[:, a : a + 1], from_start[:, b : b + 1], wide)
        ).astype(BF16)
        end_ref[0, :, cut] = lanes_of(whole[:, a : a + 1], whole[:, b : b + 1], wide)
        for head, mine in ((a, lane < wide // 2), (b, lane >= wide // 2)):
            one = jnp.where(mine, wide_dy, 0.0).astype(BF16)
            decays = decays_of(cum[:, head : head + 1], cumt[head : head + 1, :])
            mix[0] += dot_nt(one[:half], x[:half]) * decays[0]
            both = dot_nt(one[half:], x)
            mix[1] += both[:, :half] * decays[1]
            mix[2] += both[:, half:] * decays[2]
    nothing = jnp.zeros((half, half), BF16)
    top, low, end_mix = (m.astype(BF16) for m in mix)
    topt, lowt, end_mixt = (m.T.astype(BF16) for m in mix)
    mix_ref[0, :half, :half] = top
    mix_ref[0, :half, half:] = nothing
    mix_ref[0, half:, :half] = low
    mix_ref[0, half:, half:] = end_mix
    mixt_ref[0, :half, :half] = topt
    mixt_ref[0, :half, half:] = lowt
    mixt_ref[0, half:, :half] = nothing
    mixt_ref[0, half:, half:] = end_mixt


def wide_spec(width):
    return pl.BlockSpec((SPAN, width), lambda g: (0, g))


def lead_spec(*shape):
    return pl.BlockSpec((1, *shape), lambda g: (g, *(0 for _ in shape)))


def before(values, cotan, logs_t, groups):
    heads = logs_t.shape[0] // groups
    width = values.shape[1] // groups
    wide = wide_spec(width)
    return call(
        before_kernel,
        (
            jax.ShapeDtypeStruct(values.shape, BF16),
            jax.ShapeDtypeStruct(values.shape, BF16),
            jax.ShapeDtypeStruct((groups, SPAN, SPAN), BF16),
            jax.ShapeDtypeStruct((groups, SPAN, SPAN), BF16),
            jax.ShapeDtypeStruct((groups, SPAN, heads), F32),
            jax.ShapeDtypeStruct((groups, heads, SPAN), F32),
            jax.ShapeDtypeStruct((groups, 1, width), F32),
        ),
        flops=groups * heads * SPAN * SPAN * 2500,
        moved=values.size * 8,
        exps=groups * heads * SPAN * SPAN,
        grid=(groups,),
        in_specs=[wide, wide, pl.BlockSpec(logs_t.shape, lambda g: (0, 0))],
        out_specs=(
            wide, wide, lead_spec(SPAN, SPAN), lead_spec(SPAN, SPAN),
            lead_spec(SPAN, heads), lead_spec(heads, SPAN), lead_spec(1, width),
        ),
        scratch_shapes=[pltpu.VMEM((STATE, SPAN), F32)],
    )(values, cotan, logs_t)


def partial_kernel(*refs):
    (*pieces, weight_ref, sibling_weight_ref, out_ref, sibling_out_ref) = refs
    start = 0
    for piece in pieces:
        rows = slice(start, start + piece.shape[0])
        start += piece.shape[0]
        out_ref[rows, :] = dot(piece[...], weight_ref[...]).astype(BF16)
        sibling_out_ref[rows, :] = dot(piece[...], sibling_weight_ref[...]).astype(BF16)


def partials(pieces, effective, sibling_effective):
    rows, columns = sum(piece.shape[0] for piece in pieces), effective.shape[1]
    whole = pl.BlockSpec(memory_space=pltpu.VMEM)
    return call(
        partial_kernel,
        (jax.ShapeDtypeStruct((rows, columns), BF16),) * 2,
        flops=4 * rows * effective.size,
        moved=(rows * effective.shape[0] + 2 * effective.size + 2 * rows * columns) * 2,
        in_specs=[whole] * (len(pieces) + 2),
        out_specs=(whole,) * 2,
    )(*pieces, effective, sibling_effective)


def turn_kernel(*refs):
    (*pieces, out_ref) = refs
    start = 0
    for piece in pieces:
        out_ref[:, start : start + piece.shape[0]] = turned(piece[...])
        start += piece.shape[0]


def turn(pieces):
    rows, features = sum(piece.shape[0] for piece in pieces), pieces[0].shape[1]
    whole = pl.BlockSpec(memory_space=pltpu.VMEM)
    return call(
        turn_kernel,
        jax.ShapeDtypeStruct((features, rows), BF16),
        flops=rows * features * 2000,
        moved=rows * features * 4,
        in_specs=[whole] * len(pieces),
        out_specs=whole,
    )(*pieces)


def either(ahead, first, second, body):
    if ahead:
        return body(first, second)
    lower = lax.axis_index("seq") < lax.axis_size("seq") // 2

    @pl.when(lower)
    def _():
        body(first, second)

    @pl.when(jnp.logical_not(lower))
    def _():
        body(second, first)


def states_kernel(both, *refs):
    (*terms, xd_ref, yd_ref, proj_ref, near_low_ref, near_ref, far_ref) = refs
    total = terms[0][...].astype(F32)
    for term in terms[1:]:
        total += term[...].astype(F32)
    low = total.astype(BF16)
    proj_ref[...] = low
    state = dot(turned(low[:, :STATE]), xd_ref[...])
    adjoint = dot(turned(low[:, STATE:]), yd_ref[...])

    def put(near, far):
        near_low_ref[0] = near.astype(BF16)
        near_ref[0] = near
        far_ref[0] = far

    either(both, state, adjoint, put)


def states(ahead, terms, xd, yd, first, groups, width):
    pair = pl.BlockSpec((SPAN, 2 * STATE), lambda g: (0, g))
    pair_from = pl.BlockSpec((SPAN, 2 * STATE), lambda g: (0, g + first))
    wide = pl.BlockSpec((SPAN, width), lambda g: (0, g + first))
    lead = lead_spec(STATE, width)
    shape = (groups, STATE, width)
    return call(
        functools.partial(states_kernel, ahead),
        (
            jax.ShapeDtypeStruct((SPAN, groups * 2 * STATE), BF16),
            jax.ShapeDtypeStruct(shape, BF16),
            jax.ShapeDtypeStruct(shape, F32),
            jax.ShapeDtypeStruct(shape, F32),
        ),
        flops=4 * SPAN * groups * width * STATE,
        moved=groups * SPAN * (width * 4 + 4 * STATE * 5),
        grid=(groups,),
        in_specs=[pair_from] * len(terms) + [wide, wide],
        out_specs=(pair, lead, lead, lead),
    )(*terms, xd, yd)


def added(refs):
    total = refs[0][0]
    for ref in refs[1:]:
        total += ref[0]
    return total


def message_kernel(decay_ref, arrived_ref, own_ref, out_ref):
    out_ref[0] = (decay_ref[0] * arrived_ref[0].astype(F32) + own_ref[0]).astype(BF16)


def handed_on(decay, arrived, own, first):
    groups, _, width = arrived.shape
    lead = lead_spec(STATE, width)
    return call(
        message_kernel,
        jax.ShapeDtypeStruct(arrived.shape, BF16),
        flops=2 * arrived.size,
        moved=8 * arrived.size,
        grid=(groups,),
        in_specs=[pl.BlockSpec((1, 1, width), lambda g: (g + first, 0, 0)), lead, lead],
        out_specs=lead,
    )(decay, arrived, own)


def grads_kernel(ahead, proj_ref, xd_ref, yd_ref, mix_ref, mixt_ref, near_ref, *refs):
    (*far_refs, out_ref) = refs

    def body(start, adjoint):
        write, read = proj_ref[:, :STATE], proj_ref[:, STATE:]
        grad_write = dot(mixt_ref[0], read) + dot_nt(xd_ref[...], added(adjoint))
        grad_read = dot(mix_ref[0], write) + dot_nt(yd_ref[...], added(start))
        out_ref[:, :STATE] = grad_write.astype(BF16)
        out_ref[:, STATE:] = grad_read.astype(BF16)

    either(ahead, [near_ref], far_refs, body)


def grads(ahead, proj, xd, yd, mix, mixt, near, far, first):
    groups, _, width = near.shape
    pair = pl.BlockSpec((SPAN, 2 * STATE), lambda g: (0, g))
    wide = pl.BlockSpec((SPAN, width), lambda g: (0, g + first))
    square = pl.BlockSpec((1, SPAN, SPAN), lambda g: (g + first, 0, 0))
    return call(
        functools.partial(grads_kernel, ahead),
        jax.ShapeDtypeStruct(proj.shape, BF16),
        flops=4 * SPAN * groups * (width + SPAN) * STATE,
        moved=groups * SPAN * width * 8,
        grid=(groups,),
        in_specs=[pair, wide, wide, square, square]
        + [lead_spec(STATE, width)] * (1 + len(far)),
        out_specs=pair,
    )(proj, xd, yd, mix, mixt, near, *far)


def output_kernel(parts, hops, ahead, skip_ref, x_ref, cum_ref, cumt_ref, *refs):
    (*refs, out_ref, proj_ref, start_ref) = refs
    projs, nears = refs[:parts], refs[parts : 2 * parts]
    fars = [refs[2 * parts + hops * p : 2 * parts + hops * (p + 1)] for p in range(parts)]
    each = projs[0].shape[1] // (2 * STATE)
    for group in range(parts * each):
        part, at = divmod(group, each)

        @pl.when(pl.program_id(0) == group)
        def _(part=part, at=at):
            proj_ref[...] = projs[part][:, at * 2 * STATE : (at + 1) * 2 * STATE]

            def put(start, _):
                start_ref[...] = added([ref.at[at : at + 1] for ref in start])

            either(ahead, [nears[part]], fars[part], put)

    heads = cum_ref.shape[2]
    half = SPAN // 2
    wide = x_ref.shape[1] // heads * 2
    write = proj_ref[:, :STATE]
    read = proj_ref[:, STATE:]
    cum = cum_ref[0]
    cumt = cumt_ref[0]
    from_start = jnp.exp(cum)
    scores = dot_nt(read, write)
    top, low, end = scores[:half, :half], scores[half:, :half], scores[half:, half:]
    lane = lax.broadcasted_iota(jnp.int32, (half, wide), 1)
    for pair in range(heads // 2):
        a, b = 2 * pair, 2 * pair + 1
        cut = slice(pair * wide, (pair + 1) * wide)
        x = x_ref[:, cut]
        upper, lower = [], []
        for head in (a, b):
            decays = decays_of(cum[:, head : head + 1], cumt[head : head + 1, :])
            upper.append(dot((top * decays[0]).astype(BF16), x[:half]))
            lower.append(
                dot((low * decays[1]).astype(BF16), x[:half])
                + dot((end * decays[2]).astype(BF16), x[half:])
            )
        carried = dot(read, start_ref[:, cut]) * lanes_of(
            from_start[:, a : a + 1], from_start[:, b : b + 1], wide
        )
        head = pl.program_id(0) * heads + a
        gain = jnp.where(
            lax.broadcasted_iota(jnp.int32, (1, wide), 1) < wide // 2,
            skip_ref[head], skip_ref[head + 1],
        )
        rest = carried + gain * x.astype(F32)
        out_ref[:half, cut] = (
            jnp.where(lane < wide // 2, upper[0], upper[1]) + rest[:half]
        ).astype(BF16)
        out_ref[half:, cut] = (
            jnp.where(lane < wide // 2, lower[0], lower[1]) + rest[half:]
        ).astype(BF16)


def output(ahead, values, cum, cumt, skip, projs, nears, fars):
    groups, _, heads = cum.shape
    width = values.shape[1] // groups
    wide = wide_spec(width)
    pieces = [*projs, *nears, *(ref for far in fars for ref in far)]
    return call(
        functools.partial(output_kernel, len(projs), len(fars[0]), ahead),
        jax.ShapeDtypeStruct(values.shape, BF16),
        flops=groups * heads * SPAN * SPAN * 2000,
        moved=values.size * 5,
        exps=groups * heads * SPAN * SPAN,
        grid=(groups,),
        in_specs=[
            pl.BlockSpec(memory_space=pltpu.SMEM), wide, lead_spec(SPAN, heads),
            lead_spec(heads, SPAN),
        ]
        + [pl.BlockSpec(memory_space=pltpu.VMEM)] * len(pieces),
        out_specs=wide,
        scratch_shapes=[
            pltpu.VMEM((SPAN, 2 * STATE), BF16), pltpu.VMEM((STATE, width), BF16)
        ],
    )(skip, values, cum, cumt, *pieces)


def spot_of(block, spots):
    if spots == 1:
        return 0
    other_x = (lax.axis_index("head") != block % 2).astype(jnp.int32)
    other_core = (lax.axis_index("sub") != block // 2).astype(jnp.int32)
    return 2 * other_x + other_core


def update_kernel(blocks, spots, part, *refs):
    turned_refs, pieces = refs[:spots], refs[spots : spots + blocks]
    decayed_ref, keep_ref = refs[spots + blocks : spots + blocks + 2]
    weight_ref, sparse_ref, grad_ref, weight_out, sparse_out, sems = refs[-6:]
    tokens, width = pieces[0].shape
    rows = decayed_ref.shape[0]
    step = min(rows, 256)
    columns = slice(part * width, (part + 1) * width)
    for block, piece in enumerate(pieces):
        start = pl.multiple_of(spot_of(block, spots) * tokens, tokens)
        grad_ref[pl.ds(start, tokens), :] = piece[...]
    copies = []
    for number in range(rows // step):
        here = slice(number * step, (number + 1) * step)
        total = dot(turned_refs[0][here, :], grad_ref[:tokens, :])
        for spot in range(1, spots):
            total += dot(
                turned_refs[spot][here, :], grad_ref[spot * tokens : (spot + 1) * tokens, :]
            )
        weight = decayed_ref[here, columns] - (LEARN_RATE * WEIGHT_SCALE) * total
        weight_out[here, :] = weight
        sparse_out[here, :] = (weight * keep_ref[here, columns].astype(F32)).astype(BF16)
        for place, (source, target) in enumerate(
            ((weight_out, weight_ref), (sparse_out, sparse_ref))
        ):
            copies.append(
                pltpu.make_async_copy(
                    source.at[here, :], target.at[here, columns], sems.at[place, number]
                )
            )
            copies[-1].start()
    for copy in copies:
        copy.wait()


def update(turned_hidden, grad_blocks, decayed, keep, part, earlier, vmem):
    rows, columns = decayed.shape
    width = grad_blocks[0].shape[1]
    tokens = turned_hidden[0].shape[1]
    spots, blocks = len(turned_hidden), len(grad_blocks)
    earlier = earlier or ()
    whole, anywhere = pl.BlockSpec(memory_space=pltpu.VMEM), pl.BlockSpec(memory_space=pl.ANY)
    return call(
        functools.partial(update_kernel, blocks, spots, part),
        (jax.ShapeDtypeStruct((rows, columns), F32), jax.ShapeDtypeStruct((rows, columns), BF16)),
        flops=2 * spots * tokens * rows * width,
        moved=rows * width * 12 + spots * tokens * (rows + width) * 2,
        vmem=vmem,
        in_specs=[whole] * (spots + blocks + 2) + [anywhere] * len(earlier),
        out_specs=(anywhere, anywhere),
        scratch_shapes=[
            pltpu.VMEM((spots * tokens, width), BF16),
            pltpu.VMEM((rows, width), F32),
            pltpu.VMEM((rows, width), BF16),
            pltpu.SemaphoreType.DMA((2, rows // min(rows, 256))),
        ],
        input_output_aliases={spots + blocks + 2 + i: i for i in range(len(earlier))},
    )(*turned_hidden, *grad_blocks, decayed, keep, *earlier)


def held(after, *before):
    return lax.optimization_barrier((after, *before))[0]


def to_all(seq, distance):
    return [(source, (source + distance) % seq) for source in range(seq)]


def block_pairs(seq, near, same_core):
    return [
        (
            (z * 2 + x) * 2 + core,
            ((z + (x if near else 1 - x) + 2 * core) % seq * 2 + x) * 2
            + (core if same_core else 1 - core),
        )
        for z in range(seq)
        for x in range(2)
        for core in range(2)
    ]


def transpose_pairs(seq, changed):
    pairs = []
    for z in range(seq):
        for x in range(2):
            for core in range(2):
                layer = 2 * x + core
                distance = (z - layer) % seq
                source = (z * 2 + (1 - x if changed else x)) * 2 + core
                pairs.append((source, (layer * 2 + distance % 2) * 2 + distance // 2))
    return pairs


SWAP = [(0, 1), (1, 0)]


def chain(own, own_low, decay, seq, step):
    arrived = jnp.zeros_like(own_low)
    message = own_low
    first = 0 if step > 0 else seq - 1
    for hop in range(seq - 1):
        source = first + hop * step
        if hop:
            message = handed_on(decay, arrived, own, 0)
        arrived = arrived + lax.ppermute(message, "seq", [(source, source + step)])
    return arrived


def on_device_general(
    seq, hidden, inner_values, log_decay, skip_gain, cotangent, master, mask_now, mask_next
):
    groups = master.shape[1] // (2 * STATE)
    effective, decayed, keep = weights(master, mask_now, mask_next)
    features = lax.all_gather(hidden, ("head", "sub"), axis=1, tiled=True)
    layer = lax.all_to_all(features, "seq", split_axis=1, concat_axis=0, tiled=True)
    xd, yd, mix, mixt, cum, cumt, decay = before(
        inner_values, cotangent, log_decay.T, groups
    )
    part = dot(layer, effective).astype(BF16)
    terms = [lax.psum_scatter(part, "seq", scatter_dimension=0, tiled=True)]
    proj, state_low, state, adjoint = states(True, terms, xd, yd, 0, groups, decay.shape[2])
    start = chain(state, state_low, decay, seq, 1)
    adjoint_in = chain(adjoint, adjoint.astype(BF16), decay, seq, -1)
    grad = grads(True, proj, xd, yd, mix, mixt, start, [adjoint_in], 0)
    blocks = [lax.all_gather(grad, "seq", axis=0, tiled=True)]
    ssd_output = output(
        True, inner_values, cum, cumt, skip_gain, [proj], [start], [[adjoint_in]]
    )
    return ssd_output, *update([layer.T], blocks, decayed, keep, 0, None, 40 * MIB)


def on_device(
    seq, hidden, inner_values, log_decay, skip_gain, cotangent, master, mask_now, mask_next
):
    groups = master.shape[1] // (2 * STATE)
    axes = ("seq", "head", "sub")
    rows = hidden.shape[0] // 2
    beside = lax.ppermute(hidden[rows:], "head", SWAP)
    top = lax.ppermute(held(hidden[:rows], beside), axes, transpose_pairs(seq, False))
    low = lax.ppermute(beside, axes, transpose_pairs(seq, True))
    effective, decayed, keep = weights(master, mask_now, mask_next)
    sibling_effective = effective_of(
        lax.ppermute(master, "sub", SWAP), lax.ppermute(mask_now, "sub", SWAP)
    )
    xd, yd, mix, mixt, cum, cumt, decay = before(
        inner_values, cotangent, log_decay.T, groups
    )
    top, low = held(top, effective, sibling_effective), held(low, effective, sibling_effective)

    own = [top, low]
    other = [lax.ppermute(piece, "head", SWAP) for piece in own]
    same, cross = partials(own, effective, sibling_effective)
    terms = [
        lax.ppermute(same, axes, block_pairs(seq, True, True)),
        lax.ppermute(cross, axes, block_pairs(seq, True, False)),
    ]
    own_turned = turn([held(top, same), low])
    other[0] = held(other[0], xd, own_turned, *terms)
    same, cross = partials(other, effective, sibling_effective)
    terms += [
        lax.ppermute(same, axes, block_pairs(seq, False, True)),
        lax.ppermute(cross, axes, block_pairs(seq, False, False)),
    ]

    each = groups // PARTS
    spans = range(PARTS)
    projs, messages, nears, fars = zip(
        *(
            states(None, terms, xd, yd, p * each, each, decay.shape[2])
            for p in spans
        )
    )
    other_turned = turn([held(other[0], nears[0]), other[1]])
    own_turned = held(own_turned, nears[0])
    turned_hidden = [
        own_turned, lax.ppermute(own_turned, "sub", SWAP),
        other_turned, lax.ppermute(other_turned, "sub", SWAP),
    ]
    arrived = [[] for _ in spans]
    hops = (([(0, 1), (3, 2)], nears), ([(1, 2), (2, 1)], fars), ([(1, 0), (2, 3)], None))
    messages = list(messages)
    for pairs, own_terms in hops:
        for p in spans:
            message = messages[p]
            if p and not arrived[p]:
                message = held(message, arrived[p - 1][-1])
            arrived[p].append(lax.ppermute(message, "seq", pairs))
        for p in spans:
            if own_terms:
                messages[p] = handed_on(decay, arrived[p][-1], own_terms[p], p * each)
    blocks = []
    for p in spans:
        grad = grads(
            None, projs[p], xd, yd, mix, mixt, arrived[p][0], arrived[p][1:], p * each
        )
        blocks.append([grad])
        for distance in range(1, seq):
            pairs = to_all(seq, seq - distance)
            if p == 0 and distance == seq - 1:
                grad = held(grad, arrived[-1][-1])
            blocks[p].append(lax.ppermute(grad, "seq", pairs))

    ssd_output = output(
        None, inner_values, cum, cumt, skip_gain,
        projs, [a[0] for a in arrived], [a[1:] for a in arrived],
    )
    decayed = held(decayed, blocks[-1][0])
    updated = None
    for p in spans:
        updated = update(turned_hidden, blocks[p], decayed, keep, p, updated, 16 * MIB)
    return ssd_output, *updated


PARTS = 2


def solution(mesh):
    by_position = P(("grp", "seq"), ("head", "sub"))
    by_row = P("seq", ("head", "sub"))
    seq, head, sub = (mesh.shape[name] for name in ("seq", "head", "sub"))
    body = on_device if (seq, head, sub) == (4, 2, 2) else on_device_general
    return jax.shard_map(
        functools.partial(body, seq),
        mesh=mesh,
        in_specs=(
            by_position, by_position, by_position, P(("head", "sub")), by_position,
            by_row, by_row, by_row,
        ),
        out_specs=(by_position, by_position, by_position),
        check_vma=False,
    )
```

```python
import functools
import math

import jax
import jax.numpy as jnp
from jax import lax
from jax.experimental import pallas as pl
from jax.experimental.pallas import tpu as pltpu
from jax.sharding import PartitionSpec as P

D = 4096
STATE = 128
SPAN = 256
LEARN_RATE = 0.05
WEIGHT_DECAY = 10.0
WEIGHT_SCALE = 2.0 / math.sqrt(D)
KEEP_BITS = (0b000111, 0b011001, 0b101010, 0b110100)
OUT_OF_SIGHT = -1e30
MIB = 1024 * 1024

F32 = jnp.float32
BF16 = jnp.bfloat16
NT = (((1,), (1,)), ((), ()))


def call(kernel, out_shape, flops, moved, exps=0, vmem=16 * MIB, **more):
    return pl.pallas_call(
        kernel,
        out_shape=out_shape,
        compiler_params=pltpu.CompilerParams(vmem_limit_bytes=vmem),
        cost_estimate=pl.CostEstimate(flops=flops, bytes_accessed=moved, transcendentals=exps),
        **more,
    )


def dot(a, b):
    return jnp.dot(a, b, preferred_element_type=F32)


def dot_nt(a, b):
    return lax.dot_general(a, b, NT, preferred_element_type=F32)


def turned(a):
    return a.astype(F32).T.astype(BF16)


def expanded(codes, rows):
    spread = (
        lax.broadcasted_iota(jnp.int32, (rows, rows // 4), 0) // 4
        == lax.broadcasted_iota(jnp.int32, (rows, rows // 4), 1)
    ).astype(F32)
    code = dot(spread.astype(BF16), codes.astype(F32).astype(BF16)).astype(jnp.int32)
    place = lax.broadcasted_iota(jnp.int32, (rows, 1), 0) % 4
    bits = jnp.where(
        place < 2,
        jnp.where(place == 0, KEEP_BITS[0], KEEP_BITS[1]),
        jnp.where(place == 2, KEEP_BITS[2], KEEP_BITS[3]),
    )
    return lax.shift_right_logical(jnp.broadcast_to(bits, code.shape), code) & 1


def weights_kernel(master_ref, now_ref, next_ref, effective_ref, decayed_ref, keep_ref):
    rows = master_ref.shape[0]
    master = master_ref[...]
    kept = expanded(now_ref[...], rows) == 1
    effective_ref[...] = jnp.where(kept, master * WEIGHT_SCALE, 0.0).astype(BF16)
    decayed_ref[...] = jnp.where(kept, master, master * (1.0 - LEARN_RATE * WEIGHT_DECAY))
    keep_ref[...] = expanded(next_ref[...], rows).astype(F32).astype(BF16)


def weights(master, mask_now, mask_next):
    rows, columns = master.shape
    block = min(rows, 256)
    full = pl.BlockSpec((block, columns), lambda i: (i, 0))
    quarter = pl.BlockSpec((block // 4, columns), lambda i: (i, 0))
    return call(
        weights_kernel,
        (
            jax.ShapeDtypeStruct((rows, columns), BF16),
            jax.ShapeDtypeStruct((rows, columns), F32),
            jax.ShapeDtypeStruct((rows, columns), BF16),
        ),
        flops=rows * columns * 3000,
        moved=rows * columns * 14,
        grid=(rows // block,),
        in_specs=[full, quarter, quarter],
        out_specs=(full, full, full),
    )(master, mask_now, mask_next)


def effective_kernel(master_ref, now_ref, effective_ref):
    kept = expanded(now_ref[...], master_ref.shape[0]) == 1
    effective_ref[...] = jnp.where(kept, master_ref[...] * WEIGHT_SCALE, 0.0).astype(BF16)


def effective_of(master, mask_now):
    rows, columns = master.shape
    block = min(rows, 256)
    full = pl.BlockSpec((block, columns), lambda i: (i, 0))
    return call(
        effective_kernel,
        jax.ShapeDtypeStruct((rows, columns), BF16),
        flops=rows * columns * 3000,
        moved=rows * columns * 7,
        grid=(rows // block,),
        in_specs=[full, pl.BlockSpec((block // 4, columns), lambda i: (i, 0))],
        out_specs=full,
    )(master, mask_now)


def lanes_of(left, right, wide):
    lane = lax.broadcasted_iota(jnp.int32, (left.shape[0], wide), 1)
    return jnp.where(lane < wide // 2, left, right)


def decays_of(col, row):
    half = SPAN // 2
    causal = lax.broadcasted_iota(jnp.int32, (half, half), 0) >= lax.broadcasted_iota(
        jnp.int32, (half, half), 1
    )
    top = jnp.exp(jnp.where(causal, col[:half] - row[:, :half], OUT_OF_SIGHT))
    low = jnp.exp(col[half:] - row[:, :half])
    end = jnp.exp(jnp.where(causal, col[half:] - row[:, half:], OUT_OF_SIGHT))
    return top, low, end


def before_kernel(
    x_ref, dy_ref, logt_ref,
    xd_ref, yd_ref, mix_ref, mixt_ref, cum_ref, cumt_ref, end_ref, tall_ref,
):
    heads = cum_ref.shape[2]
    half = SPAN // 2
    wide = x_ref.shape[1] // heads * 2
    row = lax.broadcasted_iota(jnp.int32, (SPAN, SPAN), 0)
    col = lax.broadcasted_iota(jnp.int32, (SPAN, SPAN), 1)
    first = pl.multiple_of(pl.program_id(0) * heads, heads)
    cumt = jnp.dot(
        logt_ref[pl.ds(first, heads), :], (row <= col).astype(F32),
        precision=lax.Precision.HIGHEST, preferred_element_type=F32,
    )
    tall_ref[...] = jnp.zeros_like(tall_ref)
    tall_ref[:heads, :] = cumt
    cum = tall_ref[...].T[:, :heads]
    cum_ref[0] = cum
    cumt_ref[0] = cumt
    end = cum[SPAN - 1 :, :]
    from_start = jnp.exp(cum)
    to_end = jnp.exp(end - cum)
    whole = jnp.exp(end)
    mix = [jnp.zeros((half, half), F32) for _ in range(3)]
    lane = lax.broadcasted_iota(jnp.int32, (SPAN, wide), 1)
    for pair in range(heads // 2):
        a, b = 2 * pair, 2 * pair + 1
        cut = slice(pair * wide, (pair + 1) * wide)
        x = x_ref[:, cut]
        dy = dy_ref[:, cut]
        wide_dy = dy.astype(F32)
        xd_ref[:, cut] = (
            x.astype(F32) * lanes_of(to_end[:, a : a + 1], to_end[:, b : b + 1], wide)
        ).astype(BF16)
        yd_ref[:, cut] = (
            wide_dy * lanes_of(from_start[:, a : a + 1], from_start[:, b : b + 1], wide)
        ).astype(BF16)
        end_ref[0, :, cut] = lanes_of(whole[:, a : a + 1], whole[:, b : b + 1], wide)
        for head, mine in ((a, lane < wide // 2), (b, lane >= wide // 2)):
            one = jnp.where(mine, wide_dy, 0.0).astype(BF16)
            decays = decays_of(cum[:, head : head + 1], cumt[head : head + 1, :])
            mix[0] += dot_nt(one[:half], x[:half]) * decays[0]
            both = dot_nt(one[half:], x)
            mix[1] += both[:, :half] * decays[1]
            mix[2] += both[:, half:] * decays[2]
    nothing = jnp.zeros((half, half), BF16)
    top, low, end_mix = (m.astype(BF16) for m in mix)
    topt, lowt, end_mixt = (m.T.astype(BF16) for m in mix)
    mix_ref[0, :half, :half] = top
    mix_ref[0, :half, half:] = nothing
    mix_ref[0, half:, :half] = low
    mix_ref[0, half:, half:] = end_mix
    mixt_ref[0, :half, :half] = topt
    mixt_ref[0, :half, half:] = lowt
    mixt_ref[0, half:, :half] = nothing
    mixt_ref[0, half:, half:] = end_mixt


def wide_spec(width):
    return pl.BlockSpec((SPAN, width), lambda g: (0, g))


def lead_spec(*shape):
    return pl.BlockSpec((1, *shape), lambda g: (g, *(0 for _ in shape)))


def before(values, cotan, logs_t, groups):
    heads = logs_t.shape[0] // groups
    width = values.shape[1] // groups
    wide = wide_spec(width)
    return call(
        before_kernel,
        (
            jax.ShapeDtypeStruct(values.shape, BF16),
            jax.ShapeDtypeStruct(values.shape, BF16),
            jax.ShapeDtypeStruct((groups, SPAN, SPAN), BF16),
            jax.ShapeDtypeStruct((groups, SPAN, SPAN), BF16),
            jax.ShapeDtypeStruct((groups, SPAN, heads), F32),
            jax.ShapeDtypeStruct((groups, heads, SPAN), F32),
            jax.ShapeDtypeStruct((groups, 1, width), F32),
        ),
        flops=groups * heads * SPAN * SPAN * 2500,
        moved=values.size * 8,
        exps=groups * heads * SPAN * SPAN,
        grid=(groups,),
        in_specs=[wide, wide, pl.BlockSpec(logs_t.shape, lambda g: (0, 0))],
        out_specs=(
            wide, wide, lead_spec(SPAN, SPAN), lead_spec(SPAN, SPAN),
            lead_spec(SPAN, heads), lead_spec(heads, SPAN), lead_spec(1, width),
        ),
        scratch_shapes=[pltpu.VMEM((STATE, SPAN), F32)],
    )(values, cotan, logs_t)


def partial_kernel(spread, *refs):
    given = refs[:-1] if spread else refs
    (*pieces, weight_ref, sibling_weight_ref, out_ref, sibling_out_ref) = given
    pieces = [piece[...] for piece in pieces]
    if spread:
        refs[-1][...] = pieces[-2] + pieces[-1]
        pieces[-2:] = [refs[-1][...]]
    start = 0
    for piece in pieces:
        rows = slice(start, start + piece.shape[0])
        start += piece.shape[0]
        out_ref[rows, :] = dot(piece, weight_ref[...]).astype(BF16)
        sibling_out_ref[rows, :] = dot(piece, sibling_weight_ref[...]).astype(BF16)


def partials(pieces, effective, sibling_effective, spread=False):
    rows = sum(piece.shape[0] for piece in pieces[: -1 if spread else None])
    columns = effective.shape[1]
    whole = pl.BlockSpec(memory_space=pltpu.VMEM)
    shapes = [jax.ShapeDtypeStruct((rows, columns), BF16)] * 2
    if spread:
        shapes.append(jax.ShapeDtypeStruct(pieces[-1].shape, BF16))
    return call(
        functools.partial(partial_kernel, spread),
        tuple(shapes),
        flops=4 * rows * effective.size,
        moved=(rows * effective.shape[0] + 2 * effective.size + 2 * rows * columns) * 2,
        in_specs=[whole] * (len(pieces) + 2),
        out_specs=(whole,) * len(shapes),
    )(*pieces, effective, sibling_effective)


def turn_kernel(*refs):
    (*pieces, out_ref) = refs
    start = 0
    for piece in pieces:
        out_ref[:, start : start + piece.shape[0]] = turned(piece[...])
        start += piece.shape[0]


def turn(pieces):
    rows, features = sum(piece.shape[0] for piece in pieces), pieces[0].shape[1]
    whole = pl.BlockSpec(memory_space=pltpu.VMEM)
    return call(
        turn_kernel,
        jax.ShapeDtypeStruct((features, rows), BF16),
        flops=rows * features * 2000,
        moved=rows * features * 4,
        in_specs=[whole] * len(pieces),
        out_specs=whole,
    )(*pieces)


def either(ahead, first, second, body):
    if ahead:
        return body(first, second)
    lower = lax.axis_index("seq") < lax.axis_size("seq") // 2

    @pl.when(lower)
    def _():
        body(first, second)

    @pl.when(jnp.logical_not(lower))
    def _():
        body(second, first)


def states_kernel(both, *refs):
    (*terms, xd_ref, yd_ref, proj_ref, near_low_ref, near_ref, far_ref) = refs
    total = terms[0][...].astype(F32)
    for term in terms[1:]:
        total += term[...].astype(F32)
    low = total.astype(BF16)
    proj_ref[...] = low
    state = dot(turned(low[:, :STATE]), xd_ref[...])
    adjoint = dot(turned(low[:, STATE:]), yd_ref[...])

    def put(near, far):
        near_low_ref[0] = near.astype(BF16)
        near_ref[0] = near
        far_ref[0] = far

    either(both, state, adjoint, put)


def states(ahead, terms, xd, yd, first, groups, width):
    pair = pl.BlockSpec((SPAN, 2 * STATE), lambda g: (0, g))
    pair_from = pl.BlockSpec((SPAN, 2 * STATE), lambda g: (0, g + first))
    wide = pl.BlockSpec((SPAN, width), lambda g: (0, g + first))
    lead = lead_spec(STATE, width)
    shape = (groups, STATE, width)
    return call(
        functools.partial(states_kernel, ahead),
        (
            jax.ShapeDtypeStruct((SPAN, groups * 2 * STATE), BF16),
            jax.ShapeDtypeStruct(shape, BF16),
            jax.ShapeDtypeStruct(shape, F32),
            jax.ShapeDtypeStruct(shape, F32),
        ),
        flops=4 * SPAN * groups * width * STATE,
        moved=groups * SPAN * (width * 4 + 4 * STATE * 5),
        grid=(groups,),
        in_specs=[pair_from] * len(terms) + [wide, wide],
        out_specs=(pair, lead, lead, lead),
    )(*terms, xd, yd)


def added(refs):
    total = refs[0][0]
    for ref in refs[1:]:
        total += ref[0]
    return total


def message_kernel(decay_ref, arrived_ref, own_ref, out_ref):
    out_ref[0] = (decay_ref[0] * arrived_ref[0].astype(F32) + own_ref[0]).astype(BF16)


def handed_on(decay, arrived, own, first):
    groups, _, width = arrived.shape
    lead = lead_spec(STATE, width)
    return call(
        message_kernel,
        jax.ShapeDtypeStruct(arrived.shape, BF16),
        flops=2 * arrived.size,
        moved=8 * arrived.size,
        grid=(groups,),
        in_specs=[pl.BlockSpec((1, 1, width), lambda g: (g + first, 0, 0)), lead, lead],
        out_specs=lead,
    )(decay, arrived, own)


def grads_kernel(ahead, proj_ref, xd_ref, yd_ref, mix_ref, mixt_ref, near_ref, *refs):
    (*far_refs, out_ref) = refs

    def body(start, adjoint):
        write, read = proj_ref[:, :STATE], proj_ref[:, STATE:]
        grad_write = dot(mixt_ref[0], read) + dot_nt(xd_ref[...], added(adjoint))
        grad_read = dot(mix_ref[0], write) + dot_nt(yd_ref[...], added(start))
        out_ref[:, :STATE] = grad_write.astype(BF16)
        out_ref[:, STATE:] = grad_read.astype(BF16)

    either(ahead, [near_ref], far_refs, body)


def grads(ahead, proj, xd, yd, mix, mixt, near, far, first):
    groups, _, width = near.shape
    pair = pl.BlockSpec((SPAN, 2 * STATE), lambda g: (0, g))
    wide = pl.BlockSpec((SPAN, width), lambda g: (0, g + first))
    square = pl.BlockSpec((1, SPAN, SPAN), lambda g: (g + first, 0, 0))
    return call(
        functools.partial(grads_kernel, ahead),
        jax.ShapeDtypeStruct(proj.shape, BF16),
        flops=4 * SPAN * groups * (width + SPAN) * STATE,
        moved=groups * SPAN * width * 8,
        grid=(groups,),
        in_specs=[pair, wide, wide, square, square]
        + [lead_spec(STATE, width)] * (1 + len(far)),
        out_specs=pair,
    )(proj, xd, yd, mix, mixt, near, *far)


def output_kernel(parts, hops, ahead, skip_ref, x_ref, cum_ref, cumt_ref, *refs):
    (*refs, out_ref, proj_ref, start_ref) = refs
    projs, nears = refs[:parts], refs[parts : 2 * parts]
    fars = [refs[2 * parts + hops * p : 2 * parts + hops * (p + 1)] for p in range(parts)]
    each = projs[0].shape[1] // (2 * STATE)
    for group in range(parts * each):
        part, at = divmod(group, each)

        @pl.when(pl.program_id(0) == group)
        def _(part=part, at=at):
            proj_ref[...] = projs[part][:, at * 2 * STATE : (at + 1) * 2 * STATE]

            def put(start, _):
                start_ref[...] = added([ref.at[at : at + 1] for ref in start])

            either(ahead, [nears[part]], fars[part], put)

    heads = cum_ref.shape[2]
    half = SPAN // 2
    wide = x_ref.shape[1] // heads * 2
    write = proj_ref[:, :STATE]
    read = proj_ref[:, STATE:]
    cum = cum_ref[0]
    cumt = cumt_ref[0]
    from_start = jnp.exp(cum)
    scores = dot_nt(read, write)
    top, low, end = scores[:half, :half], scores[half:, :half], scores[half:, half:]
    lane = lax.broadcasted_iota(jnp.int32, (half, wide), 1)
    for pair in range(heads // 2):
        a, b = 2 * pair, 2 * pair + 1
        cut = slice(pair * wide, (pair + 1) * wide)
        x = x_ref[:, cut]
        upper, lower = [], []
        for head in (a, b):
            decays = decays_of(cum[:, head : head + 1], cumt[head : head + 1, :])
            upper.append(dot((top * decays[0]).astype(BF16), x[:half]))
            lower.append(
                dot((low * decays[1]).astype(BF16), x[:half])
                + dot((end * decays[2]).astype(BF16), x[half:])
            )
        carried = dot(read, start_ref[:, cut]) * lanes_of(
            from_start[:, a : a + 1], from_start[:, b : b + 1], wide
        )
        head = pl.program_id(0) * heads + a
        gain = jnp.where(
            lax.broadcasted_iota(jnp.int32, (1, wide), 1) < wide // 2,
            skip_ref[head], skip_ref[head + 1],
        )
        rest = carried + gain * x.astype(F32)
        out_ref[:half, cut] = (
            jnp.where(lane < wide // 2, upper[0], upper[1]) + rest[:half]
        ).astype(BF16)
        out_ref[half:, cut] = (
            jnp.where(lane < wide // 2, lower[0], lower[1]) + rest[half:]
        ).astype(BF16)


def output(ahead, values, cum, cumt, skip, projs, nears, fars):
    groups, _, heads = cum.shape
    width = values.shape[1] // groups
    wide = wide_spec(width)
    pieces = [*projs, *nears, *(ref for far in fars for ref in far)]
    return call(
        functools.partial(output_kernel, len(projs), len(fars[0]), ahead),
        jax.ShapeDtypeStruct(values.shape, BF16),
        flops=groups * heads * SPAN * SPAN * 2000,
        moved=values.size * 5,
        exps=groups * heads * SPAN * SPAN,
        grid=(groups,),
        in_specs=[
            pl.BlockSpec(memory_space=pltpu.SMEM), wide, lead_spec(SPAN, heads),
            lead_spec(heads, SPAN),
        ]
        + [pl.BlockSpec(memory_space=pltpu.VMEM)] * len(pieces),
        out_specs=wide,
        scratch_shapes=[
            pltpu.VMEM((SPAN, 2 * STATE), BF16), pltpu.VMEM((STATE, width), BF16)
        ],
    )(skip, values, cum, cumt, *pieces)


def spot_of(block, spots):
    if spots == 1:
        return 0
    other_x = (lax.axis_index("head") != block % 2).astype(jnp.int32)
    other_core = (lax.axis_index("sub") != block // 2).astype(jnp.int32)
    return 2 * other_x + other_core


def update_kernel(blocks, spots, part, *refs):
    turned_refs, pieces = refs[:spots], refs[spots : spots + blocks]
    decayed_ref, keep_ref = refs[spots + blocks : spots + blocks + 2]
    weight_ref, sparse_ref, grad_ref, weight_out, sparse_out, sems = refs[-6:]
    tokens, width = pieces[0].shape
    rows = decayed_ref.shape[0]
    step = min(rows, 256)
    columns = slice(part * width, (part + 1) * width)
    for block, piece in enumerate(pieces):
        start = pl.multiple_of(spot_of(block, spots) * tokens, tokens)
        grad_ref[pl.ds(start, tokens), :] = piece[...]
    copies = []
    for number in range(rows // step):
        here = slice(number * step, (number + 1) * step)
        total = dot(turned_refs[0][here, :], grad_ref[:tokens, :])
        for spot in range(1, spots):
            total += dot(
                turned_refs[spot][here, :], grad_ref[spot * tokens : (spot + 1) * tokens, :]
            )
        weight = decayed_ref[here, columns] - (LEARN_RATE * WEIGHT_SCALE) * total
        weight_out[here, :] = weight
        sparse_out[here, :] = (weight * keep_ref[here, columns].astype(F32)).astype(BF16)
        for place, (source, target) in enumerate(
            ((weight_out, weight_ref), (sparse_out, sparse_ref))
        ):
            copies.append(
                pltpu.make_async_copy(
                    source.at[here, :], target.at[here, columns], sems.at[place, number]
                )
            )
            copies[-1].start()
    for copy in copies:
        copy.wait()


def update(turned_hidden, grad_blocks, decayed, keep, part, earlier, vmem):
    rows, columns = decayed.shape
    width = grad_blocks[0].shape[1]
    tokens = turned_hidden[0].shape[1]
    spots, blocks = len(turned_hidden), len(grad_blocks)
    earlier = earlier or ()
    whole, anywhere = pl.BlockSpec(memory_space=pltpu.VMEM), pl.BlockSpec(memory_space=pl.ANY)
    return call(
        functools.partial(update_kernel, blocks, spots, part),
        (jax.ShapeDtypeStruct((rows, columns), F32), jax.ShapeDtypeStruct((rows, columns), BF16)),
        flops=2 * spots * tokens * rows * width,
        moved=rows * width * 12 + spots * tokens * (rows + width) * 2,
        vmem=vmem,
        in_specs=[whole] * (spots + blocks + 2) + [anywhere] * len(earlier),
        out_specs=(anywhere, anywhere),
        scratch_shapes=[
            pltpu.VMEM((spots * tokens, width), BF16),
            pltpu.VMEM((rows, width), F32),
            pltpu.VMEM((rows, width), BF16),
            pltpu.SemaphoreType.DMA((2, rows // min(rows, 256))),
        ],
        input_output_aliases={spots + blocks + 2 + i: i for i in range(len(earlier))},
    )(*turned_hidden, *grad_blocks, decayed, keep, *earlier)


def held(after, *before):
    return lax.optimization_barrier((after, *before))[0]


def to_all(seq, distance):
    return [(source, (source + distance) % seq) for source in range(seq)]


def block_pairs(seq, near, same_core):
    return [
        (
            (z * 2 + x) * 2 + core,
            ((z + (x if near else 1 - x) + 2 * core) % seq * 2 + x) * 2
            + (core if same_core else 1 - core),
        )
        for z in range(seq)
        for x in range(2)
        for core in range(2)
    ]


def transpose_pairs(seq):
    stays, crosses, beside, onward = [], [], [], []
    for z in range(seq):
        for x in range(2):
            for core in range(2):
                layer = 2 * x + core
                distance = (z - layer) % seq
                source, step = ((z * 2 + way) * 2 + core for way in (x, 1 - x))
                target = (layer * 2 + distance % 2) * 2 + distance // 2
                if distance % 2 == x:
                    stays.append((source, target))
                else:
                    crosses.append((source, target))
                    beside.append((source, step))
                    onward.append((step, target))
    return stays, crosses, beside, onward


SWAP = [(0, 1), (1, 0)]


def chain(own, own_low, decay, seq, step):
    arrived = jnp.zeros_like(own_low)
    message = own_low
    first = 0 if step > 0 else seq - 1
    for hop in range(seq - 1):
        source = first + hop * step
        if hop:
            message = handed_on(decay, arrived, own, 0)
        arrived = arrived + lax.ppermute(message, "seq", [(source, source + step)])
    return arrived


def on_device_general(
    seq, hidden, inner_values, log_decay, skip_gain, cotangent, master, mask_now, mask_next
):
    groups = master.shape[1] // (2 * STATE)
    effective, decayed, keep = weights(master, mask_now, mask_next)
    features = lax.all_gather(hidden, ("head", "sub"), axis=1, tiled=True)
    layer = lax.all_to_all(features, "seq", split_axis=1, concat_axis=0, tiled=True)
    xd, yd, mix, mixt, cum, cumt, decay = before(
        inner_values, cotangent, log_decay.T, groups
    )
    part = dot(layer, effective).astype(BF16)
    terms = [lax.psum_scatter(part, "seq", scatter_dimension=0, tiled=True)]
    proj, state_low, state, adjoint = states(True, terms, xd, yd, 0, groups, decay.shape[2])
    start = chain(state, state_low, decay, seq, 1)
    adjoint_in = chain(adjoint, adjoint.astype(BF16), decay, seq, -1)
    grad = grads(True, proj, xd, yd, mix, mixt, start, [adjoint_in], 0)
    blocks = [lax.all_gather(grad, "seq", axis=0, tiled=True)]
    ssd_output = output(
        True, inner_values, cum, cumt, skip_gain, [proj], [start], [[adjoint_in]]
    )
    return ssd_output, *update([layer.T], blocks, decayed, keep, 0, None, 40 * MIB)


def on_device(
    seq, hidden, inner_values, log_decay, skip_gain, cotangent, master, mask_now, mask_next
):
    groups = master.shape[1] // (2 * STATE)
    axes = ("seq", "head", "sub")
    rows = hidden.shape[0] // 2
    stays, crosses, beside, onward = transpose_pairs(seq)
    relayed = lax.ppermute(hidden[rows:], axes, beside)
    top = lax.ppermute(hidden[:rows], axes, stays + crosses)
    low = [lax.ppermute(hidden[rows:], axes, stays), lax.ppermute(relayed, axes, onward)]
    effective, decayed, keep = weights(master, mask_now, mask_next)
    sibling_effective = effective_of(
        lax.ppermute(master, "sub", SWAP), lax.ppermute(mask_now, "sub", SWAP)
    )
    xd, yd, mix, mixt, cum, cumt, decay = before(
        inner_values, cotangent, log_decay.T, groups
    )
    top = held(top, effective, sibling_effective)

    other = [lax.ppermute(top, "head", SWAP)]
    same, cross, low = partials([top, *low], effective, sibling_effective, True)
    other.append(lax.ppermute(low, "head", SWAP))
    terms = [
        lax.ppermute(same, axes, block_pairs(seq, True, True)),
        lax.ppermute(cross, axes, block_pairs(seq, True, False)),
    ]
    other[0] = held(other[0], xd, *terms)
    same, cross = partials(other, effective, sibling_effective)
    terms += [
        lax.ppermute(same, axes, block_pairs(seq, False, True)),
        lax.ppermute(cross, axes, block_pairs(seq, False, False)),
    ]

    each = groups // PARTS
    spans = range(PARTS)
    projs, messages, nears, fars = zip(
        *(
            states(None, terms, xd, yd, p * each, each, decay.shape[2])
            for p in spans
        )
    )
    arrived = [[] for _ in spans]
    hops = (([(0, 1), (3, 2)], nears), ([(1, 2), (2, 1)], fars), ([(1, 0), (2, 3)], None))
    messages = list(messages)
    for pairs, own_terms in hops:
        for p in spans:
            message = messages[p]
            if p and not arrived[p]:
                message = held(message, arrived[p - 1][-1])
            arrived[p].append(lax.ppermute(message, "seq", pairs))
        for p in spans:
            if own_terms:
                messages[p] = handed_on(decay, arrived[p][-1], own_terms[p], p * each)
    turned_hidden = []
    for first, second in ((top, low), other):
        piece = turn([held(first, arrived[0][1]), second])
        turned_hidden += [piece, lax.ppermute(piece, "sub", SWAP)]
    inputs = [held(projs[0], *turned_hidden), *projs[1:]]
    blocks = []
    for p in spans:
        grad = grads(
            None, inputs[p], xd, yd, mix, mixt, arrived[p][0], arrived[p][1:], p * each
        )
        blocks.append([grad])
        for distance in range(1, seq):
            pairs = to_all(seq, seq - distance)
            blocks[p].append(lax.ppermute(grad, "seq", pairs))

    decayed = held(decayed, blocks[-1][0])
    updated = None
    for p in spans:
        updated = update(turned_hidden, blocks[p], decayed, keep, p, updated, 16 * MIB)
        if not p:
            cum = held(cum, *updated)
    ssd_output = output(
        None, inner_values, cum, cumt, skip_gain,
        projs, [a[0] for a in arrived], [a[1:] for a in arrived],
    )
    return ssd_output, *updated


PARTS = 2


def solution(mesh):
    by_position = P(("grp", "seq"), ("head", "sub"))
    by_row = P("seq", ("head", "sub"))
    seq, head, sub = (mesh.shape[name] for name in ("seq", "head", "sub"))
    body = on_device if (seq, head, sub) == (4, 2, 2) else on_device_general
    return jax.shard_map(
        functools.partial(body, seq),
        mesh=mesh,
        in_specs=(
            by_position, by_position, by_position, P(("head", "sub")), by_position,
            by_row, by_row, by_row,
        ),
        out_specs=(by_position, by_position, by_position),
        check_vma=False,
    )
```

```python
import functools
import math

import jax
import jax.numpy as jnp
from jax import lax
from jax.experimental import pallas as pl
from jax.experimental.pallas import tpu as pltpu
from jax.sharding import PartitionSpec as P

D = 4096
STATE = 128
SPAN = 256
LEARN_RATE = 0.05
WEIGHT_DECAY = 10.0
WEIGHT_SCALE = 2.0 / math.sqrt(D)
KEEP_BITS = (0b000111, 0b011001, 0b101010, 0b110100)
OUT_OF_SIGHT = -1e30
MIB = 1024 * 1024

F32 = jnp.float32
BF16 = jnp.bfloat16
NT = (((1,), (1,)), ((), ()))


def call(kernel, out_shape, flops, moved, exps=0, vmem=16 * MIB, **more):
    return pl.pallas_call(
        kernel,
        out_shape=out_shape,
        compiler_params=pltpu.CompilerParams(vmem_limit_bytes=vmem),
        cost_estimate=pl.CostEstimate(flops=flops, bytes_accessed=moved, transcendentals=exps),
        **more,
    )


def dot(a, b):
    return jnp.dot(a, b, preferred_element_type=F32)


def dot_nt(a, b):
    return lax.dot_general(a, b, NT, preferred_element_type=F32)


def turned(a):
    return a.astype(F32).T.astype(BF16)


def expanded(codes, rows):
    spread = (
        lax.broadcasted_iota(jnp.int32, (rows, rows // 4), 0) // 4
        == lax.broadcasted_iota(jnp.int32, (rows, rows // 4), 1)
    ).astype(F32)
    code = dot(spread.astype(BF16), codes.astype(F32).astype(BF16)).astype(jnp.int32)
    place = lax.broadcasted_iota(jnp.int32, (rows, 1), 0) % 4
    bits = jnp.where(
        place < 2,
        jnp.where(place == 0, KEEP_BITS[0], KEEP_BITS[1]),
        jnp.where(place == 2, KEEP_BITS[2], KEEP_BITS[3]),
    )
    return lax.shift_right_logical(jnp.broadcast_to(bits, code.shape), code) & 1


def weights_kernel(master_ref, now_ref, next_ref, effective_ref, decayed_ref, keep_ref):
    rows = master_ref.shape[0]
    master = master_ref[...]
    kept = expanded(now_ref[...], rows) == 1
    effective_ref[...] = jnp.where(kept, master * WEIGHT_SCALE, 0.0).astype(BF16)
    decayed_ref[...] = jnp.where(kept, master, master * (1.0 - LEARN_RATE * WEIGHT_DECAY))
    keep_ref[...] = expanded(next_ref[...], rows).astype(F32).astype(BF16)


def weights(master, mask_now, mask_next):
    rows, columns = master.shape
    block = min(rows, 256)
    full = pl.BlockSpec((block, columns), lambda i: (i, 0))
    quarter = pl.BlockSpec((block // 4, columns), lambda i: (i, 0))
    return call(
        weights_kernel,
        (
            jax.ShapeDtypeStruct((rows, columns), BF16),
            jax.ShapeDtypeStruct((rows, columns), F32),
            jax.ShapeDtypeStruct((rows, columns), BF16),
        ),
        flops=rows * columns * 3000,
        moved=rows * columns * 14,
        grid=(rows // block,),
        in_specs=[full, quarter, quarter],
        out_specs=(full, full, full),
    )(master, mask_now, mask_next)


def effective_kernel(master_ref, now_ref, effective_ref):
    kept = expanded(now_ref[...], master_ref.shape[0]) == 1
    effective_ref[...] = jnp.where(kept, master_ref[...] * WEIGHT_SCALE, 0.0).astype(BF16)


def effective_of(master, mask_now):
    rows, columns = master.shape
    block = min(rows, 256)
    full = pl.BlockSpec((block, columns), lambda i: (i, 0))
    return call(
        effective_kernel,
        jax.ShapeDtypeStruct((rows, columns), BF16),
        flops=rows * columns * 3000,
        moved=rows * columns * 7,
        grid=(rows // block,),
        in_specs=[full, pl.BlockSpec((block // 4, columns), lambda i: (i, 0))],
        out_specs=full,
    )(master, mask_now)


def lanes_of(left, right, wide):
    lane = lax.broadcasted_iota(jnp.int32, (left.shape[0], wide), 1)
    return jnp.where(lane < wide // 2, left, right)


def decays_of(col, row):
    half = SPAN // 2
    causal = lax.broadcasted_iota(jnp.int32, (half, half), 0) >= lax.broadcasted_iota(
        jnp.int32, (half, half), 1
    )
    top = jnp.exp(jnp.where(causal, col[:half] - row[:, :half], OUT_OF_SIGHT))
    low = jnp.exp(col[half:] - row[:, :half])
    end = jnp.exp(jnp.where(causal, col[half:] - row[:, half:], OUT_OF_SIGHT))
    return top, low, end


def before_kernel(
    x_ref, dy_ref, logt_ref,
    xd_ref, yd_ref, mix_ref, mixt_ref, cum_ref, cumt_ref, end_ref, tall_ref,
):
    heads = cum_ref.shape[2]
    half = SPAN // 2
    wide = x_ref.shape[1] // heads * 2
    row = lax.broadcasted_iota(jnp.int32, (SPAN, SPAN), 0)
    col = lax.broadcasted_iota(jnp.int32, (SPAN, SPAN), 1)
    first = pl.multiple_of(pl.program_id(0) * heads, heads)
    cumt = jnp.dot(
        logt_ref[pl.ds(first, heads), :], (row <= col).astype(F32),
        precision=lax.Precision.HIGHEST, preferred_element_type=F32,
    )
    tall_ref[...] = jnp.zeros_like(tall_ref)
    tall_ref[:heads, :] = cumt
    cum = tall_ref[...].T[:, :heads]
    cum_ref[0] = cum
    cumt_ref[0] = cumt
    end = cum[SPAN - 1 :, :]
    from_start = jnp.exp(cum)
    to_end = jnp.exp(end - cum)
    whole = jnp.exp(end)
    mix = [jnp.zeros((half, half), F32) for _ in range(3)]
    lane = lax.broadcasted_iota(jnp.int32, (SPAN, wide), 1)
    for pair in range(heads // 2):
        a, b = 2 * pair, 2 * pair + 1
        cut = slice(pair * wide, (pair + 1) * wide)
        x = x_ref[:, cut]
        dy = dy_ref[:, cut]
        wide_dy = dy.astype(F32)
        xd_ref[:, cut] = (
            x.astype(F32) * lanes_of(to_end[:, a : a + 1], to_end[:, b : b + 1], wide)
        ).astype(BF16)
        yd_ref[:, cut] = (
            wide_dy * lanes_of(from_start[:, a : a + 1], from_start[:, b : b + 1], wide)
        ).astype(BF16)
        end_ref[0, :, cut] = lanes_of(whole[:, a : a + 1], whole[:, b : b + 1], wide)
        for head, mine in ((a, lane < wide // 2), (b, lane >= wide // 2)):
            one = jnp.where(mine, wide_dy, 0.0).astype(BF16)
            decays = decays_of(cum[:, head : head + 1], cumt[head : head + 1, :])
            mix[0] += dot_nt(one[:half], x[:half]) * decays[0]
            both = dot_nt(one[half:], x)
            mix[1] += both[:, :half] * decays[1]
            mix[2] += both[:, half:] * decays[2]
    nothing = jnp.zeros((half, half), BF16)
    top, low, end_mix = (m.astype(BF16) for m in mix)
    topt, lowt, end_mixt = (m.T.astype(BF16) for m in mix)
    mix_ref[0, :half, :half] = top
    mix_ref[0, :half, half:] = nothing
    mix_ref[0, half:, :half] = low
    mix_ref[0, half:, half:] = end_mix
    mixt_ref[0, :half, :half] = topt
    mixt_ref[0, :half, half:] = lowt
    mixt_ref[0, half:, :half] = nothing
    mixt_ref[0, half:, half:] = end_mixt


def wide_spec(width):
    return pl.BlockSpec((SPAN, width), lambda g: (0, g))


def lead_spec(*shape):
    return pl.BlockSpec((1, *shape), lambda g: (g, *(0 for _ in shape)))


def before(values, cotan, logs_t, groups):
    heads = logs_t.shape[0] // groups
    width = values.shape[1] // groups
    wide = wide_spec(width)
    return call(
        before_kernel,
        (
            jax.ShapeDtypeStruct(values.shape, BF16),
            jax.ShapeDtypeStruct(values.shape, BF16),
            jax.ShapeDtypeStruct((groups, SPAN, SPAN), BF16),
            jax.ShapeDtypeStruct((groups, SPAN, SPAN), BF16),
            jax.ShapeDtypeStruct((groups, SPAN, heads), F32),
            jax.ShapeDtypeStruct((groups, heads, SPAN), F32),
            jax.ShapeDtypeStruct((groups, 1, width), F32),
        ),
        flops=groups * heads * SPAN * SPAN * 2500,
        moved=values.size * 8,
        exps=groups * heads * SPAN * SPAN,
        grid=(groups,),
        in_specs=[wide, wide, pl.BlockSpec(logs_t.shape, lambda g: (0, 0))],
        out_specs=(
            wide, wide, lead_spec(SPAN, SPAN), lead_spec(SPAN, SPAN),
            lead_spec(SPAN, heads), lead_spec(heads, SPAN), lead_spec(1, width),
        ),
        scratch_shapes=[pltpu.VMEM((STATE, SPAN), F32)],
    )(values, cotan, logs_t)


def partial_kernel(spread, *refs):
    given = refs[:-1] if spread else refs
    (*pieces, weight_ref, sibling_weight_ref, out_ref, sibling_out_ref) = given
    pieces = [piece[...] for piece in pieces]
    if spread:
        refs[-1][...] = pieces[-2] + pieces[-1]
        pieces[-2:] = [refs[-1][...]]
    start = 0
    for piece in pieces:
        rows = slice(start, start + piece.shape[0])
        start += piece.shape[0]
        out_ref[rows, :] = dot(piece, weight_ref[...]).astype(BF16)
        sibling_out_ref[rows, :] = dot(piece, sibling_weight_ref[...]).astype(BF16)


def partials(pieces, effective, sibling_effective, spread=False):
    rows = sum(piece.shape[0] for piece in pieces[: -1 if spread else None])
    columns = effective.shape[1]
    whole = pl.BlockSpec(memory_space=pltpu.VMEM)
    shapes = [jax.ShapeDtypeStruct((rows, columns), BF16)] * 2
    if spread:
        shapes.append(jax.ShapeDtypeStruct(pieces[-1].shape, BF16))
    return call(
        functools.partial(partial_kernel, spread),
        tuple(shapes),
        flops=4 * rows * effective.size,
        moved=(rows * effective.shape[0] + 2 * effective.size + 2 * rows * columns) * 2,
        in_specs=[whole] * (len(pieces) + 2),
        out_specs=(whole,) * len(shapes),
    )(*pieces, effective, sibling_effective)


def turn_kernel(*refs):
    (*pieces, out_ref) = refs
    start = 0
    for piece in pieces:
        out_ref[:, start : start + piece.shape[0]] = turned(piece[...])
        start += piece.shape[0]


def turn(pieces):
    rows, features = sum(piece.shape[0] for piece in pieces), pieces[0].shape[1]
    whole = pl.BlockSpec(memory_space=pltpu.VMEM)
    return call(
        turn_kernel,
        jax.ShapeDtypeStruct((features, rows), BF16),
        flops=rows * features * 2000,
        moved=rows * features * 4,
        in_specs=[whole] * len(pieces),
        out_specs=whole,
    )(*pieces)


def either(ahead, first, second, body):
    if ahead:
        return body(first, second)
    lower = lax.axis_index("seq") < lax.axis_size("seq") // 2

    @pl.when(lower)
    def _():
        body(first, second)

    @pl.when(jnp.logical_not(lower))
    def _():
        body(second, first)


def states_kernel(both, *refs):
    (*terms, xd_ref, yd_ref, proj_ref, near_low_ref, near_ref, far_ref) = refs
    whole = [term for term in terms if term.shape[0] == SPAN]
    total = sum(term[...].astype(F32) for term in whole)
    cut = [term[...].astype(F32) for term in terms if term.shape[0] != SPAN]
    if cut:
        total += jnp.concatenate([a + b for a, b in zip(cut[0::2], cut[1::2])], axis=0)
    low = total.astype(BF16)
    proj_ref[...] = low
    state = dot(turned(low[:, :STATE]), xd_ref[...])
    adjoint = dot(turned(low[:, STATE:]), yd_ref[...])

    def put(near, far):
        near_low_ref[0] = near.astype(BF16)
        near_ref[0] = near
        far_ref[0] = far

    either(both, state, adjoint, put)


def states(ahead, terms, cut_terms, xd, yd, first, groups, width):
    pair = pl.BlockSpec((SPAN, 2 * STATE), lambda g: (0, g))
    pair_from = pl.BlockSpec((SPAN, 2 * STATE), lambda g: (0, g + first))
    wide = pl.BlockSpec((SPAN, width), lambda g: (0, g + first))
    lead = lead_spec(STATE, width)
    shape = (groups, STATE, width)
    return call(
        functools.partial(states_kernel, ahead),
        (
            jax.ShapeDtypeStruct((SPAN, groups * 2 * STATE), BF16),
            jax.ShapeDtypeStruct(shape, BF16),
            jax.ShapeDtypeStruct(shape, F32),
            jax.ShapeDtypeStruct(shape, F32),
        ),
        flops=4 * SPAN * groups * width * STATE,
        moved=groups * SPAN * (width * 4 + 4 * STATE * 5),
        grid=(groups,),
        in_specs=[pair_from] * len(terms)
        + [
            pl.BlockSpec((term.shape[0], 2 * STATE), lambda g: (0, g + first))
            for pieces in cut_terms
            for term in pieces
        ]
        + [wide, wide],
        out_specs=(pair, lead, lead, lead),
    )(*terms, *(term for pieces in cut_terms for term in pieces), xd, yd)


def added(refs):
    total = refs[0][0]
    for ref in refs[1:]:
        total += ref[0]
    return total


def message_kernel(decay_ref, arrived_ref, own_ref, out_ref):
    out_ref[0] = (decay_ref[0] * arrived_ref[0].astype(F32) + own_ref[0]).astype(BF16)


def handed_on(decay, arrived, own, first):
    groups, _, width = arrived.shape
    lead = lead_spec(STATE, width)
    return call(
        message_kernel,
        jax.ShapeDtypeStruct(arrived.shape, BF16),
        flops=2 * arrived.size,
        moved=8 * arrived.size,
        grid=(groups,),
        in_specs=[pl.BlockSpec((1, 1, width), lambda g: (g + first, 0, 0)), lead, lead],
        out_specs=lead,
    )(decay, arrived, own)


def grads_kernel(ahead, proj_ref, xd_ref, yd_ref, mix_ref, mixt_ref, near_ref, *refs):
    (*far_refs, out_ref) = refs

    def body(start, adjoint):
        write, read = proj_ref[:, :STATE], proj_ref[:, STATE:]
        grad_write = dot(mixt_ref[0], read) + dot_nt(xd_ref[...], added(adjoint))
        grad_read = dot(mix_ref[0], write) + dot_nt(yd_ref[...], added(start))
        out_ref[:, :STATE] = grad_write.astype(BF16)
        out_ref[:, STATE:] = grad_read.astype(BF16)

    either(ahead, [near_ref], far_refs, body)


def grads(ahead, proj, xd, yd, mix, mixt, near, far, first):
    groups, _, width = near.shape
    pair = pl.BlockSpec((SPAN, 2 * STATE), lambda g: (0, g))
    wide = pl.BlockSpec((SPAN, width), lambda g: (0, g + first))
    square = pl.BlockSpec((1, SPAN, SPAN), lambda g: (g + first, 0, 0))
    return call(
        functools.partial(grads_kernel, ahead),
        jax.ShapeDtypeStruct(proj.shape, BF16),
        flops=4 * SPAN * groups * (width + SPAN) * STATE,
        moved=groups * SPAN * width * 8,
        grid=(groups,),
        in_specs=[pair, wide, wide, square, square]
        + [lead_spec(STATE, width)] * (1 + len(far)),
        out_specs=pair,
    )(proj, xd, yd, mix, mixt, near, *far)


def output_kernel(parts, hops, ahead, skip_ref, x_ref, cum_ref, cumt_ref, *refs):
    (*refs, out_ref, proj_ref, start_ref) = refs
    projs, nears = refs[:parts], refs[parts : 2 * parts]
    fars = [refs[2 * parts + hops * p : 2 * parts + hops * (p + 1)] for p in range(parts)]
    each = projs[0].shape[1] // (2 * STATE)
    for group in range(parts * each):
        part, at = divmod(group, each)

        @pl.when(pl.program_id(0) == group)
        def _(part=part, at=at):
            proj_ref[...] = projs[part][:, at * 2 * STATE : (at + 1) * 2 * STATE]

            def put(start, _):
                start_ref[...] = added([ref.at[at : at + 1] for ref in start])

            either(ahead, [nears[part]], fars[part], put)

    heads = cum_ref.shape[2]
    half = SPAN // 2
    wide = x_ref.shape[1] // heads * 2
    write = proj_ref[:, :STATE]
    read = proj_ref[:, STATE:]
    cum = cum_ref[0]
    cumt = cumt_ref[0]
    from_start = jnp.exp(cum)
    scores = dot_nt(read, write)
    top, low, end = scores[:half, :half], scores[half:, :half], scores[half:, half:]
    lane = lax.broadcasted_iota(jnp.int32, (half, wide), 1)
    for pair in range(heads // 2):
        a, b = 2 * pair, 2 * pair + 1
        cut = slice(pair * wide, (pair + 1) * wide)
        x = x_ref[:, cut]
        upper, lower = [], []
        for head in (a, b):
            decays = decays_of(cum[:, head : head + 1], cumt[head : head + 1, :])
            upper.append(dot((top * decays[0]).astype(BF16), x[:half]))
            lower.append(
                dot((low * decays[1]).astype(BF16), x[:half])
                + dot((end * decays[2]).astype(BF16), x[half:])
            )
        carried = dot(read, start_ref[:, cut]) * lanes_of(
            from_start[:, a : a + 1], from_start[:, b : b + 1], wide
        )
        head = pl.program_id(0) * heads + a
        gain = jnp.where(
            lax.broadcasted_iota(jnp.int32, (1, wide), 1) < wide // 2,
            skip_ref[head], skip_ref[head + 1],
        )
        rest = carried + gain * x.astype(F32)
        out_ref[:half, cut] = (
            jnp.where(lane < wide // 2, upper[0], upper[1]) + rest[:half]
        ).astype(BF16)
        out_ref[half:, cut] = (
            jnp.where(lane < wide // 2, lower[0], lower[1]) + rest[half:]
        ).astype(BF16)


def output(ahead, values, cum, cumt, skip, projs, nears, fars):
    groups, _, heads = cum.shape
    width = values.shape[1] // groups
    wide = wide_spec(width)
    pieces = [*projs, *nears, *(ref for far in fars for ref in far)]
    return call(
        functools.partial(output_kernel, len(projs), len(fars[0]), ahead),
        jax.ShapeDtypeStruct(values.shape, BF16),
        flops=groups * heads * SPAN * SPAN * 2000,
        moved=values.size * 5,
        exps=groups * heads * SPAN * SPAN,
        grid=(groups,),
        in_specs=[
            pl.BlockSpec(memory_space=pltpu.SMEM), wide, lead_spec(SPAN, heads),
            lead_spec(heads, SPAN),
        ]
        + [pl.BlockSpec(memory_space=pltpu.VMEM)] * len(pieces),
        out_specs=wide,
        scratch_shapes=[
            pltpu.VMEM((SPAN, 2 * STATE), BF16), pltpu.VMEM((STATE, width), BF16)
        ],
    )(skip, values, cum, cumt, *pieces)


def spot_of(block, spots):
    if spots == 1:
        return 0
    other_x = (lax.axis_index("head") != block % 2).astype(jnp.int32)
    other_core = (lax.axis_index("sub") != block // 2).astype(jnp.int32)
    return 2 * other_x + other_core


def update_kernel(blocks, spots, part, *refs):
    turned_refs, pieces = refs[:spots], refs[spots : spots + blocks]
    decayed_ref, keep_ref = refs[spots + blocks : spots + blocks + 2]
    weight_ref, sparse_ref, grad_ref, weight_out, sparse_out, sems = refs[-6:]
    tokens, width = pieces[0].shape
    rows = decayed_ref.shape[0]
    step = min(rows, 256)
    columns = slice(part * width, (part + 1) * width)
    for block, piece in enumerate(pieces):
        start = pl.multiple_of(spot_of(block, spots) * tokens, tokens)
        grad_ref[pl.ds(start, tokens), :] = piece[...]
    copies = []
    for number in range(rows // step):
        here = slice(number * step, (number + 1) * step)
        total = dot(turned_refs[0][here, :], grad_ref[:tokens, :])
        for spot in range(1, spots):
            total += dot(
                turned_refs[spot][here, :], grad_ref[spot * tokens : (spot + 1) * tokens, :]
            )
        weight = decayed_ref[here, columns] - (LEARN_RATE * WEIGHT_SCALE) * total
        weight_out[here, :] = weight
        sparse_out[here, :] = (weight * keep_ref[here, columns].astype(F32)).astype(BF16)
        for place, (source, target) in enumerate(
            ((weight_out, weight_ref), (sparse_out, sparse_ref))
        ):
            copies.append(
                pltpu.make_async_copy(
                    source.at[here, :], target.at[here, columns], sems.at[place, number]
                )
            )
            copies[-1].start()
    for copy in copies:
        copy.wait()


def update(turned_hidden, grad_blocks, decayed, keep, part, earlier, vmem):
    rows, columns = decayed.shape
    width = grad_blocks[0].shape[1]
    tokens = turned_hidden[0].shape[1]
    spots, blocks = len(turned_hidden), len(grad_blocks)
    earlier = earlier or ()
    whole, anywhere = pl.BlockSpec(memory_space=pltpu.VMEM), pl.BlockSpec(memory_space=pl.ANY)
    return call(
        functools.partial(update_kernel, blocks, spots, part),
        (jax.ShapeDtypeStruct((rows, columns), F32), jax.ShapeDtypeStruct((rows, columns), BF16)),
        flops=2 * spots * tokens * rows * width,
        moved=rows * width * 12 + spots * tokens * (rows + width) * 2,
        vmem=vmem,
        in_specs=[whole] * (spots + blocks + 2) + [anywhere] * len(earlier),
        out_specs=(anywhere, anywhere),
        scratch_shapes=[
            pltpu.VMEM((spots * tokens, width), BF16),
            pltpu.VMEM((rows, width), F32),
            pltpu.VMEM((rows, width), BF16),
            pltpu.SemaphoreType.DMA((2, rows // min(rows, 256))),
        ],
        input_output_aliases={spots + blocks + 2 + i: i for i in range(len(earlier))},
    )(*turned_hidden, *grad_blocks, decayed, keep, *earlier)


def held(after, *before):
    return lax.optimization_barrier((after, *before))[0]


def to_all(seq, distance):
    return [(source, (source + distance) % seq) for source in range(seq)]


def block_pairs(seq, near, same_core):
    return [
        (
            (z * 2 + x) * 2 + core,
            ((z + (x if near else 1 - x) + 2 * core) % seq * 2 + x) * 2
            + (core if same_core else 1 - core),
        )
        for z in range(seq)
        for x in range(2)
        for core in range(2)
    ]


def transpose_pairs(seq):
    stays, crosses, beside, onward = [], [], [], []
    for z in range(seq):
        for x in range(2):
            for core in range(2):
                layer = 2 * x + core
                distance = (z - layer) % seq
                source, step = ((z * 2 + way) * 2 + core for way in (x, 1 - x))
                target = (layer * 2 + distance % 2) * 2 + distance // 2
                if distance % 2 == x:
                    stays.append((source, target))
                else:
                    crosses.append((source, target))
                    beside.append((source, step))
                    onward.append((step, target))
    return stays, crosses, beside, onward


SWAP = [(0, 1), (1, 0)]


def chain(own, own_low, decay, seq, step):
    arrived = jnp.zeros_like(own_low)
    message = own_low
    first = 0 if step > 0 else seq - 1
    for hop in range(seq - 1):
        source = first + hop * step
        if hop:
            message = handed_on(decay, arrived, own, 0)
        arrived = arrived + lax.ppermute(message, "seq", [(source, source + step)])
    return arrived


def on_device_general(
    seq, hidden, inner_values, log_decay, skip_gain, cotangent, master, mask_now, mask_next
):
    groups = master.shape[1] // (2 * STATE)
    effective, decayed, keep = weights(master, mask_now, mask_next)
    features = lax.all_gather(hidden, ("head", "sub"), axis=1, tiled=True)
    layer = lax.all_to_all(features, "seq", split_axis=1, concat_axis=0, tiled=True)
    xd, yd, mix, mixt, cum, cumt, decay = before(
        inner_values, cotangent, log_decay.T, groups
    )
    part = dot(layer, effective).astype(BF16)
    terms = [lax.psum_scatter(part, "seq", scatter_dimension=0, tiled=True)]
    proj, state_low, state, adjoint = states(True, terms, [], xd, yd, 0, groups, decay.shape[2])
    start = chain(state, state_low, decay, seq, 1)
    adjoint_in = chain(adjoint, adjoint.astype(BF16), decay, seq, -1)
    grad = grads(True, proj, xd, yd, mix, mixt, start, [adjoint_in], 0)
    blocks = [lax.all_gather(grad, "seq", axis=0, tiled=True)]
    ssd_output = output(
        True, inner_values, cum, cumt, skip_gain, [proj], [start], [[adjoint_in]]
    )
    return ssd_output, *update([layer.T], blocks, decayed, keep, 0, None, 40 * MIB)


def on_device(
    seq, hidden, inner_values, log_decay, skip_gain, cotangent, master, mask_now, mask_next
):
    groups = master.shape[1] // (2 * STATE)
    axes = ("seq", "head", "sub")
    rows = hidden.shape[0] // 2
    stays, crosses, beside, onward = transpose_pairs(seq)
    relayed = lax.ppermute(hidden[rows:], axes, beside)
    top = lax.ppermute(hidden[:rows], axes, stays + crosses)
    low = [lax.ppermute(hidden[rows:], axes, stays), lax.ppermute(relayed, axes, onward)]
    effective, decayed, keep = weights(master, mask_now, mask_next)
    sibling_effective = effective_of(
        lax.ppermute(master, "sub", SWAP), lax.ppermute(mask_now, "sub", SWAP)
    )
    top = held(top, effective, sibling_effective)

    other = [lax.ppermute(top, "head", SWAP)]
    same, cross, low = partials([top, *low], effective, sibling_effective, True)
    other.append(lax.ppermute(low, "head", SWAP))
    terms = [
        lax.ppermute(same, axes, block_pairs(seq, True, True)),
        lax.ppermute(cross, axes, block_pairs(seq, True, False)),
    ]
    late = []
    for number, piece in enumerate(other):
        if number:
            piece = held(piece, *terms, *late[0])
        same, cross = partials([piece], effective, sibling_effective)
        late.append((same, cross))
    far_terms = [
        [
            lax.ppermute(same, axes, block_pairs(seq, False, True)),
            lax.ppermute(cross, axes, block_pairs(seq, False, False)),
        ]
        for same, cross in late
    ]
    xd, yd, mix, mixt, cum, cumt, decay = before(
        held(inner_values, *late[-1]), cotangent, log_decay.T, groups
    )

    each = groups // PARTS
    spans = range(PARTS)
    projs, messages, nears, fars = zip(
        *(
            states(None, terms, far_terms, xd, yd, p * each, each, decay.shape[2])
            for p in spans
        )
    )
    arrived = [[] for _ in spans]
    hops = (([(0, 1), (3, 2)], nears), ([(1, 2), (2, 1)], fars), ([(1, 0), (2, 3)], None))
    messages = list(messages)
    for pairs, own_terms in hops:
        for p in spans:
            message = messages[p]
            if p and not arrived[p]:
                message = held(message, arrived[p - 1][-1])
            arrived[p].append(lax.ppermute(message, "seq", pairs))
            if not p and len(arrived[p]) == 1:
                arrived[p][0] = held(arrived[p][0], *nears)
        for p in spans:
            if own_terms:
                messages[p] = handed_on(decay, arrived[p][-1], own_terms[p], p * each)
    turned_hidden = []
    for first, second in ((top, low), other):
        piece = turn([held(first, arrived[0][1]), second])
        turned_hidden += [piece, lax.ppermute(piece, "sub", SWAP)]
    inputs = [held(projs[0], *turned_hidden), *projs[1:]]
    blocks = []
    for p in spans:
        grad = grads(
            None, inputs[p], xd, yd, mix, mixt, arrived[p][0], arrived[p][1:], p * each
        )
        blocks.append([grad])
        for distance in range(1, seq):
            pairs = to_all(seq, seq - distance)
            blocks[p].append(lax.ppermute(grad, "seq", pairs))

    decayed = held(decayed, blocks[-1][0])
    updated = None
    for p in spans:
        updated = update(turned_hidden, blocks[p], decayed, keep, p, updated, 16 * MIB)
        if not p:
            cum = held(cum, *updated)
    ssd_output = output(
        None, inner_values, cum, cumt, skip_gain,
        projs, [a[0] for a in arrived], [a[1:] for a in arrived],
    )
    return ssd_output, *updated


PARTS = 2


def solution(mesh):
    by_position = P(("grp", "seq"), ("head", "sub"))
    by_row = P("seq", ("head", "sub"))
    seq, head, sub = (mesh.shape[name] for name in ("seq", "head", "sub"))
    body = on_device if (seq, head, sub) == (4, 2, 2) else on_device_general
    return jax.shard_map(
        functools.partial(body, seq),
        mesh=mesh,
        in_specs=(
            by_position, by_position, by_position, P(("head", "sub")), by_position,
            by_row, by_row, by_row,
        ),
        out_specs=(by_position, by_position, by_position),
        check_vma=False,
    )
```

```python
import functools
import math

import jax
import jax.numpy as jnp
from jax import lax
from jax.experimental import pallas as pl
from jax.experimental.pallas import tpu as pltpu
from jax.sharding import PartitionSpec as P

D = 4096
STATE = 128
SPAN = 256
LEARN_RATE = 0.05
WEIGHT_DECAY = 10.0
WEIGHT_SCALE = 2.0 / math.sqrt(D)
KEEP_BITS = (0b000111, 0b011001, 0b101010, 0b110100)
OUT_OF_SIGHT = -1e30
MIB = 1024 * 1024

F32 = jnp.float32
BF16 = jnp.bfloat16
NT = (((1,), (1,)), ((), ()))


def call(kernel, out_shape, flops, moved, exps=0, vmem=16 * MIB, **more):
    return pl.pallas_call(
        kernel,
        out_shape=out_shape,
        compiler_params=pltpu.CompilerParams(vmem_limit_bytes=vmem),
        cost_estimate=pl.CostEstimate(flops=flops, bytes_accessed=moved, transcendentals=exps),
        **more,
    )


def dot(a, b):
    return jnp.dot(a, b, preferred_element_type=F32)


def dot_nt(a, b):
    return lax.dot_general(a, b, NT, preferred_element_type=F32)


def turned(a):
    return a.astype(F32).T.astype(BF16)


def expanded(codes, rows):
    spread = (
        lax.broadcasted_iota(jnp.int32, (rows, rows // 4), 0) // 4
        == lax.broadcasted_iota(jnp.int32, (rows, rows // 4), 1)
    ).astype(F32)
    code = dot(spread.astype(BF16), codes.astype(F32).astype(BF16)).astype(jnp.int32)
    place = lax.broadcasted_iota(jnp.int32, (rows, 1), 0) % 4
    bits = jnp.where(
        place < 2,
        jnp.where(place == 0, KEEP_BITS[0], KEEP_BITS[1]),
        jnp.where(place == 2, KEEP_BITS[2], KEEP_BITS[3]),
    )
    return lax.shift_right_logical(jnp.broadcast_to(bits, code.shape), code) & 1


def weights_kernel(master_ref, now_ref, next_ref, effective_ref, decayed_ref, keep_ref):
    rows = master_ref.shape[0]
    master = master_ref[...]
    kept = expanded(now_ref[...], rows) == 1
    effective_ref[...] = jnp.where(kept, master * WEIGHT_SCALE, 0.0).astype(BF16)
    decayed_ref[...] = jnp.where(kept, master, master * (1.0 - LEARN_RATE * WEIGHT_DECAY))
    keep_ref[...] = expanded(next_ref[...], rows).astype(F32).astype(BF16)


def weights(master, mask_now, mask_next):
    rows, columns = master.shape
    block = min(rows, 256)
    full = pl.BlockSpec((block, columns), lambda i: (i, 0))
    quarter = pl.BlockSpec((block // 4, columns), lambda i: (i, 0))
    return call(
        weights_kernel,
        (
            jax.ShapeDtypeStruct((rows, columns), BF16),
            jax.ShapeDtypeStruct((rows, columns), F32),
            jax.ShapeDtypeStruct((rows, columns), BF16),
        ),
        flops=rows * columns * 3000,
        moved=rows * columns * 14,
        grid=(rows // block,),
        in_specs=[full, quarter, quarter],
        out_specs=(full, full, full),
    )(master, mask_now, mask_next)


def effective_kernel(master_ref, now_ref, effective_ref):
    kept = expanded(now_ref[...], master_ref.shape[0]) == 1
    effective_ref[...] = jnp.where(kept, master_ref[...] * WEIGHT_SCALE, 0.0).astype(BF16)


def effective_of(master, mask_now):
    rows, columns = master.shape
    block = min(rows, 256)
    full = pl.BlockSpec((block, columns), lambda i: (i, 0))
    return call(
        effective_kernel,
        jax.ShapeDtypeStruct((rows, columns), BF16),
        flops=rows * columns * 3000,
        moved=rows * columns * 7,
        grid=(rows // block,),
        in_specs=[full, pl.BlockSpec((block // 4, columns), lambda i: (i, 0))],
        out_specs=full,
    )(master, mask_now)


def lanes_of(left, right, wide):
    lane = lax.broadcasted_iota(jnp.int32, (left.shape[0], wide), 1)
    return jnp.where(lane < wide // 2, left, right)


def decays_of(col, row):
    half = SPAN // 2
    causal = lax.broadcasted_iota(jnp.int32, (half, half), 0) >= lax.broadcasted_iota(
        jnp.int32, (half, half), 1
    )
    top = jnp.exp(jnp.where(causal, col[:half] - row[:, :half], OUT_OF_SIGHT))
    low = jnp.exp(col[half:] - row[:, :half])
    end = jnp.exp(jnp.where(causal, col[half:] - row[:, half:], OUT_OF_SIGHT))
    return top, low, end


def before_kernel(
    x_ref, dy_ref, logt_ref,
    xd_ref, yd_ref, mix_ref, mixt_ref, cum_ref, cumt_ref, end_ref, tall_ref,
):
    heads = cum_ref.shape[2]
    half = SPAN // 2
    wide = x_ref.shape[1] // heads * 2
    row = lax.broadcasted_iota(jnp.int32, (SPAN, SPAN), 0)
    col = lax.broadcasted_iota(jnp.int32, (SPAN, SPAN), 1)
    first = pl.multiple_of(pl.program_id(0) * heads, heads)
    cumt = jnp.dot(
        logt_ref[pl.ds(first, heads), :], (row <= col).astype(F32),
        precision=lax.Precision.HIGHEST, preferred_element_type=F32,
    )
    tall_ref[...] = jnp.zeros_like(tall_ref)
    tall_ref[:heads, :] = cumt
    cum = tall_ref[...].T[:, :heads]
    cum_ref[0] = cum
    cumt_ref[0] = cumt
    end = cum[SPAN - 1 :, :]
    from_start = jnp.exp(cum)
    to_end = jnp.exp(end - cum)
    whole = jnp.exp(end)
    mix = [jnp.zeros((half, half), F32) for _ in range(3)]
    lane = lax.broadcasted_iota(jnp.int32, (SPAN, wide), 1)
    for pair in range(heads // 2):
        a, b = 2 * pair, 2 * pair + 1
        cut = slice(pair * wide, (pair + 1) * wide)
        x = x_ref[:, cut]
        dy = dy_ref[:, cut]
        wide_dy = dy.astype(F32)
        xd_ref[:, cut] = (
            x.astype(F32) * lanes_of(to_end[:, a : a + 1], to_end[:, b : b + 1], wide)
        ).astype(BF16)
        yd_ref[:, cut] = (
            wide_dy * lanes_of(from_start[:, a : a + 1], from_start[:, b : b + 1], wide)
        ).astype(BF16)
        end_ref[0, :, cut] = lanes_of(whole[:, a : a + 1], whole[:, b : b + 1], wide)
        for head, mine in ((a, lane < wide // 2), (b, lane >= wide // 2)):
            one = jnp.where(mine, wide_dy, 0.0).astype(BF16)
            decays = decays_of(cum[:, head : head + 1], cumt[head : head + 1, :])
            mix[0] += dot_nt(one[:half], x[:half]) * decays[0]
            both = dot_nt(one[half:], x)
            mix[1] += both[:, :half] * decays[1]
            mix[2] += both[:, half:] * decays[2]
    nothing = jnp.zeros((half, half), BF16)
    top, low, end_mix = (m.astype(BF16) for m in mix)
    topt, lowt, end_mixt = (m.T.astype(BF16) for m in mix)
    mix_ref[0, :half, :half] = top
    mix_ref[0, :half, half:] = nothing
    mix_ref[0, half:, :half] = low
    mix_ref[0, half:, half:] = end_mix
    mixt_ref[0, :half, :half] = topt
    mixt_ref[0, :half, half:] = lowt
    mixt_ref[0, half:, :half] = nothing
    mixt_ref[0, half:, half:] = end_mixt


def wide_spec(width):
    return pl.BlockSpec((SPAN, width), lambda g: (0, g))


def lead_spec(*shape):
    return pl.BlockSpec((1, *shape), lambda g: (g, *(0 for _ in shape)))


def before(values, cotan, logs_t, groups):
    heads = logs_t.shape[0] // groups
    width = values.shape[1] // groups
    wide = wide_spec(width)
    return call(
        before_kernel,
        (
            jax.ShapeDtypeStruct(values.shape, BF16),
            jax.ShapeDtypeStruct(values.shape, BF16),
            jax.ShapeDtypeStruct((groups, SPAN, SPAN), BF16),
            jax.ShapeDtypeStruct((groups, SPAN, SPAN), BF16),
            jax.ShapeDtypeStruct((groups, SPAN, heads), F32),
            jax.ShapeDtypeStruct((groups, heads, SPAN), F32),
            jax.ShapeDtypeStruct((groups, 1, width), F32),
        ),
        flops=groups * heads * SPAN * SPAN * 2500,
        moved=values.size * 8,
        exps=groups * heads * SPAN * SPAN,
        grid=(groups,),
        in_specs=[wide, wide, pl.BlockSpec(logs_t.shape, lambda g: (0, 0))],
        out_specs=(
            wide, wide, lead_spec(SPAN, SPAN), lead_spec(SPAN, SPAN),
            lead_spec(SPAN, heads), lead_spec(heads, SPAN), lead_spec(1, width),
        ),
        scratch_shapes=[pltpu.VMEM((STATE, SPAN), F32)],
    )(values, cotan, logs_t)


def partial_kernel(spread, *refs):
    given = refs[:-1] if spread else refs
    (*pieces, weight_ref, sibling_weight_ref, out_ref, sibling_out_ref) = given
    pieces = [piece[...] for piece in pieces]
    if spread:
        refs[-1][...] = pieces[-2] + pieces[-1]
        pieces[-2:] = [refs[-1][...]]
    start = 0
    for piece in pieces:
        rows = slice(start, start + piece.shape[0])
        start += piece.shape[0]
        out_ref[rows, :] = dot(piece, weight_ref[...]).astype(BF16)
        sibling_out_ref[rows, :] = dot(piece, sibling_weight_ref[...]).astype(BF16)


def partials(pieces, effective, sibling_effective, spread=False):
    rows = sum(piece.shape[0] for piece in pieces[: -1 if spread else None])
    columns = effective.shape[1]
    whole = pl.BlockSpec(memory_space=pltpu.VMEM)
    shapes = [jax.ShapeDtypeStruct((rows, columns), BF16)] * 2
    if spread:
        shapes.append(jax.ShapeDtypeStruct(pieces[-1].shape, BF16))
    return call(
        functools.partial(partial_kernel, spread),
        tuple(shapes),
        flops=4 * rows * effective.size,
        moved=(rows * effective.shape[0] + 2 * effective.size + 2 * rows * columns) * 2,
        in_specs=[whole] * (len(pieces) + 2),
        out_specs=(whole,) * len(shapes),
    )(*pieces, effective, sibling_effective)


def turn_kernel(*refs):
    (*pieces, out_ref) = refs
    start = 0
    for piece in pieces:
        out_ref[:, start : start + piece.shape[0]] = turned(piece[...])
        start += piece.shape[0]


def turn(pieces):
    rows, features = sum(piece.shape[0] for piece in pieces), pieces[0].shape[1]
    whole = pl.BlockSpec(memory_space=pltpu.VMEM)
    return call(
        turn_kernel,
        jax.ShapeDtypeStruct((features, rows), BF16),
        flops=rows * features * 2000,
        moved=rows * features * 4,
        in_specs=[whole] * len(pieces),
        out_specs=whole,
    )(*pieces)


def either(ahead, first, second, body):
    if ahead:
        return body(first, second)
    lower = lax.axis_index("seq") < lax.axis_size("seq") // 2

    @pl.when(lower)
    def _():
        body(first, second)

    @pl.when(jnp.logical_not(lower))
    def _():
        body(second, first)


def states_kernel(both, *refs):
    (*terms, xd_ref, yd_ref, proj_ref, near_low_ref, near_ref, far_ref) = refs
    total = terms[0][...].astype(F32)
    for term in terms[1:]:
        total += term[...].astype(F32)
    low = total.astype(BF16)
    proj_ref[...] = low
    state = dot(turned(low[:, :STATE]), xd_ref[...])
    adjoint = dot(turned(low[:, STATE:]), yd_ref[...])

    def put(near, far):
        near_low_ref[0] = near.astype(BF16)
        near_ref[0] = near
        far_ref[0] = far

    either(both, state, adjoint, put)


def states(ahead, terms, xd, yd, first, groups, width):
    pair = pl.BlockSpec((SPAN, 2 * STATE), lambda g: (0, g))
    pair_from = pl.BlockSpec((SPAN, 2 * STATE), lambda g: (0, g + first))
    wide = pl.BlockSpec((SPAN, width), lambda g: (0, g + first))
    lead = lead_spec(STATE, width)
    shape = (groups, STATE, width)
    return call(
        functools.partial(states_kernel, ahead),
        (
            jax.ShapeDtypeStruct((SPAN, groups * 2 * STATE), BF16),
            jax.ShapeDtypeStruct(shape, BF16),
            jax.ShapeDtypeStruct(shape, F32),
            jax.ShapeDtypeStruct(shape, F32),
        ),
        flops=4 * SPAN * groups * width * STATE,
        moved=groups * SPAN * (width * 4 + 4 * STATE * 5),
        grid=(groups,),
        in_specs=[pair_from] * len(terms) + [wide, wide],
        out_specs=(pair, lead, lead, lead),
    )(*terms, xd, yd)


def added(refs):
    total = refs[0][0]
    for ref in refs[1:]:
        total += ref[0]
    return total


def message_kernel(decay_ref, arrived_ref, own_ref, out_ref):
    out_ref[0] = (decay_ref[0] * arrived_ref[0].astype(F32) + own_ref[0]).astype(BF16)


def handed_on(decay, arrived, own, first):
    groups, _, width = arrived.shape
    lead = lead_spec(STATE, width)
    return call(
        message_kernel,
        jax.ShapeDtypeStruct(arrived.shape, BF16),
        flops=2 * arrived.size,
        moved=8 * arrived.size,
        grid=(groups,),
        in_specs=[pl.BlockSpec((1, 1, width), lambda g: (g + first, 0, 0)), lead, lead],
        out_specs=lead,
    )(decay, arrived, own)


def grads_kernel(ahead, proj_ref, xd_ref, yd_ref, mix_ref, mixt_ref, near_ref, *refs):
    (*far_refs, out_ref) = refs

    def body(start, adjoint):
        write, read = proj_ref[:, :STATE], proj_ref[:, STATE:]
        grad_write = dot(mixt_ref[0], read) + dot_nt(xd_ref[...], added(adjoint))
        grad_read = dot(mix_ref[0], write) + dot_nt(yd_ref[...], added(start))
        out_ref[:, :STATE] = grad_write.astype(BF16)
        out_ref[:, STATE:] = grad_read.astype(BF16)

    either(ahead, [near_ref], far_refs, body)


def grads(ahead, proj, xd, yd, mix, mixt, near, far, first):
    groups, _, width = near.shape
    pair = pl.BlockSpec((SPAN, 2 * STATE), lambda g: (0, g))
    wide = pl.BlockSpec((SPAN, width), lambda g: (0, g + first))
    square = pl.BlockSpec((1, SPAN, SPAN), lambda g: (g + first, 0, 0))
    return call(
        functools.partial(grads_kernel, ahead),
        jax.ShapeDtypeStruct(proj.shape, BF16),
        flops=4 * SPAN * groups * (width + SPAN) * STATE,
        moved=groups * SPAN * width * 8,
        grid=(groups,),
        in_specs=[pair, wide, wide, square, square]
        + [lead_spec(STATE, width)] * (1 + len(far)),
        out_specs=pair,
    )(proj, xd, yd, mix, mixt, near, *far)


def output_kernel(parts, hops, ahead, skip_ref, x_ref, cum_ref, cumt_ref, *refs):
    (*refs, out_ref, proj_ref, start_ref) = refs
    projs, nears = refs[:parts], refs[parts : 2 * parts]
    fars = [refs[2 * parts + hops * p : 2 * parts + hops * (p + 1)] for p in range(parts)]
    each = projs[0].shape[1] // (2 * STATE)
    for group in range(parts * each):
        part, at = divmod(group, each)

        @pl.when(pl.program_id(0) == group)
        def _(part=part, at=at):
            proj_ref[...] = projs[part][:, at * 2 * STATE : (at + 1) * 2 * STATE]

            def put(start, _):
                start_ref[...] = added([ref.at[at : at + 1] for ref in start])

            either(ahead, [nears[part]], fars[part], put)

    heads = cum_ref.shape[2]
    half = SPAN // 2
    wide = x_ref.shape[1] // heads * 2
    write = proj_ref[:, :STATE]
    read = proj_ref[:, STATE:]
    cum = cum_ref[0]
    cumt = cumt_ref[0]
    from_start = jnp.exp(cum)
    scores = dot_nt(read, write)
    top, low, end = scores[:half, :half], scores[half:, :half], scores[half:, half:]
    lane = lax.broadcasted_iota(jnp.int32, (half, wide), 1)
    for pair in range(heads // 2):
        a, b = 2 * pair, 2 * pair + 1
        cut = slice(pair * wide, (pair + 1) * wide)
        x = x_ref[:, cut]
        upper, lower = [], []
        for head in (a, b):
            decays = decays_of(cum[:, head : head + 1], cumt[head : head + 1, :])
            upper.append(dot((top * decays[0]).astype(BF16), x[:half]))
            lower.append(
                dot((low * decays[1]).astype(BF16), x[:half])
                + dot((end * decays[2]).astype(BF16), x[half:])
            )
        carried = dot(read, start_ref[:, cut]) * lanes_of(
            from_start[:, a : a + 1], from_start[:, b : b + 1], wide
        )
        head = pl.program_id(0) * heads + a
        gain = jnp.where(
            lax.broadcasted_iota(jnp.int32, (1, wide), 1) < wide // 2,
            skip_ref[head], skip_ref[head + 1],
        )
        rest = carried + gain * x.astype(F32)
        out_ref[:half, cut] = (
            jnp.where(lane < wide // 2, upper[0], upper[1]) + rest[:half]
        ).astype(BF16)
        out_ref[half:, cut] = (
            jnp.where(lane < wide // 2, lower[0], lower[1]) + rest[half:]
        ).astype(BF16)


def output(ahead, values, cum, cumt, skip, projs, nears, fars):
    groups, _, heads = cum.shape
    width = values.shape[1] // groups
    wide = wide_spec(width)
    pieces = [*projs, *nears, *(ref for far in fars for ref in far)]
    return call(
        functools.partial(output_kernel, len(projs), len(fars[0]), ahead),
        jax.ShapeDtypeStruct(values.shape, BF16),
        flops=groups * heads * SPAN * SPAN * 2000,
        moved=values.size * 5,
        exps=groups * heads * SPAN * SPAN,
        grid=(groups,),
        in_specs=[
            pl.BlockSpec(memory_space=pltpu.SMEM), wide, lead_spec(SPAN, heads),
            lead_spec(heads, SPAN),
        ]
        + [pl.BlockSpec(memory_space=pltpu.VMEM)] * len(pieces),
        out_specs=wide,
        scratch_shapes=[
            pltpu.VMEM((SPAN, 2 * STATE), BF16), pltpu.VMEM((STATE, width), BF16)
        ],
    )(skip, values, cum, cumt, *pieces)


def spot_of(block, spots):
    if spots == 1:
        return 0
    other_x = (lax.axis_index("head") != block % 2).astype(jnp.int32)
    other_core = (lax.axis_index("sub") != block // 2).astype(jnp.int32)
    return 2 * other_x + other_core


def update_kernel(blocks, spots, part, *refs):
    turned_refs, pieces = refs[:spots], refs[spots : spots + blocks]
    decayed_ref, keep_ref = refs[spots + blocks : spots + blocks + 2]
    weight_ref, sparse_ref, grad_ref, weight_out, sparse_out, sems = refs[-6:]
    tokens, width = pieces[0].shape
    rows = decayed_ref.shape[0]
    step = min(rows, 256)
    columns = slice(part * width, (part + 1) * width)
    for block, piece in enumerate(pieces):
        start = pl.multiple_of(spot_of(block, spots) * tokens, tokens)
        grad_ref[pl.ds(start, tokens), :] = piece[...]
    copies = []
    for number in range(rows // step):
        here = slice(number * step, (number + 1) * step)
        total = dot(turned_refs[0][here, :], grad_ref[:tokens, :])
        for spot in range(1, spots):
            total += dot(
                turned_refs[spot][here, :], grad_ref[spot * tokens : (spot + 1) * tokens, :]
            )
        weight = decayed_ref[here, columns] - (LEARN_RATE * WEIGHT_SCALE) * total
        weight_out[here, :] = weight
        sparse_out[here, :] = (weight * keep_ref[here, columns].astype(F32)).astype(BF16)
        for place, (source, target) in enumerate(
            ((weight_out, weight_ref), (sparse_out, sparse_ref))
        ):
            copies.append(
                pltpu.make_async_copy(
                    source.at[here, :], target.at[here, columns], sems.at[place, number]
                )
            )
            copies[-1].start()
    for copy in copies:
        copy.wait()


def update(turned_hidden, grad_blocks, decayed, keep, part, earlier, vmem):
    rows, columns = decayed.shape
    width = grad_blocks[0].shape[1]
    tokens = turned_hidden[0].shape[1]
    spots, blocks = len(turned_hidden), len(grad_blocks)
    earlier = earlier or ()
    whole, anywhere = pl.BlockSpec(memory_space=pltpu.VMEM), pl.BlockSpec(memory_space=pl.ANY)
    return call(
        functools.partial(update_kernel, blocks, spots, part),
        (jax.ShapeDtypeStruct((rows, columns), F32), jax.ShapeDtypeStruct((rows, columns), BF16)),
        flops=2 * spots * tokens * rows * width,
        moved=rows * width * 12 + spots * tokens * (rows + width) * 2,
        vmem=vmem,
        in_specs=[whole] * (spots + blocks + 2) + [anywhere] * len(earlier),
        out_specs=(anywhere, anywhere),
        scratch_shapes=[
            pltpu.VMEM((spots * tokens, width), BF16),
            pltpu.VMEM((rows, width), F32),
            pltpu.VMEM((rows, width), BF16),
            pltpu.SemaphoreType.DMA((2, rows // min(rows, 256))),
        ],
        input_output_aliases={spots + blocks + 2 + i: i for i in range(len(earlier))},
    )(*turned_hidden, *grad_blocks, decayed, keep, *earlier)


def held(after, *before):
    return lax.optimization_barrier((after, *before))[0]


def to_all(seq, distance):
    return [(source, (source + distance) % seq) for source in range(seq)]


def block_pairs(seq, near, same_core):
    return [
        (
            (z * 2 + x) * 2 + core,
            ((z + (x if near else 1 - x) + 2 * core) % seq * 2 + x) * 2
            + (core if same_core else 1 - core),
        )
        for z in range(seq)
        for x in range(2)
        for core in range(2)
    ]


def transpose_pairs(seq):
    stays, crosses, beside, onward = [], [], [], []
    for z in range(seq):
        for x in range(2):
            for core in range(2):
                layer = 2 * x + core
                distance = (z - layer) % seq
                source, step = ((z * 2 + way) * 2 + core for way in (x, 1 - x))
                target = (layer * 2 + distance % 2) * 2 + distance // 2
                if distance % 2 == x:
                    stays.append((source, target))
                else:
                    crosses.append((source, target))
                    beside.append((source, step))
                    onward.append((step, target))
    return stays, crosses, beside, onward


SWAP = [(0, 1), (1, 0)]


def chain(own, own_low, decay, seq, step):
    arrived = jnp.zeros_like(own_low)
    message = own_low
    first = 0 if step > 0 else seq - 1
    for hop in range(seq - 1):
        source = first + hop * step
        if hop:
            message = handed_on(decay, arrived, own, 0)
        arrived = arrived + lax.ppermute(message, "seq", [(source, source + step)])
    return arrived


def on_device_general(
    seq, hidden, inner_values, log_decay, skip_gain, cotangent, master, mask_now, mask_next
):
    groups = master.shape[1] // (2 * STATE)
    effective, decayed, keep = weights(master, mask_now, mask_next)
    features = lax.all_gather(hidden, ("head", "sub"), axis=1, tiled=True)
    layer = lax.all_to_all(features, "seq", split_axis=1, concat_axis=0, tiled=True)
    xd, yd, mix, mixt, cum, cumt, decay = before(
        inner_values, cotangent, log_decay.T, groups
    )
    part = dot(layer, effective).astype(BF16)
    terms = [lax.psum_scatter(part, "seq", scatter_dimension=0, tiled=True)]
    proj, state_low, state, adjoint = states(True, terms, xd, yd, 0, groups, decay.shape[2])
    start = chain(state, state_low, decay, seq, 1)
    adjoint_in = chain(adjoint, adjoint.astype(BF16), decay, seq, -1)
    grad = grads(True, proj, xd, yd, mix, mixt, start, [adjoint_in], 0)
    blocks = [lax.all_gather(grad, "seq", axis=0, tiled=True)]
    ssd_output = output(
        True, inner_values, cum, cumt, skip_gain, [proj], [start], [[adjoint_in]]
    )
    return ssd_output, *update([layer.T], blocks, decayed, keep, 0, None, 40 * MIB)


def on_device(
    seq, hidden, inner_values, log_decay, skip_gain, cotangent, master, mask_now, mask_next
):
    groups = master.shape[1] // (2 * STATE)
    axes = ("seq", "head", "sub")
    rows = hidden.shape[0] // 2
    stays, crosses, beside, onward = transpose_pairs(seq)
    relayed = lax.ppermute(hidden[rows:], axes, beside)
    top = lax.ppermute(hidden[:rows], axes, stays + crosses)
    low = [lax.ppermute(hidden[rows:], axes, stays), lax.ppermute(relayed, axes, onward)]
    effective, decayed, keep = weights(master, mask_now, mask_next)
    sibling_effective = effective_of(
        lax.ppermute(master, "sub", SWAP), lax.ppermute(mask_now, "sub", SWAP)
    )
    top = held(top, effective, sibling_effective)

    other = [lax.ppermute(top, "head", SWAP)]
    same, cross, low = partials([top, *low], effective, sibling_effective, True)
    other.append(lax.ppermute(low, "head", SWAP))
    terms = [
        lax.ppermute(same, axes, block_pairs(seq, True, True)),
        lax.ppermute(cross, axes, block_pairs(seq, True, False)),
    ]
    other[0] = held(other[0], *terms)
    same, cross = partials(other, effective, sibling_effective)
    terms += [
        lax.ppermute(same, axes, block_pairs(seq, False, True)),
        lax.ppermute(cross, axes, block_pairs(seq, False, False)),
    ]

    xd, yd, mix, mixt, cum, cumt, decay = before(
        held(inner_values, same), cotangent, log_decay.T, groups
    )

    each = groups // PARTS
    spans = range(PARTS)
    projs, messages, nears, fars = zip(
        *(
            states(None, terms, xd, yd, p * each, each, decay.shape[2])
            for p in spans
        )
    )
    turned_hidden = []
    for first, second in ((top, low), other):
        piece = turn([held(first, nears[0]), second])
        turned_hidden += [piece, lax.ppermute(piece, "sub", SWAP)]
    fars = [*fars[:-1], held(fars[-1], *turned_hidden)]
    arrived = [[] for _ in spans]
    hops = (([(0, 1), (3, 2)], nears), ([(1, 2), (2, 1)], fars), ([(1, 0), (2, 3)], None))
    messages = list(messages)
    for pairs, own_terms in hops:
        for p in spans:
            message = messages[p]
            if p and not arrived[p]:
                message = held(message, arrived[p - 1][-1])
            arrived[p].append(lax.ppermute(message, "seq", pairs))
        for p in spans:
            if own_terms:
                messages[p] = handed_on(decay, arrived[p][-1], own_terms[p], p * each)
    blocks = []
    for p in spans:
        grad = grads(
            None, projs[p], xd, yd, mix, mixt, arrived[p][0], arrived[p][1:], p * each
        )
        blocks.append([grad])
        for distance in range(1, seq):
            pairs = to_all(seq, seq - distance)
            blocks[p].append(lax.ppermute(grad, "seq", pairs))

    decayed = held(decayed, blocks[-1][0])
    updated = None
    for p in spans:
        updated = update(turned_hidden, blocks[p], decayed, keep, p, updated, 16 * MIB)
        if not p:
            cum = held(cum, *updated)
    ssd_output = output(
        None, inner_values, cum, cumt, skip_gain,
        projs, [a[0] for a in arrived], [a[1:] for a in arrived],
    )
    return ssd_output, *updated


PARTS = 2


def solution(mesh):
    by_position = P(("grp", "seq"), ("head", "sub"))
    by_row = P("seq", ("head", "sub"))
    seq, head, sub = (mesh.shape[name] for name in ("seq", "head", "sub"))
    body = on_device if (seq, head, sub) == (4, 2, 2) else on_device_general
    return jax.shard_map(
        functools.partial(body, seq),
        mesh=mesh,
        in_specs=(
            by_position, by_position, by_position, P(("head", "sub")), by_position,
            by_row, by_row, by_row,
        ),
        out_specs=(by_position, by_position, by_position),
        check_vma=False,
    )
```

```python
import functools
import math

import jax
import jax.numpy as jnp
from jax import lax
from jax.experimental import pallas as pl
from jax.experimental.pallas import tpu as pltpu
from jax.sharding import PartitionSpec as P

D = 4096
STATE = 128
SPAN = 256
LEARN_RATE = 0.05
WEIGHT_DECAY = 10.0
WEIGHT_SCALE = 2.0 / math.sqrt(D)
KEEP_BITS = (0b000111, 0b011001, 0b101010, 0b110100)
OUT_OF_SIGHT = -1e30
MIB = 1024 * 1024

F32 = jnp.float32
BF16 = jnp.bfloat16
NT = (((1,), (1,)), ((), ()))


def call(kernel, out_shape, flops, moved, exps=0, vmem=16 * MIB, **more):
    return pl.pallas_call(
        kernel,
        out_shape=out_shape,
        compiler_params=pltpu.CompilerParams(vmem_limit_bytes=vmem),
        cost_estimate=pl.CostEstimate(flops=flops, bytes_accessed=moved, transcendentals=exps),
        **more,
    )


def dot(a, b):
    return jnp.dot(a, b, preferred_element_type=F32)


def dot_nt(a, b):
    return lax.dot_general(a, b, NT, preferred_element_type=F32)


def turned(a):
    return a.astype(F32).T.astype(BF16)


def expanded(codes, rows):
    spread = (
        lax.broadcasted_iota(jnp.int32, (rows, rows // 4), 0) // 4
        == lax.broadcasted_iota(jnp.int32, (rows, rows // 4), 1)
    ).astype(F32)
    code = dot(spread.astype(BF16), codes.astype(F32).astype(BF16)).astype(jnp.int32)
    place = lax.broadcasted_iota(jnp.int32, (rows, 1), 0) % 4
    bits = jnp.where(
        place < 2,
        jnp.where(place == 0, KEEP_BITS[0], KEEP_BITS[1]),
        jnp.where(place == 2, KEEP_BITS[2], KEEP_BITS[3]),
    )
    return lax.shift_right_logical(jnp.broadcast_to(bits, code.shape), code) & 1


def weights_kernel(master_ref, now_ref, next_ref, effective_ref, decayed_ref, keep_ref):
    rows = master_ref.shape[0]
    master = master_ref[...]
    kept = expanded(now_ref[...], rows) == 1
    effective_ref[...] = jnp.where(kept, master * WEIGHT_SCALE, 0.0).astype(BF16)
    decayed_ref[...] = jnp.where(kept, master, master * (1.0 - LEARN_RATE * WEIGHT_DECAY))
    keep_ref[...] = expanded(next_ref[...], rows).astype(F32).astype(BF16)


def weights(master, mask_now, mask_next):
    rows, columns = master.shape
    block = min(rows, 256)
    full = pl.BlockSpec((block, columns), lambda i: (i, 0))
    quarter = pl.BlockSpec((block // 4, columns), lambda i: (i, 0))
    return call(
        weights_kernel,
        (
            jax.ShapeDtypeStruct((rows, columns), BF16),
            jax.ShapeDtypeStruct((rows, columns), F32),
            jax.ShapeDtypeStruct((rows, columns), BF16),
        ),
        flops=rows * columns * 3000,
        moved=rows * columns * 14,
        grid=(rows // block,),
        in_specs=[full, quarter, quarter],
        out_specs=(full, full, full),
    )(master, mask_now, mask_next)


def effective_kernel(master_ref, now_ref, effective_ref):
    kept = expanded(now_ref[...], master_ref.shape[0]) == 1
    effective_ref[...] = jnp.where(kept, master_ref[...] * WEIGHT_SCALE, 0.0).astype(BF16)


def effective_of(master, mask_now):
    rows, columns = master.shape
    block = min(rows, 256)
    full = pl.BlockSpec((block, columns), lambda i: (i, 0))
    return call(
        effective_kernel,
        jax.ShapeDtypeStruct((rows, columns), BF16),
        flops=rows * columns * 3000,
        moved=rows * columns * 7,
        grid=(rows // block,),
        in_specs=[full, pl.BlockSpec((block // 4, columns), lambda i: (i, 0))],
        out_specs=full,
    )(master, mask_now)


def lanes_of(left, right, wide):
    lane = lax.broadcasted_iota(jnp.int32, (left.shape[0], wide), 1)
    return jnp.where(lane < wide // 2, left, right)


def decays_of(col, row):
    half = SPAN // 2
    causal = lax.broadcasted_iota(jnp.int32, (half, half), 0) >= lax.broadcasted_iota(
        jnp.int32, (half, half), 1
    )
    top = jnp.exp(jnp.where(causal, col[:half] - row[:, :half], OUT_OF_SIGHT))
    low = jnp.exp(col[half:] - row[:, :half])
    end = jnp.exp(jnp.where(causal, col[half:] - row[:, half:], OUT_OF_SIGHT))
    return top, low, end


def before_kernel(
    x_ref, dy_ref, logt_ref,
    xd_ref, yd_ref, mix_ref, mixt_ref, cum_ref, cumt_ref, end_ref, tall_ref,
):
    heads = cum_ref.shape[2]
    half = SPAN // 2
    wide = x_ref.shape[1] // heads * 2
    row = lax.broadcasted_iota(jnp.int32, (SPAN, SPAN), 0)
    col = lax.broadcasted_iota(jnp.int32, (SPAN, SPAN), 1)
    first = pl.multiple_of(pl.program_id(0) * heads, heads)
    cumt = jnp.dot(
        logt_ref[pl.ds(first, heads), :], (row <= col).astype(F32),
        precision=lax.Precision.HIGHEST, preferred_element_type=F32,
    )
    tall_ref[...] = jnp.zeros_like(tall_ref)
    tall_ref[:heads, :] = cumt
    cum = tall_ref[...].T[:, :heads]
    cum_ref[0] = cum
    cumt_ref[0] = cumt
    end = cum[SPAN - 1 :, :]
    from_start = jnp.exp(cum)
    to_end = jnp.exp(end - cum)
    whole = jnp.exp(end)
    mix = [jnp.zeros((half, half), F32) for _ in range(3)]
    lane = lax.broadcasted_iota(jnp.int32, (SPAN, wide), 1)
    for pair in range(heads // 2):
        a, b = 2 * pair, 2 * pair + 1
        cut = slice(pair * wide, (pair + 1) * wide)
        x = x_ref[:, cut]
        dy = dy_ref[:, cut]
        wide_dy = dy.astype(F32)
        xd_ref[:, cut] = (
            x.astype(F32) * lanes_of(to_end[:, a : a + 1], to_end[:, b : b + 1], wide)
        ).astype(BF16)
        yd_ref[:, cut] = (
            wide_dy * lanes_of(from_start[:, a : a + 1], from_start[:, b : b + 1], wide)
        ).astype(BF16)
        end_ref[0, :, cut] = lanes_of(whole[:, a : a + 1], whole[:, b : b + 1], wide)
        for head, mine in ((a, lane < wide // 2), (b, lane >= wide // 2)):
            one = jnp.where(mine, wide_dy, 0.0).astype(BF16)
            decays = decays_of(cum[:, head : head + 1], cumt[head : head + 1, :])
            mix[0] += dot_nt(one[:half], x[:half]) * decays[0]
            both = dot_nt(one[half:], x)
            mix[1] += both[:, :half] * decays[1]
            mix[2] += both[:, half:] * decays[2]
    nothing = jnp.zeros((half, half), BF16)
    top, low, end_mix = (m.astype(BF16) for m in mix)
    topt, lowt, end_mixt = (m.T.astype(BF16) for m in mix)
    mix_ref[0, :half, :half] = top
    mix_ref[0, :half, half:] = nothing
    mix_ref[0, half:, :half] = low
    mix_ref[0, half:, half:] = end_mix
    mixt_ref[0, :half, :half] = topt
    mixt_ref[0, :half, half:] = lowt
    mixt_ref[0, half:, :half] = nothing
    mixt_ref[0, half:, half:] = end_mixt


def wide_spec(width):
    return pl.BlockSpec((SPAN, width), lambda g: (0, g))


def lead_spec(*shape):
    return pl.BlockSpec((1, *shape), lambda g: (g, *(0 for _ in shape)))


def before(values, cotan, logs_t, groups):
    heads = logs_t.shape[0] // groups
    width = values.shape[1] // groups
    wide = wide_spec(width)
    return call(
        before_kernel,
        (
            jax.ShapeDtypeStruct(values.shape, BF16),
            jax.ShapeDtypeStruct(values.shape, BF16),
            jax.ShapeDtypeStruct((groups, SPAN, SPAN), BF16),
            jax.ShapeDtypeStruct((groups, SPAN, SPAN), BF16),
            jax.ShapeDtypeStruct((groups, SPAN, heads), F32),
            jax.ShapeDtypeStruct((groups, heads, SPAN), F32),
            jax.ShapeDtypeStruct((groups, 1, width), F32),
        ),
        flops=groups * heads * SPAN * SPAN * 2500,
        moved=values.size * 8,
        exps=groups * heads * SPAN * SPAN,
        grid=(groups,),
        in_specs=[wide, wide, pl.BlockSpec(logs_t.shape, lambda g: (0, 0))],
        out_specs=(
            wide, wide, lead_spec(SPAN, SPAN), lead_spec(SPAN, SPAN),
            lead_spec(SPAN, heads), lead_spec(heads, SPAN), lead_spec(1, width),
        ),
        scratch_shapes=[pltpu.VMEM((STATE, SPAN), F32)],
    )(values, cotan, logs_t)


def partial_kernel(spread, *refs):
    given = refs[:-1] if spread else refs
    (*pieces, weight_ref, sibling_weight_ref, out_ref, sibling_out_ref) = given
    pieces = [piece[...] for piece in pieces]
    if spread:
        refs[-1][...] = pieces[-2] + pieces[-1]
        pieces[-2:] = [refs[-1][...]]
    start = 0
    for piece in pieces:
        rows = slice(start, start + piece.shape[0])
        start += piece.shape[0]
        out_ref[rows, :] = dot(piece, weight_ref[...]).astype(BF16)
        sibling_out_ref[rows, :] = dot(piece, sibling_weight_ref[...]).astype(BF16)


def partials(pieces, effective, sibling_effective, spread=False):
    rows = sum(piece.shape[0] for piece in pieces[: -1 if spread else None])
    columns = effective.shape[1]
    whole = pl.BlockSpec(memory_space=pltpu.VMEM)
    shapes = [jax.ShapeDtypeStruct((rows, columns), BF16)] * 2
    if spread:
        shapes.append(jax.ShapeDtypeStruct(pieces[-1].shape, BF16))
    return call(
        functools.partial(partial_kernel, spread),
        tuple(shapes),
        flops=4 * rows * effective.size,
        moved=(rows * effective.shape[0] + 2 * effective.size + 2 * rows * columns) * 2,
        in_specs=[whole] * (len(pieces) + 2),
        out_specs=(whole,) * len(shapes),
    )(*pieces, effective, sibling_effective)


def turn_kernel(*refs):
    (*pieces, out_ref) = refs
    start = 0
    for piece in pieces:
        out_ref[:, start : start + piece.shape[0]] = turned(piece[...])
        start += piece.shape[0]


def turn(pieces):
    rows, features = sum(piece.shape[0] for piece in pieces), pieces[0].shape[1]
    whole = pl.BlockSpec(memory_space=pltpu.VMEM)
    return call(
        turn_kernel,
        jax.ShapeDtypeStruct((features, rows), BF16),
        flops=rows * features * 2000,
        moved=rows * features * 4,
        in_specs=[whole] * len(pieces),
        out_specs=whole,
    )(*pieces)


def either(ahead, first, second, body):
    if ahead:
        return body(first, second)
    lower = lax.axis_index("seq") < lax.axis_size("seq") // 2

    @pl.when(lower)
    def _():
        body(first, second)

    @pl.when(jnp.logical_not(lower))
    def _():
        body(second, first)


def states_kernel(both, *refs):
    (*terms, xd_ref, yd_ref, proj_ref, near_low_ref, near_ref, far_ref) = refs
    whole = [term for term in terms if term.shape[0] == SPAN]
    total = sum(term[...].astype(F32) for term in whole)
    cut = [term[...].astype(F32) for term in terms if term.shape[0] != SPAN]
    if cut:
        total += jnp.concatenate([a + b for a, b in zip(cut[0::2], cut[1::2])], axis=0)
    low = total.astype(BF16)
    proj_ref[...] = low
    state = dot(turned(low[:, :STATE]), xd_ref[...])
    adjoint = dot(turned(low[:, STATE:]), yd_ref[...])

    def put(near, far):
        near_low_ref[0] = near.astype(BF16)
        near_ref[0] = near
        far_ref[0] = far

    either(both, state, adjoint, put)


def states(ahead, terms, cut_terms, xd, yd, first, groups, width):
    pair = pl.BlockSpec((SPAN, 2 * STATE), lambda g: (0, g))
    pair_from = pl.BlockSpec((SPAN, 2 * STATE), lambda g: (0, g + first))
    wide = pl.BlockSpec((SPAN, width), lambda g: (0, g + first))
    lead = lead_spec(STATE, width)
    shape = (groups, STATE, width)
    return call(
        functools.partial(states_kernel, ahead),
        (
            jax.ShapeDtypeStruct((SPAN, groups * 2 * STATE), BF16),
            jax.ShapeDtypeStruct(shape, BF16),
            jax.ShapeDtypeStruct(shape, F32),
            jax.ShapeDtypeStruct(shape, F32),
        ),
        flops=4 * SPAN * groups * width * STATE,
        moved=groups * SPAN * (width * 4 + 4 * STATE * 5),
        grid=(groups,),
        in_specs=[pair_from] * len(terms)
        + [
            pl.BlockSpec((term.shape[0], 2 * STATE), lambda g: (0, g + first))
            for pieces in cut_terms
            for term in pieces
        ]
        + [wide, wide],
        out_specs=(pair, lead, lead, lead),
    )(*terms, *(term for pieces in cut_terms for term in pieces), xd, yd)


def added(refs):
    total = refs[0][0]
    for ref in refs[1:]:
        total += ref[0]
    return total


def message_kernel(decay_ref, arrived_ref, own_ref, out_ref):
    out_ref[0] = (decay_ref[0] * arrived_ref[0].astype(F32) + own_ref[0]).astype(BF16)


def handed_on(decay, arrived, own, first):
    groups, _, width = arrived.shape
    lead = lead_spec(STATE, width)
    return call(
        message_kernel,
        jax.ShapeDtypeStruct(arrived.shape, BF16),
        flops=2 * arrived.size,
        moved=8 * arrived.size,
        grid=(groups,),
        in_specs=[pl.BlockSpec((1, 1, width), lambda g: (g + first, 0, 0)), lead, lead],
        out_specs=lead,
    )(decay, arrived, own)


def grads_kernel(ahead, proj_ref, xd_ref, yd_ref, mix_ref, mixt_ref, near_ref, *refs):
    (*far_refs, out_ref) = refs

    def body(start, adjoint):
        write, read = proj_ref[:, :STATE], proj_ref[:, STATE:]
        grad_write = dot(mixt_ref[0], read) + dot_nt(xd_ref[...], added(adjoint))
        grad_read = dot(mix_ref[0], write) + dot_nt(yd_ref[...], added(start))
        out_ref[:, :STATE] = grad_write.astype(BF16)
        out_ref[:, STATE:] = grad_read.astype(BF16)

    either(ahead, [near_ref], far_refs, body)


def grads(ahead, proj, xd, yd, mix, mixt, near, far, first):
    groups, _, width = near.shape
    pair = pl.BlockSpec((SPAN, 2 * STATE), lambda g: (0, g))
    wide = pl.BlockSpec((SPAN, width), lambda g: (0, g + first))
    square = pl.BlockSpec((1, SPAN, SPAN), lambda g: (g + first, 0, 0))
    return call(
        functools.partial(grads_kernel, ahead),
        jax.ShapeDtypeStruct(proj.shape, BF16),
        flops=4 * SPAN * groups * (width + SPAN) * STATE,
        moved=groups * SPAN * width * 8,
        grid=(groups,),
        in_specs=[pair, wide, wide, square, square]
        + [lead_spec(STATE, width)] * (1 + len(far)),
        out_specs=pair,
    )(proj, xd, yd, mix, mixt, near, *far)


def output_kernel(parts, hops, ahead, skip_ref, x_ref, cum_ref, cumt_ref, *refs):
    (*refs, out_ref, proj_ref, start_ref) = refs
    projs, nears = refs[:parts], refs[parts : 2 * parts]
    fars = [refs[2 * parts + hops * p : 2 * parts + hops * (p + 1)] for p in range(parts)]
    each = projs[0].shape[1] // (2 * STATE)
    for group in range(parts * each):
        part, at = divmod(group, each)

        @pl.when(pl.program_id(0) == group)
        def _(part=part, at=at):
            proj_ref[...] = projs[part][:, at * 2 * STATE : (at + 1) * 2 * STATE]

            def put(start, _):
                start_ref[...] = added([ref.at[at : at + 1] for ref in start])

            either(ahead, [nears[part]], fars[part], put)

    heads = cum_ref.shape[2]
    half = SPAN // 2
    wide = x_ref.shape[1] // heads * 2
    write = proj_ref[:, :STATE]
    read = proj_ref[:, STATE:]
    cum = cum_ref[0]
    cumt = cumt_ref[0]
    from_start = jnp.exp(cum)
    scores = dot_nt(read, write)
    top, low, end = scores[:half, :half], scores[half:, :half], scores[half:, half:]
    lane = lax.broadcasted_iota(jnp.int32, (half, wide), 1)
    for pair in range(heads // 2):
        a, b = 2 * pair, 2 * pair + 1
        cut = slice(pair * wide, (pair + 1) * wide)
        x = x_ref[:, cut]
        upper, lower = [], []
        for head in (a, b):
            decays = decays_of(cum[:, head : head + 1], cumt[head : head + 1, :])
            upper.append(dot((top * decays[0]).astype(BF16), x[:half]))
            lower.append(
                dot((low * decays[1]).astype(BF16), x[:half])
                + dot((end * decays[2]).astype(BF16), x[half:])
            )
        carried = dot(read, start_ref[:, cut]) * lanes_of(
            from_start[:, a : a + 1], from_start[:, b : b + 1], wide
        )
        head = pl.program_id(0) * heads + a
        gain = jnp.where(
            lax.broadcasted_iota(jnp.int32, (1, wide), 1) < wide // 2,
            skip_ref[head], skip_ref[head + 1],
        )
        rest = carried + gain * x.astype(F32)
        out_ref[:half, cut] = (
            jnp.where(lane < wide // 2, upper[0], upper[1]) + rest[:half]
        ).astype(BF16)
        out_ref[half:, cut] = (
            jnp.where(lane < wide // 2, lower[0], lower[1]) + rest[half:]
        ).astype(BF16)


def output(ahead, values, cum, cumt, skip, projs, nears, fars):
    groups, _, heads = cum.shape
    width = values.shape[1] // groups
    wide = wide_spec(width)
    pieces = [*projs, *nears, *(ref for far in fars for ref in far)]
    return call(
        functools.partial(output_kernel, len(projs), len(fars[0]), ahead),
        jax.ShapeDtypeStruct(values.shape, BF16),
        flops=groups * heads * SPAN * SPAN * 2000,
        moved=values.size * 5,
        exps=groups * heads * SPAN * SPAN,
        grid=(groups,),
        in_specs=[
            pl.BlockSpec(memory_space=pltpu.SMEM), wide, lead_spec(SPAN, heads),
            lead_spec(heads, SPAN),
        ]
        + [pl.BlockSpec(memory_space=pltpu.VMEM)] * len(pieces),
        out_specs=wide,
        scratch_shapes=[
            pltpu.VMEM((SPAN, 2 * STATE), BF16), pltpu.VMEM((STATE, width), BF16)
        ],
    )(skip, values, cum, cumt, *pieces)


def spot_of(block, spots):
    if spots == 1:
        return 0
    other_x = (lax.axis_index("head") != block % 2).astype(jnp.int32)
    other_core = (lax.axis_index("sub") != block // 2).astype(jnp.int32)
    return 2 * other_x + other_core


def update_kernel(blocks, spots, part, *refs):
    turned_refs, pieces = refs[:spots], refs[spots : spots + blocks]
    decayed_ref, keep_ref = refs[spots + blocks : spots + blocks + 2]
    weight_ref, sparse_ref, grad_ref, weight_out, sparse_out, sems = refs[-6:]
    tokens, width = pieces[0].shape
    rows = decayed_ref.shape[0]
    step = min(rows, 256)
    columns = slice(part * width, (part + 1) * width)
    for block, piece in enumerate(pieces):
        start = pl.multiple_of(spot_of(block, spots) * tokens, tokens)
        grad_ref[pl.ds(start, tokens), :] = piece[...]
    copies = []
    for number in range(rows // step):
        here = slice(number * step, (number + 1) * step)
        total = dot(turned_refs[0][here, :], grad_ref[:tokens, :])
        for spot in range(1, spots):
            total += dot(
                turned_refs[spot][here, :], grad_ref[spot * tokens : (spot + 1) * tokens, :]
            )
        weight = decayed_ref[here, columns] - (LEARN_RATE * WEIGHT_SCALE) * total
        weight_out[here, :] = weight
        sparse_out[here, :] = (weight * keep_ref[here, columns].astype(F32)).astype(BF16)
        for place, (source, target) in enumerate(
            ((weight_out, weight_ref), (sparse_out, sparse_ref))
        ):
            copies.append(
                pltpu.make_async_copy(
                    source.at[here, :], target.at[here, columns], sems.at[place, number]
                )
            )
            copies[-1].start()
    for copy in copies:
        copy.wait()


def update(turned_hidden, grad_blocks, decayed, keep, part, earlier, vmem):
    rows, columns = decayed.shape
    width = grad_blocks[0].shape[1]
    tokens = turned_hidden[0].shape[1]
    spots, blocks = len(turned_hidden), len(grad_blocks)
    earlier = earlier or ()
    whole, anywhere = pl.BlockSpec(memory_space=pltpu.VMEM), pl.BlockSpec(memory_space=pl.ANY)
    return call(
        functools.partial(update_kernel, blocks, spots, part),
        (jax.ShapeDtypeStruct((rows, columns), F32), jax.ShapeDtypeStruct((rows, columns), BF16)),
        flops=2 * spots * tokens * rows * width,
        moved=rows * width * 12 + spots * tokens * (rows + width) * 2,
        vmem=vmem,
        in_specs=[whole] * (spots + blocks + 2) + [anywhere] * len(earlier),
        out_specs=(anywhere, anywhere),
        scratch_shapes=[
            pltpu.VMEM((spots * tokens, width), BF16),
            pltpu.VMEM((rows, width), F32),
            pltpu.VMEM((rows, width), BF16),
            pltpu.SemaphoreType.DMA((2, rows // min(rows, 256))),
        ],
        input_output_aliases={spots + blocks + 2 + i: i for i in range(len(earlier))},
    )(*turned_hidden, *grad_blocks, decayed, keep, *earlier)


def held(after, *before):
    return lax.optimization_barrier((after, *before))[0]


def to_all(seq, distance):
    return [(source, (source + distance) % seq) for source in range(seq)]


def block_pairs(seq, near, same_core):
    return [
        (
            (z * 2 + x) * 2 + core,
            ((z + (x if near else 1 - x) + 2 * core) % seq * 2 + x) * 2
            + (core if same_core else 1 - core),
        )
        for z in range(seq)
        for x in range(2)
        for core in range(2)
    ]


def transpose_pairs(seq):
    stays, crosses, beside, onward = [], [], [], []
    for z in range(seq):
        for x in range(2):
            for core in range(2):
                layer = 2 * x + core
                distance = (z - layer) % seq
                source, step = ((z * 2 + way) * 2 + core for way in (x, 1 - x))
                target = (layer * 2 + distance % 2) * 2 + distance // 2
                if distance % 2 == x:
                    stays.append((source, target))
                else:
                    crosses.append((source, target))
                    beside.append((source, step))
                    onward.append((step, target))
    return stays, crosses, beside, onward


SWAP = [(0, 1), (1, 0)]


def chain(own, own_low, decay, seq, step):
    arrived = jnp.zeros_like(own_low)
    message = own_low
    first = 0 if step > 0 else seq - 1
    for hop in range(seq - 1):
        source = first + hop * step
        if hop:
            message = handed_on(decay, arrived, own, 0)
        arrived = arrived + lax.ppermute(message, "seq", [(source, source + step)])
    return arrived


def on_device_general(
    seq, hidden, inner_values, log_decay, skip_gain, cotangent, master, mask_now, mask_next
):
    groups = master.shape[1] // (2 * STATE)
    effective, decayed, keep = weights(master, mask_now, mask_next)
    features = lax.all_gather(hidden, ("head", "sub"), axis=1, tiled=True)
    layer = lax.all_to_all(features, "seq", split_axis=1, concat_axis=0, tiled=True)
    xd, yd, mix, mixt, cum, cumt, decay = before(
        inner_values, cotangent, log_decay.T, groups
    )
    part = dot(layer, effective).astype(BF16)
    terms = [lax.psum_scatter(part, "seq", scatter_dimension=0, tiled=True)]
    proj, state_low, state, adjoint = states(True, terms, [], xd, yd, 0, groups, decay.shape[2])
    start = chain(state, state_low, decay, seq, 1)
    adjoint_in = chain(adjoint, adjoint.astype(BF16), decay, seq, -1)
    grad = grads(True, proj, xd, yd, mix, mixt, start, [adjoint_in], 0)
    blocks = [lax.all_gather(grad, "seq", axis=0, tiled=True)]
    ssd_output = output(
        True, inner_values, cum, cumt, skip_gain, [proj], [start], [[adjoint_in]]
    )
    return ssd_output, *update([layer.T], blocks, decayed, keep, 0, None, 40 * MIB)


def on_device(
    seq, hidden, inner_values, log_decay, skip_gain, cotangent, master, mask_now, mask_next
):
    groups = master.shape[1] // (2 * STATE)
    axes = ("seq", "head", "sub")
    rows = hidden.shape[0] // 2
    stays, crosses, beside, onward = transpose_pairs(seq)
    relayed = lax.ppermute(hidden[rows:], axes, beside)
    top = lax.ppermute(hidden[:rows], axes, stays + crosses)
    low = [lax.ppermute(hidden[rows:], axes, stays), lax.ppermute(relayed, axes, onward)]
    effective, decayed, keep = weights(master, mask_now, mask_next)
    sibling_effective = effective_of(
        lax.ppermute(master, "sub", SWAP), lax.ppermute(mask_now, "sub", SWAP)
    )
    top = held(top, effective, sibling_effective)

    other = [lax.ppermute(top, "head", SWAP)]
    early = []
    for number in range(2):
        if number:
            pieces = [held(low[0], *early[0]), low[1]]
            same, cross, low = partials(pieces, effective, sibling_effective, True)
            other.append(lax.ppermute(low, "head", SWAP))
        else:
            same, cross = partials([top], effective, sibling_effective)
        early.append((same, cross))
    cut_terms = [
        [
            lax.ppermute(same, axes, block_pairs(seq, True, True)),
            lax.ppermute(cross, axes, block_pairs(seq, True, False)),
        ]
        for same, cross in early
    ]
    other[0] = held(other[0], *cut_terms[0], *cut_terms[1])
    same, cross = partials(other, effective, sibling_effective)
    terms = [
        lax.ppermute(same, axes, block_pairs(seq, False, True)),
        lax.ppermute(cross, axes, block_pairs(seq, False, False)),
    ]

    xd, yd, mix, mixt, cum, cumt, decay = before(
        held(inner_values, same), cotangent, log_decay.T, groups
    )

    each = groups // PARTS
    spans = range(PARTS)
    projs, messages, nears, fars = zip(
        *(
            states(None, terms, cut_terms, xd, yd, p * each, each, decay.shape[2])
            for p in spans
        )
    )
    turned_hidden = []
    for first, second in ((top, low), other):
        piece = turn([held(first, nears[0]), second])
        turned_hidden += [piece, lax.ppermute(piece, "sub", SWAP)]
    fars = [*fars[:-1], held(fars[-1], *turned_hidden)]
    arrived = [[] for _ in spans]
    hops = (([(0, 1), (3, 2)], nears), ([(1, 2), (2, 1)], fars), ([(1, 0), (2, 3)], None))
    messages = list(messages)
    for pairs, own_terms in hops:
        for p in spans:
            message = messages[p]
            if p and not arrived[p]:
                message = held(message, arrived[p - 1][-1])
            arrived[p].append(lax.ppermute(message, "seq", pairs))
        for p in spans:
            if own_terms:
                messages[p] = handed_on(decay, arrived[p][-1], own_terms[p], p * each)
    blocks = []
    for p in spans:
        grad = grads(
            None, projs[p], xd, yd, mix, mixt, arrived[p][0], arrived[p][1:], p * each
        )
        blocks.append([grad])
        for distance in range(1, seq):
            pairs = to_all(seq, seq - distance)
            blocks[p].append(lax.ppermute(grad, "seq", pairs))

    decayed = held(decayed, blocks[-1][0])
    updated = None
    for p in spans:
        updated = update(turned_hidden, blocks[p], decayed, keep, p, updated, 16 * MIB)
        if not p:
            cum = held(cum, *updated)
    ssd_output = output(
        None, inner_values, cum, cumt, skip_gain,
        projs, [a[0] for a in arrived], [a[1:] for a in arrived],
    )
    return ssd_output, *updated


PARTS = 2


def solution(mesh):
    by_position = P(("grp", "seq"), ("head", "sub"))
    by_row = P("seq", ("head", "sub"))
    seq, head, sub = (mesh.shape[name] for name in ("seq", "head", "sub"))
    body = on_device if (seq, head, sub) == (4, 2, 2) else on_device_general
    return jax.shard_map(
        functools.partial(body, seq),
        mesh=mesh,
        in_specs=(
            by_position, by_position, by_position, P(("head", "sub")), by_position,
            by_row, by_row, by_row,
        ),
        out_specs=(by_position, by_position, by_position),
        check_vma=False,
    )
```

```python
import functools
import math

import jax
import jax.numpy as jnp
from jax import lax
from jax.experimental import pallas as pl
from jax.experimental.pallas import tpu as pltpu
from jax.sharding import PartitionSpec as P

D = 4096
STATE = 128
SPAN = 256
LEARN_RATE = 0.05
WEIGHT_DECAY = 10.0
WEIGHT_SCALE = 2.0 / math.sqrt(D)
KEEP_BITS = (0b000111, 0b011001, 0b101010, 0b110100)
OUT_OF_SIGHT = -1e30
MIB = 1024 * 1024

F32 = jnp.float32
BF16 = jnp.bfloat16
NT = (((1,), (1,)), ((), ()))


def call(kernel, out_shape, flops, moved, exps=0, vmem=16 * MIB, **more):
    return pl.pallas_call(
        kernel,
        out_shape=out_shape,
        compiler_params=pltpu.CompilerParams(vmem_limit_bytes=vmem),
        cost_estimate=pl.CostEstimate(flops=flops, bytes_accessed=moved, transcendentals=exps),
        **more,
    )


def dot(a, b):
    return jnp.dot(a, b, preferred_element_type=F32)


def dot_nt(a, b):
    return lax.dot_general(a, b, NT, preferred_element_type=F32)


def turned(a):
    return a.astype(F32).T.astype(BF16)


def expanded(codes, rows):
    spread = (
        lax.broadcasted_iota(jnp.int32, (rows, rows // 4), 0) // 4
        == lax.broadcasted_iota(jnp.int32, (rows, rows // 4), 1)
    ).astype(F32)
    code = dot(spread.astype(BF16), codes.astype(F32).astype(BF16)).astype(jnp.int32)
    place = lax.broadcasted_iota(jnp.int32, (rows, 1), 0) % 4
    bits = jnp.where(
        place < 2,
        jnp.where(place == 0, KEEP_BITS[0], KEEP_BITS[1]),
        jnp.where(place == 2, KEEP_BITS[2], KEEP_BITS[3]),
    )
    return lax.shift_right_logical(jnp.broadcast_to(bits, code.shape), code) & 1


def weights_kernel(master_ref, now_ref, next_ref, effective_ref, decayed_ref, keep_ref):
    rows = master_ref.shape[0]
    master = master_ref[...]
    kept = expanded(now_ref[...], rows) == 1
    effective_ref[...] = jnp.where(kept, master * WEIGHT_SCALE, 0.0).astype(BF16)
    decayed_ref[...] = jnp.where(kept, master, master * (1.0 - LEARN_RATE * WEIGHT_DECAY))
    keep_ref[...] = expanded(next_ref[...], rows).astype(F32).astype(BF16)


def weights(master, mask_now, mask_next):
    rows, columns = master.shape
    block = min(rows, 256)
    full = pl.BlockSpec((block, columns), lambda i: (i, 0))
    quarter = pl.BlockSpec((block // 4, columns), lambda i: (i, 0))
    return call(
        weights_kernel,
        (
            jax.ShapeDtypeStruct((rows, columns), BF16),
            jax.ShapeDtypeStruct((rows, columns), F32),
            jax.ShapeDtypeStruct((rows, columns), BF16),
        ),
        flops=rows * columns * 3000,
        moved=rows * columns * 14,
        grid=(rows // block,),
        in_specs=[full, quarter, quarter],
        out_specs=(full, full, full),
    )(master, mask_now, mask_next)


def effective_kernel(master_ref, now_ref, effective_ref):
    kept = expanded(now_ref[...], master_ref.shape[0]) == 1
    effective_ref[...] = jnp.where(kept, master_ref[...] * WEIGHT_SCALE, 0.0).astype(BF16)


def effective_of(master, mask_now):
    rows, columns = master.shape
    block = min(rows, 256)
    full = pl.BlockSpec((block, columns), lambda i: (i, 0))
    return call(
        effective_kernel,
        jax.ShapeDtypeStruct((rows, columns), BF16),
        flops=rows * columns * 3000,
        moved=rows * columns * 7,
        grid=(rows // block,),
        in_specs=[full, pl.BlockSpec((block // 4, columns), lambda i: (i, 0))],
        out_specs=full,
    )(master, mask_now)


def lanes_of(left, right, wide):
    lane = lax.broadcasted_iota(jnp.int32, (left.shape[0], wide), 1)
    return jnp.where(lane < wide // 2, left, right)


def decays_of(col, row):
    half = SPAN // 2
    causal = lax.broadcasted_iota(jnp.int32, (half, half), 0) >= lax.broadcasted_iota(
        jnp.int32, (half, half), 1
    )
    top = jnp.exp(jnp.where(causal, col[:half] - row[:, :half], OUT_OF_SIGHT))
    low = jnp.exp(col[half:] - row[:, :half])
    end = jnp.exp(jnp.where(causal, col[half:] - row[:, half:], OUT_OF_SIGHT))
    return top, low, end


def before_kernel(
    x_ref, dy_ref, logt_ref,
    xd_ref, yd_ref, mix_ref, mixt_ref, cum_ref, cumt_ref, end_ref, tall_ref,
):
    heads = cum_ref.shape[2]
    half = SPAN // 2
    wide = x_ref.shape[1] // heads * 2
    row = lax.broadcasted_iota(jnp.int32, (SPAN, SPAN), 0)
    col = lax.broadcasted_iota(jnp.int32, (SPAN, SPAN), 1)
    first = pl.multiple_of(pl.program_id(0) * heads, heads)
    cumt = jnp.dot(
        logt_ref[pl.ds(first, heads), :], (row <= col).astype(F32),
        precision=lax.Precision.HIGHEST, preferred_element_type=F32,
    )
    tall_ref[...] = jnp.zeros_like(tall_ref)
    tall_ref[:heads, :] = cumt
    cum = tall_ref[...].T[:, :heads]
    cum_ref[0] = cum
    cumt_ref[0] = cumt
    end = cum[SPAN - 1 :, :]
    from_start = jnp.exp(cum)
    to_end = jnp.exp(end - cum)
    whole = jnp.exp(end)
    mix = [jnp.zeros((half, half), F32) for _ in range(3)]
    lane = lax.broadcasted_iota(jnp.int32, (SPAN, wide), 1)
    for pair in range(heads // 2):
        a, b = 2 * pair, 2 * pair + 1
        cut = slice(pair * wide, (pair + 1) * wide)
        x = x_ref[:, cut]
        dy = dy_ref[:, cut]
        wide_dy = dy.astype(F32)
        xd_ref[:, cut] = (
            x.astype(F32) * lanes_of(to_end[:, a : a + 1], to_end[:, b : b + 1], wide)
        ).astype(BF16)
        yd_ref[:, cut] = (
            wide_dy * lanes_of(from_start[:, a : a + 1], from_start[:, b : b + 1], wide)
        ).astype(BF16)
        end_ref[0, :, cut] = lanes_of(whole[:, a : a + 1], whole[:, b : b + 1], wide)
        for head, mine in ((a, lane < wide // 2), (b, lane >= wide // 2)):
            one = jnp.where(mine, wide_dy, 0.0).astype(BF16)
            decays = decays_of(cum[:, head : head + 1], cumt[head : head + 1, :])
            mix[0] += dot_nt(one[:half], x[:half]) * decays[0]
            both = dot_nt(one[half:], x)
            mix[1] += both[:, :half] * decays[1]
            mix[2] += both[:, half:] * decays[2]
    nothing = jnp.zeros((half, half), BF16)
    top, low, end_mix = (m.astype(BF16) for m in mix)
    topt, lowt, end_mixt = (m.T.astype(BF16) for m in mix)
    mix_ref[0, :half, :half] = top
    mix_ref[0, :half, half:] = nothing
    mix_ref[0, half:, :half] = low
    mix_ref[0, half:, half:] = end_mix
    mixt_ref[0, :half, :half] = topt
    mixt_ref[0, :half, half:] = lowt
    mixt_ref[0, half:, :half] = nothing
    mixt_ref[0, half:, half:] = end_mixt


def wide_spec(width):
    return pl.BlockSpec((SPAN, width), lambda g: (0, g))


def lead_spec(*shape):
    return pl.BlockSpec((1, *shape), lambda g: (g, *(0 for _ in shape)))


def before(values, cotan, logs_t, groups):
    heads = logs_t.shape[0] // groups
    width = values.shape[1] // groups
    wide = wide_spec(width)
    return call(
        before_kernel,
        (
            jax.ShapeDtypeStruct(values.shape, BF16),
            jax.ShapeDtypeStruct(values.shape, BF16),
            jax.ShapeDtypeStruct((groups, SPAN, SPAN), BF16),
            jax.ShapeDtypeStruct((groups, SPAN, SPAN), BF16),
            jax.ShapeDtypeStruct((groups, SPAN, heads), F32),
            jax.ShapeDtypeStruct((groups, heads, SPAN), F32),
            jax.ShapeDtypeStruct((groups, 1, width), F32),
        ),
        flops=groups * heads * SPAN * SPAN * 2500,
        moved=values.size * 8,
        exps=groups * heads * SPAN * SPAN,
        grid=(groups,),
        in_specs=[wide, wide, pl.BlockSpec(logs_t.shape, lambda g: (0, 0))],
        out_specs=(
            wide, wide, lead_spec(SPAN, SPAN), lead_spec(SPAN, SPAN),
            lead_spec(SPAN, heads), lead_spec(heads, SPAN), lead_spec(1, width),
        ),
        scratch_shapes=[pltpu.VMEM((STATE, SPAN), F32)],
    )(values, cotan, logs_t)


def partial_kernel(spread, *refs):
    given = refs[:-1] if spread else refs
    (*pieces, weight_ref, sibling_weight_ref, out_ref, sibling_out_ref) = given
    pieces = [piece[...] for piece in pieces]
    if spread:
        refs[-1][...] = pieces[-2] + pieces[-1]
        pieces[-2:] = [refs[-1][...]]
    start = 0
    for piece in pieces:
        rows = slice(start, start + piece.shape[0])
        start += piece.shape[0]
        out_ref[rows, :] = dot(piece, weight_ref[...]).astype(BF16)
        sibling_out_ref[rows, :] = dot(piece, sibling_weight_ref[...]).astype(BF16)


def partials(pieces, effective, sibling_effective, spread=False):
    rows = sum(piece.shape[0] for piece in pieces[: -1 if spread else None])
    columns = effective.shape[1]
    whole = pl.BlockSpec(memory_space=pltpu.VMEM)
    shapes = [jax.ShapeDtypeStruct((rows, columns), BF16)] * 2
    if spread:
        shapes.append(jax.ShapeDtypeStruct(pieces[-1].shape, BF16))
    return call(
        functools.partial(partial_kernel, spread),
        tuple(shapes),
        flops=4 * rows * effective.size,
        moved=(rows * effective.shape[0] + 2 * effective.size + 2 * rows * columns) * 2,
        in_specs=[whole] * (len(pieces) + 2),
        out_specs=(whole,) * len(shapes),
    )(*pieces, effective, sibling_effective)


def turn_kernel(*refs):
    (*pieces, out_ref) = refs
    start = 0
    for piece in pieces:
        out_ref[:, start : start + piece.shape[0]] = turned(piece[...])
        start += piece.shape[0]


def turn(pieces):
    rows, features = sum(piece.shape[0] for piece in pieces), pieces[0].shape[1]
    whole = pl.BlockSpec(memory_space=pltpu.VMEM)
    return call(
        turn_kernel,
        jax.ShapeDtypeStruct((features, rows), BF16),
        flops=rows * features * 2000,
        moved=rows * features * 4,
        in_specs=[whole] * len(pieces),
        out_specs=whole,
    )(*pieces)


def either(ahead, first, second, body):
    if ahead:
        return body(first, second)
    lower = lax.axis_index("seq") < lax.axis_size("seq") // 2

    @pl.when(lower)
    def _():
        body(first, second)

    @pl.when(jnp.logical_not(lower))
    def _():
        body(second, first)


def states_kernel(both, *refs):
    (*terms, xd_ref, yd_ref, proj_ref, near_low_ref, near_ref, far_ref) = refs
    total = terms[0][...].astype(F32)
    for term in terms[1:]:
        total += term[...].astype(F32)
    low = total.astype(BF16)
    proj_ref[...] = low
    state = dot(turned(low[:, :STATE]), xd_ref[...])
    adjoint = dot(turned(low[:, STATE:]), yd_ref[...])

    def put(near, far):
        near_low_ref[0] = near.astype(BF16)
        near_ref[0] = near
        far_ref[0] = far

    either(both, state, adjoint, put)


def states(ahead, terms, xd, yd, first, groups, width):
    pair = pl.BlockSpec((SPAN, 2 * STATE), lambda g: (0, g))
    pair_from = pl.BlockSpec((SPAN, 2 * STATE), lambda g: (0, g + first))
    wide = pl.BlockSpec((SPAN, width), lambda g: (0, g + first))
    lead = lead_spec(STATE, width)
    shape = (groups, STATE, width)
    return call(
        functools.partial(states_kernel, ahead),
        (
            jax.ShapeDtypeStruct((SPAN, groups * 2 * STATE), BF16),
            jax.ShapeDtypeStruct(shape, BF16),
            jax.ShapeDtypeStruct(shape, F32),
            jax.ShapeDtypeStruct(shape, F32),
        ),
        flops=4 * SPAN * groups * width * STATE,
        moved=groups * SPAN * (width * 4 + 4 * STATE * 5),
        grid=(groups,),
        in_specs=[pair_from] * len(terms) + [wide, wide],
        out_specs=(pair, lead, lead, lead),
    )(*terms, xd, yd)


def added(refs):
    total = refs[0][0]
    for ref in refs[1:]:
        total += ref[0]
    return total


def message_kernel(decay_ref, arrived_ref, own_ref, out_ref):
    out_ref[0] = (decay_ref[0] * arrived_ref[0].astype(F32) + own_ref[0]).astype(BF16)


def handed_on(decay, arrived, own, first):
    groups, _, width = arrived.shape
    lead = lead_spec(STATE, width)
    return call(
        message_kernel,
        jax.ShapeDtypeStruct(arrived.shape, BF16),
        flops=2 * arrived.size,
        moved=8 * arrived.size,
        grid=(groups,),
        in_specs=[pl.BlockSpec((1, 1, width), lambda g: (g + first, 0, 0)), lead, lead],
        out_specs=lead,
    )(decay, arrived, own)


def grads_kernel(ahead, proj_ref, xd_ref, yd_ref, mix_ref, mixt_ref, near_ref, *refs):
    (*far_refs, out_ref) = refs

    def body(start, adjoint):
        write, read = proj_ref[:, :STATE], proj_ref[:, STATE:]
        grad_write = dot(mixt_ref[0], read) + dot_nt(xd_ref[...], added(adjoint))
        grad_read = dot(mix_ref[0], write) + dot_nt(yd_ref[...], added(start))
        out_ref[:, :STATE] = grad_write.astype(BF16)
        out_ref[:, STATE:] = grad_read.astype(BF16)

    either(ahead, [near_ref], far_refs, body)


def grads(ahead, proj, xd, yd, mix, mixt, near, far, first):
    groups, _, width = near.shape
    pair = pl.BlockSpec((SPAN, 2 * STATE), lambda g: (0, g))
    wide = pl.BlockSpec((SPAN, width), lambda g: (0, g + first))
    square = pl.BlockSpec((1, SPAN, SPAN), lambda g: (g + first, 0, 0))
    return call(
        functools.partial(grads_kernel, ahead),
        jax.ShapeDtypeStruct(proj.shape, BF16),
        flops=4 * SPAN * groups * (width + SPAN) * STATE,
        moved=groups * SPAN * width * 8,
        grid=(groups,),
        in_specs=[pair, wide, wide, square, square]
        + [lead_spec(STATE, width)] * (1 + len(far)),
        out_specs=pair,
    )(proj, xd, yd, mix, mixt, near, *far)


def output_kernel(parts, hops, ahead, skip_ref, x_ref, cum_ref, cumt_ref, *refs):
    (*refs, out_ref, proj_ref, start_ref) = refs
    projs, nears = refs[:parts], refs[parts : 2 * parts]
    fars = [refs[2 * parts + hops * p : 2 * parts + hops * (p + 1)] for p in range(parts)]
    each = projs[0].shape[1] // (2 * STATE)
    for group in range(parts * each):
        part, at = divmod(group, each)

        @pl.when(pl.program_id(0) == group)
        def _(part=part, at=at):
            proj_ref[...] = projs[part][:, at * 2 * STATE : (at + 1) * 2 * STATE]

            def put(start, _):
                start_ref[...] = added([ref.at[at : at + 1] for ref in start])

            either(ahead, [nears[part]], fars[part], put)

    heads = cum_ref.shape[2]
    half = SPAN // 2
    wide = x_ref.shape[1] // heads * 2
    write = proj_ref[:, :STATE]
    read = proj_ref[:, STATE:]
    cum = cum_ref[0]
    cumt = cumt_ref[0]
    from_start = jnp.exp(cum)
    scores = dot_nt(read, write)
    top, low, end = scores[:half, :half], scores[half:, :half], scores[half:, half:]
    lane = lax.broadcasted_iota(jnp.int32, (half, wide), 1)
    for pair in range(heads // 2):
        a, b = 2 * pair, 2 * pair + 1
        cut = slice(pair * wide, (pair + 1) * wide)
        x = x_ref[:, cut]
        upper, lower = [], []
        for head in (a, b):
            decays = decays_of(cum[:, head : head + 1], cumt[head : head + 1, :])
            upper.append(dot((top * decays[0]).astype(BF16), x[:half]))
            lower.append(
                dot((low * decays[1]).astype(BF16), x[:half])
                + dot((end * decays[2]).astype(BF16), x[half:])
            )
        carried = dot(read, start_ref[:, cut]) * lanes_of(
            from_start[:, a : a + 1], from_start[:, b : b + 1], wide
        )
        head = pl.program_id(0) * heads + a
        gain = jnp.where(
            lax.broadcasted_iota(jnp.int32, (1, wide), 1) < wide // 2,
            skip_ref[head], skip_ref[head + 1],
        )
        rest = carried + gain * x.astype(F32)
        out_ref[:half, cut] = (
            jnp.where(lane < wide // 2, upper[0], upper[1]) + rest[:half]
        ).astype(BF16)
        out_ref[half:, cut] = (
            jnp.where(lane < wide // 2, lower[0], lower[1]) + rest[half:]
        ).astype(BF16)


def output(ahead, values, cum, cumt, skip, projs, nears, fars):
    groups, _, heads = cum.shape
    width = values.shape[1] // groups
    wide = wide_spec(width)
    pieces = [*projs, *nears, *(ref for far in fars for ref in far)]
    return call(
        functools.partial(output_kernel, len(projs), len(fars[0]), ahead),
        jax.ShapeDtypeStruct(values.shape, BF16),
        flops=groups * heads * SPAN * SPAN * 2000,
        moved=values.size * 5,
        exps=groups * heads * SPAN * SPAN,
        grid=(groups,),
        in_specs=[
            pl.BlockSpec(memory_space=pltpu.SMEM), wide, lead_spec(SPAN, heads),
            lead_spec(heads, SPAN),
        ]
        + [pl.BlockSpec(memory_space=pltpu.VMEM)] * len(pieces),
        out_specs=wide,
        scratch_shapes=[
            pltpu.VMEM((SPAN, 2 * STATE), BF16), pltpu.VMEM((STATE, width), BF16)
        ],
    )(skip, values, cum, cumt, *pieces)


def spot_of(block, spots):
    if spots == 1:
        return 0
    other_x = (lax.axis_index("head") != block % 2).astype(jnp.int32)
    other_core = (lax.axis_index("sub") != block // 2).astype(jnp.int32)
    return 2 * other_x + other_core


def update_kernel(blocks, spots, part, *refs):
    turned_refs, pieces = refs[:spots], refs[spots : spots + blocks]
    decayed_ref, keep_ref = refs[spots + blocks : spots + blocks + 2]
    weight_ref, sparse_ref, grad_ref, weight_out, sparse_out, sems = refs[-6:]
    tokens, width = pieces[0].shape
    rows = decayed_ref.shape[0]
    step = min(rows, 256)
    columns = slice(part * width, (part + 1) * width)
    for block, piece in enumerate(pieces):
        start = pl.multiple_of(spot_of(block, spots) * tokens, tokens)
        grad_ref[pl.ds(start, tokens), :] = piece[...]
    copies = []
    for number in range(rows // step):
        here = slice(number * step, (number + 1) * step)
        total = dot(turned_refs[0][here, :], grad_ref[:tokens, :])
        for spot in range(1, spots):
            total += dot(
                turned_refs[spot][here, :], grad_ref[spot * tokens : (spot + 1) * tokens, :]
            )
        weight = decayed_ref[here, columns] - (LEARN_RATE * WEIGHT_SCALE) * total
        weight_out[here, :] = weight
        sparse_out[here, :] = (weight * keep_ref[here, columns].astype(F32)).astype(BF16)
        for place, (source, target) in enumerate(
            ((weight_out, weight_ref), (sparse_out, sparse_ref))
        ):
            copies.append(
                pltpu.make_async_copy(
                    source.at[here, :], target.at[here, columns], sems.at[place, number]
                )
            )
            copies[-1].start()
    for copy in copies:
        copy.wait()


def update(turned_hidden, grad_blocks, decayed, keep, part, earlier, vmem):
    rows, columns = decayed.shape
    width = grad_blocks[0].shape[1]
    tokens = turned_hidden[0].shape[1]
    spots, blocks = len(turned_hidden), len(grad_blocks)
    earlier = earlier or ()
    whole, anywhere = pl.BlockSpec(memory_space=pltpu.VMEM), pl.BlockSpec(memory_space=pl.ANY)
    return call(
        functools.partial(update_kernel, blocks, spots, part),
        (jax.ShapeDtypeStruct((rows, columns), F32), jax.ShapeDtypeStruct((rows, columns), BF16)),
        flops=2 * spots * tokens * rows * width,
        moved=rows * width * 12 + spots * tokens * (rows + width) * 2,
        vmem=vmem,
        in_specs=[whole] * (spots + blocks + 2) + [anywhere] * len(earlier),
        out_specs=(anywhere, anywhere),
        scratch_shapes=[
            pltpu.VMEM((spots * tokens, width), BF16),
            pltpu.VMEM((rows, width), F32),
            pltpu.VMEM((rows, width), BF16),
            pltpu.SemaphoreType.DMA((2, rows // min(rows, 256))),
        ],
        input_output_aliases={spots + blocks + 2 + i: i for i in range(len(earlier))},
    )(*turned_hidden, *grad_blocks, decayed, keep, *earlier)


def held(after, *before):
    return lax.optimization_barrier((after, *before))[0]


def to_all(seq, distance):
    return [(source, (source + distance) % seq) for source in range(seq)]


def block_pairs(seq, near, same_core):
    return [
        (
            (z * 2 + x) * 2 + core,
            ((z + (x if near else 1 - x) + 2 * core) % seq * 2 + x) * 2
            + (core if same_core else 1 - core),
        )
        for z in range(seq)
        for x in range(2)
        for core in range(2)
    ]


def transpose_pairs(seq):
    stays, crosses, beside, onward = [], [], [], []
    for z in range(seq):
        for x in range(2):
            for core in range(2):
                layer = 2 * x + core
                distance = (z - layer) % seq
                source, step = ((z * 2 + way) * 2 + core for way in (x, 1 - x))
                target = (layer * 2 + distance % 2) * 2 + distance // 2
                if distance % 2 == x:
                    stays.append((source, target))
                else:
                    crosses.append((source, target))
                    beside.append((source, step))
                    onward.append((step, target))
    return stays, crosses, beside, onward


SWAP = [(0, 1), (1, 0)]


def chain(own, own_low, decay, seq, step):
    arrived = jnp.zeros_like(own_low)
    message = own_low
    first = 0 if step > 0 else seq - 1
    for hop in range(seq - 1):
        source = first + hop * step
        if hop:
            message = handed_on(decay, arrived, own, 0)
        arrived = arrived + lax.ppermute(message, "seq", [(source, source + step)])
    return arrived


def on_device_general(
    seq, hidden, inner_values, log_decay, skip_gain, cotangent, master, mask_now, mask_next
):
    groups = master.shape[1] // (2 * STATE)
    effective, decayed, keep = weights(master, mask_now, mask_next)
    features = lax.all_gather(hidden, ("head", "sub"), axis=1, tiled=True)
    layer = lax.all_to_all(features, "seq", split_axis=1, concat_axis=0, tiled=True)
    xd, yd, mix, mixt, cum, cumt, decay = before(
        inner_values, cotangent, log_decay.T, groups
    )
    part = dot(layer, effective).astype(BF16)
    terms = [lax.psum_scatter(part, "seq", scatter_dimension=0, tiled=True)]
    proj, state_low, state, adjoint = states(True, terms, xd, yd, 0, groups, decay.shape[2])
    start = chain(state, state_low, decay, seq, 1)
    adjoint_in = chain(adjoint, adjoint.astype(BF16), decay, seq, -1)
    grad = grads(True, proj, xd, yd, mix, mixt, start, [adjoint_in], 0)
    blocks = [lax.all_gather(grad, "seq", axis=0, tiled=True)]
    ssd_output = output(
        True, inner_values, cum, cumt, skip_gain, [proj], [start], [[adjoint_in]]
    )
    return ssd_output, *update([layer.T], blocks, decayed, keep, 0, None, 40 * MIB)


def on_device(
    seq, hidden, inner_values, log_decay, skip_gain, cotangent, master, mask_now, mask_next
):
    groups = master.shape[1] // (2 * STATE)
    axes = ("seq", "head", "sub")
    rows = hidden.shape[0] // 2
    stays, crosses, beside, onward = transpose_pairs(seq)
    relayed = lax.ppermute(hidden[rows:], axes, beside)
    top = lax.ppermute(hidden[:rows], axes, stays + crosses)
    low = [lax.ppermute(hidden[rows:], axes, stays), lax.ppermute(relayed, axes, onward)]
    effective, decayed, keep = weights(master, mask_now, mask_next)
    sibling_effective = effective_of(
        lax.ppermute(master, "sub", SWAP), lax.ppermute(mask_now, "sub", SWAP)
    )
    top = held(top, effective, sibling_effective)

    other = [lax.ppermute(top, "head", SWAP)]
    same, cross, low = partials([top, *low], effective, sibling_effective, True)
    other.append(lax.ppermute(low, "head", SWAP))
    terms = [
        lax.ppermute(same, axes, block_pairs(seq, True, True)),
        lax.ppermute(cross, axes, block_pairs(seq, True, False)),
    ]
    same, cross = partials(other, effective, sibling_effective)
    terms += [
        lax.ppermute(same, axes, block_pairs(seq, False, True)),
        lax.ppermute(cross, axes, block_pairs(seq, False, False)),
    ]

    xd, yd, mix, mixt, cum, cumt, decay = before(
        held(inner_values, same), cotangent, log_decay.T, groups
    )

    each = groups // PARTS
    spans = range(PARTS)
    projs, messages, nears, fars = zip(
        *(
            states(None, terms, xd, yd, p * each, each, decay.shape[2])
            for p in spans
        )
    )
    turned_hidden = []
    for first, second in ((top, low), other):
        piece = turn([held(first, nears[0]), second])
        turned_hidden += [piece, lax.ppermute(piece, "sub", SWAP)]
    fars = [*fars[:-1], held(fars[-1], *turned_hidden)]
    arrived = [[] for _ in spans]
    hops = (([(0, 1), (3, 2)], nears), ([(1, 2), (2, 1)], fars), ([(1, 0), (2, 3)], None))
    messages = list(messages)
    for pairs, own_terms in hops:
        for p in spans:
            message = messages[p]
            if p and not arrived[p]:
                message = held(message, arrived[p - 1][-1])
            arrived[p].append(lax.ppermute(message, "seq", pairs))
        for p in spans:
            if own_terms:
                messages[p] = handed_on(decay, arrived[p][-1], own_terms[p], p * each)
    blocks = []
    for p in spans:
        grad = grads(
            None, projs[p], xd, yd, mix, mixt, arrived[p][0], arrived[p][1:], p * each
        )
        blocks.append([grad])
        for distance in range(1, seq):
            pairs = to_all(seq, seq - distance)
            blocks[p].append(lax.ppermute(grad, "seq", pairs))

    decayed = held(decayed, blocks[-1][0])
    updated = None
    for p in spans:
        updated = update(turned_hidden, blocks[p], decayed, keep, p, updated, 16 * MIB)
        if not p:
            cum = held(cum, *updated)
    ssd_output = output(
        None, inner_values, cum, cumt, skip_gain,
        projs, [a[0] for a in arrived], [a[1:] for a in arrived],
    )
    return ssd_output, *updated


PARTS = 2


def solution(mesh):
    by_position = P(("grp", "seq"), ("head", "sub"))
    by_row = P("seq", ("head", "sub"))
    seq, head, sub = (mesh.shape[name] for name in ("seq", "head", "sub"))
    body = on_device if (seq, head, sub) == (4, 2, 2) else on_device_general
    return jax.shard_map(
        functools.partial(body, seq),
        mesh=mesh,
        in_specs=(
            by_position, by_position, by_position, P(("head", "sub")), by_position,
            by_row, by_row, by_row,
        ),
        out_specs=(by_position, by_position, by_position),
        check_vma=False,
    )
```

```python
import functools
import math

import jax
import jax.numpy as jnp
from jax import lax
from jax.experimental import pallas as pl
from jax.experimental.pallas import tpu as pltpu
from jax.sharding import PartitionSpec as P

D = 4096
STATE = 128
SPAN = 256
LEARN_RATE = 0.05
WEIGHT_DECAY = 10.0
WEIGHT_SCALE = 2.0 / math.sqrt(D)
KEEP_BITS = (0b000111, 0b011001, 0b101010, 0b110100)
OUT_OF_SIGHT = -1e30
MIB = 1024 * 1024

F32 = jnp.float32
BF16 = jnp.bfloat16
NT = (((1,), (1,)), ((), ()))


def call(kernel, out_shape, flops, moved, exps=0, vmem=16 * MIB, **more):
    return pl.pallas_call(
        kernel,
        out_shape=out_shape,
        compiler_params=pltpu.CompilerParams(vmem_limit_bytes=vmem),
        cost_estimate=pl.CostEstimate(flops=flops, bytes_accessed=moved, transcendentals=exps),
        **more,
    )


def dot(a, b):
    return jnp.dot(a, b, preferred_element_type=F32)


def dot_nt(a, b):
    return lax.dot_general(a, b, NT, preferred_element_type=F32)


def turned(a):
    return a.astype(F32).T.astype(BF16)


def expanded(codes, rows):
    spread = (
        lax.broadcasted_iota(jnp.int32, (rows, rows // 4), 0) // 4
        == lax.broadcasted_iota(jnp.int32, (rows, rows // 4), 1)
    ).astype(F32)
    code = dot(spread.astype(BF16), codes.astype(F32).astype(BF16)).astype(jnp.int32)
    place = lax.broadcasted_iota(jnp.int32, (rows, 1), 0) % 4
    bits = jnp.where(
        place < 2,
        jnp.where(place == 0, KEEP_BITS[0], KEEP_BITS[1]),
        jnp.where(place == 2, KEEP_BITS[2], KEEP_BITS[3]),
    )
    return lax.shift_right_logical(jnp.broadcast_to(bits, code.shape), code) & 1


def weights_kernel(master_ref, now_ref, next_ref, effective_ref, decayed_ref, keep_ref):
    rows = master_ref.shape[0]
    master = master_ref[...]
    kept = expanded(now_ref[...], rows) == 1
    effective_ref[...] = jnp.where(kept, master * WEIGHT_SCALE, 0.0).astype(BF16)
    decayed_ref[...] = jnp.where(kept, master, master * (1.0 - LEARN_RATE * WEIGHT_DECAY))
    keep_ref[...] = expanded(next_ref[...], rows).astype(F32).astype(BF16)


def weights(master, mask_now, mask_next):
    rows, columns = master.shape
    block = min(rows, 256)
    full = pl.BlockSpec((block, columns), lambda i: (i, 0))
    quarter = pl.BlockSpec((block // 4, columns), lambda i: (i, 0))
    return call(
        weights_kernel,
        (
            jax.ShapeDtypeStruct((rows, columns), BF16),
            jax.ShapeDtypeStruct((rows, columns), F32),
            jax.ShapeDtypeStruct((rows, columns), BF16),
        ),
        flops=rows * columns * 3000,
        moved=rows * columns * 14,
        grid=(rows // block,),
        in_specs=[full, quarter, quarter],
        out_specs=(full, full, full),
    )(master, mask_now, mask_next)


def effective_kernel(master_ref, now_ref, effective_ref):
    kept = expanded(now_ref[...], master_ref.shape[0]) == 1
    effective_ref[...] = jnp.where(kept, master_ref[...] * WEIGHT_SCALE, 0.0).astype(BF16)


def effective_of(master, mask_now):
    rows, columns = master.shape
    block = min(rows, 256)
    full = pl.BlockSpec((block, columns), lambda i: (i, 0))
    return call(
        effective_kernel,
        jax.ShapeDtypeStruct((rows, columns), BF16),
        flops=rows * columns * 3000,
        moved=rows * columns * 7,
        grid=(rows // block,),
        in_specs=[full, pl.BlockSpec((block // 4, columns), lambda i: (i, 0))],
        out_specs=full,
    )(master, mask_now)


def lanes_of(left, right, wide):
    lane = lax.broadcasted_iota(jnp.int32, (left.shape[0], wide), 1)
    return jnp.where(lane < wide // 2, left, right)


def decays_of(col, row):
    half = SPAN // 2
    causal = lax.broadcasted_iota(jnp.int32, (half, half), 0) >= lax.broadcasted_iota(
        jnp.int32, (half, half), 1
    )
    top = jnp.exp(jnp.where(causal, col[:half] - row[:, :half], OUT_OF_SIGHT))
    low = jnp.exp(col[half:] - row[:, :half])
    end = jnp.exp(jnp.where(causal, col[half:] - row[:, half:], OUT_OF_SIGHT))
    return top, low, end


def before_kernel(
    x_ref, dy_ref, logt_ref,
    xd_ref, yd_ref, mix_ref, mixt_ref, cum_ref, cumt_ref, end_ref, tall_ref,
):
    heads = cum_ref.shape[2]
    half = SPAN // 2
    wide = x_ref.shape[1] // heads * 2
    row = lax.broadcasted_iota(jnp.int32, (SPAN, SPAN), 0)
    col = lax.broadcasted_iota(jnp.int32, (SPAN, SPAN), 1)
    first = pl.multiple_of(pl.program_id(0) * heads, heads)
    cumt = jnp.dot(
        logt_ref[pl.ds(first, heads), :], (row <= col).astype(F32),
        precision=lax.Precision.HIGHEST, preferred_element_type=F32,
    )
    tall_ref[...] = jnp.zeros_like(tall_ref)
    tall_ref[:heads, :] = cumt
    cum = tall_ref[...].T[:, :heads]
    cum_ref[0] = cum
    cumt_ref[0] = cumt
    end = cum[SPAN - 1 :, :]
    from_start = jnp.exp(cum)
    to_end = jnp.exp(end - cum)
    whole = jnp.exp(end)
    mix = [jnp.zeros((half, half), F32) for _ in range(3)]
    lane = lax.broadcasted_iota(jnp.int32, (SPAN, wide), 1)
    for pair in range(heads // 2):
        a, b = 2 * pair, 2 * pair + 1
        cut = slice(pair * wide, (pair + 1) * wide)
        x = x_ref[:, cut]
        dy = dy_ref[:, cut]
        wide_dy = dy.astype(F32)
        xd_ref[:, cut] = (
            x.astype(F32) * lanes_of(to_end[:, a : a + 1], to_end[:, b : b + 1], wide)
        ).astype(BF16)
        yd_ref[:, cut] = (
            wide_dy * lanes_of(from_start[:, a : a + 1], from_start[:, b : b + 1], wide)
        ).astype(BF16)
        end_ref[0, :, cut] = lanes_of(whole[:, a : a + 1], whole[:, b : b + 1], wide)
        for head, mine in ((a, lane < wide // 2), (b, lane >= wide // 2)):
            one = jnp.where(mine, wide_dy, 0.0).astype(BF16)
            decays = decays_of(cum[:, head : head + 1], cumt[head : head + 1, :])
            mix[0] += dot_nt(one[:half], x[:half]) * decays[0]
            both = dot_nt(one[half:], x)
            mix[1] += both[:, :half] * decays[1]
            mix[2] += both[:, half:] * decays[2]
    nothing = jnp.zeros((half, half), BF16)
    top, low, end_mix = (m.astype(BF16) for m in mix)
    topt, lowt, end_mixt = (m.T.astype(BF16) for m in mix)
    mix_ref[0, :half, :half] = top
    mix_ref[0, :half, half:] = nothing
    mix_ref[0, half:, :half] = low
    mix_ref[0, half:, half:] = end_mix
    mixt_ref[0, :half, :half] = topt
    mixt_ref[0, :half, half:] = lowt
    mixt_ref[0, half:, :half] = nothing
    mixt_ref[0, half:, half:] = end_mixt


def wide_spec(width):
    return pl.BlockSpec((SPAN, width), lambda g: (0, g))


def lead_spec(*shape):
    return pl.BlockSpec((1, *shape), lambda g: (g, *(0 for _ in shape)))


def before(values, cotan, logs_t, groups):
    heads = logs_t.shape[0] // groups
    width = values.shape[1] // groups
    wide = wide_spec(width)
    return call(
        before_kernel,
        (
            jax.ShapeDtypeStruct(values.shape, BF16),
            jax.ShapeDtypeStruct(values.shape, BF16),
            jax.ShapeDtypeStruct((groups, SPAN, SPAN), BF16),
            jax.ShapeDtypeStruct((groups, SPAN, SPAN), BF16),
            jax.ShapeDtypeStruct((groups, SPAN, heads), F32),
            jax.ShapeDtypeStruct((groups, heads, SPAN), F32),
            jax.ShapeDtypeStruct((groups, 1, width), F32),
        ),
        flops=groups * heads * SPAN * SPAN * 2500,
        moved=values.size * 8,
        exps=groups * heads * SPAN * SPAN,
        grid=(groups,),
        in_specs=[wide, wide, pl.BlockSpec(logs_t.shape, lambda g: (0, 0))],
        out_specs=(
            wide, wide, lead_spec(SPAN, SPAN), lead_spec(SPAN, SPAN),
            lead_spec(SPAN, heads), lead_spec(heads, SPAN), lead_spec(1, width),
        ),
        scratch_shapes=[pltpu.VMEM((STATE, SPAN), F32)],
    )(values, cotan, logs_t)


def partial_kernel(spread, *refs):
    given = refs[:-1] if spread else refs
    (*pieces, weight_ref, sibling_weight_ref, out_ref, sibling_out_ref) = given
    pieces = [piece[...] for piece in pieces]
    if spread:
        refs[-1][...] = pieces[-2] + pieces[-1]
        pieces[-2:] = [refs[-1][...]]
    start = 0
    for piece in pieces:
        rows = slice(start, start + piece.shape[0])
        start += piece.shape[0]
        out_ref[rows, :] = dot(piece, weight_ref[...]).astype(BF16)
        sibling_out_ref[rows, :] = dot(piece, sibling_weight_ref[...]).astype(BF16)


def partials(pieces, effective, sibling_effective, spread=False):
    rows = sum(piece.shape[0] for piece in pieces[: -1 if spread else None])
    columns = effective.shape[1]
    whole = pl.BlockSpec(memory_space=pltpu.VMEM)
    shapes = [jax.ShapeDtypeStruct((rows, columns), BF16)] * 2
    if spread:
        shapes.append(jax.ShapeDtypeStruct(pieces[-1].shape, BF16))
    return call(
        functools.partial(partial_kernel, spread),
        tuple(shapes),
        flops=4 * rows * effective.size,
        moved=(rows * effective.shape[0] + 2 * effective.size + 2 * rows * columns) * 2,
        in_specs=[whole] * (len(pieces) + 2),
        out_specs=(whole,) * len(shapes),
    )(*pieces, effective, sibling_effective)


def turn_kernel(*refs):
    (*pieces, out_ref) = refs
    start = 0
    for piece in pieces:
        out_ref[:, start : start + piece.shape[0]] = turned(piece[...])
        start += piece.shape[0]


def turn(pieces):
    rows, features = sum(piece.shape[0] for piece in pieces), pieces[0].shape[1]
    whole = pl.BlockSpec(memory_space=pltpu.VMEM)
    return call(
        turn_kernel,
        jax.ShapeDtypeStruct((features, rows), BF16),
        flops=rows * features * 2000,
        moved=rows * features * 4,
        in_specs=[whole] * len(pieces),
        out_specs=whole,
    )(*pieces)


def either(ahead, first, second, body):
    if ahead:
        return body(first, second)
    lower = lax.axis_index("seq") < lax.axis_size("seq") // 2

    @pl.when(lower)
    def _():
        body(first, second)

    @pl.when(jnp.logical_not(lower))
    def _():
        body(second, first)


def states_kernel(both, *refs):
    (*terms, xd_ref, yd_ref, proj_ref, near_low_ref, near_ref, far_ref) = refs
    total = terms[0][...].astype(F32)
    for term in terms[1:]:
        total += term[...].astype(F32)
    low = total.astype(BF16)
    proj_ref[...] = low
    state = dot(turned(low[:, :STATE]), xd_ref[...])
    adjoint = dot(turned(low[:, STATE:]), yd_ref[...])

    def put(near, far):
        near_low_ref[0] = near.astype(BF16)
        near_ref[0] = near
        far_ref[0] = far

    either(both, state, adjoint, put)


def states(ahead, terms, xd, yd, first, groups, width):
    pair = pl.BlockSpec((SPAN, 2 * STATE), lambda g: (0, g))
    pair_from = pl.BlockSpec((SPAN, 2 * STATE), lambda g: (0, g + first))
    wide = pl.BlockSpec((SPAN, width), lambda g: (0, g + first))
    lead = lead_spec(STATE, width)
    shape = (groups, STATE, width)
    return call(
        functools.partial(states_kernel, ahead),
        (
            jax.ShapeDtypeStruct((SPAN, groups * 2 * STATE), BF16),
            jax.ShapeDtypeStruct(shape, BF16),
            jax.ShapeDtypeStruct(shape, F32),
            jax.ShapeDtypeStruct(shape, F32),
        ),
        flops=4 * SPAN * groups * width * STATE,
        moved=groups * SPAN * (width * 4 + 4 * STATE * 5),
        grid=(groups,),
        in_specs=[pair_from] * len(terms) + [wide, wide],
        out_specs=(pair, lead, lead, lead),
    )(*terms, xd, yd)


def added(refs):
    total = refs[0][0]
    for ref in refs[1:]:
        total += ref[0]
    return total


def message_kernel(decay_ref, arrived_ref, own_ref, out_ref):
    out_ref[0] = (decay_ref[0] * arrived_ref[0].astype(F32) + own_ref[0]).astype(BF16)


def handed_on(decay, arrived, own, first):
    groups, _, width = arrived.shape
    lead = lead_spec(STATE, width)
    return call(
        message_kernel,
        jax.ShapeDtypeStruct(arrived.shape, BF16),
        flops=2 * arrived.size,
        moved=8 * arrived.size,
        grid=(groups,),
        in_specs=[pl.BlockSpec((1, 1, width), lambda g: (g + first, 0, 0)), lead, lead],
        out_specs=lead,
    )(decay, arrived, own)


def grads_kernel(ahead, proj_ref, xd_ref, yd_ref, mix_ref, mixt_ref, near_ref, *refs):
    (*far_refs, out_ref) = refs

    def body(start, adjoint):
        write, read = proj_ref[:, :STATE], proj_ref[:, STATE:]
        grad_write = dot(mixt_ref[0], read) + dot_nt(xd_ref[...], added(adjoint))
        grad_read = dot(mix_ref[0], write) + dot_nt(yd_ref[...], added(start))
        out_ref[:, :STATE] = grad_write.astype(BF16)
        out_ref[:, STATE:] = grad_read.astype(BF16)

    either(ahead, [near_ref], far_refs, body)


def grads(ahead, proj, xd, yd, mix, mixt, near, far, first):
    groups, _, width = near.shape
    pair = pl.BlockSpec((SPAN, 2 * STATE), lambda g: (0, g))
    wide = pl.BlockSpec((SPAN, width), lambda g: (0, g + first))
    square = pl.BlockSpec((1, SPAN, SPAN), lambda g: (g + first, 0, 0))
    return call(
        functools.partial(grads_kernel, ahead),
        jax.ShapeDtypeStruct(proj.shape, BF16),
        flops=4 * SPAN * groups * (width + SPAN) * STATE,
        moved=groups * SPAN * width * 8,
        grid=(groups,),
        in_specs=[pair, wide, wide, square, square]
        + [lead_spec(STATE, width)] * (1 + len(far)),
        out_specs=pair,
    )(proj, xd, yd, mix, mixt, near, *far)


def write_grad(proj_ref, xd, mixt, adjoint):
    return (dot(mixt, proj_ref[:, STATE:]) + dot_nt(xd, adjoint)).astype(BF16)


def read_grad(proj_ref, yd, mix, start):
    return (dot(mix, proj_ref[:, :STATE]) + dot_nt(yd, start)).astype(BF16)


def first_grads_kernel(
    proj_ref, next_proj_ref, xd_ref, yd_ref, mix_ref, mixt_ref, near_ref, *refs
):
    (*far_refs, next_near_ref, out_ref) = refs
    width = near_ref.shape[2]
    here, after = slice(0, width), slice(width, 2 * width)
    rest = slice(2 * STATE, 3 * STATE)
    next_near = next_near_ref[0]

    def body(start, adjoint):
        out_ref[:, :STATE] = write_grad(proj_ref, xd_ref[:, here], mixt_ref[0], added(adjoint))
        out_ref[:, STATE : 2 * STATE] = read_grad(
            proj_ref, yd_ref[:, here], mix_ref[0], added(start)
        )
        if start[0] is near_ref:
            out_ref[:, rest] = read_grad(next_proj_ref, yd_ref[:, after], mix_ref[1], next_near)
        else:
            out_ref[:, rest] = write_grad(next_proj_ref, xd_ref[:, after], mixt_ref[1], next_near)

    either(None, [near_ref], far_refs, body)


def last_grads_kernel(proj_ref, xd_ref, yd_ref, mix_ref, mixt_ref, *refs):
    (*far_refs, out_ref) = refs
    width = far_refs[0].shape[2]
    after = slice(width, 2 * width)

    def body(start, adjoint):
        if start:
            out_ref[...] = read_grad(proj_ref, yd_ref[:, after], mix_ref[1], added(start))
        else:
            out_ref[...] = write_grad(proj_ref, xd_ref[:, after], mixt_ref[1], added(adjoint))

    either(None, [], far_refs, body)


def some_grads(kernel, columns, *operands):
    whole = pl.BlockSpec(memory_space=pltpu.VMEM)
    return call(
        kernel,
        jax.ShapeDtypeStruct((SPAN, columns), BF16),
        flops=8 * SPAN * columns * (SPAN + operands[-1].shape[2]),
        moved=2 * sum(operand.size for operand in operands),
        in_specs=[whole] * len(operands),
        out_specs=whole,
    )(*operands)


def first_grads(proj, next_proj, xd, yd, mix, mixt, near, far, next_near):
    return some_grads(
        first_grads_kernel, 3 * STATE,
        proj, next_proj, xd, yd, mix, mixt, near, *far, next_near,
    )


def last_grads(proj, xd, yd, mix, mixt, far):
    return some_grads(last_grads_kernel, STATE, proj, xd, yd, mix, mixt, *far)


def output_kernel(parts, hops, ahead, skip_ref, x_ref, cum_ref, cumt_ref, *refs):
    (*refs, out_ref, proj_ref, start_ref) = refs
    projs, nears = refs[:parts], refs[parts : 2 * parts]
    fars = [refs[2 * parts + hops * p : 2 * parts + hops * (p + 1)] for p in range(parts)]
    each = projs[0].shape[1] // (2 * STATE)
    for group in range(parts * each):
        part, at = divmod(group, each)

        @pl.when(pl.program_id(0) == group)
        def _(part=part, at=at):
            proj_ref[...] = projs[part][:, at * 2 * STATE : (at + 1) * 2 * STATE]

            def put(start, _):
                start_ref[...] = added([ref.at[at : at + 1] for ref in start])

            either(ahead, [nears[part]], fars[part], put)

    heads = cum_ref.shape[2]
    half = SPAN // 2
    wide = x_ref.shape[1] // heads * 2
    write = proj_ref[:, :STATE]
    read = proj_ref[:, STATE:]
    cum = cum_ref[0]
    cumt = cumt_ref[0]
    from_start = jnp.exp(cum)
    scores = dot_nt(read, write)
    top, low, end = scores[:half, :half], scores[half:, :half], scores[half:, half:]
    lane = lax.broadcasted_iota(jnp.int32, (half, wide), 1)
    for pair in range(heads // 2):
        a, b = 2 * pair, 2 * pair + 1
        cut = slice(pair * wide, (pair + 1) * wide)
        x = x_ref[:, cut]
        upper, lower = [], []
        for head in (a, b):
            decays = decays_of(cum[:, head : head + 1], cumt[head : head + 1, :])
            upper.append(dot((top * decays[0]).astype(BF16), x[:half]))
            lower.append(
                dot((low * decays[1]).astype(BF16), x[:half])
                + dot((end * decays[2]).astype(BF16), x[half:])
            )
        carried = dot(read, start_ref[:, cut]) * lanes_of(
            from_start[:, a : a + 1], from_start[:, b : b + 1], wide
        )
        head = pl.program_id(0) * heads + a
        gain = jnp.where(
            lax.broadcasted_iota(jnp.int32, (1, wide), 1) < wide // 2,
            skip_ref[head], skip_ref[head + 1],
        )
        rest = carried + gain * x.astype(F32)
        out_ref[:half, cut] = (
            jnp.where(lane < wide // 2, upper[0], upper[1]) + rest[:half]
        ).astype(BF16)
        out_ref[half:, cut] = (
            jnp.where(lane < wide // 2, lower[0], lower[1]) + rest[half:]
        ).astype(BF16)


def output(ahead, values, cum, cumt, skip, projs, nears, fars):
    groups, _, heads = cum.shape
    width = values.shape[1] // groups
    wide = wide_spec(width)
    pieces = [*projs, *nears, *(ref for far in fars for ref in far)]
    return call(
        functools.partial(output_kernel, len(projs), len(fars[0]), ahead),
        jax.ShapeDtypeStruct(values.shape, BF16),
        flops=groups * heads * SPAN * SPAN * 2000,
        moved=values.size * 5,
        exps=groups * heads * SPAN * SPAN,
        grid=(groups,),
        in_specs=[
            pl.BlockSpec(memory_space=pltpu.SMEM), wide, lead_spec(SPAN, heads),
            lead_spec(heads, SPAN),
        ]
        + [pl.BlockSpec(memory_space=pltpu.VMEM)] * len(pieces),
        out_specs=wide,
        scratch_shapes=[
            pltpu.VMEM((SPAN, 2 * STATE), BF16), pltpu.VMEM((STATE, width), BF16)
        ],
    )(skip, values, cum, cumt, *pieces)


def spot_of(block, spots):
    if spots == 1:
        return 0
    other_x = (lax.axis_index("head") != block % 2).astype(jnp.int32)
    other_core = (lax.axis_index("sub") != block // 2).astype(jnp.int32)
    return 2 * other_x + other_core


def update_kernel(blocks, spots, part, split, *refs):
    turned_refs, refs = refs[:spots], refs[spots:]
    firsts, refs = refs[:blocks], refs[blocks:]
    lasts = refs[:blocks] if split == 1 else ()
    decayed_ref, keep_ref = refs[len(lasts) : len(lasts) + 2]
    weight_ref, sparse_ref, grad_ref, weight_out, sparse_out, sems = refs[-6:]
    tokens, width = firsts[0].shape[0], grad_ref.shape[1]
    rows = decayed_ref.shape[0]
    step = min(rows, 256)
    columns = slice(part * width, (part + 1) * width)
    for block, first in enumerate(firsts):
        start = pl.multiple_of(spot_of(block, spots) * tokens, tokens)
        here = pl.ds(start, tokens)
        if split != 1:
            grad_ref[here, :] = first[:, :width]
            continue
        last = lasts[block]
        lower = (lax.axis_index("seq") + block) % blocks < blocks // 2

        @pl.when(lower)
        def _(here=here, first=first, last=last):
            grad_ref[here, :STATE] = last[...]
            grad_ref[here, STATE:] = first[:, width:]

        @pl.when(jnp.logical_not(lower))
        def _(here=here, first=first, last=last):
            grad_ref[here, :STATE] = first[:, width:]
            grad_ref[here, STATE:] = last[...]

    copies = []
    for number in range(rows // step):
        here = slice(number * step, (number + 1) * step)
        total = dot(turned_refs[0][here, :], grad_ref[:tokens, :])
        for spot in range(1, spots):
            total += dot(
                turned_refs[spot][here, :], grad_ref[spot * tokens : (spot + 1) * tokens, :]
            )
        weight = decayed_ref[here, columns] - (LEARN_RATE * WEIGHT_SCALE) * total
        weight_out[here, :] = weight
        sparse_out[here, :] = (weight * keep_ref[here, columns].astype(F32)).astype(BF16)
        for place, (source, target) in enumerate(
            ((weight_out, weight_ref), (sparse_out, sparse_ref))
        ):
            copies.append(
                pltpu.make_async_copy(
                    source.at[here, :], target.at[here, columns], sems.at[place, number]
                )
            )
            copies[-1].start()
    for copy in copies:
        copy.wait()


def update(turned_hidden, firsts, lasts, decayed, keep, width, part, split, earlier, vmem):
    rows, columns = decayed.shape
    tokens = turned_hidden[0].shape[1]
    spots, blocks = len(turned_hidden), len(firsts)
    pieces = [*turned_hidden, *firsts, *lasts, decayed, keep]
    earlier = earlier or ()
    whole, anywhere = pl.BlockSpec(memory_space=pltpu.VMEM), pl.BlockSpec(memory_space=pl.ANY)
    return call(
        functools.partial(update_kernel, blocks, spots, part, split),
        (jax.ShapeDtypeStruct((rows, columns), F32), jax.ShapeDtypeStruct((rows, columns), BF16)),
        flops=2 * spots * tokens * rows * width,
        moved=rows * width * 12 + spots * tokens * (rows + width) * 2,
        vmem=vmem,
        in_specs=[whole] * len(pieces) + [anywhere] * len(earlier),
        out_specs=(anywhere, anywhere),
        scratch_shapes=[
            pltpu.VMEM((spots * tokens, width), BF16),
            pltpu.VMEM((rows, width), F32),
            pltpu.VMEM((rows, width), BF16),
            pltpu.SemaphoreType.DMA((2, rows // min(rows, 256))),
        ],
        input_output_aliases={len(pieces) + i: i for i in range(len(earlier))},
    )(*pieces, *earlier)


def held(after, *before):
    return lax.optimization_barrier((after, *before))[0]


def to_all(seq, distance):
    return [(source, (source + distance) % seq) for source in range(seq)]


def block_pairs(seq, near, same_core):
    return [
        (
            (z * 2 + x) * 2 + core,
            ((z + (x if near else 1 - x) + 2 * core) % seq * 2 + x) * 2
            + (core if same_core else 1 - core),
        )
        for z in range(seq)
        for x in range(2)
        for core in range(2)
    ]


def transpose_pairs(seq):
    stays, crosses, beside, onward = [], [], [], []
    for z in range(seq):
        for x in range(2):
            for core in range(2):
                layer = 2 * x + core
                distance = (z - layer) % seq
                source, step = ((z * 2 + way) * 2 + core for way in (x, 1 - x))
                target = (layer * 2 + distance % 2) * 2 + distance // 2
                if distance % 2 == x:
                    stays.append((source, target))
                else:
                    crosses.append((source, target))
                    beside.append((source, step))
                    onward.append((step, target))
    return stays, crosses, beside, onward


SWAP = [(0, 1), (1, 0)]


def chain(own, own_low, decay, seq, step):
    arrived = jnp.zeros_like(own_low)
    message = own_low
    first = 0 if step > 0 else seq - 1
    for hop in range(seq - 1):
        source = first + hop * step
        if hop:
            message = handed_on(decay, arrived, own, 0)
        arrived = arrived + lax.ppermute(message, "seq", [(source, source + step)])
    return arrived


def on_device_general(
    seq, hidden, inner_values, log_decay, skip_gain, cotangent, master, mask_now, mask_next
):
    groups = master.shape[1] // (2 * STATE)
    effective, decayed, keep = weights(master, mask_now, mask_next)
    features = lax.all_gather(hidden, ("head", "sub"), axis=1, tiled=True)
    layer = lax.all_to_all(features, "seq", split_axis=1, concat_axis=0, tiled=True)
    xd, yd, mix, mixt, cum, cumt, decay = before(
        inner_values, cotangent, log_decay.T, groups
    )
    part = dot(layer, effective).astype(BF16)
    terms = [lax.psum_scatter(part, "seq", scatter_dimension=0, tiled=True)]
    proj, state_low, state, adjoint = states(True, terms, xd, yd, 0, groups, decay.shape[2])
    start = chain(state, state_low, decay, seq, 1)
    adjoint_in = chain(adjoint, adjoint.astype(BF16), decay, seq, -1)
    grad = grads(True, proj, xd, yd, mix, mixt, start, [adjoint_in], 0)
    blocks = [lax.all_gather(grad, "seq", axis=0, tiled=True)]
    ssd_output = output(
        True, inner_values, cum, cumt, skip_gain, [proj], [start], [[adjoint_in]]
    )
    return ssd_output, *update(
        [layer.T], blocks, [], decayed, keep, grad.shape[1], 0, None, None, 40 * MIB
    )


def on_device(
    seq, hidden, inner_values, log_decay, skip_gain, cotangent, master, mask_now, mask_next
):
    groups = master.shape[1] // (2 * STATE)
    axes = ("seq", "head", "sub")
    rows = hidden.shape[0] // 2
    stays, crosses, beside, onward = transpose_pairs(seq)
    relayed = lax.ppermute(hidden[rows:], axes, beside)
    top = lax.ppermute(hidden[:rows], axes, stays + crosses)
    low = [lax.ppermute(hidden[rows:], axes, stays), lax.ppermute(relayed, axes, onward)]
    effective, decayed, keep = weights(master, mask_now, mask_next)
    sibling_effective = effective_of(
        lax.ppermute(master, "sub", SWAP), lax.ppermute(mask_now, "sub", SWAP)
    )
    top = held(top, effective, sibling_effective)

    other = [lax.ppermute(top, "head", SWAP)]
    same, cross, low = partials([top, *low], effective, sibling_effective, True)
    other.append(lax.ppermute(low, "head", SWAP))
    terms = [
        lax.ppermute(same, axes, block_pairs(seq, True, True)),
        lax.ppermute(cross, axes, block_pairs(seq, True, False)),
    ]
    same, cross = partials(other, effective, sibling_effective)
    terms += [
        lax.ppermute(same, axes, block_pairs(seq, False, True)),
        lax.ppermute(cross, axes, block_pairs(seq, False, False)),
    ]

    xd, yd, mix, mixt, cum, cumt, decay = before(
        held(inner_values, same), cotangent, log_decay.T, groups
    )

    each = groups // PARTS
    spans = range(PARTS)
    projs, messages, nears, fars = zip(
        *(
            states(None, terms, xd, yd, p * each, each, decay.shape[2])
            for p in spans
        )
    )
    turned_hidden = []
    for first, second in ((top, low), other):
        piece = turn([held(first, nears[0]), second])
        turned_hidden += [piece, lax.ppermute(piece, "sub", SWAP)]
    fars = [*fars[:-1], held(fars[-1], *turned_hidden)]
    arrived = [[] for _ in spans]
    hops = (([(0, 1), (3, 2)], nears), ([(1, 2), (2, 1)], fars), ([(1, 0), (2, 3)], None))
    messages = list(messages)
    for pairs, own_terms in hops:
        for p in spans:
            message = messages[p]
            if p and not arrived[p]:
                message = held(message, arrived[p - 1][-1])
            arrived[p].append(lax.ppermute(message, "seq", pairs))
        for p in spans:
            if own_terms:
                messages[p] = handed_on(decay, arrived[p][-1], own_terms[p], p * each)
    (near, *far), (next_near, *next_far) = arrived
    first = first_grads(*projs, xd, yd, mix, mixt, near, far, next_near)
    last = last_grads(projs[1], xd, yd, mix, mixt, next_far)
    firsts, lasts = (
        [grad]
        + [
            lax.ppermute(grad, "seq", to_all(seq, seq - distance)) for distance in range(1, seq)
        ]
        for grad in (first, last)
    )
    decayed = held(decayed, last)
    updated = None
    for p in spans:
        updated = update(
            turned_hidden, firsts, lasts if p else [], decayed, keep, 2 * STATE, p, p, updated,
            16 * MIB,
        )
        if not p:
            cum = held(cum, *updated)
    ssd_output = output(
        None, inner_values, cum, cumt, skip_gain,
        projs, [a[0] for a in arrived], [a[1:] for a in arrived],
    )
    return ssd_output, *updated


PARTS = 2


def solution(mesh):
    by_position = P(("grp", "seq"), ("head", "sub"))
    by_row = P("seq", ("head", "sub"))
    seq, head, sub = (mesh.shape[name] for name in ("seq", "head", "sub"))
    body = on_device if (seq, head, sub) == (4, 2, 2) else on_device_general
    return jax.shard_map(
        functools.partial(body, seq),
        mesh=mesh,
        in_specs=(
            by_position, by_position, by_position, P(("head", "sub")), by_position,
            by_row, by_row, by_row,
        ),
        out_specs=(by_position, by_position, by_position),
        check_vma=False,
    )
```

```python
import functools
import math

import jax
import jax.numpy as jnp
from jax import lax
from jax.experimental import pallas as pl
from jax.experimental.pallas import tpu as pltpu
from jax.sharding import PartitionSpec as P

D = 4096
STATE = 128
SPAN = 256
LEARN_RATE = 0.05
WEIGHT_DECAY = 10.0
WEIGHT_SCALE = 2.0 / math.sqrt(D)
KEEP_BITS = (0b000111, 0b011001, 0b101010, 0b110100)
OUT_OF_SIGHT = -1e30
MIB = 1024 * 1024

F32 = jnp.float32
BF16 = jnp.bfloat16
NT = (((1,), (1,)), ((), ()))


def call(kernel, out_shape, flops, moved, exps=0, vmem=16 * MIB, **more):
    return pl.pallas_call(
        kernel,
        out_shape=out_shape,
        compiler_params=pltpu.CompilerParams(vmem_limit_bytes=vmem),
        cost_estimate=pl.CostEstimate(flops=flops, bytes_accessed=moved, transcendentals=exps),
        **more,
    )


def dot(a, b):
    return jnp.dot(a, b, preferred_element_type=F32)


def dot_nt(a, b):
    return lax.dot_general(a, b, NT, preferred_element_type=F32)


def turned(a):
    return a.astype(F32).T.astype(BF16)


def expanded(codes, rows):
    spread = (
        lax.broadcasted_iota(jnp.int32, (rows, rows // 4), 0) // 4
        == lax.broadcasted_iota(jnp.int32, (rows, rows // 4), 1)
    ).astype(F32)
    code = dot(spread.astype(BF16), codes.astype(F32).astype(BF16)).astype(jnp.int32)
    place = lax.broadcasted_iota(jnp.int32, (rows, 1), 0) % 4
    bits = jnp.where(
        place < 2,
        jnp.where(place == 0, KEEP_BITS[0], KEEP_BITS[1]),
        jnp.where(place == 2, KEEP_BITS[2], KEEP_BITS[3]),
    )
    return lax.shift_right_logical(jnp.broadcast_to(bits, code.shape), code) & 1


def weights_kernel(master_ref, now_ref, next_ref, effective_ref, decayed_ref, keep_ref):
    rows = master_ref.shape[0]
    master = master_ref[...]
    kept = expanded(now_ref[...], rows) == 1
    effective_ref[...] = jnp.where(kept, master * WEIGHT_SCALE, 0.0).astype(BF16)
    decayed_ref[...] = jnp.where(kept, master, master * (1.0 - LEARN_RATE * WEIGHT_DECAY))
    keep_ref[...] = expanded(next_ref[...], rows).astype(F32).astype(BF16)


def weights(master, mask_now, mask_next):
    rows, columns = master.shape
    block = min(rows, 256)
    full = pl.BlockSpec((block, columns), lambda i: (i, 0))
    quarter = pl.BlockSpec((block // 4, columns), lambda i: (i, 0))
    return call(
        weights_kernel,
        (
            jax.ShapeDtypeStruct((rows, columns), BF16),
            jax.ShapeDtypeStruct((rows, columns), F32),
            jax.ShapeDtypeStruct((rows, columns), BF16),
        ),
        flops=rows * columns * 3000,
        moved=rows * columns * 14,
        grid=(rows // block,),
        in_specs=[full, quarter, quarter],
        out_specs=(full, full, full),
    )(master, mask_now, mask_next)


def effective_kernel(master_ref, now_ref, effective_ref):
    kept = expanded(now_ref[...], master_ref.shape[0]) == 1
    effective_ref[...] = jnp.where(kept, master_ref[...] * WEIGHT_SCALE, 0.0).astype(BF16)


def effective_of(master, mask_now):
    rows, columns = master.shape
    block = min(rows, 256)
    full = pl.BlockSpec((block, columns), lambda i: (i, 0))
    return call(
        effective_kernel,
        jax.ShapeDtypeStruct((rows, columns), BF16),
        flops=rows * columns * 3000,
        moved=rows * columns * 7,
        grid=(rows // block,),
        in_specs=[full, pl.BlockSpec((block // 4, columns), lambda i: (i, 0))],
        out_specs=full,
    )(master, mask_now)


def lanes_of(left, right, wide):
    lane = lax.broadcasted_iota(jnp.int32, (left.shape[0], wide), 1)
    return jnp.where(lane < wide // 2, left, right)


def decays_of(col, row):
    half = SPAN // 2
    causal = lax.broadcasted_iota(jnp.int32, (half, half), 0) >= lax.broadcasted_iota(
        jnp.int32, (half, half), 1
    )
    top = jnp.exp(jnp.where(causal, col[:half] - row[:, :half], OUT_OF_SIGHT))
    low = jnp.exp(col[half:] - row[:, :half])
    end = jnp.exp(jnp.where(causal, col[half:] - row[:, half:], OUT_OF_SIGHT))
    return top, low, end


def before_kernel(
    x_ref, dy_ref, logt_ref,
    xd_ref, yd_ref, mix_ref, mixt_ref, cum_ref, cumt_ref, end_ref, tall_ref,
):
    heads = cum_ref.shape[2]
    half = SPAN // 2
    wide = x_ref.shape[1] // heads * 2
    row = lax.broadcasted_iota(jnp.int32, (SPAN, SPAN), 0)
    col = lax.broadcasted_iota(jnp.int32, (SPAN, SPAN), 1)
    first = pl.multiple_of(pl.program_id(0) * heads, heads)
    cumt = jnp.dot(
        logt_ref[pl.ds(first, heads), :], (row <= col).astype(F32),
        precision=lax.Precision.HIGHEST, preferred_element_type=F32,
    )
    tall_ref[...] = jnp.zeros_like(tall_ref)
    tall_ref[:heads, :] = cumt
    cum = tall_ref[...].T[:, :heads]
    cum_ref[0] = cum
    cumt_ref[0] = cumt
    end = cum[SPAN - 1 :, :]
    from_start = jnp.exp(cum)
    to_end = jnp.exp(end - cum)
    whole = jnp.exp(end)
    mix = [jnp.zeros((half, half), F32) for _ in range(3)]
    lane = lax.broadcasted_iota(jnp.int32, (SPAN, wide), 1)
    for pair in range(heads // 2):
        a, b = 2 * pair, 2 * pair + 1
        cut = slice(pair * wide, (pair + 1) * wide)
        x = x_ref[:, cut]
        dy = dy_ref[:, cut]
        wide_dy = dy.astype(F32)
        xd_ref[:, cut] = (
            x.astype(F32) * lanes_of(to_end[:, a : a + 1], to_end[:, b : b + 1], wide)
        ).astype(BF16)
        yd_ref[:, cut] = (
            wide_dy * lanes_of(from_start[:, a : a + 1], from_start[:, b : b + 1], wide)
        ).astype(BF16)
        end_ref[0, :, cut] = lanes_of(whole[:, a : a + 1], whole[:, b : b + 1], wide)
        for head, mine in ((a, lane < wide // 2), (b, lane >= wide // 2)):
            one = jnp.where(mine, wide_dy, 0.0).astype(BF16)
            decays = decays_of(cum[:, head : head + 1], cumt[head : head + 1, :])
            mix[0] += dot_nt(one[:half], x[:half]) * decays[0]
            both = dot_nt(one[half:], x)
            mix[1] += both[:, :half] * decays[1]
            mix[2] += both[:, half:] * decays[2]
    nothing = jnp.zeros((half, half), BF16)
    top, low, end_mix = (m.astype(BF16) for m in mix)
    topt, lowt, end_mixt = (m.T.astype(BF16) for m in mix)
    mix_ref[0, :half, :half] = top
    mix_ref[0, :half, half:] = nothing
    mix_ref[0, half:, :half] = low
    mix_ref[0, half:, half:] = end_mix
    mixt_ref[0, :half, :half] = topt
    mixt_ref[0, :half, half:] = lowt
    mixt_ref[0, half:, :half] = nothing
    mixt_ref[0, half:, half:] = end_mixt


def wide_spec(width):
    return pl.BlockSpec((SPAN, width), lambda g: (0, g))


def lead_spec(*shape):
    return pl.BlockSpec((1, *shape), lambda g: (g, *(0 for _ in shape)))


def before(values, cotan, logs_t, groups):
    heads = logs_t.shape[0] // groups
    width = values.shape[1] // groups
    wide = wide_spec(width)
    return call(
        before_kernel,
        (
            jax.ShapeDtypeStruct(values.shape, BF16),
            jax.ShapeDtypeStruct(values.shape, BF16),
            jax.ShapeDtypeStruct((groups, SPAN, SPAN), BF16),
            jax.ShapeDtypeStruct((groups, SPAN, SPAN), BF16),
            jax.ShapeDtypeStruct((groups, SPAN, heads), F32),
            jax.ShapeDtypeStruct((groups, heads, SPAN), F32),
            jax.ShapeDtypeStruct((groups, 1, width), F32),
        ),
        flops=groups * heads * SPAN * SPAN * 2500,
        moved=values.size * 8,
        exps=groups * heads * SPAN * SPAN,
        grid=(groups,),
        in_specs=[wide, wide, pl.BlockSpec(logs_t.shape, lambda g: (0, 0))],
        out_specs=(
            wide, wide, lead_spec(SPAN, SPAN), lead_spec(SPAN, SPAN),
            lead_spec(SPAN, heads), lead_spec(heads, SPAN), lead_spec(1, width),
        ),
        scratch_shapes=[pltpu.VMEM((STATE, SPAN), F32)],
    )(values, cotan, logs_t)


def partial_kernel(spread, *refs):
    given = refs[:-1] if spread else refs
    (*pieces, weight_ref, sibling_weight_ref, out_ref, sibling_out_ref) = given
    pieces = [piece[...] for piece in pieces]
    if spread:
        refs[-1][...] = pieces[-2] + pieces[-1]
        pieces[-2:] = [refs[-1][...]]
    start = 0
    for piece in pieces:
        rows = slice(start, start + piece.shape[0])
        start += piece.shape[0]
        out_ref[rows, :] = dot(piece, weight_ref[...]).astype(BF16)
        sibling_out_ref[rows, :] = dot(piece, sibling_weight_ref[...]).astype(BF16)


def partials(pieces, effective, sibling_effective, spread=False):
    rows = sum(piece.shape[0] for piece in pieces[: -1 if spread else None])
    columns = effective.shape[1]
    whole = pl.BlockSpec(memory_space=pltpu.VMEM)
    shapes = [jax.ShapeDtypeStruct((rows, columns), BF16)] * 2
    if spread:
        shapes.append(jax.ShapeDtypeStruct(pieces[-1].shape, BF16))
    return call(
        functools.partial(partial_kernel, spread),
        tuple(shapes),
        flops=4 * rows * effective.size,
        moved=(rows * effective.shape[0] + 2 * effective.size + 2 * rows * columns) * 2,
        in_specs=[whole] * (len(pieces) + 2),
        out_specs=(whole,) * len(shapes),
    )(*pieces, effective, sibling_effective)


def turn_kernel(*refs):
    (*pieces, out_ref) = refs
    start = 0
    for piece in pieces:
        out_ref[:, start : start + piece.shape[0]] = turned(piece[...])
        start += piece.shape[0]


def turn(pieces):
    rows, features = sum(piece.shape[0] for piece in pieces), pieces[0].shape[1]
    whole = pl.BlockSpec(memory_space=pltpu.VMEM)
    return call(
        turn_kernel,
        jax.ShapeDtypeStruct((features, rows), BF16),
        flops=rows * features * 2000,
        moved=rows * features * 4,
        in_specs=[whole] * len(pieces),
        out_specs=whole,
    )(*pieces)


def either(ahead, first, second, body):
    if ahead:
        return body(first, second)
    lower = lax.axis_index("seq") < lax.axis_size("seq") // 2

    @pl.when(lower)
    def _():
        body(first, second)

    @pl.when(jnp.logical_not(lower))
    def _():
        body(second, first)


def states_kernel(both, *refs):
    (*terms, xd_ref, yd_ref, proj_ref, near_low_ref, near_ref, far_ref) = refs
    total = terms[0][...].astype(F32)
    for term in terms[1:]:
        total += term[...].astype(F32)
    low = total.astype(BF16)
    proj_ref[...] = low
    state = dot(turned(low[:, :STATE]), xd_ref[...])
    adjoint = dot(turned(low[:, STATE:]), yd_ref[...])

    def put(near, far):
        near_low_ref[0] = near.astype(BF16)
        near_ref[0] = near
        far_ref[0] = far

    either(both, state, adjoint, put)


def states(ahead, terms, xd, yd, first, groups, width):
    pair = pl.BlockSpec((SPAN, 2 * STATE), lambda g: (0, g))
    pair_from = pl.BlockSpec((SPAN, 2 * STATE), lambda g: (0, g + first))
    wide = pl.BlockSpec((SPAN, width), lambda g: (0, g + first))
    lead = lead_spec(STATE, width)
    shape = (groups, STATE, width)
    return call(
        functools.partial(states_kernel, ahead),
        (
            jax.ShapeDtypeStruct((SPAN, groups * 2 * STATE), BF16),
            jax.ShapeDtypeStruct(shape, BF16),
            jax.ShapeDtypeStruct(shape, F32),
            jax.ShapeDtypeStruct(shape, F32),
        ),
        flops=4 * SPAN * groups * width * STATE,
        moved=groups * SPAN * (width * 4 + 4 * STATE * 5),
        grid=(groups,),
        in_specs=[pair_from] * len(terms) + [wide, wide],
        out_specs=(pair, lead, lead, lead),
    )(*terms, xd, yd)


def added(refs):
    total = refs[0][0]
    for ref in refs[1:]:
        total += ref[0]
    return total


def message_kernel(decay_ref, arrived_ref, own_ref, out_ref):
    out_ref[0] = (decay_ref[0] * arrived_ref[0].astype(F32) + own_ref[0]).astype(BF16)


def handed_on(decay, arrived, own, first):
    groups, _, width = arrived.shape
    lead = lead_spec(STATE, width)
    return call(
        message_kernel,
        jax.ShapeDtypeStruct(arrived.shape, BF16),
        flops=2 * arrived.size,
        moved=8 * arrived.size,
        grid=(groups,),
        in_specs=[pl.BlockSpec((1, 1, width), lambda g: (g + first, 0, 0)), lead, lead],
        out_specs=lead,
    )(decay, arrived, own)


def grads_kernel(ahead, proj_ref, xd_ref, yd_ref, mix_ref, mixt_ref, near_ref, *refs):
    (*far_refs, out_ref) = refs

    def body(start, adjoint):
        write, read = proj_ref[:, :STATE], proj_ref[:, STATE:]
        grad_write = dot(mixt_ref[0], read) + dot_nt(xd_ref[...], added(adjoint))
        grad_read = dot(mix_ref[0], write) + dot_nt(yd_ref[...], added(start))
        out_ref[:, :STATE] = grad_write.astype(BF16)
        out_ref[:, STATE:] = grad_read.astype(BF16)

    either(ahead, [near_ref], far_refs, body)


def grads(ahead, proj, xd, yd, mix, mixt, near, far, first):
    groups, _, width = near.shape
    pair = pl.BlockSpec((SPAN, 2 * STATE), lambda g: (0, g))
    wide = pl.BlockSpec((SPAN, width), lambda g: (0, g + first))
    square = pl.BlockSpec((1, SPAN, SPAN), lambda g: (g + first, 0, 0))
    return call(
        functools.partial(grads_kernel, ahead),
        jax.ShapeDtypeStruct(proj.shape, BF16),
        flops=4 * SPAN * groups * (width + SPAN) * STATE,
        moved=groups * SPAN * width * 8,
        grid=(groups,),
        in_specs=[pair, wide, wide, square, square]
        + [lead_spec(STATE, width)] * (1 + len(far)),
        out_specs=pair,
    )(proj, xd, yd, mix, mixt, near, *far)


def write_grad(proj_ref, xd, mixt, adjoint):
    return (dot(mixt, proj_ref[:, STATE:]) + dot_nt(xd, adjoint)).astype(BF16)


def read_grad(proj_ref, yd, mix, start):
    return (dot(mix, proj_ref[:, :STATE]) + dot_nt(yd, start)).astype(BF16)


def first_grads_kernel(
    proj_ref, next_proj_ref, xd_ref, yd_ref, mix_ref, mixt_ref, near_ref, *refs
):
    (*far_refs, next_near_ref, out_ref) = refs
    width = near_ref.shape[2]
    here, after = slice(0, width), slice(width, 2 * width)
    rest = slice(2 * STATE, 3 * STATE)
    next_near = next_near_ref[0]

    def body(start, adjoint):
        out_ref[:, :STATE] = write_grad(proj_ref, xd_ref[:, here], mixt_ref[0], added(adjoint))
        out_ref[:, STATE : 2 * STATE] = read_grad(
            proj_ref, yd_ref[:, here], mix_ref[0], added(start)
        )
        if start[0] is near_ref:
            out_ref[:, rest] = read_grad(next_proj_ref, yd_ref[:, after], mix_ref[1], next_near)
        else:
            out_ref[:, rest] = write_grad(next_proj_ref, xd_ref[:, after], mixt_ref[1], next_near)

    either(None, [near_ref], far_refs, body)


def last_grads_kernel(proj_ref, xd_ref, yd_ref, mix_ref, mixt_ref, *refs):
    (*far_refs, out_ref) = refs
    width = far_refs[0].shape[2]
    after = slice(width, 2 * width)

    def body(start, adjoint):
        if start:
            out_ref[...] = read_grad(proj_ref, yd_ref[:, after], mix_ref[1], added(start))
        else:
            out_ref[...] = write_grad(proj_ref, xd_ref[:, after], mixt_ref[1], added(adjoint))

    either(None, [], far_refs, body)


def some_grads(kernel, columns, *operands):
    whole = pl.BlockSpec(memory_space=pltpu.VMEM)
    return call(
        kernel,
        jax.ShapeDtypeStruct((SPAN, columns), BF16),
        flops=8 * SPAN * columns * (SPAN + operands[-1].shape[2]),
        moved=2 * sum(operand.size for operand in operands),
        in_specs=[whole] * len(operands),
        out_specs=whole,
    )(*operands)


def first_grads(proj, next_proj, xd, yd, mix, mixt, near, far, next_near):
    return some_grads(
        first_grads_kernel, 3 * STATE,
        proj, next_proj, xd, yd, mix, mixt, near, *far, next_near,
    )


def last_grads(proj, xd, yd, mix, mixt, far):
    return some_grads(last_grads_kernel, STATE, proj, xd, yd, mix, mixt, *far)


def output_kernel(parts, hops, ahead, skip_ref, x_ref, cum_ref, cumt_ref, *refs):
    (*refs, out_ref, proj_ref, start_ref) = refs
    projs, nears = refs[:parts], refs[parts : 2 * parts]
    fars = [refs[2 * parts + hops * p : 2 * parts + hops * (p + 1)] for p in range(parts)]
    each = projs[0].shape[1] // (2 * STATE)
    for group in range(parts * each):
        part, at = divmod(group, each)

        @pl.when(pl.program_id(0) == group)
        def _(part=part, at=at):
            proj_ref[...] = projs[part][:, at * 2 * STATE : (at + 1) * 2 * STATE]

            def put(start, _):
                start_ref[...] = added([ref.at[at : at + 1] for ref in start])

            either(ahead, [nears[part]], fars[part], put)

    heads = cum_ref.shape[2]
    half = SPAN // 2
    wide = x_ref.shape[1] // heads * 2
    write = proj_ref[:, :STATE]
    read = proj_ref[:, STATE:]
    cum = cum_ref[0]
    cumt = cumt_ref[0]
    from_start = jnp.exp(cum)
    scores = dot_nt(read, write)
    top, low, end = scores[:half, :half], scores[half:, :half], scores[half:, half:]
    lane = lax.broadcasted_iota(jnp.int32, (half, wide), 1)
    for pair in range(heads // 2):
        a, b = 2 * pair, 2 * pair + 1
        cut = slice(pair * wide, (pair + 1) * wide)
        x = x_ref[:, cut]
        upper, lower = [], []
        for head in (a, b):
            decays = decays_of(cum[:, head : head + 1], cumt[head : head + 1, :])
            upper.append(dot((top * decays[0]).astype(BF16), x[:half]))
            lower.append(
                dot((low * decays[1]).astype(BF16), x[:half])
                + dot((end * decays[2]).astype(BF16), x[half:])
            )
        carried = dot(read, start_ref[:, cut]) * lanes_of(
            from_start[:, a : a + 1], from_start[:, b : b + 1], wide
        )
        head = pl.program_id(0) * heads + a
        gain = jnp.where(
            lax.broadcasted_iota(jnp.int32, (1, wide), 1) < wide // 2,
            skip_ref[head], skip_ref[head + 1],
        )
        rest = carried + gain * x.astype(F32)
        out_ref[:half, cut] = (
            jnp.where(lane < wide // 2, upper[0], upper[1]) + rest[:half]
        ).astype(BF16)
        out_ref[half:, cut] = (
            jnp.where(lane < wide // 2, lower[0], lower[1]) + rest[half:]
        ).astype(BF16)


def output(ahead, values, cum, cumt, skip, projs, nears, fars):
    groups, _, heads = cum.shape
    width = values.shape[1] // groups
    wide = wide_spec(width)
    pieces = [*projs, *nears, *(ref for far in fars for ref in far)]
    return call(
        functools.partial(output_kernel, len(projs), len(fars[0]), ahead),
        jax.ShapeDtypeStruct(values.shape, BF16),
        flops=groups * heads * SPAN * SPAN * 2000,
        moved=values.size * 5,
        exps=groups * heads * SPAN * SPAN,
        grid=(groups,),
        in_specs=[
            pl.BlockSpec(memory_space=pltpu.SMEM), wide, lead_spec(SPAN, heads),
            lead_spec(heads, SPAN),
        ]
        + [pl.BlockSpec(memory_space=pltpu.VMEM)] * len(pieces),
        out_specs=wide,
        scratch_shapes=[
            pltpu.VMEM((SPAN, 2 * STATE), BF16), pltpu.VMEM((STATE, width), BF16)
        ],
    )(skip, values, cum, cumt, *pieces)


def spot_of(block, spots):
    if spots == 1:
        return 0
    other_x = (lax.axis_index("head") != block % 2).astype(jnp.int32)
    other_core = (lax.axis_index("sub") != block // 2).astype(jnp.int32)
    return 2 * other_x + other_core


def update_kernel(blocks, spots, part, split, *refs):
    turned_refs, refs = refs[:spots], refs[spots:]
    firsts, refs = refs[:blocks], refs[blocks:]
    lasts = refs[:blocks] if split == 1 else ()
    decayed_ref, keep_ref = refs[len(lasts) : len(lasts) + 2]
    weight_ref, sparse_ref, grad_ref, weight_out, sparse_out, sems = refs[-6:]
    tokens, width = firsts[0].shape[0], grad_ref.shape[1]
    rows = decayed_ref.shape[0]
    step = min(rows, 256)
    columns = slice(part * width, (part + 1) * width)
    for block, first in enumerate(firsts):
        start = pl.multiple_of(spot_of(block, spots) * tokens, tokens)
        here = pl.ds(start, tokens)
        if split != 1:
            grad_ref[here, :] = first[:, :width]
            continue
        last = lasts[block]
        lower = (lax.axis_index("seq") + block) % blocks < blocks // 2

        @pl.when(lower)
        def _(here=here, first=first, last=last):
            grad_ref[here, :STATE] = last[...]
            grad_ref[here, STATE:] = first[:, width:]

        @pl.when(jnp.logical_not(lower))
        def _(here=here, first=first, last=last):
            grad_ref[here, :STATE] = first[:, width:]
            grad_ref[here, STATE:] = last[...]

    copies = []
    for number in range(rows // step):
        here = slice(number * step, (number + 1) * step)
        total = dot(turned_refs[0][here, :], grad_ref[:tokens, :])
        for spot in range(1, spots):
            total += dot(
                turned_refs[spot][here, :], grad_ref[spot * tokens : (spot + 1) * tokens, :]
            )
        weight = decayed_ref[here, columns] - (LEARN_RATE * WEIGHT_SCALE) * total
        weight_out[here, :] = weight
        sparse_out[here, :] = (weight * keep_ref[here, columns].astype(F32)).astype(BF16)
        for place, (source, target) in enumerate(
            ((weight_out, weight_ref), (sparse_out, sparse_ref))
        ):
            copies.append(
                pltpu.make_async_copy(
                    source.at[here, :], target.at[here, columns], sems.at[place, number]
                )
            )
            copies[-1].start()
    for copy in copies:
        copy.wait()


def update(turned_hidden, firsts, lasts, decayed, keep, width, part, split, earlier, vmem):
    rows, columns = decayed.shape
    tokens = turned_hidden[0].shape[1]
    spots, blocks = len(turned_hidden), len(firsts)
    pieces = [*turned_hidden, *firsts, *lasts, decayed, keep]
    earlier = earlier or ()
    whole, anywhere = pl.BlockSpec(memory_space=pltpu.VMEM), pl.BlockSpec(memory_space=pl.ANY)
    return call(
        functools.partial(update_kernel, blocks, spots, part, split),
        (jax.ShapeDtypeStruct((rows, columns), F32), jax.ShapeDtypeStruct((rows, columns), BF16)),
        flops=2 * spots * tokens * rows * width,
        moved=rows * width * 12 + spots * tokens * (rows + width) * 2,
        vmem=vmem,
        in_specs=[whole] * len(pieces) + [anywhere] * len(earlier),
        out_specs=(anywhere, anywhere),
        scratch_shapes=[
            pltpu.VMEM((spots * tokens, width), BF16),
            pltpu.VMEM((rows, width), F32),
            pltpu.VMEM((rows, width), BF16),
            pltpu.SemaphoreType.DMA((2, rows // min(rows, 256))),
        ],
        input_output_aliases={len(pieces) + i: i for i in range(len(earlier))},
    )(*pieces, *earlier)


def held(after, *before):
    return lax.optimization_barrier((after, *before))[0]


def to_all(seq, distance):
    return [(source, (source + distance) % seq) for source in range(seq)]


def block_pairs(seq, near, same_core):
    return [
        (
            (z * 2 + x) * 2 + core,
            ((z + (x if near else 1 - x) + 2 * core) % seq * 2 + x) * 2
            + (core if same_core else 1 - core),
        )
        for z in range(seq)
        for x in range(2)
        for core in range(2)
    ]


def transpose_pairs(seq):
    stays, crosses, beside, onward = [], [], [], []
    for z in range(seq):
        for x in range(2):
            for core in range(2):
                layer = 2 * x + core
                distance = (z - layer) % seq
                source, step = ((z * 2 + way) * 2 + core for way in (x, 1 - x))
                target = (layer * 2 + distance % 2) * 2 + distance // 2
                if distance % 2 == x:
                    stays.append((source, target))
                else:
                    crosses.append((source, target))
                    beside.append((source, step))
                    onward.append((step, target))
    return stays, crosses, beside, onward


SWAP = [(0, 1), (1, 0)]


def chain(own, own_low, decay, seq, step):
    arrived = jnp.zeros_like(own_low)
    message = own_low
    first = 0 if step > 0 else seq - 1
    for hop in range(seq - 1):
        source = first + hop * step
        if hop:
            message = handed_on(decay, arrived, own, 0)
        arrived = arrived + lax.ppermute(message, "seq", [(source, source + step)])
    return arrived


def on_device_general(
    seq, hidden, inner_values, log_decay, skip_gain, cotangent, master, mask_now, mask_next
):
    groups = master.shape[1] // (2 * STATE)
    effective, decayed, keep = weights(master, mask_now, mask_next)
    features = lax.all_gather(hidden, ("head", "sub"), axis=1, tiled=True)
    layer = lax.all_to_all(features, "seq", split_axis=1, concat_axis=0, tiled=True)
    xd, yd, mix, mixt, cum, cumt, decay = before(
        inner_values, cotangent, log_decay.T, groups
    )
    part = dot(layer, effective).astype(BF16)
    terms = [lax.psum_scatter(part, "seq", scatter_dimension=0, tiled=True)]
    proj, state_low, state, adjoint = states(True, terms, xd, yd, 0, groups, decay.shape[2])
    start = chain(state, state_low, decay, seq, 1)
    adjoint_in = chain(adjoint, adjoint.astype(BF16), decay, seq, -1)
    grad = grads(True, proj, xd, yd, mix, mixt, start, [adjoint_in], 0)
    blocks = [lax.all_gather(grad, "seq", axis=0, tiled=True)]
    ssd_output = output(
        True, inner_values, cum, cumt, skip_gain, [proj], [start], [[adjoint_in]]
    )
    return ssd_output, *update(
        [layer.T], blocks, [], decayed, keep, grad.shape[1], 0, None, None, 40 * MIB
    )


def on_device(
    seq, hidden, inner_values, log_decay, skip_gain, cotangent, master, mask_now, mask_next
):
    groups = master.shape[1] // (2 * STATE)
    axes = ("seq", "head", "sub")
    rows = hidden.shape[0] // 2
    stays, crosses, beside, onward = transpose_pairs(seq)
    relayed = lax.ppermute(hidden[rows:], axes, beside)
    top = lax.ppermute(hidden[:rows], axes, stays + crosses)
    low = [lax.ppermute(hidden[rows:], axes, stays), lax.ppermute(relayed, axes, onward)]
    effective, decayed, keep = weights(master, mask_now, mask_next)
    sibling_effective = effective_of(
        lax.ppermute(master, "sub", SWAP), lax.ppermute(mask_now, "sub", SWAP)
    )
    top = held(top, effective, sibling_effective)

    other = [lax.ppermute(top, "head", SWAP)]
    same, cross, low = partials([top, *low], effective, sibling_effective, True)
    other.append(lax.ppermute(low, "head", SWAP))
    terms = [
        lax.ppermute(same, axes, block_pairs(seq, True, True)),
        lax.ppermute(cross, axes, block_pairs(seq, True, False)),
    ]
    same, cross = partials(other, effective, sibling_effective)
    terms += [
        lax.ppermute(same, axes, block_pairs(seq, False, True)),
        lax.ppermute(cross, axes, block_pairs(seq, False, False)),
    ]

    xd, yd, mix, mixt, cum, cumt, decay = before(
        held(inner_values, same), cotangent, log_decay.T, groups
    )

    each = groups // PARTS
    spans = range(PARTS)
    projs, messages, nears, fars = zip(
        *(
            states(None, terms, xd, yd, p * each, each, decay.shape[2])
            for p in spans
        )
    )
    turned_hidden = []
    for first, second in ((top, low), other):
        piece = turn([held(first, nears[0]), second])
        turned_hidden += [piece, lax.ppermute(piece, "sub", SWAP)]
    fars = [*fars[:-1], held(fars[-1], *turned_hidden)]
    arrived = [[] for _ in spans]
    hops = (([(0, 1), (3, 2)], nears), ([(1, 2), (2, 1)], fars), ([(1, 0), (2, 3)], None))
    messages = list(messages)
    for pairs, own_terms in hops:
        for p in spans:
            message = messages[p]
            if p and not arrived[p]:
                message = held(message, arrived[p - 1][-1])
            arrived[p].append(lax.ppermute(message, "seq", pairs))
        for p in spans:
            if own_terms:
                messages[p] = handed_on(decay, arrived[p][-1], own_terms[p], p * each)
    (near, *far), (next_near, *next_far) = arrived
    first = first_grads(*projs, xd, yd, mix, mixt, near, far, next_near)
    last = last_grads(projs[1], xd, yd, mix, mixt, next_far)
    firsts, lasts = (
        [grad]
        + [
            lax.ppermute(grad, "seq", to_all(seq, seq - distance)) for distance in range(1, seq)
        ]
        for grad in (first, last)
    )
    ssd_output = output(
        None, inner_values, held(cum, last), cumt, skip_gain,
        projs, [a[0] for a in arrived], [a[1:] for a in arrived],
    )
    decayed = held(decayed, ssd_output)
    updated = None
    for p in spans:
        updated = update(
            turned_hidden, firsts, lasts if p else [], decayed, keep, 2 * STATE, p, p, updated,
            16 * MIB,
        )
    return ssd_output, *updated


PARTS = 2


def solution(mesh):
    by_position = P(("grp", "seq"), ("head", "sub"))
    by_row = P("seq", ("head", "sub"))
    seq, head, sub = (mesh.shape[name] for name in ("seq", "head", "sub"))
    body = on_device if (seq, head, sub) == (4, 2, 2) else on_device_general
    return jax.shard_map(
        functools.partial(body, seq),
        mesh=mesh,
        in_specs=(
            by_position, by_position, by_position, P(("head", "sub")), by_position,
            by_row, by_row, by_row,
        ),
        out_specs=(by_position, by_position, by_position),
        check_vma=False,
    )
```

```python
import functools
import math

import jax
import jax.numpy as jnp
from jax import lax
from jax.experimental import pallas as pl
from jax.experimental.pallas import tpu as pltpu
from jax.sharding import PartitionSpec as P

D = 4096
STATE = 128
SPAN = 256
LEARN_RATE = 0.05
WEIGHT_DECAY = 10.0
WEIGHT_SCALE = 2.0 / math.sqrt(D)
KEEP_BITS = (0b000111, 0b011001, 0b101010, 0b110100)
OUT_OF_SIGHT = -1e30
MIB = 1024 * 1024

F32 = jnp.float32
BF16 = jnp.bfloat16
NT = (((1,), (1,)), ((), ()))


def call(kernel, out_shape, flops, moved, exps=0, vmem=16 * MIB, **more):
    return pl.pallas_call(
        kernel,
        out_shape=out_shape,
        compiler_params=pltpu.CompilerParams(vmem_limit_bytes=vmem),
        cost_estimate=pl.CostEstimate(flops=flops, bytes_accessed=moved, transcendentals=exps),
        **more,
    )


def dot(a, b):
    return jnp.dot(a, b, preferred_element_type=F32)


def dot_nt(a, b):
    return lax.dot_general(a, b, NT, preferred_element_type=F32)


def turned(a):
    return a.astype(F32).T.astype(BF16)


def expanded(codes, rows):
    spread = (
        lax.broadcasted_iota(jnp.int32, (rows, rows // 4), 0) // 4
        == lax.broadcasted_iota(jnp.int32, (rows, rows // 4), 1)
    ).astype(F32)
    code = dot(spread.astype(BF16), codes.astype(F32).astype(BF16)).astype(jnp.int32)
    place = lax.broadcasted_iota(jnp.int32, (rows, 1), 0) % 4
    bits = jnp.where(
        place < 2,
        jnp.where(place == 0, KEEP_BITS[0], KEEP_BITS[1]),
        jnp.where(place == 2, KEEP_BITS[2], KEEP_BITS[3]),
    )
    return lax.shift_right_logical(jnp.broadcast_to(bits, code.shape), code) & 1


def weights_kernel(master_ref, now_ref, next_ref, effective_ref, decayed_ref, keep_ref):
    rows = master_ref.shape[0]
    master = master_ref[...]
    kept = expanded(now_ref[...], rows) == 1
    effective_ref[...] = jnp.where(kept, master * WEIGHT_SCALE, 0.0).astype(BF16)
    decayed_ref[...] = jnp.where(kept, master, master * (1.0 - LEARN_RATE * WEIGHT_DECAY))
    keep_ref[...] = expanded(next_ref[...], rows).astype(F32).astype(BF16)


def weights(master, mask_now, mask_next):
    rows, columns = master.shape
    block = min(rows, 256)
    full = pl.BlockSpec((block, columns), lambda i: (i, 0))
    quarter = pl.BlockSpec((block // 4, columns), lambda i: (i, 0))
    return call(
        weights_kernel,
        (
            jax.ShapeDtypeStruct((rows, columns), BF16),
            jax.ShapeDtypeStruct((rows, columns), F32),
            jax.ShapeDtypeStruct((rows, columns), BF16),
        ),
        flops=rows * columns * 3000,
        moved=rows * columns * 14,
        grid=(rows // block,),
        in_specs=[full, quarter, quarter],
        out_specs=(full, full, full),
    )(master, mask_now, mask_next)


def effective_kernel(master_ref, now_ref, effective_ref):
    kept = expanded(now_ref[...], master_ref.shape[0]) == 1
    effective_ref[...] = jnp.where(kept, master_ref[...] * WEIGHT_SCALE, 0.0).astype(BF16)


def effective_of(master, mask_now):
    rows, columns = master.shape
    block = min(rows, 256)
    full = pl.BlockSpec((block, columns), lambda i: (i, 0))
    return call(
        effective_kernel,
        jax.ShapeDtypeStruct((rows, columns), BF16),
        flops=rows * columns * 3000,
        moved=rows * columns * 7,
        grid=(rows // block,),
        in_specs=[full, pl.BlockSpec((block // 4, columns), lambda i: (i, 0))],
        out_specs=full,
    )(master, mask_now)


def lanes_of(left, right, wide):
    lane = lax.broadcasted_iota(jnp.int32, (left.shape[0], wide), 1)
    return jnp.where(lane < wide // 2, left, right)


def decays_of(col, row):
    half = SPAN // 2
    causal = lax.broadcasted_iota(jnp.int32, (half, half), 0) >= lax.broadcasted_iota(
        jnp.int32, (half, half), 1
    )
    top = jnp.exp(jnp.where(causal, col[:half] - row[:, :half], OUT_OF_SIGHT))
    low = jnp.exp(col[half:] - row[:, :half])
    end = jnp.exp(jnp.where(causal, col[half:] - row[:, half:], OUT_OF_SIGHT))
    return top, low, end


def before_kernel(
    x_ref, dy_ref, logt_ref,
    xd_ref, yd_ref, mix_ref, mixt_ref, cum_ref, cumt_ref, end_ref, tall_ref,
):
    heads = cum_ref.shape[2]
    half = SPAN // 2
    wide = x_ref.shape[1] // heads * 2
    row = lax.broadcasted_iota(jnp.int32, (SPAN, SPAN), 0)
    col = lax.broadcasted_iota(jnp.int32, (SPAN, SPAN), 1)
    first = pl.multiple_of(pl.program_id(0) * heads, heads)
    cumt = jnp.dot(
        logt_ref[pl.ds(first, heads), :], (row <= col).astype(F32),
        precision=lax.Precision.HIGHEST, preferred_element_type=F32,
    )
    tall_ref[...] = jnp.zeros_like(tall_ref)
    tall_ref[:heads, :] = cumt
    cum = tall_ref[...].T[:, :heads]
    cum_ref[0] = cum
    cumt_ref[0] = cumt
    end = cum[SPAN - 1 :, :]
    from_start = jnp.exp(cum)
    to_end = jnp.exp(end - cum)
    whole = jnp.exp(end)
    mix = [jnp.zeros((half, half), F32) for _ in range(3)]
    lane = lax.broadcasted_iota(jnp.int32, (SPAN, wide), 1)
    for pair in range(heads // 2):
        a, b = 2 * pair, 2 * pair + 1
        cut = slice(pair * wide, (pair + 1) * wide)
        x = x_ref[:, cut]
        dy = dy_ref[:, cut]
        wide_dy = dy.astype(F32)
        xd_ref[:, cut] = (
            x.astype(F32) * lanes_of(to_end[:, a : a + 1], to_end[:, b : b + 1], wide)
        ).astype(BF16)
        yd_ref[:, cut] = (
            wide_dy * lanes_of(from_start[:, a : a + 1], from_start[:, b : b + 1], wide)
        ).astype(BF16)
        end_ref[0, :, cut] = lanes_of(whole[:, a : a + 1], whole[:, b : b + 1], wide)
        for head, mine in ((a, lane < wide // 2), (b, lane >= wide // 2)):
            one = jnp.where(mine, wide_dy, 0.0).astype(BF16)
            decays = decays_of(cum[:, head : head + 1], cumt[head : head + 1, :])
            mix[0] += dot_nt(one[:half], x[:half]) * decays[0]
            both = dot_nt(one[half:], x)
            mix[1] += both[:, :half] * decays[1]
            mix[2] += both[:, half:] * decays[2]
    nothing = jnp.zeros((half, half), BF16)
    top, low, end_mix = (m.astype(BF16) for m in mix)
    topt, lowt, end_mixt = (m.T.astype(BF16) for m in mix)
    mix_ref[0, :half, :half] = top
    mix_ref[0, :half, half:] = nothing
    mix_ref[0, half:, :half] = low
    mix_ref[0, half:, half:] = end_mix
    mixt_ref[0, :half, :half] = topt
    mixt_ref[0, :half, half:] = lowt
    mixt_ref[0, half:, :half] = nothing
    mixt_ref[0, half:, half:] = end_mixt


def wide_spec(width):
    return pl.BlockSpec((SPAN, width), lambda g: (0, g))


def lead_spec(*shape):
    return pl.BlockSpec((1, *shape), lambda g: (g, *(0 for _ in shape)))


def before(values, cotan, logs_t, groups):
    heads = logs_t.shape[0] // groups
    width = values.shape[1] // groups
    wide = wide_spec(width)
    return call(
        before_kernel,
        (
            jax.ShapeDtypeStruct(values.shape, BF16),
            jax.ShapeDtypeStruct(values.shape, BF16),
            jax.ShapeDtypeStruct((groups, SPAN, SPAN), BF16),
            jax.ShapeDtypeStruct((groups, SPAN, SPAN), BF16),
            jax.ShapeDtypeStruct((groups, SPAN, heads), F32),
            jax.ShapeDtypeStruct((groups, heads, SPAN), F32),
            jax.ShapeDtypeStruct((groups, 1, width), F32),
        ),
        flops=groups * heads * SPAN * SPAN * 2500,
        moved=values.size * 8,
        exps=groups * heads * SPAN * SPAN,
        grid=(groups,),
        in_specs=[wide, wide, pl.BlockSpec(logs_t.shape, lambda g: (0, 0))],
        out_specs=(
            wide, wide, lead_spec(SPAN, SPAN), lead_spec(SPAN, SPAN),
            lead_spec(SPAN, heads), lead_spec(heads, SPAN), lead_spec(1, width),
        ),
        scratch_shapes=[pltpu.VMEM((STATE, SPAN), F32)],
    )(values, cotan, logs_t)


def partial_kernel(spread, *refs):
    given = refs[:-1] if spread else refs
    (*pieces, weight_ref, sibling_weight_ref, out_ref, sibling_out_ref) = given
    pieces = [piece[...] for piece in pieces]
    if spread:
        refs[-1][...] = pieces[-2] + pieces[-1]
        pieces[-2:] = [refs[-1][...]]
    start = 0
    for piece in pieces:
        rows = slice(start, start + piece.shape[0])
        start += piece.shape[0]
        out_ref[rows, :] = dot(piece, weight_ref[...]).astype(BF16)
        sibling_out_ref[rows, :] = dot(piece, sibling_weight_ref[...]).astype(BF16)


def partials(pieces, effective, sibling_effective, spread=False):
    rows = sum(piece.shape[0] for piece in pieces[: -1 if spread else None])
    columns = effective.shape[1]
    whole = pl.BlockSpec(memory_space=pltpu.VMEM)
    shapes = [jax.ShapeDtypeStruct((rows, columns), BF16)] * 2
    if spread:
        shapes.append(jax.ShapeDtypeStruct(pieces[-1].shape, BF16))
    return call(
        functools.partial(partial_kernel, spread),
        tuple(shapes),
        flops=4 * rows * effective.size,
        moved=(rows * effective.shape[0] + 2 * effective.size + 2 * rows * columns) * 2,
        in_specs=[whole] * (len(pieces) + 2),
        out_specs=(whole,) * len(shapes),
    )(*pieces, effective, sibling_effective)


def rest_kernel(
    ready_ref, sibling_ready_ref, piece_ref, weight_ref, sibling_weight_ref, out_ref, sibling_out_ref
):
    rows = ready_ref.shape[0]
    out_ref[:rows, :] = ready_ref[...]
    sibling_out_ref[:rows, :] = sibling_ready_ref[...]
    out_ref[rows:, :] = dot(piece_ref[...], weight_ref[...]).astype(BF16)
    sibling_out_ref[rows:, :] = dot(piece_ref[...], sibling_weight_ref[...]).astype(BF16)


def rest_of_partials(ready, piece, effective, sibling_effective):
    rows, columns = ready[0].shape[0] + piece.shape[0], effective.shape[1]
    whole = pl.BlockSpec(memory_space=pltpu.VMEM)
    return call(
        rest_kernel,
        (jax.ShapeDtypeStruct((rows, columns), BF16),) * 2,
        flops=4 * piece.shape[0] * effective.size,
        moved=(piece.size + 2 * effective.size + 2 * rows * columns) * 2,
        in_specs=[whole] * 5,
        out_specs=(whole,) * 2,
    )(*ready, piece, effective, sibling_effective)


def turn_kernel(*refs):
    (*pieces, out_ref) = refs
    start = 0
    for piece in pieces:
        out_ref[:, start : start + piece.shape[0]] = turned(piece[...])
        start += piece.shape[0]


def turn(pieces):
    rows, features = sum(piece.shape[0] for piece in pieces), pieces[0].shape[1]
    whole = pl.BlockSpec(memory_space=pltpu.VMEM)
    return call(
        turn_kernel,
        jax.ShapeDtypeStruct((features, rows), BF16),
        flops=rows * features * 2000,
        moved=rows * features * 4,
        in_specs=[whole] * len(pieces),
        out_specs=whole,
    )(*pieces)


def either(ahead, first, second, body):
    if ahead:
        return body(first, second)
    lower = lax.axis_index("seq") < lax.axis_size("seq") // 2

    @pl.when(lower)
    def _():
        body(first, second)

    @pl.when(jnp.logical_not(lower))
    def _():
        body(second, first)


def states_kernel(both, *refs):
    (*terms, xd_ref, yd_ref, proj_ref, near_low_ref, near_ref, far_ref) = refs
    total = terms[0][...].astype(F32)
    for term in terms[1:]:
        total += term[...].astype(F32)
    low = total.astype(BF16)
    proj_ref[...] = low
    state = dot(turned(low[:, :STATE]), xd_ref[...])
    adjoint = dot(turned(low[:, STATE:]), yd_ref[...])

    def put(near, far):
        near_low_ref[0] = near.astype(BF16)
        near_ref[0] = near
        far_ref[0] = far

    either(both, state, adjoint, put)


def states(ahead, terms, xd, yd, first, groups, width):
    pair = pl.BlockSpec((SPAN, 2 * STATE), lambda g: (0, g))
    pair_from = pl.BlockSpec((SPAN, 2 * STATE), lambda g: (0, g + first))
    wide = pl.BlockSpec((SPAN, width), lambda g: (0, g + first))
    lead = lead_spec(STATE, width)
    shape = (groups, STATE, width)
    return call(
        functools.partial(states_kernel, ahead),
        (
            jax.ShapeDtypeStruct((SPAN, groups * 2 * STATE), BF16),
            jax.ShapeDtypeStruct(shape, BF16),
            jax.ShapeDtypeStruct(shape, F32),
            jax.ShapeDtypeStruct(shape, F32),
        ),
        flops=4 * SPAN * groups * width * STATE,
        moved=groups * SPAN * (width * 4 + 4 * STATE * 5),
        grid=(groups,),
        in_specs=[pair_from] * len(terms) + [wide, wide],
        out_specs=(pair, lead, lead, lead),
    )(*terms, xd, yd)


def added(refs):
    total = refs[0][0]
    for ref in refs[1:]:
        total += ref[0]
    return total


def message_kernel(decay_ref, arrived_ref, own_ref, out_ref):
    out_ref[0] = (decay_ref[0] * arrived_ref[0].astype(F32) + own_ref[0]).astype(BF16)


def handed_on(decay, arrived, own, first):
    groups, _, width = arrived.shape
    lead = lead_spec(STATE, width)
    return call(
        message_kernel,
        jax.ShapeDtypeStruct(arrived.shape, BF16),
        flops=2 * arrived.size,
        moved=8 * arrived.size,
        grid=(groups,),
        in_specs=[pl.BlockSpec((1, 1, width), lambda g: (g + first, 0, 0)), lead, lead],
        out_specs=lead,
    )(decay, arrived, own)


def grads_kernel(ahead, proj_ref, xd_ref, yd_ref, mix_ref, mixt_ref, near_ref, *refs):
    (*far_refs, out_ref) = refs

    def body(start, adjoint):
        write, read = proj_ref[:, :STATE], proj_ref[:, STATE:]
        grad_write = dot(mixt_ref[0], read) + dot_nt(xd_ref[...], added(adjoint))
        grad_read = dot(mix_ref[0], write) + dot_nt(yd_ref[...], added(start))
        out_ref[:, :STATE] = grad_write.astype(BF16)
        out_ref[:, STATE:] = grad_read.astype(BF16)

    either(ahead, [near_ref], far_refs, body)


def grads(ahead, proj, xd, yd, mix, mixt, near, far, first):
    groups, _, width = near.shape
    pair = pl.BlockSpec((SPAN, 2 * STATE), lambda g: (0, g))
    wide = pl.BlockSpec((SPAN, width), lambda g: (0, g + first))
    square = pl.BlockSpec((1, SPAN, SPAN), lambda g: (g + first, 0, 0))
    return call(
        functools.partial(grads_kernel, ahead),
        jax.ShapeDtypeStruct(proj.shape, BF16),
        flops=4 * SPAN * groups * (width + SPAN) * STATE,
        moved=groups * SPAN * width * 8,
        grid=(groups,),
        in_specs=[pair, wide, wide, square, square]
        + [lead_spec(STATE, width)] * (1 + len(far)),
        out_specs=pair,
    )(proj, xd, yd, mix, mixt, near, *far)


def write_grad(proj_ref, xd, mixt, adjoint):
    return (dot(mixt, proj_ref[:, STATE:]) + dot_nt(xd, adjoint)).astype(BF16)


def read_grad(proj_ref, yd, mix, start):
    return (dot(mix, proj_ref[:, :STATE]) + dot_nt(yd, start)).astype(BF16)


def first_grads_kernel(
    proj_ref, next_proj_ref, xd_ref, yd_ref, mix_ref, mixt_ref, near_ref, *refs
):
    (*far_refs, next_near_ref, out_ref) = refs
    width = near_ref.shape[2]
    here, after = slice(0, width), slice(width, 2 * width)
    rest = slice(2 * STATE, 3 * STATE)
    next_near = next_near_ref[0]

    def body(start, adjoint):
        out_ref[:, :STATE] = write_grad(proj_ref, xd_ref[:, here], mixt_ref[0], added(adjoint))
        out_ref[:, STATE : 2 * STATE] = read_grad(
            proj_ref, yd_ref[:, here], mix_ref[0], added(start)
        )
        if start[0] is near_ref:
            out_ref[:, rest] = read_grad(next_proj_ref, yd_ref[:, after], mix_ref[1], next_near)
        else:
            out_ref[:, rest] = write_grad(next_proj_ref, xd_ref[:, after], mixt_ref[1], next_near)

    either(None, [near_ref], far_refs, body)


def last_grads_kernel(proj_ref, xd_ref, yd_ref, mix_ref, mixt_ref, *refs):
    (*far_refs, out_ref) = refs
    width = far_refs[0].shape[2]
    after = slice(width, 2 * width)

    def body(start, adjoint):
        if start:
            out_ref[...] = read_grad(proj_ref, yd_ref[:, after], mix_ref[1], added(start))
        else:
            out_ref[...] = write_grad(proj_ref, xd_ref[:, after], mixt_ref[1], added(adjoint))

    either(None, [], far_refs, body)


def some_grads(kernel, columns, *operands):
    whole = pl.BlockSpec(memory_space=pltpu.VMEM)
    return call(
        kernel,
        jax.ShapeDtypeStruct((SPAN, columns), BF16),
        flops=8 * SPAN * columns * (SPAN + operands[-1].shape[2]),
        moved=2 * sum(operand.size for operand in operands),
        in_specs=[whole] * len(operands),
        out_specs=whole,
    )(*operands)


def first_grads(proj, next_proj, xd, yd, mix, mixt, near, far, next_near):
    return some_grads(
        first_grads_kernel, 3 * STATE,
        proj, next_proj, xd, yd, mix, mixt, near, *far, next_near,
    )


def last_grads(proj, xd, yd, mix, mixt, far):
    return some_grads(last_grads_kernel, STATE, proj, xd, yd, mix, mixt, *far)


def output_kernel(parts, hops, ahead, skip_ref, x_ref, cum_ref, cumt_ref, *refs):
    (*refs, out_ref, proj_ref, start_ref) = refs
    projs, nears = refs[:parts], refs[parts : 2 * parts]
    fars = [refs[2 * parts + hops * p : 2 * parts + hops * (p + 1)] for p in range(parts)]
    each = projs[0].shape[1] // (2 * STATE)
    for group in range(parts * each):
        part, at = divmod(group, each)

        @pl.when(pl.program_id(0) == group)
        def _(part=part, at=at):
            proj_ref[...] = projs[part][:, at * 2 * STATE : (at + 1) * 2 * STATE]

            def put(start, _):
                start_ref[...] = added([ref.at[at : at + 1] for ref in start])

            either(ahead, [nears[part]], fars[part], put)

    heads = cum_ref.shape[2]
    half = SPAN // 2
    wide = x_ref.shape[1] // heads * 2
    write = proj_ref[:, :STATE]
    read = proj_ref[:, STATE:]
    cum = cum_ref[0]
    cumt = cumt_ref[0]
    from_start = jnp.exp(cum)
    scores = dot_nt(read, write)
    top, low, end = scores[:half, :half], scores[half:, :half], scores[half:, half:]
    lane = lax.broadcasted_iota(jnp.int32, (half, wide), 1)
    for pair in range(heads // 2):
        a, b = 2 * pair, 2 * pair + 1
        cut = slice(pair * wide, (pair + 1) * wide)
        x = x_ref[:, cut]
        upper, lower = [], []
        for head in (a, b):
            decays = decays_of(cum[:, head : head + 1], cumt[head : head + 1, :])
            upper.append(dot((top * decays[0]).astype(BF16), x[:half]))
            lower.append(
                dot((low * decays[1]).astype(BF16), x[:half])
                + dot((end * decays[2]).astype(BF16), x[half:])
            )
        carried = dot(read, start_ref[:, cut]) * lanes_of(
            from_start[:, a : a + 1], from_start[:, b : b + 1], wide
        )
        head = pl.program_id(0) * heads + a
        gain = jnp.where(
            lax.broadcasted_iota(jnp.int32, (1, wide), 1) < wide // 2,
            skip_ref[head], skip_ref[head + 1],
        )
        rest = carried + gain * x.astype(F32)
        out_ref[:half, cut] = (
            jnp.where(lane < wide // 2, upper[0], upper[1]) + rest[:half]
        ).astype(BF16)
        out_ref[half:, cut] = (
            jnp.where(lane < wide // 2, lower[0], lower[1]) + rest[half:]
        ).astype(BF16)


def output(ahead, values, cum, cumt, skip, projs, nears, fars):
    groups, _, heads = cum.shape
    width = values.shape[1] // groups
    wide = wide_spec(width)
    pieces = [*projs, *nears, *(ref for far in fars for ref in far)]
    return call(
        functools.partial(output_kernel, len(projs), len(fars[0]), ahead),
        jax.ShapeDtypeStruct(values.shape, BF16),
        flops=groups * heads * SPAN * SPAN * 2000,
        moved=values.size * 5,
        exps=groups * heads * SPAN * SPAN,
        grid=(groups,),
        in_specs=[
            pl.BlockSpec(memory_space=pltpu.SMEM), wide, lead_spec(SPAN, heads),
            lead_spec(heads, SPAN),
        ]
        + [pl.BlockSpec(memory_space=pltpu.VMEM)] * len(pieces),
        out_specs=wide,
        scratch_shapes=[
            pltpu.VMEM((SPAN, 2 * STATE), BF16), pltpu.VMEM((STATE, width), BF16)
        ],
    )(skip, values, cum, cumt, *pieces)


def spot_of(block, spots):
    if spots == 1:
        return 0
    other_x = (lax.axis_index("head") != block % 2).astype(jnp.int32)
    other_core = (lax.axis_index("sub") != block // 2).astype(jnp.int32)
    return 2 * other_x + other_core


def update_kernel(blocks, spots, part, split, *refs):
    turned_refs, refs = refs[:spots], refs[spots:]
    firsts, refs = refs[:blocks], refs[blocks:]
    lasts = refs[:blocks] if split == 1 else ()
    decayed_ref, keep_ref = refs[len(lasts) : len(lasts) + 2]
    weight_ref, sparse_ref, grad_ref, weight_out, sparse_out, sems = refs[-6:]
    tokens, width = firsts[0].shape[0], grad_ref.shape[1]
    rows = decayed_ref.shape[0]
    step = min(rows, 256)
    columns = slice(part * width, (part + 1) * width)
    for block, first in enumerate(firsts):
        start = pl.multiple_of(spot_of(block, spots) * tokens, tokens)
        here = pl.ds(start, tokens)
        if split != 1:
            grad_ref[here, :] = first[:, :width]
            continue
        last = lasts[block]
        lower = (lax.axis_index("seq") + block) % blocks < blocks // 2

        @pl.when(lower)
        def _(here=here, first=first, last=last):
            grad_ref[here, :STATE] = last[...]
            grad_ref[here, STATE:] = first[:, width:]

        @pl.when(jnp.logical_not(lower))
        def _(here=here, first=first, last=last):
            grad_ref[here, :STATE] = first[:, width:]
            grad_ref[here, STATE:] = last[...]

    copies = []
    for number in range(rows // step):
        here = slice(number * step, (number + 1) * step)
        total = dot(turned_refs[0][here, :], grad_ref[:tokens, :])
        for spot in range(1, spots):
            total += dot(
                turned_refs[spot][here, :], grad_ref[spot * tokens : (spot + 1) * tokens, :]
            )
        weight = decayed_ref[here, columns] - (LEARN_RATE * WEIGHT_SCALE) * total
        weight_out[here, :] = weight
        sparse_out[here, :] = (weight * keep_ref[here, columns].astype(F32)).astype(BF16)
        for place, (source, target) in enumerate(
            ((weight_out, weight_ref), (sparse_out, sparse_ref))
        ):
            copies.append(
                pltpu.make_async_copy(
                    source.at[here, :], target.at[here, columns], sems.at[place, number]
                )
            )
            copies[-1].start()
    for copy in copies:
        copy.wait()


def update(turned_hidden, firsts, lasts, decayed, keep, width, part, split, earlier, vmem):
    rows, columns = decayed.shape
    tokens = turned_hidden[0].shape[1]
    spots, blocks = len(turned_hidden), len(firsts)
    pieces = [*turned_hidden, *firsts, *lasts, decayed, keep]
    earlier = earlier or ()
    whole, anywhere = pl.BlockSpec(memory_space=pltpu.VMEM), pl.BlockSpec(memory_space=pl.ANY)
    return call(
        functools.partial(update_kernel, blocks, spots, part, split),
        (jax.ShapeDtypeStruct((rows, columns), F32), jax.ShapeDtypeStruct((rows, columns), BF16)),
        flops=2 * spots * tokens * rows * width,
        moved=rows * width * 12 + spots * tokens * (rows + width) * 2,
        vmem=vmem,
        in_specs=[whole] * len(pieces) + [anywhere] * len(earlier),
        out_specs=(anywhere, anywhere),
        scratch_shapes=[
            pltpu.VMEM((spots * tokens, width), BF16),
            pltpu.VMEM((rows, width), F32),
            pltpu.VMEM((rows, width), BF16),
            pltpu.SemaphoreType.DMA((2, rows // min(rows, 256))),
        ],
        input_output_aliases={len(pieces) + i: i for i in range(len(earlier))},
    )(*pieces, *earlier)


def held(after, *before):
    return lax.optimization_barrier((after, *before))[0]


def to_all(seq, distance):
    return [(source, (source + distance) % seq) for source in range(seq)]


def block_pairs(seq, near, same_core):
    return [
        (
            (z * 2 + x) * 2 + core,
            ((z + (x if near else 1 - x) + 2 * core) % seq * 2 + x) * 2
            + (core if same_core else 1 - core),
        )
        for z in range(seq)
        for x in range(2)
        for core in range(2)
    ]


def transpose_pairs(seq):
    stays, crosses, beside, onward = [], [], [], []
    for z in range(seq):
        for x in range(2):
            for core in range(2):
                layer = 2 * x + core
                distance = (z - layer) % seq
                source, step = ((z * 2 + way) * 2 + core for way in (x, 1 - x))
                target = (layer * 2 + distance % 2) * 2 + distance // 2
                if distance % 2 == x:
                    stays.append((source, target))
                else:
                    crosses.append((source, target))
                    beside.append((source, step))
                    onward.append((step, target))
    return stays, crosses, beside, onward


SWAP = [(0, 1), (1, 0)]


def chain(own, own_low, decay, seq, step):
    arrived = jnp.zeros_like(own_low)
    message = own_low
    first = 0 if step > 0 else seq - 1
    for hop in range(seq - 1):
        source = first + hop * step
        if hop:
            message = handed_on(decay, arrived, own, 0)
        arrived = arrived + lax.ppermute(message, "seq", [(source, source + step)])
    return arrived


def on_device_general(
    seq, hidden, inner_values, log_decay, skip_gain, cotangent, master, mask_now, mask_next
):
    groups = master.shape[1] // (2 * STATE)
    effective, decayed, keep = weights(master, mask_now, mask_next)
    features = lax.all_gather(hidden, ("head", "sub"), axis=1, tiled=True)
    layer = lax.all_to_all(features, "seq", split_axis=1, concat_axis=0, tiled=True)
    xd, yd, mix, mixt, cum, cumt, decay = before(
        inner_values, cotangent, log_decay.T, groups
    )
    part = dot(layer, effective).astype(BF16)
    terms = [lax.psum_scatter(part, "seq", scatter_dimension=0, tiled=True)]
    proj, state_low, state, adjoint = states(True, terms, xd, yd, 0, groups, decay.shape[2])
    start = chain(state, state_low, decay, seq, 1)
    adjoint_in = chain(adjoint, adjoint.astype(BF16), decay, seq, -1)
    grad = grads(True, proj, xd, yd, mix, mixt, start, [adjoint_in], 0)
    blocks = [lax.all_gather(grad, "seq", axis=0, tiled=True)]
    ssd_output = output(
        True, inner_values, cum, cumt, skip_gain, [proj], [start], [[adjoint_in]]
    )
    return ssd_output, *update(
        [layer.T], blocks, [], decayed, keep, grad.shape[1], 0, None, None, 40 * MIB
    )


def on_device(
    seq, hidden, inner_values, log_decay, skip_gain, cotangent, master, mask_now, mask_next
):
    groups = master.shape[1] // (2 * STATE)
    axes = ("seq", "head", "sub")
    rows = hidden.shape[0] // 2
    stays, crosses, beside, onward = transpose_pairs(seq)
    relayed = lax.ppermute(hidden[rows:], axes, beside)
    top = lax.ppermute(hidden[:rows], axes, stays + crosses)
    low = [lax.ppermute(hidden[rows:], axes, stays), lax.ppermute(relayed, axes, onward)]
    effective, decayed, keep = weights(master, mask_now, mask_next)
    sibling_effective = effective_of(
        lax.ppermute(master, "sub", SWAP), lax.ppermute(mask_now, "sub", SWAP)
    )
    top = held(top, effective, sibling_effective)

    other = [lax.ppermute(top, "head", SWAP)]
    same, cross, low = partials([top, *low], effective, sibling_effective, True)
    other.append(lax.ppermute(low, "head", SWAP))
    terms = [
        lax.ppermute(same, axes, block_pairs(seq, True, True)),
        lax.ppermute(cross, axes, block_pairs(seq, True, False)),
    ]
    ready = partials(other[:1], effective, sibling_effective)
    same, cross = rest_of_partials(ready, other[1], effective, sibling_effective)
    terms += [
        lax.ppermute(same, axes, block_pairs(seq, False, True)),
        lax.ppermute(cross, axes, block_pairs(seq, False, False)),
    ]

    xd, yd, mix, mixt, cum, cumt, decay = before(
        held(inner_values, same), cotangent, log_decay.T, groups
    )

    each = groups // PARTS
    spans = range(PARTS)
    projs, messages, nears, fars = zip(
        *(
            states(None, terms, xd, yd, p * each, each, decay.shape[2])
            for p in spans
        )
    )
    turned_hidden = []
    for first, second in ((top, low), other):
        piece = turn([held(first, nears[0]), second])
        turned_hidden += [piece, lax.ppermute(piece, "sub", SWAP)]
    fars = [*fars[:-1], held(fars[-1], *turned_hidden)]
    arrived = [[] for _ in spans]
    hops = (([(0, 1), (3, 2)], nears), ([(1, 2), (2, 1)], fars), ([(1, 0), (2, 3)], None))
    messages = list(messages)
    for pairs, own_terms in hops:
        for p in spans:
            message = messages[p]
            if p and not arrived[p]:
                message = held(message, arrived[p - 1][-1])
            arrived[p].append(lax.ppermute(message, "seq", pairs))
        for p in spans:
            if own_terms:
                messages[p] = handed_on(decay, arrived[p][-1], own_terms[p], p * each)
    (near, *far), (next_near, *next_far) = arrived
    first = first_grads(*projs, xd, yd, mix, mixt, near, far, next_near)
    last = last_grads(projs[1], xd, yd, mix, mixt, next_far)
    ssd_output = output(
        None, inner_values, held(cum, last), cumt, skip_gain,
        projs, [a[0] for a in arrived], [a[1:] for a in arrived],
    )
    firsts, lasts = (
        [grad]
        + [
            lax.ppermute(
                held(grad, ssd_output) if grad is last and distance == seq - 1 else grad,
                "seq", to_all(seq, seq - distance),
            )
            for distance in range(1, seq)
        ]
        for grad in (first, last)
    )
    decayed = held(decayed, ssd_output)
    updated = None
    for p in spans:
        updated = update(
            turned_hidden, firsts, lasts if p else [], decayed, keep, 2 * STATE, p, p, updated,
            16 * MIB,
        )
    return ssd_output, *updated


PARTS = 2


def solution(mesh):
    by_position = P(("grp", "seq"), ("head", "sub"))
    by_row = P("seq", ("head", "sub"))
    seq, head, sub = (mesh.shape[name] for name in ("seq", "head", "sub"))
    body = on_device if (seq, head, sub) == (4, 2, 2) else on_device_general
    return jax.shard_map(
        functools.partial(body, seq),
        mesh=mesh,
        in_specs=(
            by_position, by_position, by_position, P(("head", "sub")), by_position,
            by_row, by_row, by_row,
        ),
        out_specs=(by_position, by_position, by_position),
        check_vma=False,
    )
```

```python
import functools
import math

import jax
import jax.numpy as jnp
from jax import lax
from jax.experimental import pallas as pl
from jax.experimental.pallas import tpu as pltpu
from jax.sharding import PartitionSpec as P

D = 4096
STATE = 128
SPAN = 256
LEARN_RATE = 0.05
WEIGHT_DECAY = 10.0
WEIGHT_SCALE = 2.0 / math.sqrt(D)
KEEP_BITS = (0b000111, 0b011001, 0b101010, 0b110100)
OUT_OF_SIGHT = -1e30
MIB = 1024 * 1024

F32 = jnp.float32
BF16 = jnp.bfloat16
NT = (((1,), (1,)), ((), ()))


def call(kernel, out_shape, flops, moved, exps=0, vmem=16 * MIB, **more):
    return pl.pallas_call(
        kernel,
        out_shape=out_shape,
        compiler_params=pltpu.CompilerParams(vmem_limit_bytes=vmem),
        cost_estimate=pl.CostEstimate(flops=flops, bytes_accessed=moved, transcendentals=exps),
        **more,
    )


def dot(a, b):
    return jnp.dot(a, b, preferred_element_type=F32)


def dot_nt(a, b):
    return lax.dot_general(a, b, NT, preferred_element_type=F32)


def turned(a):
    return a.astype(F32).T.astype(BF16)


def expanded(codes, rows):
    spread = (
        lax.broadcasted_iota(jnp.int32, (rows, rows // 4), 0) // 4
        == lax.broadcasted_iota(jnp.int32, (rows, rows // 4), 1)
    ).astype(F32)
    code = dot(spread.astype(BF16), codes.astype(F32).astype(BF16)).astype(jnp.int32)
    place = lax.broadcasted_iota(jnp.int32, (rows, 1), 0) % 4
    bits = jnp.where(
        place < 2,
        jnp.where(place == 0, KEEP_BITS[0], KEEP_BITS[1]),
        jnp.where(place == 2, KEEP_BITS[2], KEEP_BITS[3]),
    )
    return lax.shift_right_logical(jnp.broadcast_to(bits, code.shape), code) & 1


def weights_kernel(master_ref, now_ref, next_ref, effective_ref, decayed_ref, keep_ref):
    rows = master_ref.shape[0]
    master = master_ref[...]
    kept = expanded(now_ref[...], rows) == 1
    effective_ref[...] = jnp.where(kept, master * WEIGHT_SCALE, 0.0).astype(BF16)
    decayed_ref[...] = jnp.where(kept, master, master * (1.0 - LEARN_RATE * WEIGHT_DECAY))
    keep_ref[...] = expanded(next_ref[...], rows).astype(F32).astype(BF16)


def weights(master, mask_now, mask_next):
    rows, columns = master.shape
    block = min(rows, 256)
    full = pl.BlockSpec((block, columns), lambda i: (i, 0))
    quarter = pl.BlockSpec((block // 4, columns), lambda i: (i, 0))
    return call(
        weights_kernel,
        (
            jax.ShapeDtypeStruct((rows, columns), BF16),
            jax.ShapeDtypeStruct((rows, columns), F32),
            jax.ShapeDtypeStruct((rows, columns), BF16),
        ),
        flops=rows * columns * 3000,
        moved=rows * columns * 14,
        grid=(rows // block,),
        in_specs=[full, quarter, quarter],
        out_specs=(full, full, full),
    )(master, mask_now, mask_next)


def effective_kernel(master_ref, now_ref, effective_ref):
    kept = expanded(now_ref[...], master_ref.shape[0]) == 1
    effective_ref[...] = jnp.where(kept, master_ref[...] * WEIGHT_SCALE, 0.0).astype(BF16)


def effective_of(master, mask_now):
    rows, columns = master.shape
    block = min(rows, 256)
    full = pl.BlockSpec((block, columns), lambda i: (i, 0))
    return call(
        effective_kernel,
        jax.ShapeDtypeStruct((rows, columns), BF16),
        flops=rows * columns * 3000,
        moved=rows * columns * 7,
        grid=(rows // block,),
        in_specs=[full, pl.BlockSpec((block // 4, columns), lambda i: (i, 0))],
        out_specs=full,
    )(master, mask_now)


def lanes_of(left, right, wide):
    lane = lax.broadcasted_iota(jnp.int32, (left.shape[0], wide), 1)
    return jnp.where(lane < wide // 2, left, right)


def decays_of(col, row):
    half = SPAN // 2
    causal = lax.broadcasted_iota(jnp.int32, (half, half), 0) >= lax.broadcasted_iota(
        jnp.int32, (half, half), 1
    )
    top = jnp.exp(jnp.where(causal, col[:half] - row[:, :half], OUT_OF_SIGHT))
    low = jnp.exp(col[half:] - row[:, :half])
    end = jnp.exp(jnp.where(causal, col[half:] - row[:, half:], OUT_OF_SIGHT))
    return top, low, end


def before_kernel(
    x_ref, dy_ref, logt_ref,
    xd_ref, yd_ref, mix_ref, mixt_ref, cum_ref, cumt_ref, end_ref, tall_ref,
):
    heads = cum_ref.shape[2]
    half = SPAN // 2
    wide = x_ref.shape[1] // heads * 2
    row = lax.broadcasted_iota(jnp.int32, (SPAN, SPAN), 0)
    col = lax.broadcasted_iota(jnp.int32, (SPAN, SPAN), 1)
    first = pl.multiple_of(pl.program_id(0) * heads, heads)
    cumt = jnp.dot(
        logt_ref[pl.ds(first, heads), :], (row <= col).astype(F32),
        precision=lax.Precision.HIGHEST, preferred_element_type=F32,
    )
    tall_ref[...] = jnp.zeros_like(tall_ref)
    tall_ref[:heads, :] = cumt
    cum = tall_ref[...].T[:, :heads]
    cum_ref[0] = cum
    cumt_ref[0] = cumt
    end = cum[SPAN - 1 :, :]
    from_start = jnp.exp(cum)
    to_end = jnp.exp(end - cum)
    whole = jnp.exp(end)
    mix = [jnp.zeros((half, half), F32) for _ in range(3)]
    lane = lax.broadcasted_iota(jnp.int32, (SPAN, wide), 1)
    for pair in range(heads // 2):
        a, b = 2 * pair, 2 * pair + 1
        cut = slice(pair * wide, (pair + 1) * wide)
        x = x_ref[:, cut]
        dy = dy_ref[:, cut]
        wide_dy = dy.astype(F32)
        xd_ref[:, cut] = (
            x.astype(F32) * lanes_of(to_end[:, a : a + 1], to_end[:, b : b + 1], wide)
        ).astype(BF16)
        yd_ref[:, cut] = (
            wide_dy * lanes_of(from_start[:, a : a + 1], from_start[:, b : b + 1], wide)
        ).astype(BF16)
        end_ref[0, :, cut] = lanes_of(whole[:, a : a + 1], whole[:, b : b + 1], wide)
        for head, mine in ((a, lane < wide // 2), (b, lane >= wide // 2)):
            one = jnp.where(mine, wide_dy, 0.0).astype(BF16)
            decays = decays_of(cum[:, head : head + 1], cumt[head : head + 1, :])
            mix[0] += dot_nt(one[:half], x[:half]) * decays[0]
            both = dot_nt(one[half:], x)
            mix[1] += both[:, :half] * decays[1]
            mix[2] += both[:, half:] * decays[2]
    nothing = jnp.zeros((half, half), BF16)
    top, low, end_mix = (m.astype(BF16) for m in mix)
    topt, lowt, end_mixt = (m.T.astype(BF16) for m in mix)
    mix_ref[0, :half, :half] = top
    mix_ref[0, :half, half:] = nothing
    mix_ref[0, half:, :half] = low
    mix_ref[0, half:, half:] = end_mix
    mixt_ref[0, :half, :half] = topt
    mixt_ref[0, :half, half:] = lowt
    mixt_ref[0, half:, :half] = nothing
    mixt_ref[0, half:, half:] = end_mixt


def wide_spec(width):
    return pl.BlockSpec((SPAN, width), lambda g: (0, g))


def lead_spec(*shape):
    return pl.BlockSpec((1, *shape), lambda g: (g, *(0 for _ in shape)))


def before(values, cotan, logs_t, groups):
    heads = logs_t.shape[0] // groups
    width = values.shape[1] // groups
    wide = wide_spec(width)
    return call(
        before_kernel,
        (
            jax.ShapeDtypeStruct(values.shape, BF16),
            jax.ShapeDtypeStruct(values.shape, BF16),
            jax.ShapeDtypeStruct((groups, SPAN, SPAN), BF16),
            jax.ShapeDtypeStruct((groups, SPAN, SPAN), BF16),
            jax.ShapeDtypeStruct((groups, SPAN, heads), F32),
            jax.ShapeDtypeStruct((groups, heads, SPAN), F32),
            jax.ShapeDtypeStruct((groups, 1, width), F32),
        ),
        flops=groups * heads * SPAN * SPAN * 2500,
        moved=values.size * 8,
        exps=groups * heads * SPAN * SPAN,
        grid=(groups,),
        in_specs=[wide, wide, pl.BlockSpec(logs_t.shape, lambda g: (0, 0))],
        out_specs=(
            wide, wide, lead_spec(SPAN, SPAN), lead_spec(SPAN, SPAN),
            lead_spec(SPAN, heads), lead_spec(heads, SPAN), lead_spec(1, width),
        ),
        scratch_shapes=[pltpu.VMEM((STATE, SPAN), F32)],
    )(values, cotan, logs_t)


def partial_kernel(spread, *refs):
    given = refs[:-1] if spread else refs
    (*pieces, weight_ref, sibling_weight_ref, out_ref, sibling_out_ref) = given
    pieces = [piece[...] for piece in pieces]
    if spread:
        refs[-1][...] = pieces[-2] + pieces[-1]
        pieces[-2:] = [refs[-1][...]]
    start = 0
    for piece in pieces:
        rows = slice(start, start + piece.shape[0])
        start += piece.shape[0]
        out_ref[rows, :] = dot(piece, weight_ref[...]).astype(BF16)
        sibling_out_ref[rows, :] = dot(piece, sibling_weight_ref[...]).astype(BF16)


def partials(pieces, effective, sibling_effective, spread=False):
    rows = sum(piece.shape[0] for piece in pieces[: -1 if spread else None])
    columns = effective.shape[1]
    whole = pl.BlockSpec(memory_space=pltpu.VMEM)
    shapes = [jax.ShapeDtypeStruct((rows, columns), BF16)] * 2
    if spread:
        shapes.append(jax.ShapeDtypeStruct(pieces[-1].shape, BF16))
    return call(
        functools.partial(partial_kernel, spread),
        tuple(shapes),
        flops=4 * rows * effective.size,
        moved=(rows * effective.shape[0] + 2 * effective.size + 2 * rows * columns) * 2,
        in_specs=[whole] * (len(pieces) + 2),
        out_specs=(whole,) * len(shapes),
    )(*pieces, effective, sibling_effective)


def rest_kernel(
    ready_ref, sibling_ready_ref, piece_ref, weight_ref, sibling_weight_ref, out_ref, sibling_out_ref
):
    rows = ready_ref.shape[0]
    out_ref[:rows, :] = ready_ref[...]
    sibling_out_ref[:rows, :] = sibling_ready_ref[...]
    out_ref[rows:, :] = dot(piece_ref[...], weight_ref[...]).astype(BF16)
    sibling_out_ref[rows:, :] = dot(piece_ref[...], sibling_weight_ref[...]).astype(BF16)


def rest_of_partials(ready, piece, effective, sibling_effective):
    rows, columns = ready[0].shape[0] + piece.shape[0], effective.shape[1]
    whole = pl.BlockSpec(memory_space=pltpu.VMEM)
    return call(
        rest_kernel,
        (jax.ShapeDtypeStruct((rows, columns), BF16),) * 2,
        flops=4 * piece.shape[0] * effective.size,
        moved=(piece.size + 2 * effective.size + 2 * rows * columns) * 2,
        in_specs=[whole] * 5,
        out_specs=(whole,) * 2,
    )(*ready, piece, effective, sibling_effective)


def turn_kernel(*refs):
    (*pieces, out_ref) = refs
    start = 0
    for piece in pieces:
        out_ref[:, start : start + piece.shape[0]] = turned(piece[...])
        start += piece.shape[0]


def turn(pieces):
    rows, features = sum(piece.shape[0] for piece in pieces), pieces[0].shape[1]
    whole = pl.BlockSpec(memory_space=pltpu.VMEM)
    return call(
        turn_kernel,
        jax.ShapeDtypeStruct((features, rows), BF16),
        flops=rows * features * 2000,
        moved=rows * features * 4,
        in_specs=[whole] * len(pieces),
        out_specs=whole,
    )(*pieces)


def either(ahead, first, second, body):
    if ahead:
        return body(first, second)
    lower = lax.axis_index("seq") < lax.axis_size("seq") // 2

    @pl.when(lower)
    def _():
        body(first, second)

    @pl.when(jnp.logical_not(lower))
    def _():
        body(second, first)


def states_kernel(both, *refs):
    (*terms, xd_ref, yd_ref, proj_ref, near_low_ref, near_ref, far_ref) = refs
    total = terms[0][...].astype(F32)
    for term in terms[1:]:
        total += term[...].astype(F32)
    low = total.astype(BF16)
    proj_ref[...] = low
    state = dot(turned(low[:, :STATE]), xd_ref[...])
    adjoint = dot(turned(low[:, STATE:]), yd_ref[...])

    def put(near, far):
        near_low_ref[0] = near.astype(BF16)
        near_ref[0] = near
        far_ref[0] = far

    either(both, state, adjoint, put)


def states(ahead, terms, xd, yd, first, groups, width):
    pair = pl.BlockSpec((SPAN, 2 * STATE), lambda g: (0, g))
    pair_from = pl.BlockSpec((SPAN, 2 * STATE), lambda g: (0, g + first))
    wide = pl.BlockSpec((SPAN, width), lambda g: (0, g + first))
    lead = lead_spec(STATE, width)
    shape = (groups, STATE, width)
    return call(
        functools.partial(states_kernel, ahead),
        (
            jax.ShapeDtypeStruct((SPAN, groups * 2 * STATE), BF16),
            jax.ShapeDtypeStruct(shape, BF16),
            jax.ShapeDtypeStruct(shape, F32),
            jax.ShapeDtypeStruct(shape, F32),
        ),
        flops=4 * SPAN * groups * width * STATE,
        moved=groups * SPAN * (width * 4 + 4 * STATE * 5),
        grid=(groups,),
        in_specs=[pair_from] * len(terms) + [wide, wide],
        out_specs=(pair, lead, lead, lead),
    )(*terms, xd, yd)


def added(refs):
    total = refs[0][0]
    for ref in refs[1:]:
        total += ref[0]
    return total


def message_kernel(decay_ref, arrived_ref, own_ref, out_ref):
    out_ref[0] = (decay_ref[0] * arrived_ref[0].astype(F32) + own_ref[0]).astype(BF16)


def handed_on(decay, arrived, own, first):
    groups, _, width = arrived.shape
    lead = lead_spec(STATE, width)
    return call(
        message_kernel,
        jax.ShapeDtypeStruct(arrived.shape, BF16),
        flops=2 * arrived.size,
        moved=8 * arrived.size,
        grid=(groups,),
        in_specs=[pl.BlockSpec((1, 1, width), lambda g: (g + first, 0, 0)), lead, lead],
        out_specs=lead,
    )(decay, arrived, own)


def grads_kernel(ahead, proj_ref, xd_ref, yd_ref, mix_ref, mixt_ref, near_ref, *refs):
    (*far_refs, out_ref) = refs

    def body(start, adjoint):
        write, read = proj_ref[:, :STATE], proj_ref[:, STATE:]
        grad_write = dot(mixt_ref[0], read) + dot_nt(xd_ref[...], added(adjoint))
        grad_read = dot(mix_ref[0], write) + dot_nt(yd_ref[...], added(start))
        out_ref[:, :STATE] = grad_write.astype(BF16)
        out_ref[:, STATE:] = grad_read.astype(BF16)

    either(ahead, [near_ref], far_refs, body)


def grads(ahead, proj, xd, yd, mix, mixt, near, far, first):
    groups, _, width = near.shape
    pair = pl.BlockSpec((SPAN, 2 * STATE), lambda g: (0, g))
    wide = pl.BlockSpec((SPAN, width), lambda g: (0, g + first))
    square = pl.BlockSpec((1, SPAN, SPAN), lambda g: (g + first, 0, 0))
    return call(
        functools.partial(grads_kernel, ahead),
        jax.ShapeDtypeStruct(proj.shape, BF16),
        flops=4 * SPAN * groups * (width + SPAN) * STATE,
        moved=groups * SPAN * width * 8,
        grid=(groups,),
        in_specs=[pair, wide, wide, square, square]
        + [lead_spec(STATE, width)] * (1 + len(far)),
        out_specs=pair,
    )(proj, xd, yd, mix, mixt, near, *far)


def output_kernel(
    ahead, first, skip_ref, x_ref, cum_ref, cumt_ref, proj_ref, near_ref, *refs
):
    (*far_refs, out_ref, start_ref) = refs
    far_refs = [ref for ref in far_refs if ref.shape[1:] == near_ref.shape[1:]]

    def put(start, _):
        start_ref[...] = added(start)

    either(ahead, [near_ref], far_refs, put)

    heads = cum_ref.shape[2]
    half = SPAN // 2
    wide = x_ref.shape[1] // heads * 2
    write = proj_ref[:, :STATE]
    read = proj_ref[:, STATE:]
    cum = cum_ref[0]
    cumt = cumt_ref[0]
    from_start = jnp.exp(cum)
    scores = dot_nt(read, write)
    top, low, end = scores[:half, :half], scores[half:, :half], scores[half:, half:]
    lane = lax.broadcasted_iota(jnp.int32, (half, wide), 1)
    for pair in range(heads // 2):
        a, b = 2 * pair, 2 * pair + 1
        cut = slice(pair * wide, (pair + 1) * wide)
        x = x_ref[:, cut]
        upper, lower = [], []
        for head in (a, b):
            decays = decays_of(cum[:, head : head + 1], cumt[head : head + 1, :])
            upper.append(dot((top * decays[0]).astype(BF16), x[:half]))
            lower.append(
                dot((low * decays[1]).astype(BF16), x[:half])
                + dot((end * decays[2]).astype(BF16), x[half:])
            )
        carried = dot(read, start_ref[:, cut]) * lanes_of(
            from_start[:, a : a + 1], from_start[:, b : b + 1], wide
        )
        head = (pl.program_id(0) + first) * heads + a
        gain = jnp.where(
            lax.broadcasted_iota(jnp.int32, (1, wide), 1) < wide // 2,
            skip_ref[head], skip_ref[head + 1],
        )
        rest = carried + gain * x.astype(F32)
        out_ref[:half, cut] = (
            jnp.where(lane < wide // 2, upper[0], upper[1]) + rest[:half]
        ).astype(BF16)
        out_ref[half:, cut] = (
            jnp.where(lane < wide // 2, lower[0], lower[1]) + rest[half:]
        ).astype(BF16)


def output(ahead, values, cum, cumt, skip, proj, near, far, first, earlier):
    groups, _, width = near.shape
    heads = cum.shape[2]
    wide = pl.BlockSpec((SPAN, width), lambda g: (0, g + first))
    lead = lead_spec(STATE, width)
    earlier = [] if earlier is None else [earlier]
    return call(
        functools.partial(output_kernel, ahead, first),
        jax.ShapeDtypeStruct(values.shape, BF16),
        flops=groups * heads * SPAN * SPAN * 2000,
        moved=groups * SPAN * width * 10,
        exps=groups * heads * SPAN * SPAN,
        grid=(groups,),
        in_specs=[
            pl.BlockSpec(memory_space=pltpu.SMEM), wide,
            pl.BlockSpec((1, SPAN, heads), lambda g: (g + first, 0, 0)),
            pl.BlockSpec((1, heads, SPAN), lambda g: (g + first, 0, 0)),
            pl.BlockSpec((SPAN, 2 * STATE), lambda g: (0, g)),
        ]
        + [lead] * (1 + len(far))
        + [pl.BlockSpec(memory_space=pl.ANY)] * len(earlier),
        out_specs=wide,
        scratch_shapes=[pltpu.VMEM((STATE, width), BF16)],
        input_output_aliases={6 + len(far): 0} if earlier else {},
    )(skip, values, cum, cumt, proj, near, *far, *earlier)


def spot_of(block, spots):
    if spots == 1:
        return 0
    other_x = (lax.axis_index("head") != block % 2).astype(jnp.int32)
    other_core = (lax.axis_index("sub") != block // 2).astype(jnp.int32)
    return 2 * other_x + other_core


def update_kernel(blocks, spots, part, *refs):
    turned_refs, pieces = refs[:spots], refs[spots : spots + blocks]
    decayed_ref, keep_ref = refs[spots + blocks : spots + blocks + 2]
    weight_ref, sparse_ref, grad_ref, weight_out, sparse_out, sems = refs[-6:]
    tokens, width = pieces[0].shape
    rows = decayed_ref.shape[0]
    step = min(rows, 256)
    columns = slice(part * width, (part + 1) * width)
    for block, piece in enumerate(pieces):
        start = pl.multiple_of(spot_of(block, spots) * tokens, tokens)
        grad_ref[pl.ds(start, tokens), :] = piece[...]
    copies = []
    for number in range(rows // step):
        here = slice(number * step, (number + 1) * step)
        total = dot(turned_refs[0][here, :], grad_ref[:tokens, :])
        for spot in range(1, spots):
            total += dot(
                turned_refs[spot][here, :], grad_ref[spot * tokens : (spot + 1) * tokens, :]
            )
        weight = decayed_ref[here, columns] - (LEARN_RATE * WEIGHT_SCALE) * total
        weight_out[here, :] = weight
        sparse_out[here, :] = (weight * keep_ref[here, columns].astype(F32)).astype(BF16)
        for place, (source, target) in enumerate(
            ((weight_out, weight_ref), (sparse_out, sparse_ref))
        ):
            copies.append(
                pltpu.make_async_copy(
                    source.at[here, :], target.at[here, columns], sems.at[place, number]
                )
            )
            copies[-1].start()
    for copy in copies:
        copy.wait()


def update(turned_hidden, grad_blocks, decayed, keep, part, earlier, vmem):
    rows, columns = decayed.shape
    width = grad_blocks[0].shape[1]
    tokens = turned_hidden[0].shape[1]
    spots, blocks = len(turned_hidden), len(grad_blocks)
    earlier = earlier or ()
    whole, anywhere = pl.BlockSpec(memory_space=pltpu.VMEM), pl.BlockSpec(memory_space=pl.ANY)
    return call(
        functools.partial(update_kernel, blocks, spots, part),
        (jax.ShapeDtypeStruct((rows, columns), F32), jax.ShapeDtypeStruct((rows, columns), BF16)),
        flops=2 * spots * tokens * rows * width,
        moved=rows * width * 12 + spots * tokens * (rows + width) * 2,
        vmem=vmem,
        in_specs=[whole] * (spots + blocks + 2) + [anywhere] * len(earlier),
        out_specs=(anywhere, anywhere),
        scratch_shapes=[
            pltpu.VMEM((spots * tokens, width), BF16),
            pltpu.VMEM((rows, width), F32),
            pltpu.VMEM((rows, width), BF16),
            pltpu.SemaphoreType.DMA((2, rows // min(rows, 256))),
        ],
        input_output_aliases={spots + blocks + 2 + i: i for i in range(len(earlier))},
    )(*turned_hidden, *grad_blocks, decayed, keep, *earlier)


def held(after, *before):
    return lax.optimization_barrier((after, *before))[0]


def to_all(seq, distance):
    return [(source, (source + distance) % seq) for source in range(seq)]


def block_pairs(seq, near, same_core):
    return [
        (
            (z * 2 + x) * 2 + core,
            ((z + (x if near else 1 - x) + 2 * core) % seq * 2 + x) * 2
            + (core if same_core else 1 - core),
        )
        for z in range(seq)
        for x in range(2)
        for core in range(2)
    ]


def transpose_pairs(seq):
    stays, crosses, beside, onward = [], [], [], []
    for z in range(seq):
        for x in range(2):
            for core in range(2):
                layer = 2 * x + core
                distance = (z - layer) % seq
                source, step = ((z * 2 + way) * 2 + core for way in (x, 1 - x))
                target = (layer * 2 + distance % 2) * 2 + distance // 2
                if distance % 2 == x:
                    stays.append((source, target))
                else:
                    crosses.append((source, target))
                    beside.append((source, step))
                    onward.append((step, target))
    return stays, crosses, beside, onward


SWAP = [(0, 1), (1, 0)]


def chain(own, own_low, decay, seq, step):
    arrived = jnp.zeros_like(own_low)
    message = own_low
    first = 0 if step > 0 else seq - 1
    for hop in range(seq - 1):
        source = first + hop * step
        if hop:
            message = handed_on(decay, arrived, own, 0)
        arrived = arrived + lax.ppermute(message, "seq", [(source, source + step)])
    return arrived


def on_device_general(
    seq, hidden, inner_values, log_decay, skip_gain, cotangent, master, mask_now, mask_next
):
    groups = master.shape[1] // (2 * STATE)
    effective, decayed, keep = weights(master, mask_now, mask_next)
    features = lax.all_gather(hidden, ("head", "sub"), axis=1, tiled=True)
    layer = lax.all_to_all(features, "seq", split_axis=1, concat_axis=0, tiled=True)
    xd, yd, mix, mixt, cum, cumt, decay = before(
        inner_values, cotangent, log_decay.T, groups
    )
    part = dot(layer, effective).astype(BF16)
    terms = [lax.psum_scatter(part, "seq", scatter_dimension=0, tiled=True)]
    proj, state_low, state, adjoint = states(True, terms, xd, yd, 0, groups, decay.shape[2])
    start = chain(state, state_low, decay, seq, 1)
    adjoint_in = chain(adjoint, adjoint.astype(BF16), decay, seq, -1)
    grad = grads(True, proj, xd, yd, mix, mixt, start, [adjoint_in], 0)
    blocks = [lax.all_gather(grad, "seq", axis=0, tiled=True)]
    ssd_output = output(
        True, inner_values, cum, cumt, skip_gain, proj, start, [adjoint_in], 0, None
    )
    return ssd_output, *update([layer.T], blocks, decayed, keep, 0, None, 40 * MIB)


def on_device(
    seq, hidden, inner_values, log_decay, skip_gain, cotangent, master, mask_now, mask_next
):
    groups = master.shape[1] // (2 * STATE)
    axes = ("seq", "head", "sub")
    rows = hidden.shape[0] // 2
    stays, crosses, beside, onward = transpose_pairs(seq)
    relayed = lax.ppermute(hidden[rows:], axes, beside)
    top = lax.ppermute(hidden[:rows], axes, stays + crosses)
    low = [lax.ppermute(hidden[rows:], axes, stays), lax.ppermute(relayed, axes, onward)]
    effective, decayed, keep = weights(master, mask_now, mask_next)
    sibling_effective = effective_of(
        lax.ppermute(master, "sub", SWAP), lax.ppermute(mask_now, "sub", SWAP)
    )
    top = held(top, effective, sibling_effective)

    other = [lax.ppermute(top, "head", SWAP)]
    same, cross, low = partials([top, *low], effective, sibling_effective, True)
    other.append(lax.ppermute(low, "head", SWAP))
    terms = [
        lax.ppermute(same, axes, block_pairs(seq, True, True)),
        lax.ppermute(cross, axes, block_pairs(seq, True, False)),
    ]
    ready = partials(other[:1], effective, sibling_effective)
    same, cross = rest_of_partials(ready, other[1], effective, sibling_effective)
    terms += [
        lax.ppermute(same, axes, block_pairs(seq, False, True)),
        lax.ppermute(cross, axes, block_pairs(seq, False, False)),
    ]

    xd, yd, mix, mixt, cum, cumt, decay = before(
        held(inner_values, same), cotangent, log_decay.T, groups
    )

    each = groups // PARTS
    spans = range(PARTS)
    projs, messages, nears, fars = zip(
        *(
            states(None, terms, xd, yd, p * each, each, decay.shape[2])
            for p in spans
        )
    )
    turned_hidden = []
    for first, second in ((top, low), other):
        piece = turn([held(first, nears[0]), second])
        turned_hidden += [piece, lax.ppermute(piece, "sub", SWAP)]
    fars = [*fars[:-1], held(fars[-1], *turned_hidden)]
    arrived = [[] for _ in spans]
    hops = (([(0, 1), (3, 2)], nears), ([(1, 2), (2, 1)], fars), ([(1, 0), (2, 3)], None))
    messages = list(messages)
    for pairs, own_terms in hops:
        for p in spans:
            message = messages[p]
            if p and not arrived[p]:
                message = held(message, arrived[p - 1][-1])
            arrived[p].append(lax.ppermute(message, "seq", pairs))
        for p in spans:
            if own_terms:
                messages[p] = handed_on(decay, arrived[p][-1], own_terms[p], p * each)
    gradients, moved, ssd_output = [], [], None
    for p in spans:
        near, far = arrived[p][0], arrived[p][1:]
        proj = projs[p] if not p else held(projs[p], ssd_output)
        grad = grads(None, proj, xd, yd, mix, mixt, near, far, p * each)
        ssd_output = output(
            None, inner_values, held(cum, grad), cumt, skip_gain, projs[p], near, far, p * each,
            ssd_output,
        )
        blocks = [grad]
        for distance in range(1, seq):
            if not p and distance == seq - 1:
                grad = held(grad, ssd_output)
            blocks.append(lax.ppermute(grad, "seq", to_all(seq, seq - distance)))
        moved.append(blocks)
    decayed = held(decayed, ssd_output)
    updated = None
    for p in spans:
        updated = update(turned_hidden, moved[p], decayed, keep, p, updated, 16 * MIB)
    return ssd_output, *updated


PARTS = 2


def solution(mesh):
    by_position = P(("grp", "seq"), ("head", "sub"))
    by_row = P("seq", ("head", "sub"))
    seq, head, sub = (mesh.shape[name] for name in ("seq", "head", "sub"))
    body = on_device if (seq, head, sub) == (4, 2, 2) else on_device_general
    return jax.shard_map(
        functools.partial(body, seq),
        mesh=mesh,
        in_specs=(
            by_position, by_position, by_position, P(("head", "sub")), by_position,
            by_row, by_row, by_row,
        ),
        out_specs=(by_position, by_position, by_position),
        check_vma=False,
    )
```

```python
import functools
import math

import jax
import jax.numpy as jnp
from jax import lax
from jax.experimental import pallas as pl
from jax.experimental.pallas import tpu as pltpu
from jax.sharding import PartitionSpec as P

D = 4096
STATE = 128
SPAN = 256
LEARN_RATE = 0.05
WEIGHT_DECAY = 10.0
WEIGHT_SCALE = 2.0 / math.sqrt(D)
KEEP_BITS = (0b000111, 0b011001, 0b101010, 0b110100)
OUT_OF_SIGHT = -1e30
MIB = 1024 * 1024

F32 = jnp.float32
BF16 = jnp.bfloat16
NT = (((1,), (1,)), ((), ()))


def call(kernel, out_shape, flops, moved, exps=0, vmem=16 * MIB, **more):
    return pl.pallas_call(
        kernel,
        out_shape=out_shape,
        compiler_params=pltpu.CompilerParams(vmem_limit_bytes=vmem),
        cost_estimate=pl.CostEstimate(flops=flops, bytes_accessed=moved, transcendentals=exps),
        **more,
    )


def dot(a, b):
    return jnp.dot(a, b, preferred_element_type=F32)


def dot_nt(a, b):
    return lax.dot_general(a, b, NT, preferred_element_type=F32)


def turned(a):
    return a.astype(F32).T.astype(BF16)


def expanded(codes, rows):
    spread = (
        lax.broadcasted_iota(jnp.int32, (rows, rows // 4), 0) // 4
        == lax.broadcasted_iota(jnp.int32, (rows, rows // 4), 1)
    ).astype(F32)
    code = dot(spread.astype(BF16), codes.astype(F32).astype(BF16)).astype(jnp.int32)
    place = lax.broadcasted_iota(jnp.int32, (rows, 1), 0) % 4
    bits = jnp.where(
        place < 2,
        jnp.where(place == 0, KEEP_BITS[0], KEEP_BITS[1]),
        jnp.where(place == 2, KEEP_BITS[2], KEEP_BITS[3]),
    )
    return lax.shift_right_logical(jnp.broadcast_to(bits, code.shape), code) & 1


def weights_kernel(master_ref, now_ref, next_ref, effective_ref, decayed_ref, keep_ref):
    rows = master_ref.shape[0]
    master = master_ref[...]
    kept = expanded(now_ref[...], rows) == 1
    effective_ref[...] = jnp.where(kept, master * WEIGHT_SCALE, 0.0).astype(BF16)
    decayed_ref[...] = jnp.where(kept, master, master * (1.0 - LEARN_RATE * WEIGHT_DECAY))
    keep_ref[...] = expanded(next_ref[...], rows).astype(F32).astype(BF16)


def weights(master, mask_now, mask_next):
    rows, columns = master.shape
    block = min(rows, 256)
    full = pl.BlockSpec((block, columns), lambda i: (i, 0))
    quarter = pl.BlockSpec((block // 4, columns), lambda i: (i, 0))
    return call(
        weights_kernel,
        (
            jax.ShapeDtypeStruct((rows, columns), BF16),
            jax.ShapeDtypeStruct((rows, columns), F32),
            jax.ShapeDtypeStruct((rows, columns), BF16),
        ),
        flops=rows * columns * 3000,
        moved=rows * columns * 14,
        grid=(rows // block,),
        in_specs=[full, quarter, quarter],
        out_specs=(full, full, full),
    )(master, mask_now, mask_next)


def effective_kernel(master_ref, now_ref, effective_ref):
    kept = expanded(now_ref[...], master_ref.shape[0]) == 1
    effective_ref[...] = jnp.where(kept, master_ref[...] * WEIGHT_SCALE, 0.0).astype(BF16)


def effective_of(master, mask_now):
    rows, columns = master.shape
    block = min(rows, 256)
    full = pl.BlockSpec((block, columns), lambda i: (i, 0))
    return call(
        effective_kernel,
        jax.ShapeDtypeStruct((rows, columns), BF16),
        flops=rows * columns * 3000,
        moved=rows * columns * 7,
        grid=(rows // block,),
        in_specs=[full, pl.BlockSpec((block // 4, columns), lambda i: (i, 0))],
        out_specs=full,
    )(master, mask_now)


def lanes_of(left, right, wide):
    lane = lax.broadcasted_iota(jnp.int32, (left.shape[0], wide), 1)
    return jnp.where(lane < wide // 2, left, right)


def decays_of(col, row):
    half = SPAN // 2
    causal = lax.broadcasted_iota(jnp.int32, (half, half), 0) >= lax.broadcasted_iota(
        jnp.int32, (half, half), 1
    )
    top = jnp.exp(jnp.where(causal, col[:half] - row[:, :half], OUT_OF_SIGHT))
    low = jnp.exp(col[half:] - row[:, :half])
    end = jnp.exp(jnp.where(causal, col[half:] - row[:, half:], OUT_OF_SIGHT))
    return top, low, end


def before_kernel(
    x_ref, dy_ref, logt_ref,
    xd_ref, yd_ref, mix_ref, mixt_ref, cum_ref, cumt_ref, end_ref, tall_ref,
):
    heads = cum_ref.shape[2]
    half = SPAN // 2
    wide = x_ref.shape[1] // heads * 2
    row = lax.broadcasted_iota(jnp.int32, (SPAN, SPAN), 0)
    col = lax.broadcasted_iota(jnp.int32, (SPAN, SPAN), 1)
    first = pl.multiple_of(pl.program_id(0) * heads, heads)
    cumt = jnp.dot(
        logt_ref[pl.ds(first, heads), :], (row <= col).astype(F32),
        precision=lax.Precision.HIGHEST, preferred_element_type=F32,
    )
    tall_ref[...] = jnp.zeros_like(tall_ref)
    tall_ref[:heads, :] = cumt
    cum = tall_ref[...].T[:, :heads]
    cum_ref[0] = cum
    cumt_ref[0] = cumt
    end = cum[SPAN - 1 :, :]
    from_start = jnp.exp(cum)
    to_end = jnp.exp(end - cum)
    whole = jnp.exp(end)
    mix = [jnp.zeros((half, half), F32) for _ in range(3)]
    lane = lax.broadcasted_iota(jnp.int32, (SPAN, wide), 1)
    for pair in range(heads // 2):
        a, b = 2 * pair, 2 * pair + 1
        cut = slice(pair * wide, (pair + 1) * wide)
        x = x_ref[:, cut]
        dy = dy_ref[:, cut]
        wide_dy = dy.astype(F32)
        xd_ref[:, cut] = (
            x.astype(F32) * lanes_of(to_end[:, a : a + 1], to_end[:, b : b + 1], wide)
        ).astype(BF16)
        yd_ref[:, cut] = (
            wide_dy * lanes_of(from_start[:, a : a + 1], from_start[:, b : b + 1], wide)
        ).astype(BF16)
        end_ref[0, :, cut] = lanes_of(whole[:, a : a + 1], whole[:, b : b + 1], wide)
        for head, mine in ((a, lane < wide // 2), (b, lane >= wide // 2)):
            one = jnp.where(mine, wide_dy, 0.0).astype(BF16)
            decays = decays_of(cum[:, head : head + 1], cumt[head : head + 1, :])
            mix[0] += dot_nt(one[:half], x[:half]) * decays[0]
            both = dot_nt(one[half:], x)
            mix[1] += both[:, :half] * decays[1]
            mix[2] += both[:, half:] * decays[2]
    nothing = jnp.zeros((half, half), BF16)
    top, low, end_mix = (m.astype(BF16) for m in mix)
    topt, lowt, end_mixt = (m.T.astype(BF16) for m in mix)
    mix_ref[0, :half, :half] = top
    mix_ref[0, :half, half:] = nothing
    mix_ref[0, half:, :half] = low
    mix_ref[0, half:, half:] = end_mix
    mixt_ref[0, :half, :half] = topt
    mixt_ref[0, :half, half:] = lowt
    mixt_ref[0, half:, :half] = nothing
    mixt_ref[0, half:, half:] = end_mixt


def wide_spec(width):
    return pl.BlockSpec((SPAN, width), lambda g: (0, g))


def lead_spec(*shape):
    return pl.BlockSpec((1, *shape), lambda g: (g, *(0 for _ in shape)))


def before(values, cotan, logs_t, groups):
    heads = logs_t.shape[0] // groups
    width = values.shape[1] // groups
    wide = wide_spec(width)
    return call(
        before_kernel,
        (
            jax.ShapeDtypeStruct(values.shape, BF16),
            jax.ShapeDtypeStruct(values.shape, BF16),
            jax.ShapeDtypeStruct((groups, SPAN, SPAN), BF16),
            jax.ShapeDtypeStruct((groups, SPAN, SPAN), BF16),
            jax.ShapeDtypeStruct((groups, SPAN, heads), F32),
            jax.ShapeDtypeStruct((groups, heads, SPAN), F32),
            jax.ShapeDtypeStruct((groups, 1, width), F32),
        ),
        flops=groups * heads * SPAN * SPAN * 2500,
        moved=values.size * 8,
        exps=groups * heads * SPAN * SPAN,
        grid=(groups,),
        in_specs=[wide, wide, pl.BlockSpec(logs_t.shape, lambda g: (0, 0))],
        out_specs=(
            wide, wide, lead_spec(SPAN, SPAN), lead_spec(SPAN, SPAN),
            lead_spec(SPAN, heads), lead_spec(heads, SPAN), lead_spec(1, width),
        ),
        scratch_shapes=[pltpu.VMEM((STATE, SPAN), F32)],
    )(values, cotan, logs_t)


def partial_kernel(spread, *refs):
    given = refs[:-1] if spread else refs
    (*pieces, weight_ref, sibling_weight_ref, out_ref, sibling_out_ref) = given
    pieces = [piece[...] for piece in pieces]
    if spread:
        refs[-1][...] = pieces[-2] + pieces[-1]
        pieces[-2:] = [refs[-1][...]]
    start = 0
    for piece in pieces:
        rows = slice(start, start + piece.shape[0])
        start += piece.shape[0]
        out_ref[rows, :] = dot(piece, weight_ref[...]).astype(BF16)
        sibling_out_ref[rows, :] = dot(piece, sibling_weight_ref[...]).astype(BF16)


def partials(pieces, effective, sibling_effective, spread=False):
    rows = sum(piece.shape[0] for piece in pieces[: -1 if spread else None])
    columns = effective.shape[1]
    whole = pl.BlockSpec(memory_space=pltpu.VMEM)
    shapes = [jax.ShapeDtypeStruct((rows, columns), BF16)] * 2
    if spread:
        shapes.append(jax.ShapeDtypeStruct(pieces[-1].shape, BF16))
    return call(
        functools.partial(partial_kernel, spread),
        tuple(shapes),
        flops=4 * rows * effective.size,
        moved=(rows * effective.shape[0] + 2 * effective.size + 2 * rows * columns) * 2,
        in_specs=[whole] * (len(pieces) + 2),
        out_specs=(whole,) * len(shapes),
    )(*pieces, effective, sibling_effective)


def rest_kernel(
    ready_ref, sibling_ready_ref, piece_ref, weight_ref, sibling_weight_ref, out_ref, sibling_out_ref
):
    rows = ready_ref.shape[0]
    out_ref[:rows, :] = ready_ref[...]
    sibling_out_ref[:rows, :] = sibling_ready_ref[...]
    out_ref[rows:, :] = dot(piece_ref[...], weight_ref[...]).astype(BF16)
    sibling_out_ref[rows:, :] = dot(piece_ref[...], sibling_weight_ref[...]).astype(BF16)


def rest_of_partials(ready, piece, effective, sibling_effective):
    rows, columns = ready[0].shape[0] + piece.shape[0], effective.shape[1]
    whole = pl.BlockSpec(memory_space=pltpu.VMEM)
    return call(
        rest_kernel,
        (jax.ShapeDtypeStruct((rows, columns), BF16),) * 2,
        flops=4 * piece.shape[0] * effective.size,
        moved=(piece.size + 2 * effective.size + 2 * rows * columns) * 2,
        in_specs=[whole] * 5,
        out_specs=(whole,) * 2,
    )(*ready, piece, effective, sibling_effective)


def turn_kernel(*refs):
    (*pieces, out_ref) = refs
    start = 0
    for piece in pieces:
        out_ref[:, start : start + piece.shape[0]] = turned(piece[...])
        start += piece.shape[0]


def turn(pieces):
    rows, features = sum(piece.shape[0] for piece in pieces), pieces[0].shape[1]
    whole = pl.BlockSpec(memory_space=pltpu.VMEM)
    return call(
        turn_kernel,
        jax.ShapeDtypeStruct((features, rows), BF16),
        flops=rows * features * 2000,
        moved=rows * features * 4,
        in_specs=[whole] * len(pieces),
        out_specs=whole,
    )(*pieces)


def either(ahead, first, second, body):
    if ahead:
        return body(first, second)
    lower = lax.axis_index("seq") < lax.axis_size("seq") // 2

    @pl.when(lower)
    def _():
        body(first, second)

    @pl.when(jnp.logical_not(lower))
    def _():
        body(second, first)


def states_kernel(both, *refs):
    (*terms, xd_ref, yd_ref, proj_ref, near_low_ref, near_ref, far_ref) = refs
    total = terms[0][...].astype(F32)
    for term in terms[1:]:
        total += term[...].astype(F32)
    low = total.astype(BF16)
    proj_ref[...] = low
    state = dot(turned(low[:, :STATE]), xd_ref[...])
    adjoint = dot(turned(low[:, STATE:]), yd_ref[...])

    def put(near, far):
        near_low_ref[0] = near.astype(BF16)
        near_ref[0] = near
        far_ref[0] = far

    either(both, state, adjoint, put)


def states(ahead, terms, xd, yd, first, groups, width):
    pair = pl.BlockSpec((SPAN, 2 * STATE), lambda g: (0, g))
    pair_from = pl.BlockSpec((SPAN, 2 * STATE), lambda g: (0, g + first))
    wide = pl.BlockSpec((SPAN, width), lambda g: (0, g + first))
    lead = lead_spec(STATE, width)
    shape = (groups, STATE, width)
    return call(
        functools.partial(states_kernel, ahead),
        (
            jax.ShapeDtypeStruct((SPAN, groups * 2 * STATE), BF16),
            jax.ShapeDtypeStruct(shape, BF16),
            jax.ShapeDtypeStruct(shape, F32),
            jax.ShapeDtypeStruct(shape, F32),
        ),
        flops=4 * SPAN * groups * width * STATE,
        moved=groups * SPAN * (width * 4 + 4 * STATE * 5),
        grid=(groups,),
        in_specs=[pair_from] * len(terms) + [wide, wide],
        out_specs=(pair, lead, lead, lead),
    )(*terms, xd, yd)


def added(refs):
    total = refs[0][0]
    for ref in refs[1:]:
        total += ref[0]
    return total


def message_kernel(decay_ref, arrived_ref, own_ref, out_ref):
    out_ref[0] = (decay_ref[0] * arrived_ref[0].astype(F32) + own_ref[0]).astype(BF16)


def handed_on(decay, arrived, own, first):
    groups, _, width = arrived.shape
    lead = lead_spec(STATE, width)
    return call(
        message_kernel,
        jax.ShapeDtypeStruct(arrived.shape, BF16),
        flops=2 * arrived.size,
        moved=8 * arrived.size,
        grid=(groups,),
        in_specs=[pl.BlockSpec((1, 1, width), lambda g: (g + first, 0, 0)), lead, lead],
        out_specs=lead,
    )(decay, arrived, own)


def grads_kernel(ahead, proj_ref, xd_ref, yd_ref, mix_ref, mixt_ref, near_ref, *refs):
    (*far_refs, out_ref) = refs

    def body(start, adjoint):
        write, read = proj_ref[:, :STATE], proj_ref[:, STATE:]
        grad_write = dot(mixt_ref[0], read) + dot_nt(xd_ref[...], added(adjoint))
        grad_read = dot(mix_ref[0], write) + dot_nt(yd_ref[...], added(start))
        out_ref[:, :STATE] = grad_write.astype(BF16)
        out_ref[:, STATE:] = grad_read.astype(BF16)

    either(ahead, [near_ref], far_refs, body)


def grads(ahead, proj, xd, yd, mix, mixt, near, far, first):
    groups, _, width = near.shape
    pair = pl.BlockSpec((SPAN, 2 * STATE), lambda g: (0, g))
    wide = pl.BlockSpec((SPAN, width), lambda g: (0, g + first))
    square = pl.BlockSpec((1, SPAN, SPAN), lambda g: (g + first, 0, 0))
    return call(
        functools.partial(grads_kernel, ahead),
        jax.ShapeDtypeStruct(proj.shape, BF16),
        flops=4 * SPAN * groups * (width + SPAN) * STATE,
        moved=groups * SPAN * width * 8,
        grid=(groups,),
        in_specs=[pair, wide, wide, square, square]
        + [lead_spec(STATE, width)] * (1 + len(far)),
        out_specs=pair,
    )(proj, xd, yd, mix, mixt, near, *far)


def output_kernel(
    ahead, first, skip_ref, x_ref, cum_ref, cumt_ref, proj_ref, near_ref, *refs
):
    (*far_refs, out_ref, start_ref) = refs
    far_refs = [ref for ref in far_refs if ref.shape[1:] == near_ref.shape[1:]]

    def put(start, _):
        start_ref[...] = added(start)

    either(ahead, [near_ref], far_refs, put)

    heads = cum_ref.shape[2]
    half = SPAN // 2
    wide = x_ref.shape[1] // heads * 2
    write = proj_ref[:, :STATE]
    read = proj_ref[:, STATE:]
    cum = cum_ref[0]
    cumt = cumt_ref[0]
    from_start = jnp.exp(cum)
    scores = dot_nt(read, write)
    top, low, end = scores[:half, :half], scores[half:, :half], scores[half:, half:]
    lane = lax.broadcasted_iota(jnp.int32, (half, wide), 1)
    for pair in range(heads // 2):
        a, b = 2 * pair, 2 * pair + 1
        cut = slice(pair * wide, (pair + 1) * wide)
        x = x_ref[:, cut]
        upper, lower = [], []
        for head in (a, b):
            decays = decays_of(cum[:, head : head + 1], cumt[head : head + 1, :])
            upper.append(dot((top * decays[0]).astype(BF16), x[:half]))
            lower.append(
                dot((low * decays[1]).astype(BF16), x[:half])
                + dot((end * decays[2]).astype(BF16), x[half:])
            )
        carried = dot(read, start_ref[:, cut]) * lanes_of(
            from_start[:, a : a + 1], from_start[:, b : b + 1], wide
        )
        head = (pl.program_id(0) + first) * heads + a
        gain = jnp.where(
            lax.broadcasted_iota(jnp.int32, (1, wide), 1) < wide // 2,
            skip_ref[head], skip_ref[head + 1],
        )
        rest = carried + gain * x.astype(F32)
        out_ref[:half, cut] = (
            jnp.where(lane < wide // 2, upper[0], upper[1]) + rest[:half]
        ).astype(BF16)
        out_ref[half:, cut] = (
            jnp.where(lane < wide // 2, lower[0], lower[1]) + rest[half:]
        ).astype(BF16)


def output(ahead, values, cum, cumt, skip, proj, near, far, first, earlier):
    groups, _, width = near.shape
    heads = cum.shape[2]
    wide = pl.BlockSpec((SPAN, width), lambda g: (0, g + first))
    lead = lead_spec(STATE, width)
    earlier = [] if earlier is None else [earlier]
    return call(
        functools.partial(output_kernel, ahead, first),
        jax.ShapeDtypeStruct(values.shape, BF16),
        flops=groups * heads * SPAN * SPAN * 2000,
        moved=groups * SPAN * width * 10,
        exps=groups * heads * SPAN * SPAN,
        grid=(groups,),
        in_specs=[
            pl.BlockSpec(memory_space=pltpu.SMEM), wide,
            pl.BlockSpec((1, SPAN, heads), lambda g: (g + first, 0, 0)),
            pl.BlockSpec((1, heads, SPAN), lambda g: (g + first, 0, 0)),
            pl.BlockSpec((SPAN, 2 * STATE), lambda g: (0, g)),
        ]
        + [lead] * (1 + len(far))
        + [pl.BlockSpec(memory_space=pl.ANY)] * len(earlier),
        out_specs=wide,
        scratch_shapes=[pltpu.VMEM((STATE, width), BF16)],
        input_output_aliases={6 + len(far): 0} if earlier else {},
    )(skip, values, cum, cumt, proj, near, *far, *earlier)


def spot_of(block, spots):
    if spots == 1:
        return 0
    other_x = (lax.axis_index("head") != block % 2).astype(jnp.int32)
    other_core = (lax.axis_index("sub") != block // 2).astype(jnp.int32)
    return 2 * other_x + other_core


def update_kernel(blocks, spots, part, *refs):
    turned_refs, pieces = refs[:spots], refs[spots : spots + blocks]
    decayed_ref, keep_ref = refs[spots + blocks : spots + blocks + 2]
    weight_ref, sparse_ref, grad_ref, weight_out, sparse_out, sems = refs[-6:]
    tokens, width = pieces[0].shape
    rows = decayed_ref.shape[0]
    step = min(rows, 256)
    columns = slice(part * width, (part + 1) * width)
    for block, piece in enumerate(pieces):
        start = pl.multiple_of(spot_of(block, spots) * tokens, tokens)
        grad_ref[pl.ds(start, tokens), :] = piece[...]
    copies = []
    for number in range(rows // step):
        here = slice(number * step, (number + 1) * step)
        total = dot(turned_refs[0][here, :], grad_ref[:tokens, :])
        for spot in range(1, spots):
            total += dot(
                turned_refs[spot][here, :], grad_ref[spot * tokens : (spot + 1) * tokens, :]
            )
        weight = decayed_ref[here, columns] - (LEARN_RATE * WEIGHT_SCALE) * total
        weight_out[here, :] = weight
        sparse_out[here, :] = (weight * keep_ref[here, columns].astype(F32)).astype(BF16)
        for place, (source, target) in enumerate(
            ((weight_out, weight_ref), (sparse_out, sparse_ref))
        ):
            copies.append(
                pltpu.make_async_copy(
                    source.at[here, :], target.at[here, columns], sems.at[place, number]
                )
            )
            copies[-1].start()
    for copy in copies:
        copy.wait()


def update(turned_hidden, grad_blocks, decayed, keep, part, earlier, vmem):
    rows, columns = decayed.shape
    width = grad_blocks[0].shape[1]
    tokens = turned_hidden[0].shape[1]
    spots, blocks = len(turned_hidden), len(grad_blocks)
    earlier = earlier or ()
    whole, anywhere = pl.BlockSpec(memory_space=pltpu.VMEM), pl.BlockSpec(memory_space=pl.ANY)
    return call(
        functools.partial(update_kernel, blocks, spots, part),
        (jax.ShapeDtypeStruct((rows, columns), F32), jax.ShapeDtypeStruct((rows, columns), BF16)),
        flops=2 * spots * tokens * rows * width,
        moved=rows * width * 12 + spots * tokens * (rows + width) * 2,
        vmem=vmem,
        in_specs=[whole] * (spots + blocks + 2) + [anywhere] * len(earlier),
        out_specs=(anywhere, anywhere),
        scratch_shapes=[
            pltpu.VMEM((spots * tokens, width), BF16),
            pltpu.VMEM((rows, width), F32),
            pltpu.VMEM((rows, width), BF16),
            pltpu.SemaphoreType.DMA((2, rows // min(rows, 256))),
        ],
        input_output_aliases={spots + blocks + 2 + i: i for i in range(len(earlier))},
    )(*turned_hidden, *grad_blocks, decayed, keep, *earlier)


def held(after, *before):
    return lax.optimization_barrier((after, *before))[0]


def to_all(seq, distance):
    return [(source, (source + distance) % seq) for source in range(seq)]


def block_pairs(seq, near, same_core):
    return [
        (
            (z * 2 + x) * 2 + core,
            ((z + (x if near else 1 - x) + 2 * core) % seq * 2 + x) * 2
            + (core if same_core else 1 - core),
        )
        for z in range(seq)
        for x in range(2)
        for core in range(2)
    ]


def transpose_pairs(seq):
    stays, crosses, beside, onward = [], [], [], []
    for z in range(seq):
        for x in range(2):
            for core in range(2):
                layer = 2 * x + core
                distance = (z - layer) % seq
                source, step = ((z * 2 + way) * 2 + core for way in (x, 1 - x))
                target = (layer * 2 + distance % 2) * 2 + distance // 2
                if distance % 2 == x:
                    stays.append((source, target))
                else:
                    crosses.append((source, target))
                    beside.append((source, step))
                    onward.append((step, target))
    return stays, crosses, beside, onward


SWAP = [(0, 1), (1, 0)]


def chain(own, own_low, decay, seq, step):
    arrived = jnp.zeros_like(own_low)
    message = own_low
    first = 0 if step > 0 else seq - 1
    for hop in range(seq - 1):
        source = first + hop * step
        if hop:
            message = handed_on(decay, arrived, own, 0)
        arrived = arrived + lax.ppermute(message, "seq", [(source, source + step)])
    return arrived


def on_device_general(
    seq, hidden, inner_values, log_decay, skip_gain, cotangent, master, mask_now, mask_next
):
    groups = master.shape[1] // (2 * STATE)
    effective, decayed, keep = weights(master, mask_now, mask_next)
    features = lax.all_gather(hidden, ("head", "sub"), axis=1, tiled=True)
    layer = lax.all_to_all(features, "seq", split_axis=1, concat_axis=0, tiled=True)
    xd, yd, mix, mixt, cum, cumt, decay = before(
        inner_values, cotangent, log_decay.T, groups
    )
    part = dot(layer, effective).astype(BF16)
    terms = [lax.psum_scatter(part, "seq", scatter_dimension=0, tiled=True)]
    proj, state_low, state, adjoint = states(True, terms, xd, yd, 0, groups, decay.shape[2])
    start = chain(state, state_low, decay, seq, 1)
    adjoint_in = chain(adjoint, adjoint.astype(BF16), decay, seq, -1)
    grad = grads(True, proj, xd, yd, mix, mixt, start, [adjoint_in], 0)
    blocks = [lax.all_gather(grad, "seq", axis=0, tiled=True)]
    ssd_output = output(
        True, inner_values, cum, cumt, skip_gain, proj, start, [adjoint_in], 0, None
    )
    return ssd_output, *update([layer.T], blocks, decayed, keep, 0, None, 40 * MIB)


def on_device(
    seq, hidden, inner_values, log_decay, skip_gain, cotangent, master, mask_now, mask_next
):
    groups = master.shape[1] // (2 * STATE)
    axes = ("seq", "head", "sub")
    rows = hidden.shape[0] // 2
    stays, crosses, beside, onward = transpose_pairs(seq)
    relayed = lax.ppermute(hidden[rows:], axes, beside)
    top = lax.ppermute(hidden[:rows], axes, stays + crosses)
    low = [lax.ppermute(hidden[rows:], axes, stays), lax.ppermute(relayed, axes, onward)]
    effective, decayed, keep = weights(master, mask_now, mask_next)
    sibling_effective = effective_of(
        lax.ppermute(master, "sub", SWAP), lax.ppermute(mask_now, "sub", SWAP)
    )
    top = held(top, effective, sibling_effective)

    other = [lax.ppermute(top, "head", SWAP)]
    same, cross, low = partials([top, *low], effective, sibling_effective, True)
    other.append(lax.ppermute(low, "head", SWAP))
    terms = [
        lax.ppermute(same, axes, block_pairs(seq, True, True)),
        lax.ppermute(cross, axes, block_pairs(seq, True, False)),
    ]
    ready = partials(other[:1], effective, sibling_effective)
    same, cross = rest_of_partials(ready, other[1], effective, sibling_effective)
    terms += [
        lax.ppermute(same, axes, block_pairs(seq, False, True)),
        lax.ppermute(cross, axes, block_pairs(seq, False, False)),
    ]

    xd, yd, mix, mixt, cum, cumt, decay = before(
        held(inner_values, same), cotangent, log_decay.T, groups
    )

    each = groups // PARTS
    spans = range(PARTS)
    projs, messages, nears, fars = zip(
        *(
            states(None, terms, xd, yd, p * each, each, decay.shape[2])
            for p in spans
        )
    )
    turned_hidden = []
    for first, second in ((top, low), other):
        piece = turn([held(first, nears[0]), second])
        turned_hidden += [piece, lax.ppermute(piece, "sub", SWAP)]
    fars = [*fars[:-1], held(fars[-1], *turned_hidden)]
    arrived = [[] for _ in spans]
    hops = (([(0, 1), (3, 2)], nears), ([(1, 2), (2, 1)], fars), ([(1, 0), (2, 3)], None))
    messages = list(messages)
    for pairs, own_terms in hops:
        for p in spans:
            message = messages[p]
            if p and not arrived[p]:
                message = held(message, arrived[p - 1][-1])
            arrived[p].append(lax.ppermute(message, "seq", pairs))
        for p in spans:
            if own_terms:
                messages[p] = handed_on(decay, arrived[p][-1], own_terms[p], p * each)
    gradients, moved, ssd_output = [], [], None
    for p in spans:
        near, far = arrived[p][0], arrived[p][1:]
        proj = projs[p] if not p else held(projs[p], ssd_output)
        grad = grads(None, proj, xd, yd, mix, mixt, near, far, p * each)
        ssd_output = output(
            None, inner_values, held(cum, grad), cumt, skip_gain, projs[p], near, far, p * each,
            ssd_output,
        )
        blocks = [grad]
        for distance in range(1, seq):
            payload = grad
            if not p and distance != seq // 2:
                payload = held(grad, ssd_output)
            blocks.append(lax.ppermute(payload, "seq", to_all(seq, seq - distance)))
        moved.append(blocks)
    decayed = held(decayed, ssd_output)
    updated = None
    for p in spans:
        updated = update(turned_hidden, moved[p], decayed, keep, p, updated, 16 * MIB)
    return ssd_output, *updated


PARTS = 2


def solution(mesh):
    by_position = P(("grp", "seq"), ("head", "sub"))
    by_row = P("seq", ("head", "sub"))
    seq, head, sub = (mesh.shape[name] for name in ("seq", "head", "sub"))
    body = on_device if (seq, head, sub) == (4, 2, 2) else on_device_general
    return jax.shard_map(
        functools.partial(body, seq),
        mesh=mesh,
        in_specs=(
            by_position, by_position, by_position, P(("head", "sub")), by_position,
            by_row, by_row, by_row,
        ),
        out_specs=(by_position, by_position, by_position),
        check_vma=False,
    )
```

```python
import functools
import math

import jax
import jax.numpy as jnp
from jax import lax
from jax.experimental import pallas as pl
from jax.experimental.pallas import tpu as pltpu
from jax.sharding import PartitionSpec as P

D = 4096
STATE = 128
SPAN = 256
LEARN_RATE = 0.05
WEIGHT_DECAY = 10.0
WEIGHT_SCALE = 2.0 / math.sqrt(D)
KEEP_BITS = (0b000111, 0b011001, 0b101010, 0b110100)
OUT_OF_SIGHT = -1e30
MIB = 1024 * 1024

F32 = jnp.float32
BF16 = jnp.bfloat16
NT = (((1,), (1,)), ((), ()))


def call(kernel, out_shape, flops, moved, exps=0, vmem=16 * MIB, **more):
    return pl.pallas_call(
        kernel,
        out_shape=out_shape,
        compiler_params=pltpu.CompilerParams(vmem_limit_bytes=vmem),
        cost_estimate=pl.CostEstimate(flops=flops, bytes_accessed=moved, transcendentals=exps),
        **more,
    )


def dot(a, b):
    return jnp.dot(a, b, preferred_element_type=F32)


def dot_nt(a, b):
    return lax.dot_general(a, b, NT, preferred_element_type=F32)


def turned(a):
    return a.astype(F32).T.astype(BF16)


def expanded(codes, rows):
    spread = (
        lax.broadcasted_iota(jnp.int32, (rows, rows // 4), 0) // 4
        == lax.broadcasted_iota(jnp.int32, (rows, rows // 4), 1)
    ).astype(F32)
    code = dot(spread.astype(BF16), codes.astype(F32).astype(BF16)).astype(jnp.int32)
    place = lax.broadcasted_iota(jnp.int32, (rows, 1), 0) % 4
    bits = jnp.where(
        place < 2,
        jnp.where(place == 0, KEEP_BITS[0], KEEP_BITS[1]),
        jnp.where(place == 2, KEEP_BITS[2], KEEP_BITS[3]),
    )
    return lax.shift_right_logical(jnp.broadcast_to(bits, code.shape), code) & 1


def weights_kernel(master_ref, now_ref, next_ref, effective_ref, decayed_ref, keep_ref):
    rows = master_ref.shape[0]
    master = master_ref[...]
    kept = expanded(now_ref[...], rows) == 1
    effective_ref[...] = jnp.where(kept, master * WEIGHT_SCALE, 0.0).astype(BF16)
    decayed_ref[...] = jnp.where(kept, master, master * (1.0 - LEARN_RATE * WEIGHT_DECAY))
    keep_ref[...] = expanded(next_ref[...], rows).astype(F32).astype(BF16)


def weights(master, mask_now, mask_next):
    rows, columns = master.shape
    block = min(rows, 256)
    full = pl.BlockSpec((block, columns), lambda i: (i, 0))
    quarter = pl.BlockSpec((block // 4, columns), lambda i: (i, 0))
    return call(
        weights_kernel,
        (
            jax.ShapeDtypeStruct((rows, columns), BF16),
            jax.ShapeDtypeStruct((rows, columns), F32),
            jax.ShapeDtypeStruct((rows, columns), BF16),
        ),
        flops=rows * columns * 3000,
        moved=rows * columns * 14,
        grid=(rows // block,),
        in_specs=[full, quarter, quarter],
        out_specs=(full, full, full),
    )(master, mask_now, mask_next)


def effective_kernel(master_ref, now_ref, effective_ref):
    kept = expanded(now_ref[...], master_ref.shape[0]) == 1
    effective_ref[...] = jnp.where(kept, master_ref[...] * WEIGHT_SCALE, 0.0).astype(BF16)


def effective_of(master, mask_now):
    rows, columns = master.shape
    block = min(rows, 256)
    full = pl.BlockSpec((block, columns), lambda i: (i, 0))
    return call(
        effective_kernel,
        jax.ShapeDtypeStruct((rows, columns), BF16),
        flops=rows * columns * 3000,
        moved=rows * columns * 7,
        grid=(rows // block,),
        in_specs=[full, pl.BlockSpec((block // 4, columns), lambda i: (i, 0))],
        out_specs=full,
    )(master, mask_now)


def lanes_of(left, right, wide):
    lane = lax.broadcasted_iota(jnp.int32, (left.shape[0], wide), 1)
    return jnp.where(lane < wide // 2, left, right)


def decays_of(col, row):
    half = SPAN // 2
    causal = lax.broadcasted_iota(jnp.int32, (half, half), 0) >= lax.broadcasted_iota(
        jnp.int32, (half, half), 1
    )
    top = jnp.exp(jnp.where(causal, col[:half] - row[:, :half], OUT_OF_SIGHT))
    low = jnp.exp(col[half:] - row[:, :half])
    end = jnp.exp(jnp.where(causal, col[half:] - row[:, half:], OUT_OF_SIGHT))
    return top, low, end


def before_kernel(
    x_ref, dy_ref, logt_ref,
    xd_ref, yd_ref, mix_ref, mixt_ref, cum_ref, cumt_ref, end_ref, tall_ref,
):
    heads = cum_ref.shape[2]
    half = SPAN // 2
    wide = x_ref.shape[1] // heads * 2
    row = lax.broadcasted_iota(jnp.int32, (SPAN, SPAN), 0)
    col = lax.broadcasted_iota(jnp.int32, (SPAN, SPAN), 1)
    first = pl.multiple_of(pl.program_id(0) * heads, heads)
    cumt = jnp.dot(
        logt_ref[pl.ds(first, heads), :], (row <= col).astype(F32),
        precision=lax.Precision.HIGHEST, preferred_element_type=F32,
    )
    tall_ref[...] = jnp.zeros_like(tall_ref)
    tall_ref[:heads, :] = cumt
    cum = tall_ref[...].T[:, :heads]
    cum_ref[0] = cum
    cumt_ref[0] = cumt
    end = cum[SPAN - 1 :, :]
    from_start = jnp.exp(cum)
    to_end = jnp.exp(end - cum)
    whole = jnp.exp(end)
    mix = [jnp.zeros((half, half), F32) for _ in range(3)]
    lane = lax.broadcasted_iota(jnp.int32, (SPAN, wide), 1)
    for pair in range(heads // 2):
        a, b = 2 * pair, 2 * pair + 1
        cut = slice(pair * wide, (pair + 1) * wide)
        x = x_ref[:, cut]
        dy = dy_ref[:, cut]
        wide_dy = dy.astype(F32)
        xd_ref[:, cut] = (
            x.astype(F32) * lanes_of(to_end[:, a : a + 1], to_end[:, b : b + 1], wide)
        ).astype(BF16)
        yd_ref[:, cut] = (
            wide_dy * lanes_of(from_start[:, a : a + 1], from_start[:, b : b + 1], wide)
        ).astype(BF16)
        end_ref[0, :, cut] = lanes_of(whole[:, a : a + 1], whole[:, b : b + 1], wide)
        for head, mine in ((a, lane < wide // 2), (b, lane >= wide // 2)):
            one = jnp.where(mine, wide_dy, 0.0).astype(BF16)
            decays = decays_of(cum[:, head : head + 1], cumt[head : head + 1, :])
            mix[0] += dot_nt(one[:half], x[:half]) * decays[0]
            both = dot_nt(one[half:], x)
            mix[1] += both[:, :half] * decays[1]
            mix[2] += both[:, half:] * decays[2]
    nothing = jnp.zeros((half, half), BF16)
    top, low, end_mix = (m.astype(BF16) for m in mix)
    topt, lowt, end_mixt = (m.T.astype(BF16) for m in mix)
    mix_ref[0, :half, :half] = top
    mix_ref[0, :half, half:] = nothing
    mix_ref[0, half:, :half] = low
    mix_ref[0, half:, half:] = end_mix
    mixt_ref[0, :half, :half] = topt
    mixt_ref[0, :half, half:] = lowt
    mixt_ref[0, half:, :half] = nothing
    mixt_ref[0, half:, half:] = end_mixt


def wide_spec(width):
    return pl.BlockSpec((SPAN, width), lambda g: (0, g))


def lead_spec(*shape):
    return pl.BlockSpec((1, *shape), lambda g: (g, *(0 for _ in shape)))


def before(values, cotan, logs_t, groups):
    heads = logs_t.shape[0] // groups
    width = values.shape[1] // groups
    wide = wide_spec(width)
    return call(
        before_kernel,
        (
            jax.ShapeDtypeStruct(values.shape, BF16),
            jax.ShapeDtypeStruct(values.shape, BF16),
            jax.ShapeDtypeStruct((groups, SPAN, SPAN), BF16),
            jax.ShapeDtypeStruct((groups, SPAN, SPAN), BF16),
            jax.ShapeDtypeStruct((groups, SPAN, heads), F32),
            jax.ShapeDtypeStruct((groups, heads, SPAN), F32),
            jax.ShapeDtypeStruct((groups, 1, width), F32),
        ),
        flops=groups * heads * SPAN * SPAN * 2500,
        moved=values.size * 8,
        exps=groups * heads * SPAN * SPAN,
        grid=(groups,),
        in_specs=[wide, wide, pl.BlockSpec(logs_t.shape, lambda g: (0, 0))],
        out_specs=(
            wide, wide, lead_spec(SPAN, SPAN), lead_spec(SPAN, SPAN),
            lead_spec(SPAN, heads), lead_spec(heads, SPAN), lead_spec(1, width),
        ),
        scratch_shapes=[pltpu.VMEM((STATE, SPAN), F32)],
    )(values, cotan, logs_t)


def partial_kernel(spread, *refs):
    given = refs[:-1] if spread else refs
    (*pieces, weight_ref, sibling_weight_ref, out_ref, sibling_out_ref) = given
    pieces = [piece[...] for piece in pieces]
    if spread:
        refs[-1][...] = pieces[-2] + pieces[-1]
        pieces[-2:] = [refs[-1][...]]
    start = 0
    for piece in pieces:
        rows = slice(start, start + piece.shape[0])
        start += piece.shape[0]
        out_ref[rows, :] = dot(piece, weight_ref[...]).astype(BF16)
        sibling_out_ref[rows, :] = dot(piece, sibling_weight_ref[...]).astype(BF16)


def partials(pieces, effective, sibling_effective, spread=False):
    rows = sum(piece.shape[0] for piece in pieces[: -1 if spread else None])
    columns = effective.shape[1]
    whole = pl.BlockSpec(memory_space=pltpu.VMEM)
    shapes = [jax.ShapeDtypeStruct((rows, columns), BF16)] * 2
    if spread:
        shapes.append(jax.ShapeDtypeStruct(pieces[-1].shape, BF16))
    return call(
        functools.partial(partial_kernel, spread),
        tuple(shapes),
        flops=4 * rows * effective.size,
        moved=(rows * effective.shape[0] + 2 * effective.size + 2 * rows * columns) * 2,
        in_specs=[whole] * (len(pieces) + 2),
        out_specs=(whole,) * len(shapes),
    )(*pieces, effective, sibling_effective)


def rest_kernel(
    ready_ref, sibling_ready_ref, piece_ref, weight_ref, sibling_weight_ref, out_ref, sibling_out_ref
):
    rows = ready_ref.shape[0]
    out_ref[:rows, :] = ready_ref[...]
    sibling_out_ref[:rows, :] = sibling_ready_ref[...]
    out_ref[rows:, :] = dot(piece_ref[...], weight_ref[...]).astype(BF16)
    sibling_out_ref[rows:, :] = dot(piece_ref[...], sibling_weight_ref[...]).astype(BF16)


def rest_of_partials(ready, piece, effective, sibling_effective):
    rows, columns = ready[0].shape[0] + piece.shape[0], effective.shape[1]
    whole = pl.BlockSpec(memory_space=pltpu.VMEM)
    return call(
        rest_kernel,
        (jax.ShapeDtypeStruct((rows, columns), BF16),) * 2,
        flops=4 * piece.shape[0] * effective.size,
        moved=(piece.size + 2 * effective.size + 2 * rows * columns) * 2,
        in_specs=[whole] * 5,
        out_specs=(whole,) * 2,
    )(*ready, piece, effective, sibling_effective)


def turn_kernel(*refs):
    (*pieces, out_ref) = refs
    start = 0
    for piece in pieces:
        out_ref[:, start : start + piece.shape[0]] = turned(piece[...])
        start += piece.shape[0]


def turn(pieces):
    rows, features = sum(piece.shape[0] for piece in pieces), pieces[0].shape[1]
    whole = pl.BlockSpec(memory_space=pltpu.VMEM)
    return call(
        turn_kernel,
        jax.ShapeDtypeStruct((features, rows), BF16),
        flops=rows * features * 2000,
        moved=rows * features * 4,
        in_specs=[whole] * len(pieces),
        out_specs=whole,
    )(*pieces)


def either(ahead, first, second, body):
    if ahead:
        return body(first, second)
    lower = lax.axis_index("seq") < lax.axis_size("seq") // 2

    @pl.when(lower)
    def _():
        body(first, second)

    @pl.when(jnp.logical_not(lower))
    def _():
        body(second, first)


def states_kernel(both, *refs):
    (*terms, xd_ref, yd_ref, proj_ref, near_low_ref, near_ref, far_ref) = refs
    total = terms[0][...].astype(F32)
    for term in terms[1:]:
        total += term[...].astype(F32)
    low = total.astype(BF16)
    proj_ref[...] = low
    state = dot(turned(low[:, :STATE]), xd_ref[...])
    adjoint = dot(turned(low[:, STATE:]), yd_ref[...])

    def put(near, far):
        near_low_ref[0] = near.astype(BF16)
        near_ref[0] = near
        far_ref[0] = far

    either(both, state, adjoint, put)


def states(ahead, terms, xd, yd, first, groups, width):
    pair = pl.BlockSpec((SPAN, 2 * STATE), lambda g: (0, g))
    pair_from = pl.BlockSpec((SPAN, 2 * STATE), lambda g: (0, g + first))
    wide = pl.BlockSpec((SPAN, width), lambda g: (0, g + first))
    lead = lead_spec(STATE, width)
    shape = (groups, STATE, width)
    return call(
        functools.partial(states_kernel, ahead),
        (
            jax.ShapeDtypeStruct((SPAN, groups * 2 * STATE), BF16),
            jax.ShapeDtypeStruct(shape, BF16),
            jax.ShapeDtypeStruct(shape, F32),
            jax.ShapeDtypeStruct(shape, F32),
        ),
        flops=4 * SPAN * groups * width * STATE,
        moved=groups * SPAN * (width * 4 + 4 * STATE * 5),
        grid=(groups,),
        in_specs=[pair_from] * len(terms) + [wide, wide],
        out_specs=(pair, lead, lead, lead),
    )(*terms, xd, yd)


def added(refs):
    total = refs[0][0]
    for ref in refs[1:]:
        total += ref[0]
    return total


def message_kernel(decay_ref, arrived_ref, own_ref, out_ref):
    out_ref[0] = (decay_ref[0] * arrived_ref[0].astype(F32) + own_ref[0]).astype(BF16)


def handed_on(decay, arrived, own, first):
    groups, _, width = arrived.shape
    lead = lead_spec(STATE, width)
    return call(
        message_kernel,
        jax.ShapeDtypeStruct(arrived.shape, BF16),
        flops=2 * arrived.size,
        moved=8 * arrived.size,
        grid=(groups,),
        in_specs=[pl.BlockSpec((1, 1, width), lambda g: (g + first, 0, 0)), lead, lead],
        out_specs=lead,
    )(decay, arrived, own)


def grads_kernel(ahead, proj_ref, xd_ref, yd_ref, mix_ref, mixt_ref, near_ref, *refs):
    (*far_refs, out_ref) = refs

    def body(start, adjoint):
        write, read = proj_ref[:, :STATE], proj_ref[:, STATE:]
        grad_write = dot(mixt_ref[0], read) + dot_nt(xd_ref[...], added(adjoint))
        grad_read = dot(mix_ref[0], write) + dot_nt(yd_ref[...], added(start))
        out_ref[:, :STATE] = grad_write.astype(BF16)
        out_ref[:, STATE:] = grad_read.astype(BF16)

    either(ahead, [near_ref], far_refs, body)


def grads(ahead, proj, xd, yd, mix, mixt, near, far, first):
    groups, _, width = near.shape
    pair = pl.BlockSpec((SPAN, 2 * STATE), lambda g: (0, g))
    wide = pl.BlockSpec((SPAN, width), lambda g: (0, g + first))
    square = pl.BlockSpec((1, SPAN, SPAN), lambda g: (g + first, 0, 0))
    return call(
        functools.partial(grads_kernel, ahead),
        jax.ShapeDtypeStruct(proj.shape, BF16),
        flops=4 * SPAN * groups * (width + SPAN) * STATE,
        moved=groups * SPAN * width * 8,
        grid=(groups,),
        in_specs=[pair, wide, wide, square, square]
        + [lead_spec(STATE, width)] * (1 + len(far)),
        out_specs=pair,
    )(proj, xd, yd, mix, mixt, near, *far)


def output_kernel(
    ahead, first, skip_ref, x_ref, cum_ref, cumt_ref, proj_ref, near_ref, *refs
):
    (*far_refs, out_ref, start_ref) = refs
    far_refs = [ref for ref in far_refs if ref.shape[1:] == near_ref.shape[1:]]

    def put(start, _):
        start_ref[...] = added(start)

    either(ahead, [near_ref], far_refs, put)

    heads = cum_ref.shape[2]
    half = SPAN // 2
    wide = x_ref.shape[1] // heads * 2
    write = proj_ref[:, :STATE]
    read = proj_ref[:, STATE:]
    cum = cum_ref[0]
    cumt = cumt_ref[0]
    from_start = jnp.exp(cum)
    scores = dot_nt(read, write)
    top, low, end = scores[:half, :half], scores[half:, :half], scores[half:, half:]
    lane = lax.broadcasted_iota(jnp.int32, (half, wide), 1)
    for pair in range(heads // 2):
        a, b = 2 * pair, 2 * pair + 1
        cut = slice(pair * wide, (pair + 1) * wide)
        x = x_ref[:, cut]
        upper, lower = [], []
        for head in (a, b):
            decays = decays_of(cum[:, head : head + 1], cumt[head : head + 1, :])
            upper.append(dot((top * decays[0]).astype(BF16), x[:half]))
            lower.append(
                dot((low * decays[1]).astype(BF16), x[:half])
                + dot((end * decays[2]).astype(BF16), x[half:])
            )
        carried = dot(read, start_ref[:, cut]) * lanes_of(
            from_start[:, a : a + 1], from_start[:, b : b + 1], wide
        )
        head = (pl.program_id(0) + first) * heads + a
        gain = jnp.where(
            lax.broadcasted_iota(jnp.int32, (1, wide), 1) < wide // 2,
            skip_ref[head], skip_ref[head + 1],
        )
        rest = carried + gain * x.astype(F32)
        out_ref[:half, cut] = (
            jnp.where(lane < wide // 2, upper[0], upper[1]) + rest[:half]
        ).astype(BF16)
        out_ref[half:, cut] = (
            jnp.where(lane < wide // 2, lower[0], lower[1]) + rest[half:]
        ).astype(BF16)


def output(ahead, values, cum, cumt, skip, proj, near, far, first, earlier):
    groups, _, width = near.shape
    heads = cum.shape[2]
    wide = pl.BlockSpec((SPAN, width), lambda g: (0, g + first))
    lead = lead_spec(STATE, width)
    earlier = [] if earlier is None else [earlier]
    return call(
        functools.partial(output_kernel, ahead, first),
        jax.ShapeDtypeStruct(values.shape, BF16),
        flops=groups * heads * SPAN * SPAN * 2000,
        moved=groups * SPAN * width * 10,
        exps=groups * heads * SPAN * SPAN,
        grid=(groups,),
        in_specs=[
            pl.BlockSpec(memory_space=pltpu.SMEM), wide,
            pl.BlockSpec((1, SPAN, heads), lambda g: (g + first, 0, 0)),
            pl.BlockSpec((1, heads, SPAN), lambda g: (g + first, 0, 0)),
            pl.BlockSpec((SPAN, 2 * STATE), lambda g: (0, g)),
        ]
        + [lead] * (1 + len(far))
        + [pl.BlockSpec(memory_space=pl.ANY)] * len(earlier),
        out_specs=wide,
        scratch_shapes=[pltpu.VMEM((STATE, width), BF16)],
        input_output_aliases={6 + len(far): 0} if earlier else {},
    )(skip, values, cum, cumt, proj, near, *far, *earlier)


def spot_of(block, spots):
    if spots == 1:
        return 0
    other_x = (lax.axis_index("head") != block % 2).astype(jnp.int32)
    other_core = (lax.axis_index("sub") != block // 2).astype(jnp.int32)
    return 2 * other_x + other_core


def update_kernel(blocks, spots, part, *refs):
    turned_refs, pieces = refs[:spots], refs[spots : spots + blocks]
    decayed_ref, keep_ref = refs[spots + blocks : spots + blocks + 2]
    weight_ref, sparse_ref, grad_ref, weight_out, sparse_out, sems = refs[-6:]
    tokens, width = pieces[0].shape
    rows = decayed_ref.shape[0]
    step = min(rows, 256)
    columns = slice(part * width, (part + 1) * width)
    for block, piece in enumerate(pieces):
        start = pl.multiple_of(spot_of(block, spots) * tokens, tokens)
        grad_ref[pl.ds(start, tokens), :] = piece[...]
    copies = []
    for number in range(rows // step):
        here = slice(number * step, (number + 1) * step)
        total = dot(turned_refs[0][here, :], grad_ref[:tokens, :])
        for spot in range(1, spots):
            total += dot(
                turned_refs[spot][here, :], grad_ref[spot * tokens : (spot + 1) * tokens, :]
            )
        weight = decayed_ref[here, columns] - (LEARN_RATE * WEIGHT_SCALE) * total
        weight_out[here, :] = weight
        sparse_out[here, :] = (weight * keep_ref[here, columns].astype(F32)).astype(BF16)
        for place, (source, target) in enumerate(
            ((weight_out, weight_ref), (sparse_out, sparse_ref))
        ):
            copies.append(
                pltpu.make_async_copy(
                    source.at[here, :], target.at[here, columns], sems.at[place, number]
                )
            )
            copies[-1].start()
    for copy in copies:
        copy.wait()


def update(turned_hidden, grad_blocks, decayed, keep, part, earlier, vmem):
    rows, columns = decayed.shape
    width = grad_blocks[0].shape[1]
    tokens = turned_hidden[0].shape[1]
    spots, blocks = len(turned_hidden), len(grad_blocks)
    earlier = earlier or ()
    whole, anywhere = pl.BlockSpec(memory_space=pltpu.VMEM), pl.BlockSpec(memory_space=pl.ANY)
    return call(
        functools.partial(update_kernel, blocks, spots, part),
        (jax.ShapeDtypeStruct((rows, columns), F32), jax.ShapeDtypeStruct((rows, columns), BF16)),
        flops=2 * spots * tokens * rows * width,
        moved=rows * width * 12 + spots * tokens * (rows + width) * 2,
        vmem=vmem,
        in_specs=[whole] * (spots + blocks + 2) + [anywhere] * len(earlier),
        out_specs=(anywhere, anywhere),
        scratch_shapes=[
            pltpu.VMEM((spots * tokens, width), BF16),
            pltpu.VMEM((rows, width), F32),
            pltpu.VMEM((rows, width), BF16),
            pltpu.SemaphoreType.DMA((2, rows // min(rows, 256))),
        ],
        input_output_aliases={spots + blocks + 2 + i: i for i in range(len(earlier))},
    )(*turned_hidden, *grad_blocks, decayed, keep, *earlier)


def held(after, *before):
    return lax.optimization_barrier((after, *before))[0]


def to_all(seq, distance):
    return [(source, (source + distance) % seq) for source in range(seq)]


def block_pairs(seq, near, same_core):
    return [
        (
            (z * 2 + x) * 2 + core,
            ((z + (x if near else 1 - x) + 2 * core) % seq * 2 + x) * 2
            + (core if same_core else 1 - core),
        )
        for z in range(seq)
        for x in range(2)
        for core in range(2)
    ]


def transpose_pairs(seq):
    stays, crosses, beside, onward = [], [], [], []
    for z in range(seq):
        for x in range(2):
            for core in range(2):
                layer = 2 * x + core
                distance = (z - layer) % seq
                source, step = ((z * 2 + way) * 2 + core for way in (x, 1 - x))
                target = (layer * 2 + distance % 2) * 2 + distance // 2
                if distance % 2 == x:
                    stays.append((source, target))
                else:
                    crosses.append((source, target))
                    beside.append((source, step))
                    onward.append((step, target))
    return stays, crosses, beside, onward


SWAP = [(0, 1), (1, 0)]


def chain(own, own_low, decay, seq, step):
    arrived = jnp.zeros_like(own_low)
    message = own_low
    first = 0 if step > 0 else seq - 1
    for hop in range(seq - 1):
        source = first + hop * step
        if hop:
            message = handed_on(decay, arrived, own, 0)
        arrived = arrived + lax.ppermute(message, "seq", [(source, source + step)])
    return arrived


def on_device_general(
    seq, hidden, inner_values, log_decay, skip_gain, cotangent, master, mask_now, mask_next
):
    groups = master.shape[1] // (2 * STATE)
    effective, decayed, keep = weights(master, mask_now, mask_next)
    features = lax.all_gather(hidden, ("head", "sub"), axis=1, tiled=True)
    layer = lax.all_to_all(features, "seq", split_axis=1, concat_axis=0, tiled=True)
    xd, yd, mix, mixt, cum, cumt, decay = before(
        inner_values, cotangent, log_decay.T, groups
    )
    part = dot(layer, effective).astype(BF16)
    terms = [lax.psum_scatter(part, "seq", scatter_dimension=0, tiled=True)]
    proj, state_low, state, adjoint = states(True, terms, xd, yd, 0, groups, decay.shape[2])
    start = chain(state, state_low, decay, seq, 1)
    adjoint_in = chain(adjoint, adjoint.astype(BF16), decay, seq, -1)
    grad = grads(True, proj, xd, yd, mix, mixt, start, [adjoint_in], 0)
    blocks = [lax.all_gather(grad, "seq", axis=0, tiled=True)]
    ssd_output = output(
        True, inner_values, cum, cumt, skip_gain, proj, start, [adjoint_in], 0, None
    )
    return ssd_output, *update([layer.T], blocks, decayed, keep, 0, None, 40 * MIB)


def on_device(
    seq, hidden, inner_values, log_decay, skip_gain, cotangent, master, mask_now, mask_next
):
    groups = master.shape[1] // (2 * STATE)
    axes = ("seq", "head", "sub")
    rows = hidden.shape[0] * 3 // 8
    stays, crosses, beside, onward = transpose_pairs(seq)
    relayed = lax.ppermute(hidden[rows:], axes, beside)
    top = lax.ppermute(hidden[:rows], axes, stays + crosses)
    low = [lax.ppermute(hidden[rows:], axes, stays), lax.ppermute(relayed, axes, onward)]
    effective, decayed, keep = weights(master, mask_now, mask_next)
    sibling_effective = effective_of(
        lax.ppermute(master, "sub", SWAP), lax.ppermute(mask_now, "sub", SWAP)
    )
    top = held(top, effective, sibling_effective)

    other = [lax.ppermute(top, "head", SWAP)]
    same, cross, low = partials([top, *low], effective, sibling_effective, True)
    other.append(lax.ppermute(low, "head", SWAP))
    terms = [
        lax.ppermute(same, axes, block_pairs(seq, True, True)),
        lax.ppermute(cross, axes, block_pairs(seq, True, False)),
    ]
    ready = partials(other[:1], effective, sibling_effective)
    same, cross = rest_of_partials(ready, other[1], effective, sibling_effective)
    terms += [
        lax.ppermute(same, axes, block_pairs(seq, False, True)),
        lax.ppermute(cross, axes, block_pairs(seq, False, False)),
    ]

    xd, yd, mix, mixt, cum, cumt, decay = before(
        held(inner_values, same), cotangent, log_decay.T, groups
    )

    each = groups // PARTS
    spans = range(PARTS)
    projs, messages, nears, fars = zip(
        *(
            states(None, terms, xd, yd, p * each, each, decay.shape[2])
            for p in spans
        )
    )
    turned_hidden = []
    for first, second in ((top, low), other):
        piece = turn([held(first, nears[0]), second])
        turned_hidden += [piece, lax.ppermute(piece, "sub", SWAP)]
    fars = [*fars[:-1], held(fars[-1], *turned_hidden)]
    arrived = [[] for _ in spans]
    hops = (([(0, 1), (3, 2)], nears), ([(1, 2), (2, 1)], fars), ([(1, 0), (2, 3)], None))
    messages = list(messages)
    for pairs, own_terms in hops:
        for p in spans:
            message = messages[p]
            if p and not arrived[p]:
                message = held(message, arrived[p - 1][-1])
            arrived[p].append(lax.ppermute(message, "seq", pairs))
        for p in spans:
            if own_terms:
                messages[p] = handed_on(decay, arrived[p][-1], own_terms[p], p * each)
    gradients, moved, ssd_output = [], [], None
    for p in spans:
        near, far = arrived[p][0], arrived[p][1:]
        proj = projs[p] if not p else held(projs[p], ssd_output)
        grad = grads(None, proj, xd, yd, mix, mixt, near, far, p * each)
        ssd_output = output(
            None, inner_values, held(cum, grad), cumt, skip_gain, projs[p], near, far, p * each,
            ssd_output,
        )
        blocks = [grad]
        for distance in range(1, seq):
            payload = grad
            if not p and distance != seq // 2:
                payload = held(grad, ssd_output)
            blocks.append(lax.ppermute(payload, "seq", to_all(seq, seq - distance)))
        moved.append(blocks)
    decayed = held(decayed, ssd_output)
    updated = None
    for p in spans:
        updated = update(turned_hidden, moved[p], decayed, keep, p, updated, 16 * MIB)
    return ssd_output, *updated


PARTS = 2


def solution(mesh):
    by_position = P(("grp", "seq"), ("head", "sub"))
    by_row = P("seq", ("head", "sub"))
    seq, head, sub = (mesh.shape[name] for name in ("seq", "head", "sub"))
    body = on_device if (seq, head, sub) == (4, 2, 2) else on_device_general
    return jax.shard_map(
        functools.partial(body, seq),
        mesh=mesh,
        in_specs=(
            by_position, by_position, by_position, P(("head", "sub")), by_position,
            by_row, by_row, by_row,
        ),
        out_specs=(by_position, by_position, by_position),
        check_vma=False,
    )
```

```python
import functools
import math

import jax
import jax.numpy as jnp
from jax import lax
from jax.experimental import pallas as pl
from jax.experimental.pallas import tpu as pltpu
from jax.sharding import PartitionSpec as P

D = 4096
STATE = 128
SPAN = 256
LEARN_RATE = 0.05
WEIGHT_DECAY = 10.0
WEIGHT_SCALE = 2.0 / math.sqrt(D)
KEEP_BITS = (0b000111, 0b011001, 0b101010, 0b110100)
OUT_OF_SIGHT = -1e30
MIB = 1024 * 1024

F32 = jnp.float32
BF16 = jnp.bfloat16
NT = (((1,), (1,)), ((), ()))


def call(kernel, out_shape, flops, moved, exps=0, vmem=16 * MIB, **more):
    return pl.pallas_call(
        kernel,
        out_shape=out_shape,
        compiler_params=pltpu.CompilerParams(vmem_limit_bytes=vmem),
        cost_estimate=pl.CostEstimate(flops=flops, bytes_accessed=moved, transcendentals=exps),
        **more,
    )


def dot(a, b):
    return jnp.dot(a, b, preferred_element_type=F32)


def dot_nt(a, b):
    return lax.dot_general(a, b, NT, preferred_element_type=F32)


def turned(a):
    return a.astype(F32).T.astype(BF16)


def expanded(codes, rows):
    spread = (
        lax.broadcasted_iota(jnp.int32, (rows, rows // 4), 0) // 4
        == lax.broadcasted_iota(jnp.int32, (rows, rows // 4), 1)
    ).astype(F32)
    code = dot(spread.astype(BF16), codes.astype(F32).astype(BF16)).astype(jnp.int32)
    place = lax.broadcasted_iota(jnp.int32, (rows, 1), 0) % 4
    bits = jnp.where(
        place < 2,
        jnp.where(place == 0, KEEP_BITS[0], KEEP_BITS[1]),
        jnp.where(place == 2, KEEP_BITS[2], KEEP_BITS[3]),
    )
    return lax.shift_right_logical(jnp.broadcast_to(bits, code.shape), code) & 1


def weights_kernel(master_ref, now_ref, next_ref, effective_ref, decayed_ref, keep_ref):
    rows = master_ref.shape[0]
    master = master_ref[...]
    kept = expanded(now_ref[...], rows) == 1
    effective_ref[...] = jnp.where(kept, master * WEIGHT_SCALE, 0.0).astype(BF16)
    decayed_ref[...] = jnp.where(kept, master, master * (1.0 - LEARN_RATE * WEIGHT_DECAY))
    keep_ref[...] = expanded(next_ref[...], rows).astype(F32).astype(BF16)


def weights(master, mask_now, mask_next):
    rows, columns = master.shape
    block = min(rows, 256)
    full = pl.BlockSpec((block, columns), lambda i: (i, 0))
    quarter = pl.BlockSpec((block // 4, columns), lambda i: (i, 0))
    return call(
        weights_kernel,
        (
            jax.ShapeDtypeStruct((rows, columns), BF16),
            jax.ShapeDtypeStruct((rows, columns), F32),
            jax.ShapeDtypeStruct((rows, columns), BF16),
        ),
        flops=rows * columns * 3000,
        moved=rows * columns * 14,
        grid=(rows // block,),
        in_specs=[full, quarter, quarter],
        out_specs=(full, full, full),
    )(master, mask_now, mask_next)


def effective_kernel(master_ref, now_ref, effective_ref):
    kept = expanded(now_ref[...], master_ref.shape[0]) == 1
    effective_ref[...] = jnp.where(kept, master_ref[...] * WEIGHT_SCALE, 0.0).astype(BF16)


def effective_of(master, mask_now):
    rows, columns = master.shape
    block = min(rows, 256)
    full = pl.BlockSpec((block, columns), lambda i: (i, 0))
    return call(
        effective_kernel,
        jax.ShapeDtypeStruct((rows, columns), BF16),
        flops=rows * columns * 3000,
        moved=rows * columns * 7,
        grid=(rows // block,),
        in_specs=[full, pl.BlockSpec((block // 4, columns), lambda i: (i, 0))],
        out_specs=full,
    )(master, mask_now)


def lanes_of(left, right, wide):
    lane = lax.broadcasted_iota(jnp.int32, (left.shape[0], wide), 1)
    return jnp.where(lane < wide // 2, left, right)


def decays_of(col, row):
    half = SPAN // 2
    causal = lax.broadcasted_iota(jnp.int32, (half, half), 0) >= lax.broadcasted_iota(
        jnp.int32, (half, half), 1
    )
    top = jnp.exp(jnp.where(causal, col[:half] - row[:, :half], OUT_OF_SIGHT))
    low = jnp.exp(col[half:] - row[:, :half])
    end = jnp.exp(jnp.where(causal, col[half:] - row[:, half:], OUT_OF_SIGHT))
    return top, low, end


def before_kernel(
    x_ref, dy_ref, logt_ref,
    xd_ref, yd_ref, mix_ref, mixt_ref, cum_ref, cumt_ref, end_ref, tall_ref,
):
    heads = cum_ref.shape[2]
    half = SPAN // 2
    wide = x_ref.shape[1] // heads * 2
    row = lax.broadcasted_iota(jnp.int32, (SPAN, SPAN), 0)
    col = lax.broadcasted_iota(jnp.int32, (SPAN, SPAN), 1)
    first = pl.multiple_of(pl.program_id(0) * heads, heads)
    cumt = jnp.dot(
        logt_ref[pl.ds(first, heads), :], (row <= col).astype(F32),
        precision=lax.Precision.HIGHEST, preferred_element_type=F32,
    )
    tall_ref[...] = jnp.zeros_like(tall_ref)
    tall_ref[:heads, :] = cumt
    cum = tall_ref[...].T[:, :heads]
    cum_ref[0] = cum
    cumt_ref[0] = cumt
    end = cum[SPAN - 1 :, :]
    from_start = jnp.exp(cum)
    to_end = jnp.exp(end - cum)
    whole = jnp.exp(end)
    mix = [jnp.zeros((half, half), F32) for _ in range(3)]
    lane = lax.broadcasted_iota(jnp.int32, (SPAN, wide), 1)
    for pair in range(heads // 2):
        a, b = 2 * pair, 2 * pair + 1
        cut = slice(pair * wide, (pair + 1) * wide)
        x = x_ref[:, cut]
        dy = dy_ref[:, cut]
        wide_dy = dy.astype(F32)
        xd_ref[:, cut] = (
            x.astype(F32) * lanes_of(to_end[:, a : a + 1], to_end[:, b : b + 1], wide)
        ).astype(BF16)
        yd_ref[:, cut] = (
            wide_dy * lanes_of(from_start[:, a : a + 1], from_start[:, b : b + 1], wide)
        ).astype(BF16)
        end_ref[0, :, cut] = lanes_of(whole[:, a : a + 1], whole[:, b : b + 1], wide)
        for head, mine in ((a, lane < wide // 2), (b, lane >= wide // 2)):
            one = jnp.where(mine, wide_dy, 0.0).astype(BF16)
            decays = decays_of(cum[:, head : head + 1], cumt[head : head + 1, :])
            mix[0] += dot_nt(one[:half], x[:half]) * decays[0]
            both = dot_nt(one[half:], x)
            mix[1] += both[:, :half] * decays[1]
            mix[2] += both[:, half:] * decays[2]
    nothing = jnp.zeros((half, half), BF16)
    top, low, end_mix = (m.astype(BF16) for m in mix)
    topt, lowt, end_mixt = (m.T.astype(BF16) for m in mix)
    mix_ref[0, :half, :half] = top
    mix_ref[0, :half, half:] = nothing
    mix_ref[0, half:, :half] = low
    mix_ref[0, half:, half:] = end_mix
    mixt_ref[0, :half, :half] = topt
    mixt_ref[0, :half, half:] = lowt
    mixt_ref[0, half:, :half] = nothing
    mixt_ref[0, half:, half:] = end_mixt


def wide_spec(width):
    return pl.BlockSpec((SPAN, width), lambda g: (0, g))


def lead_spec(*shape):
    return pl.BlockSpec((1, *shape), lambda g: (g, *(0 for _ in shape)))


def before(values, cotan, logs_t, groups):
    heads = logs_t.shape[0] // groups
    width = values.shape[1] // groups
    wide = wide_spec(width)
    return call(
        before_kernel,
        (
            jax.ShapeDtypeStruct(values.shape, BF16),
            jax.ShapeDtypeStruct(values.shape, BF16),
            jax.ShapeDtypeStruct((groups, SPAN, SPAN), BF16),
            jax.ShapeDtypeStruct((groups, SPAN, SPAN), BF16),
            jax.ShapeDtypeStruct((groups, SPAN, heads), F32),
            jax.ShapeDtypeStruct((groups, heads, SPAN), F32),
            jax.ShapeDtypeStruct((groups, 1, width), F32),
        ),
        flops=groups * heads * SPAN * SPAN * 2500,
        moved=values.size * 8,
        exps=groups * heads * SPAN * SPAN,
        grid=(groups,),
        in_specs=[wide, wide, pl.BlockSpec(logs_t.shape, lambda g: (0, 0))],
        out_specs=(
            wide, wide, lead_spec(SPAN, SPAN), lead_spec(SPAN, SPAN),
            lead_spec(SPAN, heads), lead_spec(heads, SPAN), lead_spec(1, width),
        ),
        scratch_shapes=[pltpu.VMEM((STATE, SPAN), F32)],
    )(values, cotan, logs_t)


def partial_kernel(spread, *refs):
    given = refs[:-1] if spread else refs
    (*pieces, weight_ref, sibling_weight_ref, out_ref, sibling_out_ref) = given
    pieces = [piece[...] for piece in pieces]
    if spread:
        refs[-1][...] = pieces[-2] + pieces[-1]
        pieces[-2:] = [refs[-1][...]]
    start = 0
    for piece in pieces:
        rows = slice(start, start + piece.shape[0])
        start += piece.shape[0]
        out_ref[rows, :] = dot(piece, weight_ref[...]).astype(BF16)
        sibling_out_ref[rows, :] = dot(piece, sibling_weight_ref[...]).astype(BF16)


def partials(pieces, effective, sibling_effective, spread=False):
    rows = sum(piece.shape[0] for piece in pieces[: -1 if spread else None])
    columns = effective.shape[1]
    whole = pl.BlockSpec(memory_space=pltpu.VMEM)
    shapes = [jax.ShapeDtypeStruct((rows, columns), BF16)] * 2
    if spread:
        shapes.append(jax.ShapeDtypeStruct(pieces[-1].shape, BF16))
    return call(
        functools.partial(partial_kernel, spread),
        tuple(shapes),
        flops=4 * rows * effective.size,
        moved=(rows * effective.shape[0] + 2 * effective.size + 2 * rows * columns) * 2,
        in_specs=[whole] * (len(pieces) + 2),
        out_specs=(whole,) * len(shapes),
    )(*pieces, effective, sibling_effective)


def rest_kernel(
    ready_ref, sibling_ready_ref, piece_ref, weight_ref, sibling_weight_ref, out_ref, sibling_out_ref
):
    rows = ready_ref.shape[0]
    out_ref[:rows, :] = ready_ref[...]
    sibling_out_ref[:rows, :] = sibling_ready_ref[...]
    out_ref[rows:, :] = dot(piece_ref[...], weight_ref[...]).astype(BF16)
    sibling_out_ref[rows:, :] = dot(piece_ref[...], sibling_weight_ref[...]).astype(BF16)


def rest_of_partials(ready, piece, effective, sibling_effective):
    rows, columns = ready[0].shape[0] + piece.shape[0], effective.shape[1]
    whole = pl.BlockSpec(memory_space=pltpu.VMEM)
    return call(
        rest_kernel,
        (jax.ShapeDtypeStruct((rows, columns), BF16),) * 2,
        flops=4 * piece.shape[0] * effective.size,
        moved=(piece.size + 2 * effective.size + 2 * rows * columns) * 2,
        in_specs=[whole] * 5,
        out_specs=(whole,) * 2,
    )(*ready, piece, effective, sibling_effective)


def turn_kernel(*refs):
    (*pieces, out_ref) = refs
    start = 0
    for piece in pieces:
        out_ref[:, start : start + piece.shape[0]] = turned(piece[...])
        start += piece.shape[0]


def turn(pieces):
    rows, features = sum(piece.shape[0] for piece in pieces), pieces[0].shape[1]
    whole = pl.BlockSpec(memory_space=pltpu.VMEM)
    return call(
        turn_kernel,
        jax.ShapeDtypeStruct((features, rows), BF16),
        flops=rows * features * 2000,
        moved=rows * features * 4,
        in_specs=[whole] * len(pieces),
        out_specs=whole,
    )(*pieces)


def either(ahead, first, second, body):
    if ahead:
        return body(first, second)
    lower = lax.axis_index("seq") < lax.axis_size("seq") // 2

    @pl.when(lower)
    def _():
        body(first, second)

    @pl.when(jnp.logical_not(lower))
    def _():
        body(second, first)


def states_kernel(both, *refs):
    (*terms, xd_ref, yd_ref, proj_ref, near_low_ref, near_ref, far_ref) = refs
    total = terms[0][...].astype(F32)
    for term in terms[1:]:
        total += term[...].astype(F32)
    low = total.astype(BF16)
    proj_ref[...] = low
    state = dot(turned(low[:, :STATE]), xd_ref[...])
    adjoint = dot(turned(low[:, STATE:]), yd_ref[...])

    def put(near, far):
        near_low_ref[0] = near.astype(BF16)
        near_ref[0] = near
        far_ref[0] = far

    either(both, state, adjoint, put)


def states(ahead, terms, xd, yd, first, groups, width):
    pair = pl.BlockSpec((SPAN, 2 * STATE), lambda g: (0, g))
    pair_from = pl.BlockSpec((SPAN, 2 * STATE), lambda g: (0, g + first))
    wide = pl.BlockSpec((SPAN, width), lambda g: (0, g + first))
    lead = lead_spec(STATE, width)
    shape = (groups, STATE, width)
    return call(
        functools.partial(states_kernel, ahead),
        (
            jax.ShapeDtypeStruct((SPAN, groups * 2 * STATE), BF16),
            jax.ShapeDtypeStruct(shape, BF16),
            jax.ShapeDtypeStruct(shape, F32),
            jax.ShapeDtypeStruct(shape, F32),
        ),
        flops=4 * SPAN * groups * width * STATE,
        moved=groups * SPAN * (width * 4 + 4 * STATE * 5),
        grid=(groups,),
        in_specs=[pair_from] * len(terms) + [wide, wide],
        out_specs=(pair, lead, lead, lead),
    )(*terms, xd, yd)


def added(refs):
    total = refs[0][0]
    for ref in refs[1:]:
        total += ref[0]
    return total


def message_kernel(decay_ref, arrived_ref, own_ref, out_ref):
    out_ref[0] = (decay_ref[0] * arrived_ref[0].astype(F32) + own_ref[0]).astype(BF16)


def handed_on(decay, arrived, own, first):
    groups, _, width = arrived.shape
    lead = lead_spec(STATE, width)
    return call(
        message_kernel,
        jax.ShapeDtypeStruct(arrived.shape, BF16),
        flops=2 * arrived.size,
        moved=8 * arrived.size,
        grid=(groups,),
        in_specs=[pl.BlockSpec((1, 1, width), lambda g: (g + first, 0, 0)), lead, lead],
        out_specs=lead,
    )(decay, arrived, own)


def grads_kernel(ahead, proj_ref, xd_ref, yd_ref, mix_ref, mixt_ref, near_ref, *refs):
    (*far_refs, out_ref) = refs

    def body(start, adjoint):
        write, read = proj_ref[:, :STATE], proj_ref[:, STATE:]
        grad_write = dot(mixt_ref[0], read) + dot_nt(xd_ref[...], added(adjoint))
        grad_read = dot(mix_ref[0], write) + dot_nt(yd_ref[...], added(start))
        out_ref[:, :STATE] = grad_write.astype(BF16)
        out_ref[:, STATE:] = grad_read.astype(BF16)

    either(ahead, [near_ref], far_refs, body)


def grads(ahead, proj, xd, yd, mix, mixt, near, far, first):
    groups, _, width = near.shape
    pair = pl.BlockSpec((SPAN, 2 * STATE), lambda g: (0, g))
    wide = pl.BlockSpec((SPAN, width), lambda g: (0, g + first))
    square = pl.BlockSpec((1, SPAN, SPAN), lambda g: (g + first, 0, 0))
    return call(
        functools.partial(grads_kernel, ahead),
        jax.ShapeDtypeStruct(proj.shape, BF16),
        flops=4 * SPAN * groups * (width + SPAN) * STATE,
        moved=groups * SPAN * width * 8,
        grid=(groups,),
        in_specs=[pair, wide, wide, square, square]
        + [lead_spec(STATE, width)] * (1 + len(far)),
        out_specs=pair,
    )(proj, xd, yd, mix, mixt, near, *far)


def output_kernel(
    ahead, first, skip_ref, x_ref, cum_ref, cumt_ref, proj_ref, near_ref, *refs
):
    (*far_refs, out_ref, start_ref) = refs
    far_refs = [ref for ref in far_refs if ref.shape[1:] == near_ref.shape[1:]]

    def put(start, _):
        start_ref[...] = added(start)

    either(ahead, [near_ref], far_refs, put)

    heads = cum_ref.shape[2]
    half = SPAN // 2
    wide = x_ref.shape[1] // heads * 2
    write = proj_ref[:, :STATE]
    read = proj_ref[:, STATE:]
    cum = cum_ref[0]
    cumt = cumt_ref[0]
    from_start = jnp.exp(cum)
    scores = dot_nt(read, write)
    top, low, end = scores[:half, :half], scores[half:, :half], scores[half:, half:]
    lane = lax.broadcasted_iota(jnp.int32, (half, wide), 1)
    for pair in range(heads // 2):
        a, b = 2 * pair, 2 * pair + 1
        cut = slice(pair * wide, (pair + 1) * wide)
        x = x_ref[:, cut]
        upper, lower = [], []
        for head in (a, b):
            decays = decays_of(cum[:, head : head + 1], cumt[head : head + 1, :])
            upper.append(dot((top * decays[0]).astype(BF16), x[:half]))
            lower.append(
                dot((low * decays[1]).astype(BF16), x[:half])
                + dot((end * decays[2]).astype(BF16), x[half:])
            )
        carried = dot(read, start_ref[:, cut]) * lanes_of(
            from_start[:, a : a + 1], from_start[:, b : b + 1], wide
        )
        head = (pl.program_id(0) + first) * heads + a
        gain = jnp.where(
            lax.broadcasted_iota(jnp.int32, (1, wide), 1) < wide // 2,
            skip_ref[head], skip_ref[head + 1],
        )
        rest = carried + gain * x.astype(F32)
        out_ref[:half, cut] = (
            jnp.where(lane < wide // 2, upper[0], upper[1]) + rest[:half]
        ).astype(BF16)
        out_ref[half:, cut] = (
            jnp.where(lane < wide // 2, lower[0], lower[1]) + rest[half:]
        ).astype(BF16)


def output(ahead, values, cum, cumt, skip, proj, near, far, first, earlier):
    groups, _, width = near.shape
    heads = cum.shape[2]
    wide = pl.BlockSpec((SPAN, width), lambda g: (0, g + first))
    lead = lead_spec(STATE, width)
    earlier = [] if earlier is None else [earlier]
    return call(
        functools.partial(output_kernel, ahead, first),
        jax.ShapeDtypeStruct(values.shape, BF16),
        flops=groups * heads * SPAN * SPAN * 2000,
        moved=groups * SPAN * width * 10,
        exps=groups * heads * SPAN * SPAN,
        grid=(groups,),
        in_specs=[
            pl.BlockSpec(memory_space=pltpu.SMEM), wide,
            pl.BlockSpec((1, SPAN, heads), lambda g: (g + first, 0, 0)),
            pl.BlockSpec((1, heads, SPAN), lambda g: (g + first, 0, 0)),
            pl.BlockSpec((SPAN, 2 * STATE), lambda g: (0, g)),
        ]
        + [lead] * (1 + len(far))
        + [pl.BlockSpec(memory_space=pl.ANY)] * len(earlier),
        out_specs=wide,
        scratch_shapes=[pltpu.VMEM((STATE, width), BF16)],
        input_output_aliases={6 + len(far): 0} if earlier else {},
    )(skip, values, cum, cumt, proj, near, *far, *earlier)


def spot_of(block, spots):
    if spots == 1:
        return 0
    other_x = (lax.axis_index("head") != block % 2).astype(jnp.int32)
    other_core = (lax.axis_index("sub") != block // 2).astype(jnp.int32)
    return 2 * other_x + other_core


def update_kernel(blocks, spots, part, *refs):
    turned_refs, pieces = refs[:spots], refs[spots : spots + blocks]
    decayed_ref, keep_ref = refs[spots + blocks : spots + blocks + 2]
    weight_ref, sparse_ref, grad_ref, weight_out, sparse_out, sems = refs[-6:]
    tokens, width = pieces[0].shape
    rows = decayed_ref.shape[0]
    step = min(rows, 256)
    columns = slice(part * width, (part + 1) * width)
    for block, piece in enumerate(pieces):
        start = pl.multiple_of(spot_of(block, spots) * tokens, tokens)
        grad_ref[pl.ds(start, tokens), :] = piece[...]
    copies = []
    for number in range(rows // step):
        here = slice(number * step, (number + 1) * step)
        total = dot(turned_refs[0][here, :], grad_ref[:tokens, :])
        for spot in range(1, spots):
            total += dot(
                turned_refs[spot][here, :], grad_ref[spot * tokens : (spot + 1) * tokens, :]
            )
        weight = decayed_ref[here, columns] - (LEARN_RATE * WEIGHT_SCALE) * total
        weight_out[here, :] = weight
        sparse_out[here, :] = (weight * keep_ref[here, columns].astype(F32)).astype(BF16)
        for place, (source, target) in enumerate(
            ((weight_out, weight_ref), (sparse_out, sparse_ref))
        ):
            copies.append(
                pltpu.make_async_copy(
                    source.at[here, :], target.at[here, columns], sems.at[place, number]
                )
            )
            copies[-1].start()
    for copy in copies:
        copy.wait()


def update(turned_hidden, grad_blocks, decayed, keep, part, earlier, vmem):
    rows, columns = decayed.shape
    width = grad_blocks[0].shape[1]
    tokens = turned_hidden[0].shape[1]
    spots, blocks = len(turned_hidden), len(grad_blocks)
    earlier = earlier or ()
    whole, anywhere = pl.BlockSpec(memory_space=pltpu.VMEM), pl.BlockSpec(memory_space=pl.ANY)
    return call(
        functools.partial(update_kernel, blocks, spots, part),
        (jax.ShapeDtypeStruct((rows, columns), F32), jax.ShapeDtypeStruct((rows, columns), BF16)),
        flops=2 * spots * tokens * rows * width,
        moved=rows * width * 12 + spots * tokens * (rows + width) * 2,
        vmem=vmem,
        in_specs=[whole] * (spots + blocks + 2) + [anywhere] * len(earlier),
        out_specs=(anywhere, anywhere),
        scratch_shapes=[
            pltpu.VMEM((spots * tokens, width), BF16),
            pltpu.VMEM((rows, width), F32),
            pltpu.VMEM((rows, width), BF16),
            pltpu.SemaphoreType.DMA((2, rows // min(rows, 256))),
        ],
        input_output_aliases={spots + blocks + 2 + i: i for i in range(len(earlier))},
    )(*turned_hidden, *grad_blocks, decayed, keep, *earlier)


def held(after, *before):
    return lax.optimization_barrier((after, *before))[0]


def to_all(seq, distance):
    return [(source, (source + distance) % seq) for source in range(seq)]


def block_pairs(seq, near, same_core):
    return [
        (
            (z * 2 + x) * 2 + core,
            ((z + (x if near else 1 - x) + 2 * core) % seq * 2 + x) * 2
            + (core if same_core else 1 - core),
        )
        for z in range(seq)
        for x in range(2)
        for core in range(2)
    ]


def transpose_pairs(seq):
    stays, crosses, beside, onward = [], [], [], []
    for z in range(seq):
        for x in range(2):
            for core in range(2):
                layer = 2 * x + core
                distance = (z - layer) % seq
                source, step = ((z * 2 + way) * 2 + core for way in (x, 1 - x))
                target = (layer * 2 + distance % 2) * 2 + distance // 2
                if distance % 2 == x:
                    stays.append((source, target))
                else:
                    crosses.append((source, target))
                    beside.append((source, step))
                    onward.append((step, target))
    return stays, crosses, beside, onward


SWAP = [(0, 1), (1, 0)]


def chain(own, own_low, decay, seq, step):
    arrived = jnp.zeros_like(own_low)
    message = own_low
    first = 0 if step > 0 else seq - 1
    for hop in range(seq - 1):
        source = first + hop * step
        if hop:
            message = handed_on(decay, arrived, own, 0)
        arrived = arrived + lax.ppermute(message, "seq", [(source, source + step)])
    return arrived


def on_device_general(
    seq, hidden, inner_values, log_decay, skip_gain, cotangent, master, mask_now, mask_next
):
    groups = master.shape[1] // (2 * STATE)
    effective, decayed, keep = weights(master, mask_now, mask_next)
    features = lax.all_gather(hidden, ("head", "sub"), axis=1, tiled=True)
    layer = lax.all_to_all(features, "seq", split_axis=1, concat_axis=0, tiled=True)
    xd, yd, mix, mixt, cum, cumt, decay = before(
        inner_values, cotangent, log_decay.T, groups
    )
    part = dot(layer, effective).astype(BF16)
    terms = [lax.psum_scatter(part, "seq", scatter_dimension=0, tiled=True)]
    proj, state_low, state, adjoint = states(True, terms, xd, yd, 0, groups, decay.shape[2])
    start = chain(state, state_low, decay, seq, 1)
    adjoint_in = chain(adjoint, adjoint.astype(BF16), decay, seq, -1)
    grad = grads(True, proj, xd, yd, mix, mixt, start, [adjoint_in], 0)
    blocks = [lax.all_gather(grad, "seq", axis=0, tiled=True)]
    ssd_output = output(
        True, inner_values, cum, cumt, skip_gain, proj, start, [adjoint_in], 0, None
    )
    return ssd_output, *update([layer.T], blocks, decayed, keep, 0, None, 40 * MIB)


def on_device(
    seq, hidden, inner_values, log_decay, skip_gain, cotangent, master, mask_now, mask_next
):
    groups = master.shape[1] // (2 * STATE)
    axes = ("seq", "head", "sub")
    rows = hidden.shape[0] * 5 // 8
    stays, crosses, beside, onward = transpose_pairs(seq)
    relayed = lax.ppermute(hidden[rows:], axes, beside)
    top = lax.ppermute(hidden[:rows], axes, stays + crosses)
    low = [lax.ppermute(hidden[rows:], axes, stays), lax.ppermute(relayed, axes, onward)]
    effective, decayed, keep = weights(master, mask_now, mask_next)
    sibling_effective = effective_of(
        lax.ppermute(master, "sub", SWAP), lax.ppermute(mask_now, "sub", SWAP)
    )
    top = held(top, effective, sibling_effective)

    other = [lax.ppermute(top, "head", SWAP)]
    same, cross, low = partials([top, *low], effective, sibling_effective, True)
    other.append(lax.ppermute(low, "head", SWAP))
    terms = [
        lax.ppermute(same, axes, block_pairs(seq, True, True)),
        lax.ppermute(cross, axes, block_pairs(seq, True, False)),
    ]
    ready = partials(other[:1], effective, sibling_effective)
    same, cross = rest_of_partials(ready, other[1], effective, sibling_effective)
    terms += [
        lax.ppermute(same, axes, block_pairs(seq, False, True)),
        lax.ppermute(cross, axes, block_pairs(seq, False, False)),
    ]

    xd, yd, mix, mixt, cum, cumt, decay = before(
        held(inner_values, same), cotangent, log_decay.T, groups
    )

    each = groups // PARTS
    spans = range(PARTS)
    projs, messages, nears, fars = zip(
        *(
            states(None, terms, xd, yd, p * each, each, decay.shape[2])
            for p in spans
        )
    )
    turned_hidden = []
    for first, second in ((top, low), other):
        piece = turn([held(first, nears[0]), second])
        turned_hidden += [piece, lax.ppermute(piece, "sub", SWAP)]
    fars = [*fars[:-1], held(fars[-1], *turned_hidden)]
    arrived = [[] for _ in spans]
    hops = (([(0, 1), (3, 2)], nears), ([(1, 2), (2, 1)], fars), ([(1, 0), (2, 3)], None))
    messages = list(messages)
    for pairs, own_terms in hops:
        for p in spans:
            message = messages[p]
            if p and not arrived[p]:
                message = held(message, arrived[p - 1][-1])
            arrived[p].append(lax.ppermute(message, "seq", pairs))
        for p in spans:
            if own_terms:
                messages[p] = handed_on(decay, arrived[p][-1], own_terms[p], p * each)
    gradients, moved, ssd_output = [], [], None
    for p in spans:
        near, far = arrived[p][0], arrived[p][1:]
        proj = projs[p] if not p else held(projs[p], ssd_output)
        grad = grads(None, proj, xd, yd, mix, mixt, near, far, p * each)
        ssd_output = output(
            None, inner_values, held(cum, grad), cumt, skip_gain, projs[p], near, far, p * each,
            ssd_output,
        )
        blocks = [grad]
        for distance in range(1, seq):
            payload = grad
            if not p and distance != seq // 2:
                payload = held(grad, ssd_output)
            blocks.append(lax.ppermute(payload, "seq", to_all(seq, seq - distance)))
        moved.append(blocks)
    decayed = held(decayed, ssd_output)
    updated = None
    for p in spans:
        updated = update(turned_hidden, moved[p], decayed, keep, p, updated, 16 * MIB)
    return ssd_output, *updated


PARTS = 2


def solution(mesh):
    by_position = P(("grp", "seq"), ("head", "sub"))
    by_row = P("seq", ("head", "sub"))
    seq, head, sub = (mesh.shape[name] for name in ("seq", "head", "sub"))
    body = on_device if (seq, head, sub) == (4, 2, 2) else on_device_general
    return jax.shard_map(
        functools.partial(body, seq),
        mesh=mesh,
        in_specs=(
            by_position, by_position, by_position, P(("head", "sub")), by_position,
            by_row, by_row, by_row,
        ),
        out_specs=(by_position, by_position, by_position),
        check_vma=False,
    )
```

```python
import functools
import math

import jax
import jax.numpy as jnp
from jax import lax
from jax.experimental import pallas as pl
from jax.experimental.pallas import tpu as pltpu
from jax.sharding import PartitionSpec as P

D = 4096
STATE = 128
SPAN = 256
LEARN_RATE = 0.05
WEIGHT_DECAY = 10.0
WEIGHT_SCALE = 2.0 / math.sqrt(D)
KEEP_BITS = (0b000111, 0b011001, 0b101010, 0b110100)
OUT_OF_SIGHT = -1e30
MIB = 1024 * 1024

F32 = jnp.float32
BF16 = jnp.bfloat16
NT = (((1,), (1,)), ((), ()))


def call(kernel, out_shape, flops, moved, exps=0, vmem=16 * MIB, **more):
    return pl.pallas_call(
        kernel,
        out_shape=out_shape,
        compiler_params=pltpu.CompilerParams(vmem_limit_bytes=vmem),
        cost_estimate=pl.CostEstimate(flops=flops, bytes_accessed=moved, transcendentals=exps),
        **more,
    )


def dot(a, b):
    return jnp.dot(a, b, preferred_element_type=F32)


def dot_nt(a, b):
    return lax.dot_general(a, b, NT, preferred_element_type=F32)


def turned(a):
    return a.astype(F32).T.astype(BF16)


def expanded(codes, rows):
    spread = (
        lax.broadcasted_iota(jnp.int32, (rows, rows // 4), 0) // 4
        == lax.broadcasted_iota(jnp.int32, (rows, rows // 4), 1)
    ).astype(F32)
    code = dot(spread.astype(BF16), codes.astype(F32).astype(BF16)).astype(jnp.int32)
    place = lax.broadcasted_iota(jnp.int32, (rows, 1), 0) % 4
    bits = jnp.where(
        place < 2,
        jnp.where(place == 0, KEEP_BITS[0], KEEP_BITS[1]),
        jnp.where(place == 2, KEEP_BITS[2], KEEP_BITS[3]),
    )
    return lax.shift_right_logical(jnp.broadcast_to(bits, code.shape), code) & 1


def weights_kernel(master_ref, now_ref, next_ref, effective_ref, decayed_ref, keep_ref):
    rows = master_ref.shape[0]
    master = master_ref[...]
    kept = expanded(now_ref[...], rows) == 1
    effective_ref[...] = jnp.where(kept, master * WEIGHT_SCALE, 0.0).astype(BF16)
    decayed_ref[...] = jnp.where(kept, master, master * (1.0 - LEARN_RATE * WEIGHT_DECAY))
    keep_ref[...] = expanded(next_ref[...], rows).astype(F32).astype(BF16)


def weights(master, mask_now, mask_next):
    rows, columns = master.shape
    block = min(rows, 256)
    full = pl.BlockSpec((block, columns), lambda i: (i, 0))
    quarter = pl.BlockSpec((block // 4, columns), lambda i: (i, 0))
    return call(
        weights_kernel,
        (
            jax.ShapeDtypeStruct((rows, columns), BF16),
            jax.ShapeDtypeStruct((rows, columns), F32),
            jax.ShapeDtypeStruct((rows, columns), BF16),
        ),
        flops=rows * columns * 3000,
        moved=rows * columns * 14,
        grid=(rows // block,),
        in_specs=[full, quarter, quarter],
        out_specs=(full, full, full),
    )(master, mask_now, mask_next)


def effective_kernel(master_ref, now_ref, effective_ref):
    kept = expanded(now_ref[...], master_ref.shape[0]) == 1
    effective_ref[...] = jnp.where(kept, master_ref[...] * WEIGHT_SCALE, 0.0).astype(BF16)


def effective_of(master, mask_now):
    rows, columns = master.shape
    block = min(rows, 256)
    full = pl.BlockSpec((block, columns), lambda i: (i, 0))
    return call(
        effective_kernel,
        jax.ShapeDtypeStruct((rows, columns), BF16),
        flops=rows * columns * 3000,
        moved=rows * columns * 7,
        grid=(rows // block,),
        in_specs=[full, pl.BlockSpec((block // 4, columns), lambda i: (i, 0))],
        out_specs=full,
    )(master, mask_now)


def lanes_of(left, right, wide):
    lane = lax.broadcasted_iota(jnp.int32, (left.shape[0], wide), 1)
    return jnp.where(lane < wide // 2, left, right)


def decays_of(col, row):
    half = SPAN // 2
    causal = lax.broadcasted_iota(jnp.int32, (half, half), 0) >= lax.broadcasted_iota(
        jnp.int32, (half, half), 1
    )
    top = jnp.exp(jnp.where(causal, col[:half] - row[:, :half], OUT_OF_SIGHT))
    low = jnp.exp(col[half:] - row[:, :half])
    end = jnp.exp(jnp.where(causal, col[half:] - row[:, half:], OUT_OF_SIGHT))
    return top, low, end


def before_kernel(
    x_ref, dy_ref, logt_ref,
    xd_ref, yd_ref, mix_ref, mixt_ref, cum_ref, cumt_ref, end_ref, tall_ref,
):
    heads = cum_ref.shape[2]
    half = SPAN // 2
    wide = x_ref.shape[1] // heads * 2
    row = lax.broadcasted_iota(jnp.int32, (SPAN, SPAN), 0)
    col = lax.broadcasted_iota(jnp.int32, (SPAN, SPAN), 1)
    first = pl.multiple_of(pl.program_id(0) * heads, heads)
    cumt = jnp.dot(
        logt_ref[pl.ds(first, heads), :], (row <= col).astype(F32),
        precision=lax.Precision.HIGHEST, preferred_element_type=F32,
    )
    tall_ref[...] = jnp.zeros_like(tall_ref)
    tall_ref[:heads, :] = cumt
    cum = tall_ref[...].T[:, :heads]
    cum_ref[0] = cum
    cumt_ref[0] = cumt
    end = cum[SPAN - 1 :, :]
    from_start = jnp.exp(cum)
    to_end = jnp.exp(end - cum)
    whole = jnp.exp(end)
    mix = [jnp.zeros((half, half), F32) for _ in range(3)]
    lane = lax.broadcasted_iota(jnp.int32, (SPAN, wide), 1)
    for pair in range(heads // 2):
        a, b = 2 * pair, 2 * pair + 1
        cut = slice(pair * wide, (pair + 1) * wide)
        x = x_ref[:, cut]
        dy = dy_ref[:, cut]
        wide_dy = dy.astype(F32)
        xd_ref[:, cut] = (
            x.astype(F32) * lanes_of(to_end[:, a : a + 1], to_end[:, b : b + 1], wide)
        ).astype(BF16)
        yd_ref[:, cut] = (
            wide_dy * lanes_of(from_start[:, a : a + 1], from_start[:, b : b + 1], wide)
        ).astype(BF16)
        end_ref[0, :, cut] = lanes_of(whole[:, a : a + 1], whole[:, b : b + 1], wide)
        for head, mine in ((a, lane < wide // 2), (b, lane >= wide // 2)):
            one = jnp.where(mine, wide_dy, 0.0).astype(BF16)
            decays = decays_of(cum[:, head : head + 1], cumt[head : head + 1, :])
            mix[0] += dot_nt(one[:half], x[:half]) * decays[0]
            both = dot_nt(one[half:], x)
            mix[1] += both[:, :half] * decays[1]
            mix[2] += both[:, half:] * decays[2]
    nothing = jnp.zeros((half, half), BF16)
    top, low, end_mix = (m.astype(BF16) for m in mix)
    topt, lowt, end_mixt = (m.T.astype(BF16) for m in mix)
    mix_ref[0, :half, :half] = top
    mix_ref[0, :half, half:] = nothing
    mix_ref[0, half:, :half] = low
    mix_ref[0, half:, half:] = end_mix
    mixt_ref[0, :half, :half] = topt
    mixt_ref[0, :half, half:] = lowt
    mixt_ref[0, half:, :half] = nothing
    mixt_ref[0, half:, half:] = end_mixt


def wide_spec(width):
    return pl.BlockSpec((SPAN, width), lambda g: (0, g))


def lead_spec(*shape):
    return pl.BlockSpec((1, *shape), lambda g: (g, *(0 for _ in shape)))


def before(values, cotan, logs_t, groups):
    heads = logs_t.shape[0] // groups
    width = values.shape[1] // groups
    wide = wide_spec(width)
    return call(
        before_kernel,
        (
            jax.ShapeDtypeStruct(values.shape, BF16),
            jax.ShapeDtypeStruct(values.shape, BF16),
            jax.ShapeDtypeStruct((groups, SPAN, SPAN), BF16),
            jax.ShapeDtypeStruct((groups, SPAN, SPAN), BF16),
            jax.ShapeDtypeStruct((groups, SPAN, heads), F32),
            jax.ShapeDtypeStruct((groups, heads, SPAN), F32),
            jax.ShapeDtypeStruct((groups, 1, width), F32),
        ),
        flops=groups * heads * SPAN * SPAN * 2500,
        moved=values.size * 8,
        exps=groups * heads * SPAN * SPAN,
        grid=(groups,),
        in_specs=[wide, wide, pl.BlockSpec(logs_t.shape, lambda g: (0, 0))],
        out_specs=(
            wide, wide, lead_spec(SPAN, SPAN), lead_spec(SPAN, SPAN),
            lead_spec(SPAN, heads), lead_spec(heads, SPAN), lead_spec(1, width),
        ),
        scratch_shapes=[pltpu.VMEM((STATE, SPAN), F32)],
    )(values, cotan, logs_t)


def partial_kernel(spread, *refs):
    given = refs[:-1] if spread else refs
    (*pieces, weight_ref, sibling_weight_ref, out_ref, sibling_out_ref) = given
    pieces = [piece[...] for piece in pieces]
    if spread:
        refs[-1][...] = pieces[-2] + pieces[-1]
        pieces[-2:] = [refs[-1][...]]
    start = 0
    for piece in pieces:
        rows = slice(start, start + piece.shape[0])
        start += piece.shape[0]
        out_ref[rows, :] = dot(piece, weight_ref[...]).astype(BF16)
        sibling_out_ref[rows, :] = dot(piece, sibling_weight_ref[...]).astype(BF16)


def partials(pieces, effective, sibling_effective, spread=False):
    rows = sum(piece.shape[0] for piece in pieces[: -1 if spread else None])
    columns = effective.shape[1]
    whole = pl.BlockSpec(memory_space=pltpu.VMEM)
    shapes = [jax.ShapeDtypeStruct((rows, columns), BF16)] * 2
    if spread:
        shapes.append(jax.ShapeDtypeStruct(pieces[-1].shape, BF16))
    return call(
        functools.partial(partial_kernel, spread),
        tuple(shapes),
        flops=4 * rows * effective.size,
        moved=(rows * effective.shape[0] + 2 * effective.size + 2 * rows * columns) * 2,
        in_specs=[whole] * (len(pieces) + 2),
        out_specs=(whole,) * len(shapes),
    )(*pieces, effective, sibling_effective)


def rest_kernel(
    ready_ref, sibling_ready_ref, piece_ref, weight_ref, sibling_weight_ref, out_ref, sibling_out_ref
):
    rows = ready_ref.shape[0]
    out_ref[:rows, :] = ready_ref[...]
    sibling_out_ref[:rows, :] = sibling_ready_ref[...]
    out_ref[rows:, :] = dot(piece_ref[...], weight_ref[...]).astype(BF16)
    sibling_out_ref[rows:, :] = dot(piece_ref[...], sibling_weight_ref[...]).astype(BF16)


def rest_of_partials(ready, piece, effective, sibling_effective):
    rows, columns = ready[0].shape[0] + piece.shape[0], effective.shape[1]
    whole = pl.BlockSpec(memory_space=pltpu.VMEM)
    return call(
        rest_kernel,
        (jax.ShapeDtypeStruct((rows, columns), BF16),) * 2,
        flops=4 * piece.shape[0] * effective.size,
        moved=(piece.size + 2 * effective.size + 2 * rows * columns) * 2,
        in_specs=[whole] * 5,
        out_specs=(whole,) * 2,
    )(*ready, piece, effective, sibling_effective)


def turn_kernel(*refs):
    (*pieces, out_ref) = refs
    start = 0
    for piece in pieces:
        out_ref[:, start : start + piece.shape[0]] = turned(piece[...])
        start += piece.shape[0]


def turn(pieces):
    rows, features = sum(piece.shape[0] for piece in pieces), pieces[0].shape[1]
    whole = pl.BlockSpec(memory_space=pltpu.VMEM)
    return call(
        turn_kernel,
        jax.ShapeDtypeStruct((features, rows), BF16),
        flops=rows * features * 2000,
        moved=rows * features * 4,
        in_specs=[whole] * len(pieces),
        out_specs=whole,
    )(*pieces)


def either(ahead, first, second, body):
    if ahead:
        return body(first, second)
    lower = lax.axis_index("seq") < lax.axis_size("seq") // 2

    @pl.when(lower)
    def _():
        body(first, second)

    @pl.when(jnp.logical_not(lower))
    def _():
        body(second, first)


def states_kernel(both, *refs):
    (*terms, xd_ref, yd_ref, proj_ref, near_low_ref, near_ref, far_ref) = refs
    total = terms[0][...].astype(F32)
    for term in terms[1:]:
        total += term[...].astype(F32)
    low = total.astype(BF16)
    proj_ref[...] = low
    state = dot(turned(low[:, :STATE]), xd_ref[...])
    adjoint = dot(turned(low[:, STATE:]), yd_ref[...])

    def put(near, far):
        near_low_ref[0] = near.astype(BF16)
        near_ref[0] = near
        far_ref[0] = far

    either(both, state, adjoint, put)


def states(ahead, terms, xd, yd, first, groups, width):
    pair = pl.BlockSpec((SPAN, 2 * STATE), lambda g: (0, g))
    pair_from = pl.BlockSpec((SPAN, 2 * STATE), lambda g: (0, g + first))
    wide = pl.BlockSpec((SPAN, width), lambda g: (0, g + first))
    lead = lead_spec(STATE, width)
    shape = (groups, STATE, width)
    return call(
        functools.partial(states_kernel, ahead),
        (
            jax.ShapeDtypeStruct((SPAN, groups * 2 * STATE), BF16),
            jax.ShapeDtypeStruct(shape, BF16),
            jax.ShapeDtypeStruct(shape, F32),
            jax.ShapeDtypeStruct(shape, F32),
        ),
        flops=4 * SPAN * groups * width * STATE,
        moved=groups * SPAN * (width * 4 + 4 * STATE * 5),
        grid=(groups,),
        in_specs=[pair_from] * len(terms) + [wide, wide],
        out_specs=(pair, lead, lead, lead),
    )(*terms, xd, yd)


def added(refs):
    total = refs[0][0]
    for ref in refs[1:]:
        total += ref[0]
    return total


def message_kernel(decay_ref, arrived_ref, own_ref, out_ref):
    out_ref[0] = (decay_ref[0] * arrived_ref[0].astype(F32) + own_ref[0]).astype(BF16)


def handed_on(decay, arrived, own, first):
    groups, _, width = arrived.shape
    lead = lead_spec(STATE, width)
    return call(
        message_kernel,
        jax.ShapeDtypeStruct(arrived.shape, BF16),
        flops=2 * arrived.size,
        moved=8 * arrived.size,
        grid=(groups,),
        in_specs=[pl.BlockSpec((1, 1, width), lambda g: (g + first, 0, 0)), lead, lead],
        out_specs=lead,
    )(decay, arrived, own)


def grads_kernel(ahead, proj_ref, xd_ref, yd_ref, mix_ref, mixt_ref, near_ref, *refs):
    (*far_refs, out_ref) = refs

    def body(start, adjoint):
        write, read = proj_ref[:, :STATE], proj_ref[:, STATE:]
        grad_write = dot(mixt_ref[0], read) + dot_nt(xd_ref[...], added(adjoint))
        grad_read = dot(mix_ref[0], write) + dot_nt(yd_ref[...], added(start))
        out_ref[:, :STATE] = grad_write.astype(BF16)
        out_ref[:, STATE:] = grad_read.astype(BF16)

    either(ahead, [near_ref], far_refs, body)


def grads(ahead, proj, xd, yd, mix, mixt, near, far, first):
    groups, _, width = near.shape
    pair = pl.BlockSpec((SPAN, 2 * STATE), lambda g: (0, g))
    wide = pl.BlockSpec((SPAN, width), lambda g: (0, g + first))
    square = pl.BlockSpec((1, SPAN, SPAN), lambda g: (g + first, 0, 0))
    return call(
        functools.partial(grads_kernel, ahead),
        jax.ShapeDtypeStruct(proj.shape, BF16),
        flops=4 * SPAN * groups * (width + SPAN) * STATE,
        moved=groups * SPAN * width * 8,
        grid=(groups,),
        in_specs=[pair, wide, wide, square, square]
        + [lead_spec(STATE, width)] * (1 + len(far)),
        out_specs=pair,
    )(proj, xd, yd, mix, mixt, near, *far)


def output_kernel(
    ahead, first, skip_ref, x_ref, cum_ref, cumt_ref, proj_ref, near_ref, *refs
):
    (*far_refs, out_ref, start_ref) = refs
    far_refs = [ref for ref in far_refs if ref.shape[1:] == near_ref.shape[1:]]

    def put(start, _):
        start_ref[...] = added(start)

    either(ahead, [near_ref], far_refs, put)

    heads = cum_ref.shape[2]
    half = SPAN // 2
    wide = x_ref.shape[1] // heads * 2
    write = proj_ref[:, :STATE]
    read = proj_ref[:, STATE:]
    cum = cum_ref[0]
    cumt = cumt_ref[0]
    from_start = jnp.exp(cum)
    scores = dot_nt(read, write)
    top, low, end = scores[:half, :half], scores[half:, :half], scores[half:, half:]
    lane = lax.broadcasted_iota(jnp.int32, (half, wide), 1)
    for pair in range(heads // 2):
        a, b = 2 * pair, 2 * pair + 1
        cut = slice(pair * wide, (pair + 1) * wide)
        x = x_ref[:, cut]
        upper, lower = [], []
        for head in (a, b):
            decays = decays_of(cum[:, head : head + 1], cumt[head : head + 1, :])
            upper.append(dot((top * decays[0]).astype(BF16), x[:half]))
            lower.append(
                dot((low * decays[1]).astype(BF16), x[:half])
                + dot((end * decays[2]).astype(BF16), x[half:])
            )
        carried = dot(read, start_ref[:, cut]) * lanes_of(
            from_start[:, a : a + 1], from_start[:, b : b + 1], wide
        )
        head = (pl.program_id(0) + first) * heads + a
        gain = jnp.where(
            lax.broadcasted_iota(jnp.int32, (1, wide), 1) < wide // 2,
            skip_ref[head], skip_ref[head + 1],
        )
        rest = carried + gain * x.astype(F32)
        out_ref[:half, cut] = (
            jnp.where(lane < wide // 2, upper[0], upper[1]) + rest[:half]
        ).astype(BF16)
        out_ref[half:, cut] = (
            jnp.where(lane < wide // 2, lower[0], lower[1]) + rest[half:]
        ).astype(BF16)


def output(ahead, values, cum, cumt, skip, proj, near, far, first, earlier):
    groups, _, width = near.shape
    heads = cum.shape[2]
    wide = pl.BlockSpec((SPAN, width), lambda g: (0, g + first))
    lead = lead_spec(STATE, width)
    earlier = [] if earlier is None else [earlier]
    return call(
        functools.partial(output_kernel, ahead, first),
        jax.ShapeDtypeStruct(values.shape, BF16),
        flops=groups * heads * SPAN * SPAN * 2000,
        moved=groups * SPAN * width * 10,
        exps=groups * heads * SPAN * SPAN,
        grid=(groups,),
        in_specs=[
            pl.BlockSpec(memory_space=pltpu.SMEM), wide,
            pl.BlockSpec((1, SPAN, heads), lambda g: (g + first, 0, 0)),
            pl.BlockSpec((1, heads, SPAN), lambda g: (g + first, 0, 0)),
            pl.BlockSpec((SPAN, 2 * STATE), lambda g: (0, g)),
        ]
        + [lead] * (1 + len(far))
        + [pl.BlockSpec(memory_space=pl.ANY)] * len(earlier),
        out_specs=wide,
        scratch_shapes=[pltpu.VMEM((STATE, width), BF16)],
        input_output_aliases={6 + len(far): 0} if earlier else {},
    )(skip, values, cum, cumt, proj, near, *far, *earlier)


def spot_of(block, spots):
    if spots == 1:
        return 0
    other_x = (lax.axis_index("head") != block % 2).astype(jnp.int32)
    other_core = (lax.axis_index("sub") != block // 2).astype(jnp.int32)
    return 2 * other_x + other_core


def update_kernel(blocks, spots, part, *refs):
    turned_refs, pieces = refs[:spots], refs[spots : spots + blocks]
    decayed_ref, keep_ref = refs[spots + blocks : spots + blocks + 2]
    weight_ref, sparse_ref, grad_ref, weight_out, sparse_out, sems = refs[-6:]
    tokens, width = pieces[0].shape
    rows = decayed_ref.shape[0]
    step = min(rows, 256)
    columns = slice(part * width, (part + 1) * width)
    for block, piece in enumerate(pieces):
        start = pl.multiple_of(spot_of(block, spots) * tokens, tokens)
        grad_ref[pl.ds(start, tokens), :] = piece[...]
    copies = []
    for number in range(rows // step):
        here = slice(number * step, (number + 1) * step)
        total = dot(turned_refs[0][here, :], grad_ref[:tokens, :])
        for spot in range(1, spots):
            total += dot(
                turned_refs[spot][here, :], grad_ref[spot * tokens : (spot + 1) * tokens, :]
            )
        weight = decayed_ref[here, columns] - (LEARN_RATE * WEIGHT_SCALE) * total
        weight_out[here, :] = weight
        sparse_out[here, :] = (weight * keep_ref[here, columns].astype(F32)).astype(BF16)
        for place, (source, target) in enumerate(
            ((weight_out, weight_ref), (sparse_out, sparse_ref))
        ):
            copies.append(
                pltpu.make_async_copy(
                    source.at[here, :], target.at[here, columns], sems.at[place, number]
                )
            )
            copies[-1].start()
    for copy in copies:
        copy.wait()


def update(turned_hidden, grad_blocks, decayed, keep, part, earlier, vmem):
    rows, columns = decayed.shape
    width = grad_blocks[0].shape[1]
    tokens = turned_hidden[0].shape[1]
    spots, blocks = len(turned_hidden), len(grad_blocks)
    earlier = earlier or ()
    whole, anywhere = pl.BlockSpec(memory_space=pltpu.VMEM), pl.BlockSpec(memory_space=pl.ANY)
    return call(
        functools.partial(update_kernel, blocks, spots, part),
        (jax.ShapeDtypeStruct((rows, columns), F32), jax.ShapeDtypeStruct((rows, columns), BF16)),
        flops=2 * spots * tokens * rows * width,
        moved=rows * width * 12 + spots * tokens * (rows + width) * 2,
        vmem=vmem,
        in_specs=[whole] * (spots + blocks + 2) + [anywhere] * len(earlier),
        out_specs=(anywhere, anywhere),
        scratch_shapes=[
            pltpu.VMEM((spots * tokens, width), BF16),
            pltpu.VMEM((rows, width), F32),
            pltpu.VMEM((rows, width), BF16),
            pltpu.SemaphoreType.DMA((2, rows // min(rows, 256))),
        ],
        input_output_aliases={spots + blocks + 2 + i: i for i in range(len(earlier))},
    )(*turned_hidden, *grad_blocks, decayed, keep, *earlier)


def held(after, *before):
    return lax.optimization_barrier((after, *before))[0]


def to_all(seq, distance):
    return [(source, (source + distance) % seq) for source in range(seq)]


def block_pairs(seq, near, same_core):
    return [
        (
            (z * 2 + x) * 2 + core,
            ((z + (x if near else 1 - x) + 2 * core) % seq * 2 + x) * 2
            + (core if same_core else 1 - core),
        )
        for z in range(seq)
        for x in range(2)
        for core in range(2)
    ]


def transpose_pairs(seq):
    stays, crosses, beside, onward = [], [], [], []
    for z in range(seq):
        for x in range(2):
            for core in range(2):
                layer = 2 * x + core
                distance = (z - layer) % seq
                source, step = ((z * 2 + way) * 2 + core for way in (x, 1 - x))
                target = (layer * 2 + distance % 2) * 2 + distance // 2
                if distance % 2 == x:
                    stays.append((source, target))
                else:
                    crosses.append((source, target))
                    beside.append((source, step))
                    onward.append((step, target))
    return stays, crosses, beside, onward


SWAP = [(0, 1), (1, 0)]


def chain(own, own_low, decay, seq, step):
    arrived = jnp.zeros_like(own_low)
    message = own_low
    first = 0 if step > 0 else seq - 1
    for hop in range(seq - 1):
        source = first + hop * step
        if hop:
            message = handed_on(decay, arrived, own, 0)
        arrived = arrived + lax.ppermute(message, "seq", [(source, source + step)])
    return arrived


def on_device_general(
    seq, hidden, inner_values, log_decay, skip_gain, cotangent, master, mask_now, mask_next
):
    groups = master.shape[1] // (2 * STATE)
    effective, decayed, keep = weights(master, mask_now, mask_next)
    features = lax.all_gather(hidden, ("head", "sub"), axis=1, tiled=True)
    layer = lax.all_to_all(features, "seq", split_axis=1, concat_axis=0, tiled=True)
    xd, yd, mix, mixt, cum, cumt, decay = before(
        inner_values, cotangent, log_decay.T, groups
    )
    part = dot(layer, effective).astype(BF16)
    terms = [lax.psum_scatter(part, "seq", scatter_dimension=0, tiled=True)]
    proj, state_low, state, adjoint = states(True, terms, xd, yd, 0, groups, decay.shape[2])
    start = chain(state, state_low, decay, seq, 1)
    adjoint_in = chain(adjoint, adjoint.astype(BF16), decay, seq, -1)
    grad = grads(True, proj, xd, yd, mix, mixt, start, [adjoint_in], 0)
    blocks = [lax.all_gather(grad, "seq", axis=0, tiled=True)]
    ssd_output = output(
        True, inner_values, cum, cumt, skip_gain, proj, start, [adjoint_in], 0, None
    )
    return ssd_output, *update([layer.T], blocks, decayed, keep, 0, None, 40 * MIB)


def on_device(
    seq, hidden, inner_values, log_decay, skip_gain, cotangent, master, mask_now, mask_next
):
    groups = master.shape[1] // (2 * STATE)
    axes = ("seq", "head", "sub")
    rows = hidden.shape[0] // 2
    stays, crosses, beside, onward = transpose_pairs(seq)
    relayed = lax.ppermute(hidden[rows:], axes, beside)
    top = lax.ppermute(hidden[:rows], axes, stays + crosses)
    low = [lax.ppermute(hidden[rows:], axes, stays), lax.ppermute(relayed, axes, onward)]
    effective, decayed, keep = weights(master, mask_now, mask_next)
    sibling_effective = effective_of(
        lax.ppermute(held(master, relayed), "sub", SWAP),
        lax.ppermute(held(mask_now, relayed), "sub", SWAP),
    )
    top = held(top, effective, sibling_effective)

    other = [lax.ppermute(top, "head", SWAP)]
    same, cross, low = partials([top, *low], effective, sibling_effective, True)
    other.append(lax.ppermute(low, "head", SWAP))
    terms = [
        lax.ppermute(same, axes, block_pairs(seq, True, True)),
        lax.ppermute(cross, axes, block_pairs(seq, True, False)),
    ]
    ready = partials(other[:1], effective, sibling_effective)
    same, cross = rest_of_partials(ready, other[1], effective, sibling_effective)
    terms += [
        lax.ppermute(same, axes, block_pairs(seq, False, True)),
        lax.ppermute(cross, axes, block_pairs(seq, False, False)),
    ]

    xd, yd, mix, mixt, cum, cumt, decay = before(
        held(inner_values, same), cotangent, log_decay.T, groups
    )

    each = groups // PARTS
    spans = range(PARTS)
    projs, messages, nears, fars = zip(
        *(
            states(None, terms, xd, yd, p * each, each, decay.shape[2])
            for p in spans
        )
    )
    turned_hidden = []
    for first, second in ((top, low), other):
        piece = turn([held(first, nears[0]), second])
        turned_hidden += [piece, lax.ppermute(piece, "sub", SWAP)]
    fars = [*fars[:-1], held(fars[-1], *turned_hidden)]
    arrived = [[] for _ in spans]
    hops = (([(0, 1), (3, 2)], nears), ([(1, 2), (2, 1)], fars), ([(1, 0), (2, 3)], None))
    messages = list(messages)
    for pairs, own_terms in hops:
        for p in spans:
            message = messages[p]
            if p and not arrived[p]:
                message = held(message, arrived[p - 1][-1])
            arrived[p].append(lax.ppermute(message, "seq", pairs))
        for p in spans:
            if own_terms:
                messages[p] = handed_on(decay, arrived[p][-1], own_terms[p], p * each)
    gradients, moved, ssd_output = [], [], None
    for p in spans:
        near, far = arrived[p][0], arrived[p][1:]
        proj = projs[p] if not p else held(projs[p], ssd_output)
        grad = grads(None, proj, xd, yd, mix, mixt, near, far, p * each)
        ssd_output = output(
            None, inner_values, held(cum, grad), cumt, skip_gain, projs[p], near, far, p * each,
            ssd_output,
        )
        blocks = [grad]
        for distance in range(1, seq):
            payload = grad
            if not p and distance != seq // 2:
                payload = held(grad, ssd_output)
            blocks.append(lax.ppermute(payload, "seq", to_all(seq, seq - distance)))
        moved.append(blocks)
    decayed = held(decayed, ssd_output)
    updated = None
    for p in spans:
        updated = update(turned_hidden, moved[p], decayed, keep, p, updated, 16 * MIB)
    return ssd_output, *updated


PARTS = 2


def solution(mesh):
    by_position = P(("grp", "seq"), ("head", "sub"))
    by_row = P("seq", ("head", "sub"))
    seq, head, sub = (mesh.shape[name] for name in ("seq", "head", "sub"))
    body = on_device if (seq, head, sub) == (4, 2, 2) else on_device_general
    return jax.shard_map(
        functools.partial(body, seq),
        mesh=mesh,
        in_specs=(
            by_position, by_position, by_position, P(("head", "sub")), by_position,
            by_row, by_row, by_row,
        ),
        out_specs=(by_position, by_position, by_position),
        check_vma=False,
    )
```
